32 devices in a mesh: dp: 16 (over z, x, core), shard: 2 (over y).
Axes of the slice: x: 2, y: 2, z: 4, core: 2. Of those that a mesh axis runs over, the one named last changes fastest.
Arguments:
- tokens: bfloat16 [32, 128, 576], P(('dp', 'shard')), may hold values from -6 to 6
- segments: int32 [32, 128], P(('dp', 'shard')), may hold values from 0 to 1, never falling along the last dimension, each value on 1 to 96 neighbouring positions
- cotangent: bfloat16 [32, 128, 576], P(('dp', 'shard')), may hold values from -6 to 6
- w_qkv: float32 [576, 960], P('shard'), may hold values from -0.25 to 0.25
- w_out: float32 [576, 576], P('shard'), may hold values from -1 to 1
- w_gate_up: float32 [576, 3072], P('shard'), may hold values from -0.25 to 0.25
- w_down: float32 [1536, 576], P('shard'), may hold values from -0.15625 to 0.15625
- norm_gains: float32 [2, 576], P(None, 'shard'), may hold values from 0.5 to 1.5
- first_qkv: float32 [576, 960], P('shard'), may hold values from -12 to 12
- first_out: float32 [576, 576], P('shard'), may hold values from -8 to 8
- first_gate_up: float32 [576, 3072], P('shard'), may hold values from -16 to 16
- first_down: float32 [1536, 576], P('shard'), may hold values from -24 to 24
- first_gains: float32 [2, 576], P(None, 'shard'), may hold values from -32 to 32
- second_qkv: float32 [576, 960], P('shard'), may hold values from 18.432 to 73.728
- second_out: float32 [576, 576], P('shard'), may hold values from 8.192 to 32.768
- second_gate_up: float32 [576, 3072], P('shard'), may hold values from 32.768 to 131.072
- second_down: float32 [1536, 576], P('shard'), may hold values from 73.728 to 294.912
- second_gains: float32 [2, 576], P(None, 'shard'), may hold values from 102.4 to 409.6
Outputs:
- output: bfloat16 [32, 128, 576], P(('dp', 'shard'))
- token_grad: bfloat16 [32, 128, 576], P(('dp', 'shard'))
- new_first_qkv: float32 [576, 960], P('shard')
- new_first_out: float32 [576, 576], P('shard')
- new_first_gate_up: float32 [576, 3072], P('shard')
- new_first_down: float32 [1536, 576], P('shard')
- new_first_gains: float32 [2, 576], P(None, 'shard')
- new_second_qkv: float32 [576, 960], P('shard')
- new_second_out: float32 [576, 576], P('shard')
- new_second_gate_up: float32 [576, 3072], P('shard')
- new_second_down: float32 [1536, 576], P('shard')
- new_second_gains: float32 [2, 576], P(None, 'shard')
- new_qkv: float32 [576, 960], P('shard')
- new_out: float32 [576, 576], P('shard')
- new_gate_up: float32 [576, 3072], P('shard')
- new_down: float32 [1536, 576], P('shard')
- new_gains: float32 [2, 576], P(None, 'shard')
The draws below stay inside these ranges and needn't reach their ends.
Inputs may be any that keep to these rules, and one draw needn't show every extreme that they name: `segments`: within each sequence segment numbers start at 0, never fall and rise by at most one from token to token; each document has at most 96 tokens.
All inputs are finite; a program needn't handle non-finite values.
Results may differ from the reference program's by a relative error of at most 0.012.
The reference program's roundings to bfloat16 on the way count: a program that leaves them out, or rounds other values in their place, can miss the bound.
Values may be sent and summed in bfloat16 or wider, within the bound.
No kernel may reach another device: no remote copies, remote signals or barrier semaphores. Data moves between devices by JAX's collectives and lax.ppermute only.
A program may use at most 192 MiB of HBM per device.

```python
import math
import jax
import jax.numpy as jnp
import numpy as np
from jax import lax

D = 576
HEADS = 9
KV_HEADS = 3
HEAD = 64
FF = 1536
SEQ = 128
STEP = 10
SEQS = 32
TOKENS = 4096
QKV = 960


def block_scale(rng, dims, shards, smallest, top_value):
    def one(axis_at, shards_of):
        draws = jax.random.uniform(jax.random.fold_in(jax.random.fold_in(rng, 6), axis_at), (shards_of,), jnp.float32, smallest / len(shards), top_value / len(shards))
        return jnp.repeat(jnp.exp(draws), dims[axis_at] // shards_of).reshape((-1,) + (1,) * (len(dims) - axis_at - 1))

    loudness = one(*shards[0])
    for cut in shards[1:]:
        loudness = loudness * one(*cut)
    return loudness


def length_profile(amount, total, reach, lean):
    portions = [(1 << 20) // math.isqrt(grade ** lean) + 1 for grade in range(2, amount + 1)]
    spare, counts = total - reach - (amount - 1), [1] * (amount - 1)
    while spare > 0:
        movable = [i for i in range(amount - 1) if counts[i] < reach]
        mass, budget = sum([portions[i] for i in movable]), spare
        for i in movable:
            addition = min(reach - counts[i], max(1, budget * portions[i] // mass), spare)
            counts[i] = counts[i] + addition
            spare = spare - addition
    return np.array([reach] + counts)


def uneven_parts(rng, count, total, reach, skew):
    if count == 2:
        one = jax.random.randint(rng, (), max(1, total - reach), min(reach, total - 1) + 1)
        return jnp.stack([one, total - one])
    sizes = jnp.asarray(length_profile(count, total, reach, skew), jnp.int32)
    couples = (count - 1) // 2
    source_of, sink = sizes[1:1 + 2 * couples:2], sizes[2:2 + 2 * couples:2]
    room = jnp.minimum(source_of - 1, reach - sink)
    passed = jax.random.randint(jax.random.fold_in(rng, 1), (couples,), 0, 1 << 20) % (room + 1)
    sizes = sizes.at[1:1 + 2 * couples:2].set(source_of - passed).at[2:2 + 2 * couples:2].set(sink + passed)
    return sizes[jax.random.permutation(jax.random.fold_in(rng, 2), count)]


def noise(key, extent, deviation, bound, split=(), kind=jnp.bfloat16):
    values = jax.random.normal(key, extent, jnp.float32) * deviation
    if len(split) > 0:
        values = block_scale(key, extent, split, -0.22, 0.18) * values
    return jnp.clip(values, min=-bound, max=bound).astype(kind)


def setup_inputs(seed: int = 0) -> dict:
    key_of = jax.random.split(jax.random.key(seed), 19)
    tokens = noise(key_of[0], (SEQS, SEQ, D), 1.0, 6.0, ((0, 32),))
    segments = jax.vmap(lambda own: jnp.searchsorted(jnp.cumsum(uneven_parts(own, max(2, SEQ // 64), SEQ, SEQ // 2 + SEQ // 4, 0)), jnp.arange(SEQ), side="right"))(jax.random.split(key_of[1], SEQS)).reshape((SEQS, SEQ)).astype(jnp.int32)
    cotangent = noise(key_of[2], (SEQS, SEQ, D), 1.0, 6.0, ((0, 32),))
    w_qkv = noise(key_of[3], (D, QKV), D ** -0.5, 0.25, ((0, 2),), jnp.float32)
    w_out = noise(key_of[4], (D, D), (max(1, D // 16)) ** -0.5, 1.0, ((0, 2),), jnp.float32)
    w_gate_up = noise(key_of[5], (D, 2 * FF), D ** -0.5, 0.25, ((0, 2),), jnp.float32)
    w_down = noise(key_of[6], (FF, D), FF ** -0.5, 0.15625, ((0, 2),), jnp.float32)
    norm_gains = jnp.clip(1.0 + 0.1 * jax.random.normal(key_of[7], (2, D), jnp.float32), 0.5, 1.5)
    first_qkv = noise(key_of[8], (D, QKV), (0.033 * TOKENS ** 0.5), 12.0, ((0, 2),), jnp.float32)
    first_out = noise(key_of[9], (D, D), (0.022 * TOKENS ** 0.5), 8.0, ((0, 2),), jnp.float32)
    first_gate_up = noise(key_of[10], (D, 2 * FF), (0.044 * TOKENS ** 0.5), 16.0, ((0, 2),), jnp.float32)
    first_down = noise(key_of[11], (FF, D), (0.066 * TOKENS ** 0.5), 24.0, ((0, 2),), jnp.float32)
    first_gains = noise(key_of[12], (2, D), (0.077 * TOKENS ** 0.5), 32.0, ((1, 2),), jnp.float32)
    second_qkv = jnp.clip(jnp.exp(math.log(73.728) - 1.3862944 * jax.random.uniform(key_of[13], (D, QKV), jnp.float32) ** block_scale(key_of[13], (D, QKV), ((0, 2),), -0.2, 0.2)), 18.432, 73.728)
    second_out = jnp.clip(jnp.exp(math.log(32.768) - 1.3862944 * jax.random.uniform(key_of[14], (D, D), jnp.float32) ** block_scale(key_of[14], (D, D), ((0, 2),), -0.2, 0.2)), 8.192, 32.768)
    second_gate_up = jnp.clip(jnp.exp(math.log(131.072) - 1.3862944 * jax.random.uniform(key_of[15], (D, 2 * FF), jnp.float32) ** block_scale(key_of[15], (D, 2 * FF), ((0, 2),), -0.2, 0.2)), 32.768, 131.072)
    second_down = jnp.clip(jnp.exp(math.log(294.912) - 1.3862944 * jax.random.uniform(key_of[16], (FF, D), jnp.float32) ** block_scale(key_of[16], (FF, D), ((0, 2),), -0.2, 0.2)), 73.728, 294.912)
    second_gains = jnp.clip(jnp.exp(math.log(409.6) - 1.3862944 * jax.random.uniform(key_of[17], (2, D), jnp.float32) ** block_scale(key_of[17], (2, D), ((1, 2),), -0.2, 0.2)), 102.4, 409.6)
    return dict(tokens=tokens, segments=segments, cotangent=cotangent, w_qkv=w_qkv, w_out=w_out, w_gate_up=w_gate_up, w_down=w_down, norm_gains=norm_gains, first_qkv=first_qkv, first_out=first_out, first_gate_up=first_gate_up, first_down=first_down, first_gains=first_gains, second_qkv=second_qkv, second_out=second_out, second_gate_up=second_gate_up, second_down=second_down, second_gains=second_gains)


EPS_NORM = 1e-05
ROPE_BASE = 100000.0
BETA_ONE = 0.9
BETA_TWO = 0.95
RATE_MATRIX = 0.1
RATE_GAIN = 0.3
DECAY_MATRIX = 0.1
EPS_ADAM = 1e-08
MASKED = -1e+30
HIGHEST = lax.Precision.HIGHEST

@jax.custom_vjp
def low(v):
    return lax.optimization_barrier(v.astype(jnp.bfloat16)).astype(jnp.float32)

@jax.custom_vjp
def low_back(v):
    return v

def low_keep(v):
    return (low(v), None)

def low_pass(kept, grad):
    return (grad,)

def back_keep(v):
    return (v, None)

def back_low(kept, grad):
    return (low(grad),)
low.defvjp(low_keep, low_pass)
low_back.defvjp(back_keep, back_low)

def doc_positions(segments):
    seq_length = segments.shape[-1]
    token_index = jnp.arange(seq_length, dtype=jnp.int32)
    earlier = jnp.concatenate([segments[..., :1] - 1, segments[..., :-1]], axis=-1)
    starts = jnp.where(segments != earlier, token_index, jnp.zeros_like(token_index))
    return token_index - lax.cummax(starts, axis=segments.ndim - 1)

def rope_tables(segments):
    positions = doc_positions(segments).astype(jnp.float32)
    half_size = HEAD // 2
    frequency = ROPE_BASE ** (-(jnp.arange(half_size, dtype=jnp.float32) * 2.0 / HEAD))
    angles = positions[..., None] * frequency
    return (jnp.cos(angles), jnp.sin(angles))

def rotate(values, cosine, sine_table):
    half_size = values.shape[-1] // 2
    first_half = values[..., :half_size]
    second_half = values[..., half_size:]
    return jnp.concatenate([first_half * cosine - second_half * sine_table, second_half * cosine + first_half * sine_table], axis=-1)

def layer(token_values, mat_qkv, mat_out, mat_gate_up, mat_down, gain_pair, cosine, sine_table, allowed):
    seq_count, seq_length, model_width = token_values.shape
    group_size = HEADS // KV_HEADS
    scale_score = float(HEAD) ** (-0.5)
    scale_one = lax.rsqrt(lax.optimization_barrier(jnp.mean(token_values * token_values, axis=-1, keepdims=True)) + EPS_NORM)
    normed_one = low(token_values * scale_one * gain_pair[0])
    projected = low_back(jnp.einsum('bld,de->ble', normed_one, mat_qkv, precision=HIGHEST))
    query_part = projected[..., :HEADS * HEAD].reshape(seq_count, seq_length, KV_HEADS, group_size, HEAD)
    key_part = projected[..., HEADS * HEAD:(HEADS + KV_HEADS) * HEAD].reshape(seq_count, seq_length, KV_HEADS, HEAD)
    value_part = projected[..., (HEADS + KV_HEADS) * HEAD:].reshape(seq_count, seq_length, KV_HEADS, HEAD)
    query_low = low(rotate(query_part, cosine[:, :, None, None], sine_table[:, :, None, None]))
    key_low = low(rotate(key_part, cosine[:, :, None], sine_table[:, :, None]))
    value_low = low(value_part)
    scores = low_back(jnp.einsum('blhrc,bmhc->bhrlm', query_low, key_low, precision=HIGHEST) * scale_score)
    scores = jnp.where(allowed[:, None, None], scores, MASKED)
    row_top = lax.optimization_barrier(jnp.max(scores, axis=-1, keepdims=True))
    exponent = jnp.exp(scores - row_top)
    attn_probs = low(exponent / lax.optimization_barrier(jnp.sum(exponent, axis=-1, keepdims=True)))
    attended = jnp.einsum('bhrlm,bmhc->blhrc', attn_probs, value_low, precision=HIGHEST).reshape(seq_count, seq_length, HEADS * HEAD)
    attended = low(low_back(attended))
    branch = low_back(jnp.einsum('blk,kd->bld', attended, mat_out, precision=HIGHEST))
    middle = token_values + branch
    scale_two = lax.rsqrt(lax.optimization_barrier(jnp.mean(middle * middle, axis=-1, keepdims=True)) + EPS_NORM)
    normed_two = low(middle * scale_two * gain_pair[1])
    gate_up_out = low_back(jnp.einsum('bld,de->ble', normed_two, mat_gate_up, precision=HIGHEST))
    gate_part = gate_up_out[..., :FF]
    up_part = gate_up_out[..., FF:]
    hidden_low = low(gate_part * jax.nn.sigmoid(gate_part) * up_part)
    result = low_back(jnp.einsum('blf,fd->bld', hidden_low, mat_down, precision=HIGHEST))
    return middle + result

def adamw(weight, first_moment, second_moment, gradient, step_rate, weight_decay):
    first_new = BETA_ONE * first_moment + (1.0 - BETA_ONE) * gradient
    second_new = BETA_TWO * second_moment + (1.0 - BETA_TWO) * gradient * gradient
    fix_one = 1.0 - BETA_ONE ** STEP
    fix_two = 1.0 - BETA_TWO ** STEP
    update = first_new / fix_one / (jnp.sqrt(second_new / fix_two) + EPS_ADAM)
    return (first_new, second_new, weight - step_rate * (update + weight_decay * weight))

def reference(tokens, segments, cotangent, w_qkv, w_out, w_gate_up, w_down, norm_gains, first_qkv, first_out, first_gate_up, first_down, first_gains, second_qkv, second_out, second_gate_up, second_down, second_gains):
    masters = (w_qkv, w_out, w_gate_up, w_down, norm_gains)
    low_qkv, low_out, low_gate_up, low_down, low_gains = tuple((low(weight) for weight in masters))
    group_size = max(1, min(SEQS, 4096 // SEQ))
    block_count = SEQS // group_size
    token_blocks = tokens.astype(jnp.float32).reshape(block_count, group_size, SEQ, D)
    cot_blocks = cotangent.astype(jnp.float32).reshape(block_count, group_size, SEQ, D)
    segment_blocks = segments.reshape(block_count, group_size, SEQ)
    token_index = jnp.arange(SEQ, dtype=jnp.int32)
    causal = token_index[:, None] >= token_index[None, :]

    def step_block(totals, block_data):
        block_tokens, block_segments, block_cot = block_data
        cosine, sine_table = rope_tables(block_segments)
        allowed = (block_segments[:, :, None] == block_segments[:, None, :]) & causal

        def forward(values, mat_qkv, mat_out, mat_gate_up, mat_down, gain_pair):
            return layer(values, mat_qkv, mat_out, mat_gate_up, mat_down, gain_pair, cosine, sine_table, allowed)
        outputs, pull_back = jax.vjp(forward, block_tokens, low_qkv, low_out, low_gate_up, low_down, low_gains)
        grad_values = pull_back(block_cot)
        totals = tuple((total_grad + part_grad for total_grad, part_grad in zip(totals, grad_values[1:])))
        return (totals, (outputs.astype(jnp.bfloat16), grad_values[0].astype(jnp.bfloat16)))
    zero_grads = tuple((jnp.zeros(weight.shape, jnp.float32) for weight in masters))
    totals, (outputs, token_grads) = lax.scan(step_block, zero_grads, (token_blocks, segment_blocks, cot_blocks))
    grad_qkv, grad_out, grad_gate_up, grad_down, grad_gains = totals
    one_qkv, two_qkv, next_qkv = adamw(w_qkv, first_qkv, second_qkv, grad_qkv, RATE_MATRIX, DECAY_MATRIX)
    one_out, two_out, next_out = adamw(w_out, first_out, second_out, grad_out, RATE_MATRIX, DECAY_MATRIX)
    one_gate_up, two_gate_up, next_gate_up = adamw(w_gate_up, first_gate_up, second_gate_up, grad_gate_up, RATE_MATRIX, DECAY_MATRIX)
    one_down, two_down, next_down = adamw(w_down, first_down, second_down, grad_down, RATE_MATRIX, DECAY_MATRIX)
    one_gains, two_gains, next_gains = adamw(norm_gains, first_gains, second_gains, grad_gains, RATE_GAIN, 0.0)
    return (outputs.reshape(SEQS, SEQ, D), token_grads.reshape(SEQS, SEQ, D), one_qkv, one_out, one_gate_up, one_down, one_gains, two_qkv, two_out, two_gate_up, two_down, two_gains, next_qkv, next_out, next_gate_up, next_down, next_gains)
```

```python
import functools

import jax
import jax.numpy as jnp
from jax import lax
from jax.experimental import pallas as pl
from jax.experimental.pallas import tpu as pltpu
from jax.sharding import PartitionSpec as P

HEADS = 9
KV_HEADS = 3
GROUP = HEADS // KV_HEADS
HEAD = 64
FF = 1536
STEP = 10
QUERY = HEADS * HEAD
ROPED = (HEADS + KV_HEADS) * HEAD
QKV = (HEADS + 2 * KV_HEADS) * HEAD
LANES = 128

EPS_NORM = 1e-05
ROPE_BASE = 100000.0
BETA_ONE = 0.9
BETA_TWO = 0.95
RATE_MATRIX = 0.1
RATE_GAIN = 0.3
DECAY_MATRIX = 0.1
EPS_ADAM = 1e-08
MASKED = -1e30
SCALE = float(HEAD) ** (-0.5)
VMEM_LIMIT = 56 * 1024 * 1024
F32 = jnp.float32
BF16 = jnp.bfloat16


def doc_positions(segments):
    seq_length = segments.shape[-1]
    token_index = jnp.arange(seq_length, dtype=jnp.int32)
    earlier = jnp.concatenate([segments[..., :1] - 1, segments[..., :-1]], axis=-1)
    starts = jnp.where(segments != earlier, token_index, jnp.zeros_like(token_index))
    return token_index - lax.cummax(starts, axis=segments.ndim - 1)


def rope_tables(segments):
    positions = doc_positions(segments).astype(F32)
    half_size = HEAD // 2
    frequency = ROPE_BASE ** (-(jnp.arange(half_size, dtype=F32) * 2.0 / HEAD))
    angles = positions[:, None] * frequency
    cosine, sine = jnp.cos(angles), jnp.sin(angles)
    return (
        jnp.concatenate([cosine] * 4, axis=-1),
        jnp.concatenate([-sine, sine, -sine, sine], axis=-1),
    )


def rotate_block(values, cosine, signed_sine):
    lane = lax.broadcasted_iota(jnp.int32, values.shape, 1)
    swapped = jnp.where(
        lane % HEAD < HEAD // 2,
        pltpu.roll(values, LANES - HEAD // 2, 1),
        pltpu.roll(values, HEAD // 2, 1),
    )
    return values * cosine + swapped * signed_sine


def adamw(weight, first_moment, second_moment, gradient, step_rate, weight_decay):
    first_new = BETA_ONE * first_moment + (1.0 - BETA_ONE) * gradient
    second_new = BETA_TWO * second_moment + (1.0 - BETA_TWO) * gradient * gradient
    fix_one = 1.0 - BETA_ONE**STEP
    fix_two = 1.0 - BETA_TWO**STEP
    update = first_new / fix_one / (jnp.sqrt(second_new / fix_two) + EPS_ADAM)
    return (first_new, second_new, weight - step_rate * (update + weight_decay * weight))


def dot(left, right):
    return lax.dot_general(left, right, (((1,), (0,)), ((), ())), preferred_element_type=F32)


def dot_right_t(left, right):
    return lax.dot_general(left, right, (((1,), (1,)), ((), ())), preferred_element_type=F32)


def dot_left_t(left, right):
    return lax.dot_general(left, right, (((0,), (0,)), ((), ())), preferred_element_type=F32)


def norm_scale(values):
    return lax.rsqrt(jnp.mean(values * values, axis=-1, keepdims=True) + EPS_NORM)


def norm_back(grad_normed, normed, scale_rows):
    return scale_rows * (
        grad_normed - normed * jnp.mean(grad_normed * normed, axis=-1, keepdims=True)
    )


class Weight:
    def __init__(self, shape, whole=None, own=None, parts=(), rels=(), place=None):
        self.shape, self.place, self.rels = shape, place, rels
        self.arrays = [whole] if whole is not None else [own, *parts]
        self.split = whole is None

    def scratch(self):
        return [pltpu.VMEM(self.shape, BF16)] if self.split else []

    def load(self, idx, refs, scratch):
        if not self.split:
            return refs[0]
        full, own, parts = scratch[0], refs[0], refs[1:]
        rows = own.shape[0]
        full[pl.ds(pl.multiple_of(idx[0] * rows, 16), rows), :] = own[...].astype(BF16)
        base = (1 - idx[0]) * rows
        for part, (core, x) in zip(parts, self.rels):
            row, col = self.place(idx[1] ^ core, idx[2] ^ x)
            height, width = part.shape
            row = pl.multiple_of(base + row, 16)
            if width == self.shape[1]:
                full[pl.ds(row, height), :] = part[...]
            else:
                full[pl.ds(row, height), pl.ds(pl.multiple_of(col, LANES), width)] = part[...]
        return full


def call(body, idx, arrays, weights, outs, scratch, flops, name):
    counts = [len(w.arrays) for w in weights]
    flat = list(arrays) + [a for w in weights for a in w.arrays]
    weight_scratch = [w.scratch() for w in weights]

    def kernel(*refs):
        refs = list(refs)
        idx_ref = refs.pop(0)
        take = lambda n: [refs.pop(0) for _ in range(n)]
        array_refs = take(len(arrays))
        weight_refs = [take(n) for n in counts]
        out_refs = take(len(outs))
        own_scratch = take(len(scratch))
        scratch_refs = [take(len(s)) for s in weight_scratch]
        loads = [
            functools.partial(w.load, idx_ref, r, s)
            for w, r, s in zip(weights, weight_refs, scratch_refs)
        ]
        body(idx_ref, array_refs, loads, out_refs, own_scratch)

    moved = sum(a.size * a.dtype.itemsize for a in flat)
    moved += sum(o.size * o.dtype.itemsize for o in outs)
    return pl.pallas_call(
        kernel,
        out_shape=tuple(outs),
        in_specs=[pl.BlockSpec(memory_space=pltpu.SMEM)]
        + [pl.BlockSpec(memory_space=pltpu.VMEM)] * len(flat),
        out_specs=tuple([pl.BlockSpec(memory_space=pltpu.VMEM)] * len(outs)),
        scratch_shapes=list(scratch) + [s for group in weight_scratch for s in group],
        compiler_params=pltpu.CompilerParams(vmem_limit_bytes=VMEM_LIMIT),
        cost_estimate=pl.CostEstimate(flops=flops, bytes_accessed=moved, transcendentals=0),
        name=name,
    )(idx, *flat)


def sds(shape, dtype):
    return jax.ShapeDtypeStruct(shape, dtype)


class Pieces:
    def __init__(self, rows, height, width, place):
        self.rows, self.height, self.width, self.place = rows, height, width, place

    def outs(self):
        return [sds((2, 8, self.height, self.width), BF16)] * 2

    def emit(self, idx, full, outs):
        for other_core, out in enumerate((outs[1], outs[0])):
            for owner in range(2):
                for slot in range(8):
                    row, col = self.place(
                        idx[1] ^ other_core, idx[2] ^ (slot >> 2), idx[3] ^ (slot & 3)
                    )
                    row = pl.multiple_of((idx[0] ^ owner) * self.rows + row, 8)
                    rows = pl.ds(row, self.height)
                    if self.width == full.shape[1]:
                        piece = full[rows, :]
                    else:
                        piece = full[rows, pl.ds(pl.multiple_of(col, LANES), self.width)]
                    out[owner, slot] = piece.astype(BF16)


def attention_mask(segment_column, segment_row):
    seq_length = segment_column.shape[0]
    shape = (seq_length, seq_length)
    token = lax.broadcasted_iota(jnp.int32, shape, 0)
    seen = lax.broadcasted_iota(jnp.int32, shape, 1)
    allowed = (segment_column == segment_row) & (token >= seen)
    return jnp.concatenate([allowed] * GROUP, axis=0)


def head_stack(values, kv_head):
    first = kv_head * GROUP
    return jnp.concatenate(
        [values[:, (first + i) * HEAD : (first + i + 1) * HEAD] for i in range(GROUP)], axis=0
    )


def softmax_rows(query, key, allowed):
    scores = jnp.where(allowed, dot_right_t(query, key) * SCALE, MASKED)
    top = jnp.max(scores, axis=-1, keepdims=True)
    exponent = jnp.exp(scores - top)
    return exponent / jnp.sum(exponent, axis=-1, keepdims=True)


def attention_forward(idx, tokens, tables, segs, gains, w_qkv):
    seq_length, width = tokens.shape

    def body(idx_ref, arrays, loads, outs, scratch):
        x_ref, cos_ref, sin_ref, col_ref, row_ref, gains_ref = arrays
        qkv_ref, o_ref = outs
        x = x_ref[...].astype(F32)
        h1 = (x * norm_scale(x) * gains_ref[0:1, :]).astype(BF16)
        projected = dot(h1, loads[0]()[...])
        for start in range(0, ROPED, LANES):
            block = projected[:, start : start + LANES]
            qkv_ref[:, start : start + LANES] = rotate_block(
                block, cos_ref[...], sin_ref[...]
            ).astype(BF16)
        qkv_ref[:, ROPED:QKV] = projected[:, ROPED:QKV].astype(BF16)
        allowed = attention_mask(col_ref[...], row_ref[...])
        qkv = qkv_ref[...]
        for kv in range(KV_HEADS):
            key = qkv[:, QUERY + kv * HEAD : QUERY + (kv + 1) * HEAD]
            value = qkv[:, ROPED + kv * HEAD : ROPED + (kv + 1) * HEAD]
            probs = softmax_rows(head_stack(qkv, kv), key, allowed).astype(BF16)
            attended = dot(probs, value).astype(BF16)
            for i in range(GROUP):
                start = (kv * GROUP + i) * HEAD
                o_ref[:, start : start + HEAD] = attended[i * seq_length : (i + 1) * seq_length]

    outs = [sds((seq_length, QKV), BF16), sds((seq_length, QUERY), BF16)]
    return call(
        body, idx, [tokens, *tables, *segs, gains], [w_qkv], outs, [], 2 * 128 * 576 * 960, "attention"
    )


def feed_forward(idx, tokens, attended, gains, cotangent, w_out, w_gate_up, pieces):
    seq_length, width = tokens.shape

    def body(idx_ref, arrays, loads, outs, scratch):
        x_ref, o_ref, gains_ref, y_ref = arrays
        u_ref, h2_ref, ab_ref, z_ref = outs[:4]
        u = x_ref[...].astype(F32) + dot(o_ref[...], loads[0]()[...])
        u_ref[...] = u
        h2 = (u * norm_scale(u) * gains_ref[1:2, :]).astype(BF16)
        h2_ref[...] = h2
        ab = dot(h2, loads[1]()[...])
        ab_ref[...] = ab
        gate, up = ab[:, :FF], ab[:, FF:]
        z = (gate * jax.nn.sigmoid(gate) * up).astype(BF16)
        z_ref[...] = z
        if pieces is None:
            outs[4][...] = dot_left_t(z, y_ref[...])
        else:
            scratch[0][...] = dot_left_t(z, y_ref[...]).astype(BF16)
            pieces.emit(idx_ref, scratch[0], outs[4:])

    outs = [
        sds((seq_length, width), F32),
        sds((seq_length, width), BF16),
        sds((seq_length, 2 * FF), F32),
        sds((seq_length, FF), BF16),
    ]
    outs += [sds((FF, width), F32)] if pieces is None else pieces.outs()
    scratch = [] if pieces is None else [pltpu.VMEM((FF, width), BF16)]
    return call(
        body,
        idx,
        [tokens, attended, gains, cotangent],
        [w_out, w_gate_up],
        outs,
        scratch,
        2 * 128 * 576 * 5200,
        "feed_forward",
    )


def feed_back(idx, ab, normed_low, cotangent, w_down, pieces):
    seq_length, width = cotangent.shape

    def body(idx_ref, arrays, loads, outs, scratch):
        ab_ref, h2_ref, y_ref = arrays
        gg_ref = outs[0]
        gate, up = ab_ref[:, :FF], ab_ref[:, FF:]
        sig = jax.nn.sigmoid(gate)
        grad_hidden = dot_right_t(y_ref[...], loads[0]()[...])
        gg_ref[:, :FF] = (grad_hidden * up * sig * (1.0 + gate * (1.0 - sig))).astype(BF16)
        gg_ref[:, FF:] = (grad_hidden * gate * sig).astype(BF16)
        grad = dot_left_t(h2_ref[...], gg_ref[...])
        if pieces is None:
            outs[1][...] = grad
        else:
            scratch[0][...] = grad.astype(BF16)
            pieces.emit(idx_ref, scratch[0], outs[1:])

    outs = [sds((seq_length, 2 * FF), BF16)]
    outs += [sds((width, 2 * FF), F32)] if pieces is None else pieces.outs()
    scratch = [] if pieces is None else [pltpu.VMEM((width, 2 * FF), BF16)]
    return call(
        body, idx, [ab, normed_low, cotangent], [w_down], outs, scratch, 2 * 128 * 576 * 4700, "feed_back"
    )


def attention_back(
    idx, tokens, cotangent, middle, gated, qkv, attended, tables, segs, gains, w_gate_up, w_out, pieces
):
    seq_length, width = tokens.shape

    def body(idx_ref, arrays, loads, outs, scratch):
        x_ref, y_ref, u_ref, gg_ref, qkv_ref, o_ref = arrays[:6]
        cos_ref, sin_ref, col_ref, row_ref, gains_ref = arrays[6:]
        gu_ref, gp_ref, gain_ref = outs[:3]
        full, grad_proj = scratch
        u = u_ref[...]
        scale_two = norm_scale(u)
        normed = u * scale_two
        grad_normed = dot_right_t(gg_ref[...], loads[0]()[...])
        gain_ref[...] = jnp.sum(grad_normed * normed, axis=0, keepdims=True)
        gu = y_ref[...].astype(F32) + norm_back(
            grad_normed * gains_ref[1:2, :], normed, scale_two
        )
        gu_ref[...] = gu
        gu_low = gu.astype(BF16)
        go = dot_right_t(gu_low, loads[1]()[...]).astype(BF16)
        allowed = attention_mask(col_ref[...], row_ref[...])
        qkv_values = qkv_ref[...]
        for kv in range(KV_HEADS):
            key = qkv_values[:, QUERY + kv * HEAD : QUERY + (kv + 1) * HEAD]
            value = qkv_values[:, ROPED + kv * HEAD : ROPED + (kv + 1) * HEAD]
            query = head_stack(qkv_values, kv)
            grad_out = head_stack(go, kv)
            probs = softmax_rows(query, key, allowed)
            grad_probs = dot_right_t(grad_out, value)
            row_delta = jnp.sum(probs * grad_probs, axis=-1, keepdims=True)
            gs = (probs * (grad_probs - row_delta)).astype(BF16)
            grad_query = dot(gs, key) * SCALE
            for i in range(GROUP):
                start = (kv * GROUP + i) * HEAD
                grad_proj[:, start : start + HEAD] = grad_query[
                    i * seq_length : (i + 1) * seq_length
                ]
            start = QUERY + kv * HEAD
            grad_proj[:, start : start + HEAD] = dot_left_t(gs, query) * SCALE
            start = ROPED + kv * HEAD
            grad_proj[:, start : start + HEAD] = dot_left_t(probs.astype(BF16), grad_out)
        for start in range(0, ROPED, LANES):
            gp_ref[:, start : start + LANES] = rotate_block(
                grad_proj[:, start : start + LANES], cos_ref[...], -sin_ref[...]
            ).astype(BF16)
        gp_ref[:, ROPED:QKV] = grad_proj[:, ROPED:QKV].astype(BF16)
        x = x_ref[...].astype(F32)
        h1 = (x * norm_scale(x) * gains_ref[0:1, :]).astype(BF16)
        full[:, :QKV] = dot_left_t(h1, gp_ref[...])
        full[:, QKV:] = dot_left_t(o_ref[...], gu_low)
        if pieces is None:
            outs[3][...] = full[...]
        else:
            pieces.emit(idx_ref, full, outs[3:])

    outs = [sds((seq_length, width), F32), sds((seq_length, QKV), BF16), sds((1, width), F32)]
    outs += [sds((width, QKV + width), F32)] if pieces is None else pieces.outs()
    scratch = [pltpu.VMEM((width, QKV + width), F32), pltpu.VMEM((seq_length, QKV), F32)]
    return call(
        body,
        idx,
        [tokens, cotangent, middle, gated, qkv, attended, *tables, *segs, gains],
        [w_gate_up, w_out],
        outs,
        scratch,
        2 * 128 * 576 * 6500,
        "attention_back",
    )


def finish_tokens(idx, tokens, middle, hidden, grad_middle, grad_proj, gains, w_down, w_qkv):
    seq_length, width = tokens.shape

    def body(idx_ref, arrays, loads, outs, scratch):
        x_ref, u_ref, z_ref, gu_ref, gp_ref, gains_ref = arrays
        out_ref, grad_ref, gain_ref = outs
        out_ref[...] = (u_ref[...] + dot(z_ref[...], loads[0]()[...])).astype(BF16)
        x = x_ref[...].astype(F32)
        scale_one = norm_scale(x)
        normed = x * scale_one
        grad_normed = dot_right_t(gp_ref[...], loads[1]()[...])
        gain_ref[...] = jnp.sum(grad_normed * normed, axis=0, keepdims=True)
        grad_ref[...] = (
            gu_ref[...] + norm_back(grad_normed * gains_ref[0:1, :], normed, scale_one)
        ).astype(BF16)

    outs = [sds((seq_length, width), BF16), sds((seq_length, width), BF16), sds((1, width), F32)]
    return call(
        body,
        idx,
        [tokens, middle, hidden, grad_middle, grad_proj, gains],
        [w_down, w_qkv],
        outs,
        [],
        2 * 128 * 576 * 2500,
        "finish_tokens",
    )


def update_state(idx, parts, weights, firsts, seconds, blocks, assemble, name):
    count = len(weights)
    height, width = parts[0].shape[1:]
    full_shape, put = assemble

    def kernel(idx_ref, *refs):
        part_refs = refs[:4]
        w_refs = refs[4 : 4 + count]
        f_refs = refs[4 + count : 4 + 2 * count]
        s_refs = refs[4 + 2 * count : 4 + 3 * count]
        outs = refs[4 + 3 * count : 4 + 6 * count]
        full = refs[4 + 6 * count]
        rel = pl.program_id(0) ^ (idx_ref[1] * 2 + idx_ref[2])
        for k in range(4):

            @pl.when(rel == k)
            def _(k=k):
                for z in range(4):
                    put(full, z, part_refs[k][idx_ref[3] ^ z].astype(F32))

        start = 0
        for i in range(count):
            columns = w_refs[i].shape[1]
            first, second, new = adamw(
                w_refs[i][...],
                f_refs[i][...],
                s_refs[i][...],
                full[:, start : start + columns],
                RATE_MATRIX,
                DECAY_MATRIX,
            )
            start += columns
            outs[i][...] = first
            outs[count + i][...] = second
            outs[2 * count + i][...] = new

    state = [*weights, *firsts, *seconds]
    state_specs = [pl.BlockSpec(*blocks[i]) for i in range(count)] * 3
    moved = sum(a.size * 8 for a in state)
    return pl.pallas_call(
        kernel,
        grid_spec=pltpu.PrefetchScalarGridSpec(
            num_scalar_prefetch=1,
            grid=(4,),
            in_specs=[pl.BlockSpec((4, height, width), lambda t, _: (0, 0, 0))] * 4 + state_specs,
            out_specs=tuple(state_specs),
            scratch_shapes=[pltpu.VMEM(full_shape, F32)],
        ),
        out_shape=tuple(sds(a.shape, F32) for a in state),
        compiler_params=pltpu.CompilerParams(vmem_limit_bytes=VMEM_LIMIT),
        cost_estimate=pl.CostEstimate(flops=0, bytes_accessed=moved, transcendentals=0),
        name=name,
    )(idx, *parts, *state)


def swap(values, axis, mask):
    size = lax.axis_size(axis)
    return lax.ppermute(values, axis, [(i, i ^ mask) for i in range(size)])


def sum_and_share(send, keep):
    arrived = swap(send, "dp", 1)
    across = (keep[1].astype(F32) + arrived[1].astype(F32)).astype(BF16)
    arrived_across = swap(across, "shard", 1)
    total = keep[0].astype(F32) + arrived[0].astype(F32) + arrived_across.astype(F32)
    arrived_x = swap(total[4:].astype(BF16), "dp", 2)
    total = total[:4] + arrived_x.astype(F32)
    arrived_z = [swap(total[m].astype(BF16), "dp", 4 * m) for m in (1, 2, 3)]
    piece = total[0] + sum(a.astype(F32) for a in arrived_z)
    piece = piece.astype(BF16)
    near = jnp.stack([piece] + [swap(piece, "dp", 4 * m) for m in (1, 2, 3)])
    near_x = swap(near, "dp", 2)
    return [near, near_x, swap(near, "dp", 1), swap(near_x, "dp", 1)]


def gather_two(own, place, shape, core):
    rows = own.shape[0] // 2
    mine = lax.dynamic_slice_in_dim(own, core * rows, rows, 0).astype(BF16)
    near = swap(mine, "shard", 1)
    far = swap(near, "dp", 1)
    return Weight(shape, own=own, parts=[near, far], rels=[(0, 0), (1, 0)], place=place)


def gather_four(own, mine, place, shape):
    near = swap(mine, "shard", 1)
    near_x = swap(near, "dp", 2)
    parts = [near, near_x, swap(near, "dp", 1), swap(near_x, "dp", 1)]
    rels = [(0, 0), (0, 1), (1, 0), (1, 1)]
    return Weight(shape, own=own, parts=parts, rels=rels, place=place)


def per_device(
    tokens,
    segments,
    cotangent,
    w_qkv,
    w_out,
    w_gate_up,
    w_down,
    norm_gains,
    first_qkv,
    first_out,
    first_gate_up,
    first_down,
    first_gains,
    second_qkv,
    second_out,
    second_gate_up,
    second_down,
    second_gains,
):
    groups = lax.axis_size("shard")
    replicas = lax.axis_size("dp")
    fast = groups == 2 and replicas == 16
    place_dp = lax.axis_index("dp")
    owner = lax.axis_index("shard")
    core, x_bit, z_bits = place_dp & 1, (place_dp >> 1) & 1, place_dp >> 2
    idx = jnp.stack([owner, core, x_bit, z_bits]).astype(jnp.int32)
    x, y = tokens[0], cotangent[0]
    width = x.shape[1]
    rows, down_rows = w_qkv.shape[0], w_down.shape[0]
    masters = (w_qkv, w_out, w_gate_up, w_down)
    shapes = [(m.shape[0] * groups, m.shape[1]) for m in masters]
    if fast:
        own_gains = norm_gains.astype(BF16)
        other_gains = swap(own_gains, "shard", 1)
        gains = jnp.where(
            owner == 0,
            jnp.concatenate([own_gains, other_gains], axis=1),
            jnp.concatenate([other_gains, own_gains], axis=1),
        ).astype(F32)
        half = rows // 2
        mat_qkv = gather_two(w_qkv, lambda c, x: (c * half, 0), shapes[0], core)
        mat_out = gather_two(w_out, lambda c, x: (c * half, 0), shapes[1], core)
        mine = lax.dynamic_slice_in_dim(w_gate_up, core * half, half, 0)
        mine = jnp.where(x_bit == 0, mine[:, :FF], mine[:, FF:]).astype(BF16)
        mat_gate_up = gather_four(w_gate_up, mine, lambda c, x: (c * half, x * FF), shapes[2])
        quarter = down_rows // 4
        mine = lax.dynamic_slice_in_dim(
            w_down, (core * 2 + x_bit) * quarter, quarter, 0
        ).astype(BF16)
        mat_down = gather_four(w_down, mine, lambda c, x: ((c * 2 + x) * quarter, 0), shapes[3])
        eighth = rows // 4
        cut_qkv_out = Pieces(rows, eighth, 384, lambda c, x, z: ((c * 2 + x) * eighth, z * 384))
        cut_gate_up = Pieces(rows, half, 384, lambda c, x, z: (c * half, (x * 4 + z) * 384))
        thin = down_rows // 16
        cut_down = Pieces(down_rows, thin, width, lambda c, x, z: ((c * 8 + x * 4 + z) * thin, 0))
    else:
        gains = lax.all_gather(norm_gains.astype(BF16), "shard", axis=1, tiled=True).astype(F32)
        mat_qkv, mat_out, mat_gate_up, mat_down = [
            Weight(s, whole=lax.all_gather(m.astype(BF16), "shard", axis=0, tiled=True))
            for s, m in zip(shapes, masters)
        ]
        cut_qkv_out = cut_gate_up = cut_down = None

    tables = rope_tables(segments[0])
    segs = (segments.reshape(-1, 1), segments.reshape(1, -1))
    qkv, attended = attention_forward(idx, x, tables, segs, gains, mat_qkv)
    middle, normed_low, ab, hidden, *grad_down = feed_forward(
        idx, x, attended, gains, y, mat_out, mat_gate_up, cut_down
    )
    gated, *grad_gate_up = feed_back(idx, ab, normed_low, y, mat_down, cut_gate_up)
    grad_middle, grad_proj, grad_gain_two, *grad_qkv_out = attention_back(
        idx, x, y, middle, gated, qkv, attended, tables, segs, gains, mat_gate_up, mat_out, cut_qkv_out
    )
    output, token_grad, grad_gain_one = finish_tokens(
        idx, x, middle, hidden, grad_middle, grad_proj, gains, mat_down, mat_qkv
    )
    gain_grads = lax.psum(
        jnp.concatenate([grad_gain_one, grad_gain_two], axis=0), ("dp", "shard")
    )
    gain_grads = lax.dynamic_slice_in_dim(
        gain_grads, owner * norm_gains.shape[1], norm_gains.shape[1], 1
    )
    one_gains, two_gains, next_gains = adamw(
        norm_gains, first_gains, second_gains, gain_grads, RATE_GAIN, 0.0
    )
    if fast:

        def put_rows(full, z, piece):
            full[pl.ds(z * thin, thin), :] = piece

        def put_columns(full, z, piece):
            full[:, pl.ds(z * 384, 384)] = piece

        by_row = lambda t, _: (t, 0)
        one_down, two_down, next_down = update_state(
            idx,
            sum_and_share(*grad_down),
            [w_down],
            [first_down],
            [second_down],
            [((quarter, width), by_row)],
            ((quarter, width), put_rows),
            "update_down",
        )
        one_gate_up, two_gate_up, next_gate_up = update_state(
            idx,
            sum_and_share(*grad_gate_up),
            [w_gate_up],
            [first_gate_up],
            [second_gate_up],
            [((half, FF), lambda t, _: (t // 2, t % 2))],
            ((half, FF), put_columns),
            "update_gate_up",
        )
        one_qkv, one_out, two_qkv, two_out, next_qkv, next_out = update_state(
            idx,
            sum_and_share(*grad_qkv_out),
            [w_qkv, w_out],
            [first_qkv, first_out],
            [second_qkv, second_out],
            [((eighth, QKV), by_row), ((eighth, width), by_row)],
            ((eighth, QKV + width), put_columns),
            "update_qkv_out",
        )
    else:
        sums = lax.psum((grad_qkv_out[0], grad_gate_up[0], grad_down[0]), ("dp", "shard"))
        mine = [lax.dynamic_slice_in_dim(g, owner * (g.shape[0] // groups), g.shape[0] // groups, 0) for g in sums]
        one_qkv, two_qkv, next_qkv = adamw(
            w_qkv, first_qkv, second_qkv, mine[0][:, :QKV], RATE_MATRIX, DECAY_MATRIX
        )
        one_out, two_out, next_out = adamw(
            w_out, first_out, second_out, mine[0][:, QKV:], RATE_MATRIX, DECAY_MATRIX
        )
        one_gate_up, two_gate_up, next_gate_up = adamw(
            w_gate_up, first_gate_up, second_gate_up, mine[1], RATE_MATRIX, DECAY_MATRIX
        )
        one_down, two_down, next_down = adamw(
            w_down, first_down, second_down, mine[2], RATE_MATRIX, DECAY_MATRIX
        )
    return (
        output[None],
        token_grad[None],
        one_qkv,
        one_out,
        one_gate_up,
        one_down,
        one_gains,
        two_qkv,
        two_out,
        two_gate_up,
        two_down,
        two_gains,
        next_qkv,
        next_out,
        next_gate_up,
        next_down,
        next_gains,
    )


def solution(mesh):
    return jax.shard_map(
        per_device,
        mesh=mesh,
        in_specs=(
            P(("dp", "shard"), None, None),
            P(("dp", "shard"), None),
            P(("dp", "shard"), None, None),
            P("shard", None),
            P("shard", None),
            P("shard", None),
            P("shard", None),
            P(None, "shard"),
            P("shard", None),
            P("shard", None),
            P("shard", None),
            P("shard", None),
            P(None, "shard"),
            P("shard", None),
            P("shard", None),
            P("shard", None),
            P("shard", None),
            P(None, "shard"),
        ),
        out_specs=(
            P(("dp", "shard"), None, None),
            P(("dp", "shard"), None, None),
            P("shard", None),
            P("shard", None),
            P("shard", None),
            P("shard", None),
            P(None, "shard"),
            P("shard", None),
            P("shard", None),
            P("shard", None),
            P("shard", None),
            P(None, "shard"),
            P("shard", None),
            P("shard", None),
            P("shard", None),
            P("shard", None),
            P(None, "shard"),
        ),
        check_vma=False,
    )
```

```python
import functools

import jax
import jax.numpy as jnp
import numpy as np
from jax import lax
from jax.experimental import pallas as pl
from jax.experimental.pallas import tpu as pltpu
from jax.sharding import PartitionSpec as P

HEADS = 9
KV_HEADS = 3
GROUP = HEADS // KV_HEADS
HEAD = 64
FF = 1536
STEP = 10
QUERY = HEADS * HEAD
ROPED = (HEADS + KV_HEADS) * HEAD
QKV = (HEADS + 2 * KV_HEADS) * HEAD
LANES = 128

EPS_NORM = 1e-05
ROPE_BASE = 100000.0
BETA_ONE = 0.9
BETA_TWO = 0.95
RATE_MATRIX = 0.1
RATE_GAIN = 0.3
DECAY_MATRIX = 0.1
EPS_ADAM = 1e-08
MASKED = -1e30
SCALE = float(HEAD) ** (-0.5)
VMEM_LIMIT = 56 * 1024 * 1024
HALF = 144
CUT_ROWS = 72
CUT_COLUMNS = 384
F32 = jnp.float32
BF16 = jnp.bfloat16


def rotate_block(values, cosine, signed_sine):
    lane = lax.broadcasted_iota(jnp.int32, values.shape, 1)
    swapped = jnp.where(
        lane % HEAD < HEAD // 2,
        pltpu.roll(values, LANES - HEAD // 2, 1),
        pltpu.roll(values, HEAD // 2, 1),
    )
    return values * cosine + swapped * signed_sine


def adamw(weight, first_moment, second_moment, gradient, step_rate, weight_decay):
    first_new = BETA_ONE * first_moment + (1.0 - BETA_ONE) * gradient
    second_new = BETA_TWO * second_moment + (1.0 - BETA_TWO) * gradient * gradient
    fix_one = 1.0 - BETA_ONE**STEP
    fix_two = 1.0 - BETA_TWO**STEP
    update = first_new / fix_one / (jnp.sqrt(second_new / fix_two) + EPS_ADAM)
    return (first_new, second_new, weight - step_rate * (update + weight_decay * weight))


def dot(left, right):
    return lax.dot_general(left, right, (((1,), (0,)), ((), ())), preferred_element_type=F32)


def dot_right_t(left, right):
    return lax.dot_general(left, right, (((1,), (1,)), ((), ())), preferred_element_type=F32)


def dot_left_t(left, right):
    return lax.dot_general(left, right, (((0,), (0,)), ((), ())), preferred_element_type=F32)


def norm_scale(values):
    return lax.rsqrt(jnp.mean(values * values, axis=-1, keepdims=True) + EPS_NORM)


def norm_back(grad_normed, normed, scale_rows):
    return scale_rows * (
        grad_normed - normed * jnp.mean(grad_normed * normed, axis=-1, keepdims=True)
    )


class Weight:
    def __init__(self, shape, whole=None, own=None, parts=(), place=None, own_place=None):
        self.shape, self.place, self.own_place = shape, place, own_place
        self.parts = parts
        self.arrays = [whole] if whole is not None else [own] + [p[0] for p in parts]
        self.split = whole is None

    def scratch(self):
        return [pltpu.VMEM(self.shape, BF16)] if self.split else []

    def load(self, idx, refs, scratch):
        if not self.split:
            return refs[0]
        full = scratch[0]
        self.put(full, self.own_place(idx[0]), refs[0][...].astype(BF16))
        for ref, (_, columns, (core, x)) in zip(refs[1:], self.parts):
            value = ref[...] if columns is None else ref[:HALF, columns[0] : columns[1]]
            self.put(full, self.place(1 - idx[0], idx[1] ^ core, idx[2] ^ x), value)
        return full

    def put(self, full, position, value):
        rows, columns = slice(None), slice(None)
        if value.shape[0] < self.shape[0]:
            rows = pl.ds(pl.multiple_of(position[0], 16), value.shape[0])
        if value.shape[1] < self.shape[1]:
            columns = pl.ds(pl.multiple_of(position[1], LANES), value.shape[1])
        full[rows, columns] = value


def call(body, idx, arrays, weights, outs, scratch, flops, name):
    counts = [len(w.arrays) for w in weights]
    flat = list(arrays) + [a for w in weights for a in w.arrays]
    weight_scratch = [w.scratch() for w in weights]

    def kernel(*refs):
        refs = list(refs)
        idx_ref = refs.pop(0)
        take = lambda n: [refs.pop(0) for _ in range(n)]
        array_refs = take(len(arrays))
        weight_refs = [take(n) for n in counts]
        out_refs = take(len(outs))
        own_scratch = take(len(scratch))
        scratch_refs = [take(len(s)) for s in weight_scratch]
        loads = [
            functools.partial(w.load, idx_ref, r, s)
            for w, r, s in zip(weights, weight_refs, scratch_refs)
        ]
        body(idx_ref, array_refs, loads, out_refs, own_scratch)

    moved = sum(a.size * a.dtype.itemsize for a in flat)
    moved += sum(o.size * o.dtype.itemsize for o in outs)
    return pl.pallas_call(
        kernel,
        out_shape=tuple(outs),
        in_specs=[pl.BlockSpec(memory_space=pltpu.SMEM)]
        + [pl.BlockSpec(memory_space=pltpu.VMEM)] * len(flat),
        out_specs=tuple([pl.BlockSpec(memory_space=pltpu.VMEM)] * len(outs)),
        scratch_shapes=list(scratch) + [s for group in weight_scratch for s in group],
        compiler_params=pltpu.CompilerParams(vmem_limit_bytes=VMEM_LIMIT),
        cost_estimate=pl.CostEstimate(flops=flops, bytes_accessed=moved, transcendentals=0),
        name=name,
    )(idx, *flat)


def sds(shape, dtype):
    return jax.ShapeDtypeStruct(shape, dtype)


class Pieces:
    def __init__(self, place, parts=1, extra=0):
        self.place, self.parts, self.extra = place, parts, extra

    def outs(self):
        return [sds((self.parts, 2, 8, CUT_ROWS + self.extra, CUT_COLUMNS), BF16)] * 2

    def scratch(self, columns):
        return pltpu.VMEM((8, CUT_ROWS, columns), BF16)

    def store(self, blocks, grad, start=0):
        for i in range(8):
            rows = grad[i * CUT_ROWS : (i + 1) * CUT_ROWS].astype(BF16)
            blocks[i, :, start : start + grad.shape[1]] = rows

    def emit(self, idx, blocks, outs, under=None):
        for other_core, out in enumerate((outs[1], outs[0])):
            for part in range(self.parts):
                for owner in range(2):
                    for slot in range(8):
                        z = ((slot >> 1) & 1) | ((slot & 1) << 1)
                        block, column = self.place(
                            idx[0] ^ owner, idx[1] ^ other_core, idx[2] ^ (slot >> 2), idx[3] ^ z, part
                        )
                        columns = pl.ds(pl.multiple_of(column * CUT_COLUMNS, LANES), CUT_COLUMNS)
                        piece = blocks[block, :, columns]
                        if under is not None:
                            piece = jnp.concatenate(
                                [piece.astype(F32), under[idx[0] ^ owner]], axis=0
                            ).astype(BF16)
                        out[part, owner, slot] = piece


def head_stack(values, kv_head):
    first = kv_head * GROUP
    return jnp.concatenate(
        [values[:, (first + i) * HEAD : (first + i + 1) * HEAD] for i in range(GROUP)], axis=0
    )


def softmax_rows(query, key, allowed):
    scores = jnp.where(allowed, dot_right_t(query, key) * SCALE, MASKED)
    top = jnp.max(scores, axis=-1, keepdims=True)
    exponent = jnp.exp(scores - top)
    return exponent / jnp.sum(exponent, axis=-1, keepdims=True)


def pack_weights(idx, w_qkv, w_out, w_gate_up, down_t, norm_gains):
    width = w_out.shape[1]

    def kernel(idx_ref, q_ref, o_ref, g_ref, d_ref, gains_ref, qo_out, g_out, d_out):
        g_out[...] = g_ref[...].astype(BF16)
        qo_out[:HALF, :QKV] = q_ref[...].astype(BF16)
        qo_out[:HALF, QKV:] = o_ref[...].astype(BF16)
        qo_out[HALF:, :] = jnp.zeros((16, QKV + width), BF16)
        qo_out[HALF : HALF + 2, : gains_ref.shape[1]] = gains_ref[...].astype(BF16)
        d_out[...] = d_ref[...].astype(BF16)

    outs = (
        sds((HALF + 16, QKV + width), BF16),
        sds((HALF, FF), BF16),
        sds((HALF, down_t.shape[1]), BF16),
    )
    return pl.pallas_call(
        kernel,
        grid_spec=pltpu.PrefetchScalarGridSpec(
            num_scalar_prefetch=1,
            grid=(1,),
            in_specs=[
                pl.BlockSpec((HALF, QKV), lambda t, i: (i[1], 0)),
                pl.BlockSpec((HALF, width), lambda t, i: (i[1], 0)),
                pl.BlockSpec((HALF, FF), lambda t, i: (i[1], i[2])),
                pl.BlockSpec((HALF, down_t.shape[1]), lambda t, i: (i[1] * 2 + i[2], 0)),
                pl.BlockSpec(norm_gains.shape, lambda t, i: (0, 0)),
            ],
            out_specs=tuple(pl.BlockSpec(o.shape, lambda t, i: (0, 0)) for o in outs),
        ),
        out_shape=outs,
        compiler_params=pltpu.CompilerParams(vmem_limit_bytes=VMEM_LIMIT),
        name="pack_weights",
    )(idx, w_qkv, w_out, w_gate_up, down_t, norm_gains)


def attention_forward(idx, tokens_t, segments, frequency, gains, w_qkv):
    width, seq_length = tokens_t.shape
    split_gains = len(gains) > 1

    def body(idx_ref, arrays, loads, outs, scratch):
        x_ref, seg_ref, freq_ref = arrays[:3]
        qkv_ref, o_ref, cos_ref, sin_ref, allowed_ref, gains_ref = outs
        if split_gains:
            own = arrays[3][...].astype(BF16).astype(F32)
            other = arrays[4][HALF : HALF + 8, : width // 2].astype(F32)[:2]
            gains_ref[...] = jnp.where(
                idx_ref[0] == 0,
                jnp.concatenate([own, other], axis=1),
                jnp.concatenate([other, own], axis=1),
            )
        else:
            gains_ref[...] = arrays[3][...]
        seen_doc = jnp.broadcast_to(seg_ref[...], (seq_length, seq_length))
        own_doc = seen_doc.T
        token = lax.broadcasted_iota(jnp.int32, (seq_length, seq_length), 0)
        seen = lax.broadcasted_iota(jnp.int32, (seq_length, seq_length), 1)
        begin = jnp.sum((seen_doc < own_doc).astype(F32), axis=-1, keepdims=True)
        angles = (token.astype(F32) - begin) * freq_ref[...]
        cosine, sine = jnp.cos(angles), jnp.sin(angles)
        sine = jnp.where(seen % HEAD < HEAD // 2, -sine, sine)
        cos_ref[...] = cosine
        sin_ref[...] = sine
        allowed = ((seen_doc == own_doc) & (token >= seen)).astype(F32)
        allowed_ref[...] = allowed
        allowed = jnp.concatenate([allowed] * GROUP, axis=0) > 0.5
        x = x_ref[...].astype(F32).T
        h1 = (x * norm_scale(x) * gains_ref[0:1, :]).astype(BF16)
        projected = dot(h1, loads[0]()[...])
        for start in range(0, ROPED, LANES):
            block = projected[:, start : start + LANES]
            qkv_ref[:, start : start + LANES] = rotate_block(block, cosine, sine).astype(BF16)
        qkv_ref[:, ROPED:QKV] = projected[:, ROPED:QKV].astype(BF16)
        qkv = qkv_ref[...]
        for kv in range(KV_HEADS):
            key = qkv[:, QUERY + kv * HEAD : QUERY + (kv + 1) * HEAD]
            value = qkv[:, ROPED + kv * HEAD : ROPED + (kv + 1) * HEAD]
            probs = softmax_rows(head_stack(qkv, kv), key, allowed).astype(BF16)
            attended = dot(probs, value).astype(BF16)
            for i in range(GROUP):
                start = (kv * GROUP + i) * HEAD
                o_ref[:, start : start + HEAD] = attended[i * seq_length : (i + 1) * seq_length]

    square = sds((seq_length, seq_length), F32)
    outs = [sds((seq_length, QKV), BF16), sds((seq_length, QUERY), BF16)]
    outs += [square, square, square, sds((2, width), F32)]
    return call(
        body,
        idx,
        [tokens_t, segments, frequency, *gains],
        [w_qkv],
        outs,
        [],
        2 * 128 * 576 * 960,
        "attention",
    )


def feed_forward(idx, tokens_t, attended, gains, cotangent_t, w_out, w_gate_up, pieces):
    width, seq_length = tokens_t.shape

    def body(idx_ref, arrays, loads, outs, scratch):
        x_ref, o_ref, gains_ref, y_ref = arrays
        u_ref, h2_ref, ab_ref, z_ref = outs[:4]
        u = x_ref[...].astype(F32).T + dot(o_ref[...], loads[0]()[...])
        u_ref[...] = u
        h2 = (u * norm_scale(u) * gains_ref[1:2, :]).astype(BF16)
        h2_ref[...] = h2
        ab = dot(h2, loads[1]()[...])
        ab_ref[...] = ab
        gate, up = ab[:, :FF], ab[:, FF:]
        z = (gate * jax.nn.sigmoid(gate) * up).astype(BF16)
        z_ref[...] = z
        grad = dot(y_ref[...], z)
        if pieces is None:
            outs[4][...] = grad
        else:
            pieces.store(scratch[0], grad)
            pieces.emit(idx_ref, scratch[0], outs[4:])

    outs = [
        sds((seq_length, width), F32),
        sds((seq_length, width), BF16),
        sds((seq_length, 2 * FF), F32),
        sds((seq_length, FF), BF16),
    ]
    outs += [sds((width, FF), F32)] if pieces is None else pieces.outs()
    scratch = [] if pieces is None else [pieces.scratch(FF)]
    return call(
        body,
        idx,
        [tokens_t, attended, gains, cotangent_t],
        [w_out, w_gate_up],
        outs,
        scratch,
        2 * 128 * 576 * 5200,
        "feed_forward",
    )


def feed_back(idx, ab, normed_low, hidden, middle, cotangent_t, down_t, pieces):
    width, seq_length = cotangent_t.shape

    def body(idx_ref, arrays, loads, outs, scratch):
        ab_ref, h2_ref, z_ref, u_ref, y_ref = arrays
        gg_ref, out_ref = outs[:2]
        down = loads[0]()
        gate, up = ab_ref[:, :FF], ab_ref[:, FF:]
        sig = jax.nn.sigmoid(gate)
        grad_hidden = dot_left_t(y_ref[...], down[...])
        gg_ref[:, :FF] = (grad_hidden * up * sig * (1.0 + gate * (1.0 - sig))).astype(BF16)
        gg_ref[:, FF:] = (grad_hidden * gate * sig).astype(BF16)
        grad = dot_left_t(h2_ref[...], gg_ref[...])
        if pieces is None:
            outs[2][...] = grad
        else:
            pieces.store(scratch[0], grad)
            pieces.emit(idx_ref, scratch[0], outs[2:])
        out_ref[...] = (u_ref[...] + dot_right_t(z_ref[...], down[...])).T.astype(BF16)

    outs = [sds((seq_length, 2 * FF), BF16), sds((width, seq_length), BF16)]
    outs += [sds((width, 2 * FF), F32)] if pieces is None else pieces.outs()
    scratch = [] if pieces is None else [pieces.scratch(2 * FF)]
    return call(
        body,
        idx,
        [ab, normed_low, hidden, middle, cotangent_t],
        [down_t],
        outs,
        scratch,
        2 * 128 * 576 * 6200,
        "feed_back",
    )


def attention_back(
    idx, tokens_t, cotangent_t, middle, gated, qkv, attended, tables, gains, weights, pieces
):
    width, seq_length = tokens_t.shape

    def body(idx_ref, arrays, loads, outs, scratch):
        x_ref, y_ref, u_ref, gg_ref, qkv_ref, o_ref = arrays[:6]
        cos_ref, sin_ref, allowed_ref, gains_ref = arrays[6:]
        grad_ref = outs[0]
        grad_proj, gp_ref, gain_rows, *blocks = scratch
        u = u_ref[...]
        scale_two = norm_scale(u)
        normed = u * scale_two
        grad_normed = dot_right_t(gg_ref[...], loads[0]()[...])
        grad_gain_two = jnp.sum(grad_normed * normed, axis=0, keepdims=True)
        gu = y_ref[...].astype(F32).T + norm_back(
            grad_normed * gains_ref[1:2, :], normed, scale_two
        )
        gu_low = gu.astype(BF16)
        go = dot_right_t(gu_low, loads[1]()[...]).astype(BF16)
        allowed = jnp.concatenate([allowed_ref[...]] * GROUP, axis=0) > 0.5
        qkv_values = qkv_ref[...]
        for kv in range(KV_HEADS):
            key = qkv_values[:, QUERY + kv * HEAD : QUERY + (kv + 1) * HEAD]
            value = qkv_values[:, ROPED + kv * HEAD : ROPED + (kv + 1) * HEAD]
            query = head_stack(qkv_values, kv)
            grad_out = head_stack(go, kv)
            probs = softmax_rows(query, key, allowed)
            grad_probs = dot_right_t(grad_out, value)
            row_delta = jnp.sum(probs * grad_probs, axis=-1, keepdims=True)
            gs = (probs * (grad_probs - row_delta)).astype(BF16)
            grad_query = dot(gs, key) * SCALE
            for i in range(GROUP):
                start = (kv * GROUP + i) * HEAD
                grad_proj[:, start : start + HEAD] = grad_query[
                    i * seq_length : (i + 1) * seq_length
                ]
            start = QUERY + kv * HEAD
            grad_proj[:, start : start + HEAD] = dot_left_t(gs, query) * SCALE
            start = ROPED + kv * HEAD
            grad_proj[:, start : start + HEAD] = dot_left_t(probs.astype(BF16), grad_out)
        for start in range(0, ROPED, LANES):
            gp_ref[:, start : start + LANES] = rotate_block(
                grad_proj[:, start : start + LANES], cos_ref[...], -sin_ref[...]
            ).astype(BF16)
        gp_ref[:, ROPED:QKV] = grad_proj[:, ROPED:QKV].astype(BF16)
        x = x_ref[...].astype(F32).T
        scale_one = norm_scale(x)
        normed = x * scale_one
        h1 = (normed * gains_ref[0:1, :]).astype(BF16)
        grad_qkv = dot_left_t(h1, gp_ref[...])
        grad_out = dot_left_t(o_ref[...], gu_low)
        grad_normed = dot_right_t(gp_ref[...], loads[2]()[...])
        grad_gain_one = jnp.sum(grad_normed * normed, axis=0, keepdims=True)
        if pieces is None:
            outs[1][:, :QKV] = grad_qkv
            outs[1][:, QKV:] = grad_out
            outs[2][0:1, :] = grad_gain_one
            outs[2][1:2, :] = grad_gain_two
        else:
            pieces.store(blocks[0], grad_qkv)
            pieces.store(blocks[0], grad_out, QKV)
            half = width // 2
            gain_rows[...] = jnp.zeros_like(gain_rows)
            for owner in range(2):
                columns = slice(owner * half, (owner + 1) * half)
                gain_rows[owner, 0:1, :half] = grad_gain_one[:, columns]
                gain_rows[owner, 1:2, :half] = grad_gain_two[:, columns]
            pieces.emit(idx_ref, blocks[0], outs[1:], gain_rows)
        grad_ref[...] = (
            (gu + norm_back(grad_normed * gains_ref[0:1, :], normed, scale_one)).T
        ).astype(BF16)

    outs = [sds((width, seq_length), BF16)]
    scratch = [
        pltpu.VMEM((seq_length, QKV), F32),
        pltpu.VMEM((seq_length, QKV), BF16),
        pltpu.VMEM((2, 8, CUT_COLUMNS), F32),
    ]
    if pieces is None:
        outs += [sds((width, QKV + width), F32), sds((2, width), F32)]
    else:
        outs += pieces.outs()
        scratch += [pieces.scratch(QKV + width)]
    return call(
        body,
        idx,
        [tokens_t, cotangent_t, middle, gated, qkv, attended, *tables, gains],
        weights,
        outs,
        scratch,
        2 * 128 * 576 * 8000,
        "attention_back",
    )


def update_state(summed, parts, blocks, puts, state, shape, name, gains=()):
    count = len(state) // 3
    height, width = summed.shape[2:]
    by_z = summed.reshape(4, 4, *summed.shape[1:])

    def kernel(*refs):
        part_refs, refs = refs[: len(parts)], refs[len(parts) :]
        state_refs, refs = refs[: 3 * count], refs[3 * count :]
        gain_refs, refs = refs[: len(gains)], refs[len(gains) :]
        outs, refs = refs[: 3 * count], refs[3 * count :]
        gain_outs, full = refs[: len(gains)], refs[-1]
        for ref, put in zip(part_refs, puts):
            for z in range(4):
                put(full, z, ref[z, 0, 0].astype(F32))
        start = 0
        for i in range(count):
            columns = state_refs[i].shape[1]
            first, second, new = adamw(
                state_refs[i][...],
                state_refs[count + i][...],
                state_refs[2 * count + i][...],
                full[: state_refs[i].shape[0], start : start + columns],
                RATE_MATRIX,
                DECAY_MATRIX,
            )
            start += columns
            outs[i][...] = first
            outs[count + i][...] = second
            outs[2 * count + i][...] = new
        if gains:

            @pl.when(pl.program_id(0) == 0)
            def _():
                gradient = full[CUT_ROWS : CUT_ROWS + 2, : gain_refs[0].shape[1]]
                first, second, new = adamw(
                    gain_refs[0][...], gain_refs[1][...], gain_refs[2][...], gradient, RATE_GAIN, 0.0
                )
                gain_outs[0][...] = first
                gain_outs[1][...] = second
                gain_outs[2][...] = new

    state_specs = [pl.BlockSpec(*blocks[i]) for i in range(count)] * 3
    gain_specs = [pl.BlockSpec(g.shape, lambda t: (0, 0)) for g in gains]
    part_specs = [
        pl.BlockSpec((4, 1, 1, height, width), lambda t, p=p: (0, t, p, 0, 0)) for p in parts
    ]
    moved = sum(a.size * 8 for a in state)
    return pl.pallas_call(
        kernel,
        grid=(4,),
        in_specs=part_specs + state_specs + gain_specs,
        out_specs=tuple(state_specs + gain_specs),
        scratch_shapes=[pltpu.VMEM(shape, F32)],
        out_shape=tuple(sds(a.shape, F32) for a in [*state, *gains]),
        compiler_params=pltpu.CompilerParams(vmem_limit_bytes=VMEM_LIMIT),
        cost_estimate=pl.CostEstimate(flops=0, bytes_accessed=moved, transcendentals=0),
        name=name,
    )(*[by_z] * len(parts), *state, *gains)


def swap(values, axis, mask):
    size = lax.axis_size(axis)
    return lax.ppermute(values, axis, [(i, i ^ mask) for i in range(size)])


def sum_over_plane(keep, arrived, across_first):
    total = keep.astype(F32) + arrived.astype(F32)
    if across_first:
        total = total[0] + swap(total[1].astype(BF16), "shard", 1).astype(F32)
        return total[:4] + swap(total[4:].astype(BF16), "dp", 2).astype(F32)
    total = total[:, :4] + swap(total[:, 4:].astype(BF16), "dp", 2).astype(F32)
    return total[0] + swap(total[1].astype(BF16), "shard", 1).astype(F32)


def sum_over_line(totals):
    totals = totals[:, :2] + swap(totals[:, 2:].astype(BF16), "dp", 4).astype(F32)
    piece = totals[:, 0] + swap(totals[:, 1].astype(BF16), "dp", 8).astype(F32)
    return lax.all_gather(piece.astype(BF16), "dp", axis=0)


def spread(mine):
    near = swap(mine, "shard", 1)
    near_x = swap(near, "dp", 2)
    return [
        (near, None, (0, 0)),
        (near_x, None, (0, 1)),
        (swap(near, "dp", 1), None, (1, 0)),
        (swap(near_x, "dp", 1), None, (1, 1)),
    ]


def per_device(
    tokens,
    segments,
    cotangent,
    w_qkv,
    w_out,
    w_gate_up,
    w_down,
    norm_gains,
    first_qkv,
    first_out,
    first_gate_up,
    first_down,
    first_gains,
    second_qkv,
    second_out,
    second_gate_up,
    second_down,
    second_gains,
):
    groups = lax.axis_size("shard")
    replicas = lax.axis_size("dp")
    fast = groups == 2 and replicas == 16
    place_dp = lax.axis_index("dp")
    owner = lax.axis_index("shard")
    idx = jnp.stack([owner, place_dp & 1, (place_dp >> 1) & 1, place_dp >> 2]).astype(jnp.int32)
    x_t, y_t = tokens[0].T, cotangent[0].T
    width, seq_length = x_t.shape
    rows, down_rows = w_qkv.shape[0], w_down.shape[0]
    down_t, first_down_t, second_down_t = w_down.T, first_down.T, second_down.T
    half_size = HEAD // 2
    frequency = ROPE_BASE ** (-(np.arange(half_size) * 2.0 / HEAD))
    frequency = jnp.asarray(np.tile(frequency, 4)[None], F32)
    if fast:
        qo, gate_up, down = pack_weights(idx, w_qkv, w_out, w_gate_up, down_t, norm_gains)
        gate_up_parts = spread(gate_up)
        qo_near = swap(qo, "shard", 1)
        qo_far = swap(qo_near, "dp", 1)
        down_parts = spread(down)
        gains = (norm_gains, qo_near)
        by_rows = lambda o, c, x: (o * rows + c * HALF, 0)
        own_rows = lambda o: (o * rows, 0)
        rels = ((0, 0), (1, 0))
        mat_qkv = Weight(
            (width, QKV),
            own=w_qkv,
            parts=[(a, (0, QKV), r) for a, r in zip((qo_near, qo_far), rels)],
            place=by_rows,
            own_place=own_rows,
        )
        mat_out = Weight(
            (width, width),
            own=w_out,
            parts=[(a, (QKV, QKV + width), r) for a, r in zip((qo_near, qo_far), rels)],
            place=by_rows,
            own_place=own_rows,
        )
        mat_gate_up = Weight(
            (width, 2 * FF),
            own=w_gate_up,
            parts=gate_up_parts,
            place=lambda o, c, x: (o * rows + c * HALF, x * FF),
            own_place=own_rows,
        )
        mat_down = Weight(
            (width, FF),
            own=down_t,
            parts=down_parts,
            place=lambda o, c, x: ((c * 2 + x) * HALF, o * down_rows),
            own_place=lambda o: (0, o * down_rows),
        )
        cut_qkv_out = Pieces(lambda o, c, x, z, p: (o * 4 + c * 2 + x, z), extra=8)
        cut_gate_up = Pieces(lambda o, c, x, z, p: (o * 4 + c * 2 + p, x * 4 + z), parts=2)
        cut_down = Pieces(lambda o, c, x, z, p: (c * 4 + x * 2 + (z >> 1), o * 2 + (z & 1)))
    else:
        gains = (
            lax.all_gather(norm_gains.astype(BF16), "shard", axis=1, tiled=True).astype(F32),
        )
        mat_qkv, mat_out, mat_gate_up, mat_down = [
            lax.all_gather(m.astype(BF16), "shard", axis=0, tiled=True)
            for m in (w_qkv, w_out, w_gate_up, w_down)
        ]
        mat_qkv, mat_out, mat_gate_up, mat_down = [
            Weight(m.shape, whole=m) for m in (mat_qkv, mat_out, mat_gate_up, mat_down.T)
        ]
        cut_qkv_out = cut_gate_up = cut_down = None

    qkv, attended, *tables, gains = attention_forward(idx, x_t, segments, frequency, gains, mat_qkv)
    middle, normed_low, ab, hidden, *grad_down = feed_forward(
        idx, x_t, attended, gains, y_t, mat_out, mat_gate_up, cut_down
    )
    gated, output, *grad_gate_up = feed_back(
        idx, ab, normed_low, hidden, middle, y_t, mat_down, cut_gate_up
    )
    token_grad, *grad_qkv_out = attention_back(
        idx,
        x_t,
        y_t,
        middle,
        gated,
        qkv,
        attended,
        tables,
        gains,
        [mat_gate_up, mat_out, mat_qkv],
        cut_qkv_out,
    )
    if fast:

        def put_down(full, z, piece):
            full[(z >> 1) * CUT_ROWS : ((z >> 1) + 1) * CUT_ROWS, pl.ds((z & 1) * 384, 384)] = piece

        def put_upper(full, z, piece):
            full[:CUT_ROWS, pl.ds(z * 384, 384)] = piece

        def put_lower(full, z, piece):
            full[CUT_ROWS:, pl.ds(z * 384, 384)] = piece

        def put_columns(full, z, piece):
            full[:, pl.ds(z * 384, 384)] = piece

        arrived_down = swap(grad_down[0], "dp", 1)
        plane_down = sum_over_plane(grad_down[1][0], arrived_down[0], True)
        arrived_gate_up = swap(grad_gate_up[0], "dp", 1)
        plane_upper = sum_over_plane(grad_gate_up[1][0], arrived_gate_up[0], False)
        plane_lower = sum_over_plane(grad_gate_up[1][1], arrived_gate_up[1], True)
        summed = sum_over_line(jnp.stack([plane_down, plane_upper, plane_lower]))
        arrived_qkv_out = swap(grad_qkv_out[0], "dp", 1)
        plane_qkv_out = sum_over_plane(grad_qkv_out[1][0], arrived_qkv_out[0], False)
        summed_qkv_out = sum_over_line(plane_qkv_out[None])
        by_row = lambda t: ((t % 2) * 2 + t // 2, 0)
        one_down, two_down, next_down = update_state(
            summed,
            (0,),
            [((HALF, down_rows), by_row)],
            (put_down,),
            [down_t, first_down_t, second_down_t],
            (HALF, down_rows),
            "update_down",
        )
        one_gate_up, two_gate_up, next_gate_up = update_state(
            summed,
            (1, 2),
            [((HALF, FF), lambda t: (t % 2, t // 2))],
            (put_upper, put_lower),
            [w_gate_up, first_gate_up, second_gate_up],
            (HALF, FF),
            "update_gate_up",
        )
        updated = update_state(
            summed_qkv_out,
            (0,),
            [((CUT_ROWS, QKV), by_row), ((CUT_ROWS, width), by_row)],
            (put_columns,),
            [w_qkv, w_out, first_qkv, first_out, second_qkv, second_out],
            (CUT_ROWS + 8, QKV + width),
            "update_qkv_out",
            (norm_gains, first_gains, second_gains),
        )
        one_qkv, one_out, two_qkv, two_out, next_qkv, next_out = updated[:6]
        one_gains, two_gains, next_gains = updated[6:]
    else:
        sums = lax.psum((*grad_qkv_out, grad_gate_up[0], grad_down[0].T), ("dp", "shard"))
        grad_qkv_out, grad_gains, grad_gate_up, grad_down = sums

        def own(grad, axis=0):
            size = grad.shape[axis] // groups
            return lax.dynamic_slice_in_dim(grad, owner * size, size, axis)

        one_qkv, two_qkv, next_qkv = adamw(
            w_qkv, first_qkv, second_qkv, own(grad_qkv_out[:, :QKV]), RATE_MATRIX, DECAY_MATRIX
        )
        one_out, two_out, next_out = adamw(
            w_out, first_out, second_out, own(grad_qkv_out[:, QKV:]), RATE_MATRIX, DECAY_MATRIX
        )
        one_gate_up, two_gate_up, next_gate_up = adamw(
            w_gate_up, first_gate_up, second_gate_up, own(grad_gate_up), RATE_MATRIX, DECAY_MATRIX
        )
        one_down, two_down, next_down = [
            a.T
            for a in adamw(
                w_down, first_down, second_down, own(grad_down), RATE_MATRIX, DECAY_MATRIX
            )
        ]
        one_gains, two_gains, next_gains = adamw(
            norm_gains, first_gains, second_gains, own(grad_gains, 1), RATE_GAIN, 0.0
        )
    one_down, two_down, next_down = one_down.T, two_down.T, next_down.T
    return (
        output.T[None],
        token_grad.T[None],
        one_qkv,
        one_out,
        one_gate_up,
        one_down,
        one_gains,
        two_qkv,
        two_out,
        two_gate_up,
        two_down,
        two_gains,
        next_qkv,
        next_out,
        next_gate_up,
        next_down,
        next_gains,
    )


def solution(mesh):
    return jax.shard_map(
        per_device,
        mesh=mesh,
        in_specs=(
            P(("dp", "shard"), None, None),
            P(("dp", "shard"), None),
            P(("dp", "shard"), None, None),
            P("shard", None),
            P("shard", None),
            P("shard", None),
            P("shard", None),
            P(None, "shard"),
            P("shard", None),
            P("shard", None),
            P("shard", None),
            P("shard", None),
            P(None, "shard"),
            P("shard", None),
            P("shard", None),
            P("shard", None),
            P("shard", None),
            P(None, "shard"),
        ),
        out_specs=(
            P(("dp", "shard"), None, None),
            P(("dp", "shard"), None, None),
            P("shard", None),
            P("shard", None),
            P("shard", None),
            P("shard", None),
            P(None, "shard"),
            P("shard", None),
            P("shard", None),
            P("shard", None),
            P("shard", None),
            P(None, "shard"),
            P("shard", None),
            P("shard", None),
            P("shard", None),
            P("shard", None),
            P(None, "shard"),
        ),
        check_vma=False,
    )
```

```python
import functools

import jax
import jax.numpy as jnp
import numpy as np
from jax import lax
from jax.experimental import pallas as pl
from jax.experimental.pallas import tpu as pltpu
from jax.sharding import PartitionSpec as P

HEADS = 9
KV_HEADS = 3
GROUP = HEADS // KV_HEADS
HEAD = 64
FF = 1536
STEP = 10
QUERY = HEADS * HEAD
ROPED = (HEADS + KV_HEADS) * HEAD
QKV = (HEADS + 2 * KV_HEADS) * HEAD
LANES = 128

EPS_NORM = 1e-05
ROPE_BASE = 100000.0
BETA_ONE = 0.9
BETA_TWO = 0.95
RATE_MATRIX = 0.1
RATE_GAIN = 0.3
DECAY_MATRIX = 0.1
EPS_ADAM = 1e-08
MASKED = -1e30
SCALE = float(HEAD) ** (-0.5)
VMEM_LIMIT = 32 * 1024 * 1024
HALF = 144
CUT_ROWS = 72
CUT_COLUMNS = 384
F32 = jnp.float32
BF16 = jnp.bfloat16


def rotate_block(values, cosine, signed_sine):
    lane = lax.broadcasted_iota(jnp.int32, values.shape, 1)
    swapped = jnp.where(
        lane % HEAD < HEAD // 2,
        pltpu.roll(values, LANES - HEAD // 2, 1),
        pltpu.roll(values, HEAD // 2, 1),
    )
    return values * cosine + swapped * signed_sine


def adamw(weight, first_moment, second_moment, gradient, step_rate, weight_decay):
    first_new = BETA_ONE * first_moment + (1.0 - BETA_ONE) * gradient
    second_new = BETA_TWO * second_moment + (1.0 - BETA_TWO) * gradient * gradient
    fix_one = 1.0 - BETA_ONE**STEP
    fix_two = 1.0 - BETA_TWO**STEP
    update = first_new / fix_one / (jnp.sqrt(second_new / fix_two) + EPS_ADAM)
    return (first_new, second_new, weight - step_rate * (update + weight_decay * weight))


def dot(left, right):
    return lax.dot_general(left, right, (((1,), (0,)), ((), ())), preferred_element_type=F32)


def dot_right_t(left, right):
    return lax.dot_general(left, right, (((1,), (1,)), ((), ())), preferred_element_type=F32)


def dot_left_t(left, right):
    return lax.dot_general(left, right, (((0,), (0,)), ((), ())), preferred_element_type=F32)


def norm_scale(values):
    return lax.rsqrt(jnp.mean(values * values, axis=-1, keepdims=True) + EPS_NORM)


def norm_back(grad_normed, normed, scale_rows):
    return scale_rows * (
        grad_normed - normed * jnp.mean(grad_normed * normed, axis=-1, keepdims=True)
    )


class Weight:
    def __init__(self, shape, whole=None, own=None, parts=(), place=None, own_place=None):
        self.shape, self.place, self.own_place = shape, place, own_place
        self.parts = parts
        self.arrays = [whole] if whole is not None else [own] + [p[0] for p in parts]
        self.split = whole is None

    def scratch(self):
        return [pltpu.VMEM(self.shape, BF16)] if self.split else []

    def load(self, idx, refs, scratch):
        if not self.split:
            return refs[0]
        full = scratch[0]
        self.put(full, self.own_place(idx[0]), refs[0][...].astype(BF16))
        for ref, (_, columns, (core, x)) in zip(refs[1:], self.parts):
            value = ref[...] if columns is None else ref[:HALF, columns[0] : columns[1]]
            self.put(full, self.place(1 - idx[0], idx[1] ^ core, idx[2] ^ x), value)
        return full

    def put(self, full, position, value):
        rows, columns = slice(None), slice(None)
        if value.shape[0] < self.shape[0]:
            rows = pl.ds(pl.multiple_of(position[0], 16), value.shape[0])
        if value.shape[1] < self.shape[1]:
            columns = pl.ds(pl.multiple_of(position[1], LANES), value.shape[1])
        full[rows, columns] = value


def call(body, idx, arrays, weights, outs, scratch, flops, name, after=()):
    counts = [len(w.arrays) for w in weights]
    flat = list(arrays) + [a for w in weights for a in w.arrays]
    weight_scratch = [w.scratch() for w in weights]

    def kernel(*refs):
        refs = list(refs)
        idx_ref = refs.pop(0)
        take = lambda n: [refs.pop(0) for _ in range(n)]
        array_refs = take(len(arrays))
        weight_refs = [take(n) for n in counts]
        take(len(after))
        out_refs = take(len(outs))
        own_scratch = take(len(scratch))
        scratch_refs = [take(len(s)) for s in weight_scratch]
        loads = [
            functools.partial(w.load, idx_ref, r, s)
            for w, r, s in zip(weights, weight_refs, scratch_refs)
        ]
        body(idx_ref, array_refs, loads, out_refs, own_scratch)

    moved = sum(a.size * a.dtype.itemsize for a in flat)
    moved += sum(o.size * o.dtype.itemsize for o in outs)
    return pl.pallas_call(
        kernel,
        out_shape=tuple(outs),
        in_specs=[pl.BlockSpec(memory_space=pltpu.SMEM)]
        + [pl.BlockSpec(memory_space=pltpu.VMEM)] * len(flat)
        + [pl.BlockSpec(memory_space=pl.ANY)] * len(after),
        out_specs=tuple([pl.BlockSpec(memory_space=pltpu.VMEM)] * len(outs)),
        scratch_shapes=list(scratch) + [s for group in weight_scratch for s in group],
        compiler_params=pltpu.CompilerParams(vmem_limit_bytes=VMEM_LIMIT),
        cost_estimate=pl.CostEstimate(flops=flops, bytes_accessed=moved, transcendentals=0),
        name=name,
    )(idx, *flat, *after)


def sds(shape, dtype):
    return jax.ShapeDtypeStruct(shape, dtype)


class Pieces:
    def __init__(self, place, parts=1, extra=0):
        self.place, self.parts, self.extra = place, parts, extra

    def outs(self):
        return [sds((self.parts, 2, 8, CUT_ROWS + self.extra, CUT_COLUMNS), BF16)] * 2

    def scratch(self, columns):
        return pltpu.VMEM((8, CUT_ROWS, columns), BF16)

    def store(self, blocks, grad, start=0):
        for i in range(8):
            rows = grad[i * CUT_ROWS : (i + 1) * CUT_ROWS].astype(BF16)
            blocks[i, :, start : start + grad.shape[1]] = rows

    def emit(self, idx, blocks, outs, under=None):
        for other_core, out in enumerate((outs[1], outs[0])):
            for part in range(self.parts):
                for owner in range(2):
                    for slot in range(8):
                        z = ((slot >> 1) & 1) | ((slot & 1) << 1)
                        block, column = self.place(
                            idx[0] ^ owner, idx[1] ^ other_core, idx[2] ^ (slot >> 2), idx[3] ^ z, part
                        )
                        columns = pl.ds(pl.multiple_of(column * CUT_COLUMNS, LANES), CUT_COLUMNS)
                        piece = blocks[block, :, columns]
                        if under is not None:
                            piece = jnp.concatenate(
                                [piece.astype(F32), under[idx[0] ^ owner]], axis=0
                            ).astype(BF16)
                        out[part, owner, slot] = piece


def head_stack(values, kv_head):
    first = kv_head * GROUP
    return jnp.concatenate(
        [values[:, (first + i) * HEAD : (first + i + 1) * HEAD] for i in range(GROUP)], axis=0
    )


def softmax_rows(query, key, allowed):
    scores = jnp.where(allowed, dot_right_t(query, key) * SCALE, MASKED)
    top = jnp.max(scores, axis=-1, keepdims=True)
    exponent = jnp.exp(scores - top)
    return exponent / jnp.sum(exponent, axis=-1, keepdims=True)


def pack_weights(idx, w_qkv, w_out, w_gate_up, down_t, norm_gains):
    width = w_out.shape[1]

    def kernel(idx_ref, q_ref, o_ref, g_ref, d_ref, gains_ref, qo_out, g_out, d_out):
        g_out[...] = g_ref[...].astype(BF16)
        qo_out[:HALF, :QKV] = q_ref[...].astype(BF16)
        qo_out[:HALF, QKV:] = o_ref[...].astype(BF16)
        qo_out[HALF:, :] = jnp.zeros((16, QKV + width), BF16)
        qo_out[HALF : HALF + 2, : gains_ref.shape[1]] = gains_ref[...].astype(BF16)
        d_out[...] = d_ref[...].astype(BF16)

    outs = (
        sds((HALF + 16, QKV + width), BF16),
        sds((HALF, FF), BF16),
        sds((2 * HALF, down_t.shape[1]), BF16),
    )
    return pl.pallas_call(
        kernel,
        grid_spec=pltpu.PrefetchScalarGridSpec(
            num_scalar_prefetch=1,
            grid=(1,),
            in_specs=[
                pl.BlockSpec((HALF, QKV), lambda t, i: (i[1], 0)),
                pl.BlockSpec((HALF, width), lambda t, i: (i[1], 0)),
                pl.BlockSpec((HALF, FF), lambda t, i: (i[1], i[2])),
                pl.BlockSpec((2 * HALF, down_t.shape[1]), lambda t, i: (i[1], 0)),
                pl.BlockSpec(norm_gains.shape, lambda t, i: (0, 0)),
            ],
            out_specs=tuple(pl.BlockSpec(o.shape, lambda t, i: (0, 0)) for o in outs),
        ),
        out_shape=outs,
        compiler_params=pltpu.CompilerParams(vmem_limit_bytes=VMEM_LIMIT),
        name="pack_weights",
    )(idx, w_qkv, w_out, w_gate_up, down_t, norm_gains)


def attention_forward(idx, tokens_t, segments, frequency, gains, w_qkv):
    width, seq_length = tokens_t.shape
    split_gains = len(gains) > 1

    def body(idx_ref, arrays, loads, outs, scratch):
        x_ref, seg_ref, freq_ref = arrays[:3]
        qkv_ref, o_ref, cos_ref, sin_ref, allowed_ref, gains_ref = outs
        if split_gains:
            own = arrays[3][...].astype(BF16).astype(F32)
            other = arrays[4][HALF : HALF + 8, : width // 2].astype(F32)[:2]
            gains_ref[...] = jnp.where(
                idx_ref[0] == 0,
                jnp.concatenate([own, other], axis=1),
                jnp.concatenate([other, own], axis=1),
            )
        else:
            gains_ref[...] = arrays[3][...]
        seen_doc = jnp.broadcast_to(seg_ref[...], (seq_length, seq_length))
        own_doc = seen_doc.T
        token = lax.broadcasted_iota(jnp.int32, (seq_length, seq_length), 0)
        seen = lax.broadcasted_iota(jnp.int32, (seq_length, seq_length), 1)
        begin = jnp.sum((seen_doc < own_doc).astype(F32), axis=-1, keepdims=True)
        angles = (token.astype(F32) - begin) * freq_ref[...]
        cosine, sine = jnp.cos(angles), jnp.sin(angles)
        sine = jnp.where(seen % HEAD < HEAD // 2, -sine, sine)
        cos_ref[...] = cosine
        sin_ref[...] = sine
        allowed = ((seen_doc == own_doc) & (token >= seen)).astype(F32)
        allowed_ref[...] = allowed
        allowed = jnp.concatenate([allowed] * GROUP, axis=0) > 0.5
        x = x_ref[...].astype(F32).T
        h1 = (x * norm_scale(x) * gains_ref[0:1, :]).astype(BF16)
        projected = dot(h1, loads[0]()[...])
        for start in range(0, ROPED, LANES):
            block = projected[:, start : start + LANES]
            qkv_ref[:, start : start + LANES] = rotate_block(block, cosine, sine).astype(BF16)
        qkv_ref[:, ROPED:QKV] = projected[:, ROPED:QKV].astype(BF16)
        qkv = qkv_ref[...]
        for kv in range(KV_HEADS):
            key = qkv[:, QUERY + kv * HEAD : QUERY + (kv + 1) * HEAD]
            value = qkv[:, ROPED + kv * HEAD : ROPED + (kv + 1) * HEAD]
            probs = softmax_rows(head_stack(qkv, kv), key, allowed).astype(BF16)
            attended = dot(probs, value).astype(BF16)
            for i in range(GROUP):
                start = (kv * GROUP + i) * HEAD
                o_ref[:, start : start + HEAD] = attended[i * seq_length : (i + 1) * seq_length]

    square = sds((seq_length, seq_length), F32)
    outs = [sds((seq_length, QKV), BF16), sds((seq_length, QUERY), BF16)]
    outs += [square, square, square, sds((2, width), F32)]
    return call(
        body,
        idx,
        [tokens_t, segments, frequency, *gains],
        [w_qkv],
        outs,
        [],
        2 * 128 * 576 * 960,
        "attention",
    )


def feed_forward(idx, tokens_t, attended, gains, cotangent_t, w_out, w_gate_up, pieces, after):
    width, seq_length = tokens_t.shape

    def body(idx_ref, arrays, loads, outs, scratch):
        x_ref, o_ref, gains_ref, y_ref = arrays
        u_ref, h2_ref, ab_ref, z_ref = outs[:4]
        u = x_ref[...].astype(F32).T + dot(o_ref[...], loads[0]()[...])
        u_ref[...] = u
        h2 = (u * norm_scale(u) * gains_ref[1:2, :]).astype(BF16)
        h2_ref[...] = h2
        ab = dot(h2, loads[1]()[...])
        ab_ref[...] = ab
        gate, up = ab[:, :FF], ab[:, FF:]
        z = (gate * jax.nn.sigmoid(gate) * up).astype(BF16)
        z_ref[...] = z
        grad = dot(y_ref[...], z)
        if pieces is None:
            outs[4][...] = grad
        else:
            pieces.store(scratch[0], grad)
            pieces.emit(idx_ref, scratch[0], outs[4:])

    outs = [
        sds((seq_length, width), F32),
        sds((seq_length, width), BF16),
        sds((seq_length, 2 * FF), F32),
        sds((seq_length, FF), BF16),
    ]
    outs += [sds((width, FF), F32)] if pieces is None else pieces.outs()
    scratch = [] if pieces is None else [pieces.scratch(FF)]
    return call(
        body,
        idx,
        [tokens_t, attended, gains, cotangent_t],
        [w_out, w_gate_up],
        outs,
        scratch,
        2 * 128 * 576 * 5200,
        "feed_forward",
        after,
    )


def feed_back(idx, ab, normed_low, hidden, middle, cotangent_t, down_t, pieces):
    width, seq_length = cotangent_t.shape

    def body(idx_ref, arrays, loads, outs, scratch):
        ab_ref, h2_ref, z_ref, u_ref, y_ref = arrays
        gg_ref, out_ref = outs[:2]
        down = loads[0]()
        gate, up = ab_ref[:, :FF], ab_ref[:, FF:]
        sig = jax.nn.sigmoid(gate)
        grad_hidden = dot_left_t(y_ref[...], down[...])
        gg_ref[:, :FF] = (grad_hidden * up * sig * (1.0 + gate * (1.0 - sig))).astype(BF16)
        gg_ref[:, FF:] = (grad_hidden * gate * sig).astype(BF16)
        grad = dot_left_t(h2_ref[...], gg_ref[...])
        if pieces is None:
            outs[2][...] = grad
        else:
            pieces.store(scratch[0], grad)
            pieces.emit(idx_ref, scratch[0], outs[2:])
        out_ref[...] = (u_ref[...] + dot_right_t(z_ref[...], down[...])).T.astype(BF16)

    outs = [sds((seq_length, 2 * FF), BF16), sds((width, seq_length), BF16)]
    outs += [sds((width, 2 * FF), F32)] if pieces is None else pieces.outs()
    scratch = [] if pieces is None else [pieces.scratch(2 * FF)]
    return call(
        body,
        idx,
        [ab, normed_low, hidden, middle, cotangent_t],
        [down_t],
        outs,
        scratch,
        2 * 128 * 576 * 6200,
        "feed_back",
    )


def middle_back(idx, cotangent_t, middle, gated, gains, w_gate_up, w_out, after):
    width, seq_length = cotangent_t.shape

    def body(idx_ref, arrays, loads, outs, scratch):
        y_ref, u_ref, gg_ref, gains_ref = arrays
        gu_ref, go_ref, gain_ref = outs
        u = u_ref[...]
        scale_two = norm_scale(u)
        normed = u * scale_two
        grad_normed = dot_right_t(gg_ref[...], loads[0]()[...])
        gain_ref[...] = jnp.sum(grad_normed * normed, axis=0, keepdims=True)
        gu = y_ref[...].astype(F32).T + norm_back(
            grad_normed * gains_ref[1:2, :], normed, scale_two
        )
        gu_ref[...] = gu
        go_ref[...] = dot_right_t(gu.astype(BF16), loads[1]()[...]).astype(BF16)

    outs = [sds((seq_length, width), F32), sds((seq_length, width), BF16), sds((1, width), F32)]
    return call(
        body,
        idx,
        [cotangent_t, middle, gated, gains],
        [w_gate_up, w_out],
        outs,
        [],
        2 * 128 * 576 * 3700,
        "middle_back",
        after,
    )


def attention_back(
    idx, tokens_t, grad_middle, grad_attended, gain_two, qkv, attended, tables, gains, w_qkv, pieces, after
):
    width, seq_length = tokens_t.shape

    def body(idx_ref, arrays, loads, outs, scratch):
        x_ref, gu_ref, go_ref, gain_two_ref, qkv_ref, o_ref = arrays[:6]
        cos_ref, sin_ref, allowed_ref, gains_ref = arrays[6:]
        grad_ref = outs[0]
        grad_proj, gp_ref, gain_rows, *blocks = scratch
        gu, go = gu_ref[...], go_ref[...]
        gu_low = gu.astype(BF16)
        grad_gain_two = gain_two_ref[...]
        allowed = jnp.concatenate([allowed_ref[...]] * GROUP, axis=0) > 0.5
        qkv_values = qkv_ref[...]
        for kv in range(KV_HEADS):
            key = qkv_values[:, QUERY + kv * HEAD : QUERY + (kv + 1) * HEAD]
            value = qkv_values[:, ROPED + kv * HEAD : ROPED + (kv + 1) * HEAD]
            query = head_stack(qkv_values, kv)
            grad_out = head_stack(go, kv)
            probs = softmax_rows(query, key, allowed)
            grad_probs = dot_right_t(grad_out, value)
            row_delta = jnp.sum(probs * grad_probs, axis=-1, keepdims=True)
            gs = (probs * (grad_probs - row_delta)).astype(BF16)
            grad_query = dot(gs, key) * SCALE
            for i in range(GROUP):
                start = (kv * GROUP + i) * HEAD
                grad_proj[:, start : start + HEAD] = grad_query[
                    i * seq_length : (i + 1) * seq_length
                ]
            start = QUERY + kv * HEAD
            grad_proj[:, start : start + HEAD] = dot_left_t(gs, query) * SCALE
            start = ROPED + kv * HEAD
            grad_proj[:, start : start + HEAD] = dot_left_t(probs.astype(BF16), grad_out)
        for start in range(0, ROPED, LANES):
            gp_ref[:, start : start + LANES] = rotate_block(
                grad_proj[:, start : start + LANES], cos_ref[...], -sin_ref[...]
            ).astype(BF16)
        gp_ref[:, ROPED:QKV] = grad_proj[:, ROPED:QKV].astype(BF16)
        x = x_ref[...].astype(F32).T
        scale_one = norm_scale(x)
        normed = x * scale_one
        h1 = (normed * gains_ref[0:1, :]).astype(BF16)
        grad_qkv = dot_left_t(h1, gp_ref[...])
        grad_out = dot_left_t(o_ref[...], gu_low)
        grad_normed = dot_right_t(gp_ref[...], loads[0]()[...])
        grad_gain_one = jnp.sum(grad_normed * normed, axis=0, keepdims=True)
        if pieces is None:
            outs[1][:, :QKV] = grad_qkv
            outs[1][:, QKV:] = grad_out
            outs[2][0:1, :] = grad_gain_one
            outs[2][1:2, :] = grad_gain_two
        else:
            pieces.store(blocks[0], grad_qkv)
            pieces.store(blocks[0], grad_out, QKV)
            half = width // 2
            gain_rows[...] = jnp.zeros_like(gain_rows)
            for owner in range(2):
                columns = slice(owner * half, (owner + 1) * half)
                gain_rows[owner, 0:1, :half] = grad_gain_one[:, columns]
                gain_rows[owner, 1:2, :half] = grad_gain_two[:, columns]
            pieces.emit(idx_ref, blocks[0], outs[1:], gain_rows)
        grad_ref[...] = (
            (gu + norm_back(grad_normed * gains_ref[0:1, :], normed, scale_one)).T
        ).astype(BF16)

    outs = [sds((width, seq_length), BF16)]
    scratch = [
        pltpu.VMEM((seq_length, QKV), F32),
        pltpu.VMEM((seq_length, QKV), BF16),
        pltpu.VMEM((2, 8, CUT_COLUMNS), F32),
    ]
    if pieces is None:
        outs += [sds((width, QKV + width), F32), sds((2, width), F32)]
    else:
        outs += pieces.outs()
        scratch += [pieces.scratch(QKV + width)]
    return call(
        body,
        idx,
        [tokens_t, grad_middle, grad_attended, gain_two, qkv, attended, *tables, gains],
        [w_qkv],
        outs,
        scratch,
        2 * 128 * 576 * 4300,
        "attention_back",
        after,
    )


def step(body, arrays, outs, name, after=()):
    def kernel(*refs):
        body(refs[: len(arrays)], refs[len(arrays) + len(after) :])

    return pl.pallas_call(
        kernel,
        out_shape=tuple(outs),
        in_specs=[pl.BlockSpec(memory_space=pltpu.VMEM)] * len(arrays)
        + [pl.BlockSpec(memory_space=pl.ANY)] * len(after),
        out_specs=tuple([pl.BlockSpec(memory_space=pltpu.VMEM)] * len(outs)),
        compiler_params=pltpu.CompilerParams(vmem_limit_bytes=VMEM_LIMIT),
        name=name,
    )(*arrays, *after)


def add_split(keep, arrived, axis, send_ref, keep_ref):
    total = keep[...].astype(F32) + arrived[...].astype(F32)
    low, high = lax.index_in_dim(total, 0, axis, False), lax.index_in_dim(total, 1, axis, False)
    send_ref[...] = high.astype(BF16)
    keep_ref[...] = low


def add_step(jobs, name, after):
    arrays, outs = [], []
    for keep, arrived, axis in jobs:
        arrays += [keep, arrived]
        shape = keep.shape[:axis] + keep.shape[axis + 1 :]
        outs += [sds(shape, BF16), sds(shape, F32)]

    def body(ins, out_refs):
        for i, (_, _, axis) in enumerate(jobs):
            add_split(ins[2 * i], ins[2 * i + 1], axis, out_refs[2 * i], out_refs[2 * i + 1])

    flat = step(body, arrays, outs, name, after)
    return [(flat[2 * i], flat[2 * i + 1]) for i in range(len(jobs))]


def update_state(idx, near, far, parts, blocks, puts, state, shape, name, gains=(), after=()):
    count = len(state) // 3
    height, width = near.shape[3:]

    def kernel(idx_ref, *refs):
        part_refs, refs = refs[: 2 * len(parts)], refs[2 * len(parts) :]
        state_refs, refs = refs[: 3 * count], refs[3 * count :]
        gain_refs, refs = refs[: len(gains)], refs[len(gains) + len(after) :]
        outs, refs = refs[: 3 * count], refs[3 * count :]
        gain_outs, full = refs[: len(gains)], refs[-1]
        is_near = pl.program_id(0) % 2 == idx_ref[1]
        for i, put in enumerate(puts):
            for z in range(4):
                rel = z ^ idx_ref[3]
                slot = (rel & 1) * 2 + (rel >> 1)
                piece = jnp.where(
                    is_near,
                    part_refs[2 * i][0, 0, slot].astype(F32),
                    part_refs[2 * i + 1][0, 0, slot].astype(F32),
                )
                put(full, z, piece)
        start = 0
        for i in range(count):
            columns = state_refs[i].shape[1]
            first, second, new = adamw(
                state_refs[i][...],
                state_refs[count + i][...],
                state_refs[2 * count + i][...],
                full[: state_refs[i].shape[0], start : start + columns],
                RATE_MATRIX,
                DECAY_MATRIX,
            )
            start += columns
            outs[i][...] = first
            outs[count + i][...] = second
            outs[2 * count + i][...] = new
        if gains:

            @pl.when(pl.program_id(0) == 0)
            def _():
                gradient = full[CUT_ROWS : CUT_ROWS + 2, : gain_refs[0].shape[1]]
                first, second, new = adamw(
                    gain_refs[0][...], gain_refs[1][...], gain_refs[2][...], gradient, RATE_GAIN, 0.0
                )
                gain_outs[0][...] = first
                gain_outs[1][...] = second
                gain_outs[2][...] = new

    state_specs = [pl.BlockSpec(*blocks[i]) for i in range(count)] * 3
    gain_specs = [pl.BlockSpec(g.shape, lambda t, _: (0, 0)) for g in gains]
    part_specs = [
        pl.BlockSpec((1, 1, 4, height, width), lambda t, i, p=p: (p, (t // 2) ^ i[2], 0, 0, 0))
        for p in parts
        for _ in range(2)
    ]
    moved = sum(a.size * 8 for a in state)
    return pl.pallas_call(
        kernel,
        grid_spec=pltpu.PrefetchScalarGridSpec(
            num_scalar_prefetch=1,
            grid=(4,),
            in_specs=part_specs
            + state_specs
            + gain_specs
            + [pl.BlockSpec(memory_space=pl.ANY)] * len(after),
            out_specs=tuple(state_specs + gain_specs),
            scratch_shapes=[pltpu.VMEM(shape, F32)],
        ),
        out_shape=tuple(sds(a.shape, F32) for a in [*state, *gains]),
        compiler_params=pltpu.CompilerParams(vmem_limit_bytes=VMEM_LIMIT),
        cost_estimate=pl.CostEstimate(flops=0, bytes_accessed=moved, transcendentals=0),
        name=name,
    )(idx, *[near, far] * len(parts), *state, *gains, *after)


def swap(values, axis, mask):
    size = lax.axis_size(axis)
    return lax.ppermute(values, axis, [(i, i ^ mask) for i in range(size)])


over_y = functools.partial(swap, axis="shard", mask=1)
over_core = functools.partial(swap, axis="dp", mask=1)
over_x = functools.partial(swap, axis="dp", mask=2)
over_z_low = functools.partial(swap, axis="dp", mask=4)
over_z_high = functools.partial(swap, axis="dp", mask=8)


def per_device(
    tokens,
    segments,
    cotangent,
    w_qkv,
    w_out,
    w_gate_up,
    w_down,
    norm_gains,
    first_qkv,
    first_out,
    first_gate_up,
    first_down,
    first_gains,
    second_qkv,
    second_out,
    second_gate_up,
    second_down,
    second_gains,
):
    groups = lax.axis_size("shard")
    replicas = lax.axis_size("dp")
    fast = groups == 2 and replicas == 16
    place_dp = lax.axis_index("dp")
    owner = lax.axis_index("shard")
    idx = jnp.stack([owner, place_dp & 1, (place_dp >> 1) & 1, place_dp >> 2]).astype(jnp.int32)
    x_t, y_t = tokens[0].T, cotangent[0].T
    width, seq_length = x_t.shape
    rows, down_rows = w_qkv.shape[0], w_down.shape[0]
    down_t, first_down_t, second_down_t = w_down.T, first_down.T, second_down.T
    half_size = HEAD // 2
    frequency = ROPE_BASE ** (-(np.arange(half_size) * 2.0 / HEAD))
    frequency = jnp.asarray(np.tile(frequency, 4)[None], F32)
    if fast:
        qo, gate_up, down = pack_weights(idx, w_qkv, w_out, w_gate_up, down_t, norm_gains)
        gate_up_near = over_y(gate_up)
        qo_near = over_y(qo)
        down_near = over_y(down)
        gate_up_near_x = over_x(gate_up_near)
        gate_up_parts = [
            (gate_up_near, None, (0, 0)),
            (gate_up_near_x, None, (0, 1)),
            (over_core(gate_up_near), None, (1, 0)),
            (over_core(gate_up_near_x), None, (1, 1)),
        ]
        qo_far = over_core(qo_near)
        gains = (norm_gains, qo_near)
        by_rows = lambda o, c, x: (o * rows + c * HALF, 0)
        own_rows = lambda o: (o * rows, 0)
        rels = ((0, 0), (1, 0))
        mat_qkv = Weight(
            (width, QKV),
            own=w_qkv,
            parts=[(a, (0, QKV), r) for a, r in zip((qo_near, qo_far), rels)],
            place=by_rows,
            own_place=own_rows,
        )
        mat_out = Weight(
            (width, width),
            own=w_out,
            parts=[(a, (QKV, QKV + width), r) for a, r in zip((qo_near, qo_far), rels)],
            place=by_rows,
            own_place=own_rows,
        )
        mat_gate_up = Weight(
            (width, 2 * FF),
            own=w_gate_up,
            parts=gate_up_parts,
            place=lambda o, c, x: (o * rows + c * HALF, x * FF),
            own_place=own_rows,
        )
        mat_down = Weight(
            (width, FF),
            own=down_t,
            parts=(),
            place=lambda o, c, x: (c * 2 * HALF, o * down_rows),
            own_place=lambda o: (0, o * down_rows),
        )
        cut_qkv_out = Pieces(lambda o, c, x, z, p: (o * 4 + c * 2 + x, z), extra=8)
        cut_gate_up = Pieces(lambda o, c, x, z, p: (o * 4 + c * 2 + p, x * 4 + z), parts=2)
        cut_down = Pieces(lambda o, c, x, z, p: (c * 4 + x * 2 + (z >> 1), o * 2 + (z & 1)))
    else:
        gains = (
            lax.all_gather(norm_gains.astype(BF16), "shard", axis=1, tiled=True).astype(F32),
        )
        mat_qkv, mat_out, mat_gate_up, mat_down = [
            lax.all_gather(m.astype(BF16), "shard", axis=0, tiled=True)
            for m in (w_qkv, w_out, w_gate_up, w_down)
        ]
        mat_qkv, mat_out, mat_gate_up, mat_down = [
            Weight(m.shape, whole=m) for m in (mat_qkv, mat_out, mat_gate_up, mat_down.T)
        ]
        cut_qkv_out = cut_gate_up = cut_down = None

    qkv, attended, *tables, gains = attention_forward(idx, x_t, segments, frequency, gains, mat_qkv)
    after = ()
    if fast:

        def pass_on(ins, outs):
            outs[0][...] = ins[0][...]

        (down_near,) = step(pass_on, [down_near], [sds(down_near.shape, BF16)], "pass_on", (attended,))
        mat_down.parts = [(down_near, None, (0, 0)), (over_core(down_near), None, (1, 0))]
        mat_down.arrays = [down_t] + [p[0] for p in mat_down.parts]
        after = (down_near,)
    middle, normed_low, ab, hidden, *grad_down = feed_forward(
        idx, x_t, attended, gains, y_t, mat_out, mat_gate_up, cut_down, after
    )
    if fast:
        arrived_down = over_core(grad_down[0])
    gated, output, *grad_gate_up = feed_back(
        idx, ab, normed_low, hidden, middle, y_t, mat_down, cut_gate_up
    )
    if fast:
        cut = lambda a, *lead: a.reshape(*lead, *a.shape[-2:])
        arrived_gate_up = over_core(grad_gate_up[0])
        ((send, keep_down),) = add_step(
            [(grad_down[1][0], arrived_down[0], 0)], "down_core", (gated,)
        )
        arrived_down = over_y(send)
        after = (keep_down,)
    grad_middle, grad_attended, gain_two = middle_back(
        idx, y_t, middle, gated, gains, mat_gate_up, mat_out, after
    )
    if fast:
        halves = [
            [cut(a[p], *lead) for a in (grad_gate_up[1], arrived_gate_up)]
            for p, lead in ((0, (2, 2, 4)), (1, (4, 2, 2)))
        ]
        (send_up, keep_up), (send_low, keep_low) = add_step(
            [(*halves[0], 1), (*halves[1], 1)], "gate_up_core", (grad_middle,)
        )
        arrived_up, arrived_low = over_x(send_up), over_z_low(send_low)
        after = (keep_up,)
    token_grad, *grad_qkv_out = attention_back(
        idx,
        x_t,
        grad_middle,
        grad_attended,
        gain_two,
        qkv,
        attended,
        tables,
        gains,
        mat_qkv,
        cut_qkv_out,
        after,
    )
    if fast:

        def put_down(full, z, piece):
            full[(z >> 1) * CUT_ROWS : ((z >> 1) + 1) * CUT_ROWS, pl.ds((z & 1) * 384, 384)] = piece

        def put_upper(full, z, piece):
            full[:CUT_ROWS, pl.ds(z * 384, 384)] = piece

        def put_lower(full, z, piece):
            full[CUT_ROWS:, pl.ds(z * 384, 384)] = piece

        def put_columns(full, z, piece):
            full[:, pl.ds(z * 384, 384)] = piece

        arrived_qkv_out = over_core(grad_qkv_out[0])
        ((send, keep_down),) = add_step(
            [(cut(keep_down, 2, 4), cut(arrived_down, 2, 4), 0)], "down_y", (token_grad,)
        )
        arrived_down = over_x(send)
        ((send, keep_qkv_out),) = add_step(
            [(grad_qkv_out[1][0], arrived_qkv_out[0], 0)], "qkv_out_core", (keep_down,)
        )
        arrived_qkv_out = over_y(send)
        (send_up, keep_up), (send_low, keep_low) = add_step(
            [
                (cut(keep_up, 2, 2, 2), cut(arrived_up, 2, 2, 2), 1),
                (cut(keep_low, 2, 2, 2), cut(arrived_low, 2, 2, 2), 0),
            ],
            "up_x_low_z",
            (keep_qkv_out,),
        )
        arrived_up, arrived_low = over_z_low(send_up), over_y(send_low)
        (send, keep_down), (send_up, keep_up), (send_low, keep_low) = add_step(
            [
                (cut(keep_down, 2, 2), cut(arrived_down, 2, 2), 0),
                (keep_up, arrived_up, 0),
                (keep_low, arrived_low, 0),
            ],
            "down_x_up_z_low_y",
            (keep_up,),
        )
        arrived_down, arrived_up, arrived_low = over_z_low(send), over_y(send_up), over_x(send_low)
        ((send, keep_qkv_out),) = add_step(
            [(cut(keep_qkv_out, 2, 4), cut(arrived_qkv_out, 2, 4), 0)], "qkv_out_y", (keep_down,)
        )
        arrived_qkv_out = over_x(send)

        piece = (CUT_ROWS, CUT_COLUMNS)
        taller = (CUT_ROWS + 8, CUT_COLUMNS)

        def last_sums(ins, outs):
            for i in range(3):
                total = ins[2 * i][...] + ins[2 * i + 1][...].astype(F32)
                outs[0][i] = total[1].astype(BF16)
                outs[1][i] = total[0]

        send, keep = step(
            last_sums,
            [keep_down, arrived_down, keep_up, arrived_up, keep_low, arrived_low],
            [sds((3, *piece), BF16), sds((3, *piece), F32)],
            "down_z_up_y_low_x",
            (keep_qkv_out,),
        )
        arrived = over_z_high(send)
        ((send, keep_qkv_out),) = add_step(
            [(cut(keep_qkv_out, 2, 2), cut(arrived_qkv_out, 2, 2), 0)], "qkv_out_x", (keep,)
        )
        arrived_qkv_out = over_z_low(send)

        def make_pieces(ins, outs):
            outs[0][...] = (ins[0][...] + ins[1][...].astype(F32)).astype(BF16)
            total = ins[2][...] + ins[3][...].astype(F32)
            outs[1][...] = total[1].astype(BF16)
            outs[2][...] = total[0]

        pieces, send, keep_qkv_out = step(
            make_pieces,
            [keep, arrived, keep_qkv_out, arrived_qkv_out],
            [sds((3, *piece), BF16), sds(taller, BF16), sds(taller, F32)],
            "pieces_qkv_out_z",
        )
        pieces_high, arrived_qkv_out = over_z_high(pieces), over_z_high(send)

        def share_high(ins, outs):
            outs[0][0], outs[0][1] = ins[0][0], ins[1][0]
            for part in range(2):
                outs[1][part, 0], outs[1][part, 1] = ins[0][part + 1], ins[1][part + 1]
            outs[2][...] = (ins[2][...] + ins[3][...].astype(F32)).astype(BF16)

        near_down, near_gate_up, piece_qkv_out = step(
            share_high,
            [pieces, pieces_high, keep_qkv_out, arrived_qkv_out],
            [sds((2, *piece), BF16), sds((2, 2, *piece), BF16), sds(taller, BF16)],
            "share_z_high",
        )
        down_low, gate_up_x = over_z_low(near_down), over_x(near_gate_up)
        qkv_out_high = over_z_high(piece_qkv_out)

        def share_next(ins, outs):
            outs[0][0], outs[0][1] = ins[0][...], ins[1][...]
            for part in range(2):
                outs[1][part, 0], outs[1][part, 1] = ins[2][part], ins[3][part]
            outs[2][0], outs[2][1] = ins[4][...], ins[5][...]

        near_down, near_gate_up, near_qkv_out = step(
            share_next,
            [near_down, down_low, near_gate_up, gate_up_x, piece_qkv_out, qkv_out_high],
            [sds((2, 2, *piece), BF16), sds((2, 2, 2, *piece), BF16), sds((2, *taller), BF16)],
            "share_next",
        )
        down_x, gate_up_low = over_x(near_down), over_z_low(near_gate_up)
        qkv_out_x = over_x(near_qkv_out)

        def share_last(ins, outs):
            for x in range(2):
                for low in range(2):
                    for high in range(2):
                        slot = low * 2 + high
                        outs[0][0, x, slot] = ins[x][low, high]
                        for part in range(2):
                            outs[1][part, x, slot] = ins[2 + low][part, x, high]
            outs[2][0], outs[2][1] = ins[4][...], ins[5][...]

        near_down, near_gate_up, near_qkv_out = step(
            share_last,
            [near_down, down_x, near_gate_up, gate_up_low, near_qkv_out, qkv_out_x],
            [sds((1, 2, 4, *piece), BF16), sds((2, 2, 4, *piece), BF16), sds((2, 2, *taller), BF16)],
            "share_last",
        )
        far_down, far_gate_up = over_core(near_down), over_core(near_gate_up)
        qkv_out_low = over_z_low(near_qkv_out)
        by_row = lambda t, _: ((t % 2) * 2 + t // 2, 0)
        one_down, two_down, next_down = update_state(
            idx,
            near_down,
            far_down,
            (0,),
            [((HALF, down_rows), by_row)],
            (put_down,),
            [down_t, first_down_t, second_down_t],
            (HALF, down_rows),
            "update_down",
        )

        def share_qkv_out(ins, outs):
            for x in range(2):
                for low in range(2):
                    for high in range(2):
                        outs[0][0, x, low * 2 + high] = ins[low][x, high]

        (near_qkv_out,) = step(
            share_qkv_out,
            [near_qkv_out, qkv_out_low],
            [sds((1, 2, 4, *taller), BF16)],
            "share_qkv_out",
            (one_down,),
        )
        far_qkv_out = over_core(near_qkv_out)
        one_gate_up, two_gate_up, next_gate_up = update_state(
            idx,
            near_gate_up,
            far_gate_up,
            (0, 1),
            [((HALF, FF), lambda t, _: (t % 2, t // 2))],
            (put_upper, put_lower),
            [w_gate_up, first_gate_up, second_gate_up],
            (HALF, FF),
            "update_gate_up",
            (),
            (near_qkv_out,),
        )
        updated = update_state(
            idx,
            near_qkv_out,
            far_qkv_out,
            (0,),
            [((CUT_ROWS, QKV), by_row), ((CUT_ROWS, width), by_row)],
            (put_columns,),
            [w_qkv, w_out, first_qkv, first_out, second_qkv, second_out],
            (CUT_ROWS + 8, QKV + width),
            "update_qkv_out",
            (norm_gains, first_gains, second_gains),
            (one_gate_up,),
        )
        one_qkv, one_out, two_qkv, two_out, next_qkv, next_out = updated[:6]
        one_gains, two_gains, next_gains = updated[6:]
    else:
        sums = lax.psum((*grad_qkv_out, grad_gate_up[0], grad_down[0].T), ("dp", "shard"))
        grad_qkv_out, grad_gains, grad_gate_up, grad_down = sums

        def own(grad, axis=0):
            size = grad.shape[axis] // groups
            return lax.dynamic_slice_in_dim(grad, owner * size, size, axis)

        one_qkv, two_qkv, next_qkv = adamw(
            w_qkv, first_qkv, second_qkv, own(grad_qkv_out[:, :QKV]), RATE_MATRIX, DECAY_MATRIX
        )
        one_out, two_out, next_out = adamw(
            w_out, first_out, second_out, own(grad_qkv_out[:, QKV:]), RATE_MATRIX, DECAY_MATRIX
        )
        one_gate_up, two_gate_up, next_gate_up = adamw(
            w_gate_up, first_gate_up, second_gate_up, own(grad_gate_up), RATE_MATRIX, DECAY_MATRIX
        )
        one_down, two_down, next_down = [
            a.T
            for a in adamw(
                w_down, first_down, second_down, own(grad_down), RATE_MATRIX, DECAY_MATRIX
            )
        ]
        one_gains, two_gains, next_gains = adamw(
            norm_gains, first_gains, second_gains, own(grad_gains, 1), RATE_GAIN, 0.0
        )
    one_down, two_down, next_down = one_down.T, two_down.T, next_down.T
    return (
        output.T[None],
        token_grad.T[None],
        one_qkv,
        one_out,
        one_gate_up,
        one_down,
        one_gains,
        two_qkv,
        two_out,
        two_gate_up,
        two_down,
        two_gains,
        next_qkv,
        next_out,
        next_gate_up,
        next_down,
        next_gains,
    )


def solution(mesh):
    return jax.shard_map(
        per_device,
        mesh=mesh,
        in_specs=(
            P(("dp", "shard"), None, None),
            P(("dp", "shard"), None),
            P(("dp", "shard"), None, None),
            P("shard", None),
            P("shard", None),
            P("shard", None),
            P("shard", None),
            P(None, "shard"),
            P("shard", None),
            P("shard", None),
            P("shard", None),
            P("shard", None),
            P(None, "shard"),
            P("shard", None),
            P("shard", None),
            P("shard", None),
            P("shard", None),
            P(None, "shard"),
        ),
        out_specs=(
            P(("dp", "shard"), None, None),
            P(("dp", "shard"), None, None),
            P("shard", None),
            P("shard", None),
            P("shard", None),
            P("shard", None),
            P(None, "shard"),
            P("shard", None),
            P("shard", None),
            P("shard", None),
            P("shard", None),
            P(None, "shard"),
            P("shard", None),
            P("shard", None),
            P("shard", None),
            P("shard", None),
            P(None, "shard"),
        ),
        check_vma=False,
    )
```

```python
import functools

import jax
import jax.numpy as jnp
import numpy as np
from jax import lax
from jax.experimental import pallas as pl
from jax.experimental.pallas import tpu as pltpu
from jax.sharding import PartitionSpec as P

HEADS = 9
KV_HEADS = 3
GROUP = HEADS // KV_HEADS
HEAD = 64
FF = 1536
STEP = 10
QUERY = HEADS * HEAD
ROPED = (HEADS + KV_HEADS) * HEAD
QKV = (HEADS + 2 * KV_HEADS) * HEAD
LANES = 128

EPS_NORM = 1e-05
ROPE_BASE = 100000.0
BETA_ONE = 0.9
BETA_TWO = 0.95
RATE_MATRIX = 0.1
RATE_GAIN = 0.3
DECAY_MATRIX = 0.1
EPS_ADAM = 1e-08
MASKED = -1e30
SCALE = float(HEAD) ** (-0.5)
VMEM_LIMIT = 32 * 1024 * 1024
HALF = 144
CUT_ROWS = 72
CUT_COLUMNS = 384
F32 = jnp.float32
BF16 = jnp.bfloat16


def rotate_block(values, cosine, signed_sine):
    lane = lax.broadcasted_iota(jnp.int32, values.shape, 1)
    swapped = jnp.where(
        lane % HEAD < HEAD // 2,
        pltpu.roll(values, LANES - HEAD // 2, 1),
        pltpu.roll(values, HEAD // 2, 1),
    )
    return values * cosine + swapped * signed_sine


def adamw(weight, first_moment, second_moment, gradient, step_rate, weight_decay):
    first_new = BETA_ONE * first_moment + (1.0 - BETA_ONE) * gradient
    second_new = BETA_TWO * second_moment + (1.0 - BETA_TWO) * gradient * gradient
    fix_one = 1.0 - BETA_ONE**STEP
    fix_two = 1.0 - BETA_TWO**STEP
    update = first_new / fix_one / (jnp.sqrt(second_new / fix_two) + EPS_ADAM)
    return (first_new, second_new, weight - step_rate * (update + weight_decay * weight))


def dot(left, right):
    return lax.dot_general(left, right, (((1,), (0,)), ((), ())), preferred_element_type=F32)


def dot_right_t(left, right):
    return lax.dot_general(left, right, (((1,), (1,)), ((), ())), preferred_element_type=F32)


def dot_left_t(left, right):
    return lax.dot_general(left, right, (((0,), (0,)), ((), ())), preferred_element_type=F32)


def norm_scale(values):
    return lax.rsqrt(jnp.mean(values * values, axis=-1, keepdims=True) + EPS_NORM)


def norm_back(grad_normed, normed, scale_rows):
    return scale_rows * (
        grad_normed - normed * jnp.mean(grad_normed * normed, axis=-1, keepdims=True)
    )


class Weight:
    def __init__(self, shape, whole=None, own=(), parts=(), place=None):
        self.shape, self.own, self.parts, self.place = shape, own, parts, place
        self.arrays = [whole] if whole is not None else [a[0] for a in (*own, *parts)]
        self.split = whole is None

    def load(self, idx, refs, full):
        if not self.split:
            return refs[0]
        for ref, (_, place) in zip(refs, self.own):
            self.put(full, place(idx[0]), ref[...].astype(BF16))
        for ref, (_, (core, x, low)) in zip(refs[len(self.own) :], self.parts):
            place = self.place(1 - idx[0], idx[1] ^ core, idx[2] ^ x, (idx[3] & 1) ^ low)
            rows = ref.shape[0] // HALF * HALF
            self.put(full, place, ref[:rows, :])
        return full

    def put(self, full, position, value):
        where = []
        for axis, tile in ((0, 16), (1, LANES)):
            at, size = position[axis], value.shape[axis]
            if size == self.shape[axis]:
                where.append(slice(None))
            elif isinstance(at, int):
                where.append(slice(at, at + size))
            else:
                where.append(pl.ds(pl.multiple_of(at, tile), size))
        full[tuple(where)] = value


def call(body, idx, arrays, weights, outs, scratch, busy, name, after=(), hand_on=False):
    counts = [len(w.arrays) for w in weights]
    flat = list(arrays) + [a for w in weights for a in w.arrays]
    outs = list(outs)
    split = [w for w in weights if w.split]
    hand_on = hand_on and bool(split)
    if hand_on:
        outs += [sds(split[-1].shape, BF16)]
    made = [pltpu.VMEM(w.shape, BF16) for w in (split[:-1] if hand_on else split)]

    def kernel(*refs):
        refs = list(refs)
        idx_ref = refs.pop(0)
        take = lambda n: [refs.pop(0) for _ in range(n)]
        array_refs = take(len(arrays))
        weight_refs = [take(n) for n in counts]
        take(len(after))
        out_refs = take(len(outs))
        own_scratch = take(len(scratch))
        fulls = take(len(made)) + ([out_refs.pop()] if hand_on else [])
        loads = [
            functools.partial(w.load, idx_ref, r, fulls.pop(0) if w.split else None)
            for w, r in zip(weights, weight_refs)
        ]
        body(idx_ref, array_refs, loads, out_refs, own_scratch)

    return pl.pallas_call(
        kernel,
        out_shape=tuple(outs),
        in_specs=[pl.BlockSpec(memory_space=pltpu.SMEM)]
        + [pl.BlockSpec(memory_space=pltpu.VMEM)] * len(flat)
        + [pl.BlockSpec(memory_space=pl.ANY)] * len(after),
        out_specs=tuple([pl.BlockSpec(memory_space=pltpu.VMEM)] * len(outs)),
        scratch_shapes=list(scratch) + made,
        compiler_params=pltpu.CompilerParams(vmem_limit_bytes=VMEM_LIMIT),
        cost_estimate=busy_for(busy),
        name=name,
    )(idx, *flat, *after)


def busy_for(microseconds):
    return pl.CostEstimate(flops=int(microseconds * 1e9), bytes_accessed=0, transcendentals=0)


def sds(shape, dtype):
    return jax.ShapeDtypeStruct(shape, dtype)


class Pieces:
    def __init__(self, place, parts=1, extra=0):
        self.place, self.parts, self.extra = place, parts, extra

    def outs(self):
        return [sds((self.parts, 2, 8, CUT_ROWS + self.extra, CUT_COLUMNS), BF16)] * 2

    def scratch(self, columns):
        return pltpu.VMEM((8, CUT_ROWS, columns), BF16)

    def store(self, blocks, grad, start=0):
        for i in range(8):
            rows = grad[i * CUT_ROWS : (i + 1) * CUT_ROWS].astype(BF16)
            blocks[i, :, start : start + grad.shape[1]] = rows

    def emit(self, idx, blocks, outs, under=None):
        for other_core, out in enumerate((outs[1], outs[0])):
            for part in range(self.parts):
                for owner in range(2):
                    for slot in range(8):
                        z = ((slot >> 1) & 1) | ((slot & 1) << 1)
                        block, column = self.place(
                            idx[0] ^ owner, idx[1] ^ other_core, idx[2] ^ (slot >> 2), idx[3] ^ z, part
                        )
                        columns = pl.ds(pl.multiple_of(column * CUT_COLUMNS, LANES), CUT_COLUMNS)
                        piece = blocks[block, :, columns]
                        if under is not None:
                            piece = jnp.concatenate(
                                [piece.astype(F32), under[idx[0] ^ owner]], axis=0
                            ).astype(BF16)
                        out[part, owner, slot] = piece


def head_stack(values, kv_head):
    first = kv_head * GROUP
    return jnp.concatenate(
        [values[:, (first + i) * HEAD : (first + i + 1) * HEAD] for i in range(GROUP)], axis=0
    )


def softmax_rows(query, key, allowed):
    scores = jnp.where(allowed, dot_right_t(query, key) * SCALE, MASKED)
    top = jnp.max(scores, axis=-1, keepdims=True)
    exponent = jnp.exp(scores - top)
    return exponent / jnp.sum(exponent, axis=-1, keepdims=True)


def pack_kernel(body, idx, sources, places, outs, name, after=()):
    windows = [shape for shape, _ in places]

    def kernel(idx_ref, *refs):
        sources_in, refs = refs[: len(sources)], refs[len(sources) + len(after) :]
        out_refs, buffers, sem = refs[: len(outs)], refs[len(outs) : -1], refs[-1]
        copies = []
        for i, (source, (shape, place)) in enumerate(zip(sources_in, places)):
            where = []
            for axis, tile in ((0, 8), (1, LANES)):
                if shape[axis] == source.shape[axis]:
                    where.append(slice(None))
                else:
                    where.append(pl.ds(pl.multiple_of(place(idx_ref)[axis], tile), shape[axis]))
            copies.append(pltpu.make_async_copy(source.at[tuple(where)], buffers[i], sem.at[i]))
        for copy in copies:
            copy.start()
        for copy in copies:
            copy.wait()
        body(idx_ref, buffers, out_refs)

    return pl.pallas_call(
        kernel,
        out_shape=tuple(outs),
        in_specs=[pl.BlockSpec(memory_space=pltpu.SMEM)]
        + [pl.BlockSpec(memory_space=pltpu.HBM)] * len(sources)
        + [pl.BlockSpec(memory_space=pl.ANY)] * len(after),
        out_specs=tuple([pl.BlockSpec(memory_space=pltpu.VMEM)] * len(outs)),
        scratch_shapes=[pltpu.VMEM(w, F32) for w in windows]
        + [pltpu.SemaphoreType.DMA((len(sources),))],
        compiler_params=pltpu.CompilerParams(vmem_limit_bytes=VMEM_LIMIT),
        cost_estimate=busy_for(10),
        name=name,
    )(idx, *sources, *after)


def cast_out(idx_ref, buffers, outs):
    outs[0][...] = buffers[0][...].astype(BF16)


def pack_gate_up(idx, w_gate_up):
    window = ((HALF, FF), lambda i: (i[1] * HALF, i[2] * FF))
    return pack_kernel(
        cast_out, idx, [w_gate_up], [window], [sds((HALF, FF), BF16)], "pack_gate_up"
    )[0]


def pack_down(idx, down_t, after):
    shape = (HALF, down_t.shape[1])
    window = (shape, lambda i: ((i[1] * 2 + (i[3] & 1)) * HALF, 0))
    return pack_kernel(cast_out, idx, [down_t], [window], [sds(shape, BF16)], "pack_down", after)[0]


def pack_qkv_out(idx, w_qkv, w_out, norm_gains, after):
    columns = (QKV + w_out.shape[1]) // 2
    windows = [((HALF, m.shape[1]), lambda i: (i[1] * HALF, 0)) for m in (w_qkv, w_out)]
    windows.append((norm_gains.shape, lambda i: (0, 0)))

    def body(idx_ref, buffers, outs):
        q_ref, o_ref, gains_ref = buffers
        both = jnp.concatenate([q_ref[:, columns:], o_ref[...]], axis=1)
        outs[0][:HALF, :] = jnp.where((idx_ref[3] & 1) == 0, q_ref[:, :columns], both).astype(BF16)
        outs[0][HALF:, :] = jnp.zeros((16, columns), BF16)
        outs[0][HALF : HALF + 2, : gains_ref.shape[1]] = gains_ref[...].astype(BF16)

    outs = [sds((HALF + 16, columns), BF16)]
    return pack_kernel(
        body, idx, [w_qkv, w_out, norm_gains], windows, outs, "pack_qkv_out", after
    )[0]


def attention_forward(idx, tokens_t, segments, frequency, gains, w_qkv_out):
    width, seq_length = tokens_t.shape
    split_gains = len(gains) > 1

    def body(idx_ref, arrays, loads, outs, scratch):
        x_ref, seg_ref, freq_ref = arrays[:3]
        qkv_ref, o_ref, cos_ref, sin_ref, allowed_ref, gains_ref = outs
        if split_gains:
            own = arrays[3][...].astype(BF16).astype(F32)
            other = arrays[4][HALF : HALF + 8, : width // 2].astype(F32)[:2]
            gains_ref[...] = jnp.where(
                idx_ref[0] == 0,
                jnp.concatenate([own, other], axis=1),
                jnp.concatenate([other, own], axis=1),
            )
        else:
            gains_ref[...] = arrays[3][...]
        seen_doc = jnp.broadcast_to(seg_ref[...], (seq_length, seq_length))
        own_doc = seen_doc.T
        token = lax.broadcasted_iota(jnp.int32, (seq_length, seq_length), 0)
        seen = lax.broadcasted_iota(jnp.int32, (seq_length, seq_length), 1)
        begin = jnp.sum((seen_doc < own_doc).astype(F32), axis=-1, keepdims=True)
        angles = (token.astype(F32) - begin) * freq_ref[...]
        cosine, sine = jnp.cos(angles), jnp.sin(angles)
        sine = jnp.where(seen % HEAD < HEAD // 2, -sine, sine)
        cos_ref[...] = cosine
        sin_ref[...] = sine
        allowed = ((seen_doc == own_doc) & (token >= seen)).astype(F32)
        allowed_ref[...] = allowed
        allowed = jnp.concatenate([allowed] * GROUP, axis=0) > 0.5
        x = x_ref[...].astype(F32).T
        h1 = (x * norm_scale(x) * gains_ref[0:1, :]).astype(BF16)
        projected = dot(h1, loads[0]()[:, :QKV])
        for start in range(0, ROPED, LANES):
            block = projected[:, start : start + LANES]
            qkv_ref[:, start : start + LANES] = rotate_block(block, cosine, sine).astype(BF16)
        qkv_ref[:, ROPED:QKV] = projected[:, ROPED:QKV].astype(BF16)
        qkv = qkv_ref[...]
        for kv in range(KV_HEADS):
            key = qkv[:, QUERY + kv * HEAD : QUERY + (kv + 1) * HEAD]
            value = qkv[:, ROPED + kv * HEAD : ROPED + (kv + 1) * HEAD]
            probs = softmax_rows(head_stack(qkv, kv), key, allowed).astype(BF16)
            attended = dot(probs, value).astype(BF16)
            for i in range(GROUP):
                start = (kv * GROUP + i) * HEAD
                o_ref[:, start : start + HEAD] = attended[i * seq_length : (i + 1) * seq_length]

    square = sds((seq_length, seq_length), F32)
    outs = [sds((seq_length, QKV), BF16), sds((seq_length, QUERY), BF16)]
    outs += [square, square, square, sds((2, width), F32)]
    return call(
        body,
        idx,
        [tokens_t, segments, frequency, *gains],
        [w_qkv_out],
        outs,
        [],
        10,
        "attention",
        hand_on=True,
    )


def feed_forward(idx, tokens_t, attended, gains, cotangent_t, w_qkv_out, w_gate_up, pieces, after):
    width, seq_length = tokens_t.shape

    def body(idx_ref, arrays, loads, outs, scratch):
        x_ref, o_ref, gains_ref, y_ref = arrays
        u_ref, h2_ref, ab_ref, z_ref = outs[:4]
        u = x_ref[...].astype(F32).T + dot(o_ref[...], loads[0]()[:, QKV:])
        u_ref[...] = u
        h2 = (u * norm_scale(u) * gains_ref[1:2, :]).astype(BF16)
        h2_ref[...] = h2
        ab = dot(h2, loads[1]()[...])
        ab_ref[...] = ab
        gate, up = ab[:, :FF], ab[:, FF:]
        z = (gate * jax.nn.sigmoid(gate) * up).astype(BF16)
        z_ref[...] = z
        grad = dot(y_ref[...], z)
        if pieces is None:
            outs[4][...] = grad
        else:
            pieces.store(scratch[0], grad)
            pieces.emit(idx_ref, scratch[0], outs[4:])

    outs = [
        sds((seq_length, width), F32),
        sds((seq_length, width), BF16),
        sds((seq_length, 2 * FF), F32),
        sds((seq_length, FF), BF16),
    ]
    outs += [sds((width, FF), F32)] if pieces is None else pieces.outs()
    scratch = [] if pieces is None else [pieces.scratch(FF)]
    return call(
        body,
        idx,
        [tokens_t, attended, gains, cotangent_t],
        [w_qkv_out, w_gate_up],
        outs,
        scratch,
        20,
        "feed_forward",
        after,
        True,
    )


def feed_back(idx, ab, normed_low, hidden, middle, cotangent_t, down_t, pieces):
    width, seq_length = cotangent_t.shape

    def body(idx_ref, arrays, loads, outs, scratch):
        ab_ref, h2_ref, z_ref, u_ref, y_ref = arrays
        gg_ref, out_ref = outs[:2]
        down = loads[0]()
        gate, up = ab_ref[:, :FF], ab_ref[:, FF:]
        sig = jax.nn.sigmoid(gate)
        grad_hidden = dot_left_t(y_ref[...], down[...])
        gg_ref[:, :FF] = (grad_hidden * up * sig * (1.0 + gate * (1.0 - sig))).astype(BF16)
        gg_ref[:, FF:] = (grad_hidden * gate * sig).astype(BF16)
        grad = dot_left_t(h2_ref[...], gg_ref[...])
        if pieces is None:
            outs[2][...] = grad
        else:
            pieces.store(scratch[0], grad)
            pieces.emit(idx_ref, scratch[0], outs[2:])
        out_ref[...] = (u_ref[...] + dot_right_t(z_ref[...], down[...])).T.astype(BF16)

    outs = [sds((seq_length, 2 * FF), BF16), sds((width, seq_length), BF16)]
    outs += [sds((width, 2 * FF), F32)] if pieces is None else pieces.outs()
    scratch = [] if pieces is None else [pieces.scratch(2 * FF)]
    return call(
        body,
        idx,
        [ab, normed_low, hidden, middle, cotangent_t],
        [down_t],
        outs,
        scratch,
        20,
        "feed_back",
    )


def middle_back(idx, cotangent_t, middle, gated, gains, w_gate_up, w_qkv_out, after):
    width, seq_length = cotangent_t.shape

    def body(idx_ref, arrays, loads, outs, scratch):
        y_ref, u_ref, gg_ref, gains_ref = arrays
        gu_ref, go_ref, gain_ref = outs
        u = u_ref[...]
        scale_two = norm_scale(u)
        normed = u * scale_two
        grad_normed = dot_right_t(gg_ref[...], loads[0]()[...])
        gain_ref[...] = jnp.sum(grad_normed * normed, axis=0, keepdims=True)
        gu = y_ref[...].astype(F32).T + norm_back(
            grad_normed * gains_ref[1:2, :], normed, scale_two
        )
        gu_ref[...] = gu
        go_ref[...] = dot_right_t(gu.astype(BF16), loads[1]()[:, QKV:]).astype(BF16)

    outs = [sds((seq_length, width), F32), sds((seq_length, width), BF16), sds((1, width), F32)]
    return call(
        body,
        idx,
        [cotangent_t, middle, gated, gains],
        [w_gate_up, w_qkv_out],
        outs,
        [],
        20,
        "middle_back",
        after,
    )


def attention_back(
    idx, tokens_t, grad_middle, grad_attended, gain_two, qkv, attended, tables, gains, w_qkv, pieces, after
):
    width, seq_length = tokens_t.shape

    def body(idx_ref, arrays, loads, outs, scratch):
        x_ref, gu_ref, go_ref, gain_two_ref, qkv_ref, o_ref = arrays[:6]
        cos_ref, sin_ref, allowed_ref, gains_ref = arrays[6:]
        grad_ref = outs[0]
        grad_proj, gp_ref, gain_rows, *blocks = scratch
        gu, go = gu_ref[...], go_ref[...]
        gu_low = gu.astype(BF16)
        grad_gain_two = gain_two_ref[...]
        allowed = jnp.concatenate([allowed_ref[...]] * GROUP, axis=0) > 0.5
        qkv_values = qkv_ref[...]
        for kv in range(KV_HEADS):
            key = qkv_values[:, QUERY + kv * HEAD : QUERY + (kv + 1) * HEAD]
            value = qkv_values[:, ROPED + kv * HEAD : ROPED + (kv + 1) * HEAD]
            query = head_stack(qkv_values, kv)
            grad_out = head_stack(go, kv)
            probs = softmax_rows(query, key, allowed)
            grad_probs = dot_right_t(grad_out, value)
            row_delta = jnp.sum(probs * grad_probs, axis=-1, keepdims=True)
            gs = (probs * (grad_probs - row_delta)).astype(BF16)
            grad_query = dot(gs, key) * SCALE
            for i in range(GROUP):
                start = (kv * GROUP + i) * HEAD
                grad_proj[:, start : start + HEAD] = grad_query[
                    i * seq_length : (i + 1) * seq_length
                ]
            start = QUERY + kv * HEAD
            grad_proj[:, start : start + HEAD] = dot_left_t(gs, query) * SCALE
            start = ROPED + kv * HEAD
            grad_proj[:, start : start + HEAD] = dot_left_t(probs.astype(BF16), grad_out)
        for start in range(0, ROPED, LANES):
            gp_ref[:, start : start + LANES] = rotate_block(
                grad_proj[:, start : start + LANES], cos_ref[...], -sin_ref[...]
            ).astype(BF16)
        gp_ref[:, ROPED:QKV] = grad_proj[:, ROPED:QKV].astype(BF16)
        x = x_ref[...].astype(F32).T
        scale_one = norm_scale(x)
        normed = x * scale_one
        h1 = (normed * gains_ref[0:1, :]).astype(BF16)
        grad_qkv = dot_left_t(h1, gp_ref[...])
        grad_out = dot_left_t(o_ref[...], gu_low)
        grad_normed = dot_right_t(gp_ref[...], loads[0]()[:, :QKV])
        grad_gain_one = jnp.sum(grad_normed * normed, axis=0, keepdims=True)
        if pieces is None:
            outs[1][:, :QKV] = grad_qkv
            outs[1][:, QKV:] = grad_out
            outs[2][0:1, :] = grad_gain_one
            outs[2][1:2, :] = grad_gain_two
        else:
            pieces.store(blocks[0], grad_qkv)
            pieces.store(blocks[0], grad_out, QKV)
            half = width // 2
            gain_rows[...] = jnp.zeros_like(gain_rows)
            for owner in range(2):
                columns = slice(owner * half, (owner + 1) * half)
                gain_rows[owner, 0:1, :half] = grad_gain_one[:, columns]
                gain_rows[owner, 1:2, :half] = grad_gain_two[:, columns]
            pieces.emit(idx_ref, blocks[0], outs[1:], gain_rows)
        grad_ref[...] = (
            (gu + norm_back(grad_normed * gains_ref[0:1, :], normed, scale_one)).T
        ).astype(BF16)

    outs = [sds((width, seq_length), BF16)]
    scratch = [
        pltpu.VMEM((seq_length, QKV), F32),
        pltpu.VMEM((seq_length, QKV), BF16),
        pltpu.VMEM((2, 8, CUT_COLUMNS), F32),
    ]
    if pieces is None:
        outs += [sds((width, QKV + width), F32), sds((2, width), F32)]
    else:
        outs += pieces.outs()
        scratch += [pieces.scratch(QKV + width)]
    return call(
        body,
        idx,
        [tokens_t, grad_middle, grad_attended, gain_two, qkv, attended, *tables, gains],
        [w_qkv],
        outs,
        scratch,
        20,
        "attention_back",
        after,
    )


def step(body, arrays, outs, name, after=()):
    def kernel(*refs):
        body(refs[: len(arrays)], refs[len(arrays) + len(after) :])

    return pl.pallas_call(
        kernel,
        out_shape=tuple(outs),
        in_specs=[pl.BlockSpec(memory_space=pltpu.VMEM)] * len(arrays)
        + [pl.BlockSpec(memory_space=pl.ANY)] * len(after),
        out_specs=tuple([pl.BlockSpec(memory_space=pltpu.VMEM)] * len(outs)),
        compiler_params=pltpu.CompilerParams(vmem_limit_bytes=VMEM_LIMIT),
        cost_estimate=busy_for(4),
        name=name,
    )(*arrays, *after)


def add_split(keep, arrived, axis, send_ref, keep_ref):
    total = keep[...].astype(F32) + arrived[...].astype(F32)
    low, high = lax.index_in_dim(total, 0, axis, False), lax.index_in_dim(total, 1, axis, False)
    send_ref[...] = high.astype(BF16)
    keep_ref[...] = low


def add_step(jobs, name, after):
    arrays, outs = [], []
    for keep, arrived, axis in jobs:
        arrays += [keep, arrived]
        shape = keep.shape[:axis] + keep.shape[axis + 1 :]
        outs += [sds(shape, BF16), sds(shape, F32)]

    def body(ins, out_refs):
        for i, (_, _, axis) in enumerate(jobs):
            add_split(ins[2 * i], ins[2 * i + 1], axis, out_refs[2 * i], out_refs[2 * i + 1])

    flat = step(body, arrays, outs, name, after)
    return [(flat[2 * i], flat[2 * i + 1]) for i in range(len(jobs))]


def update_state(idx, near, far, parts, blocks, puts, state, shape, name, gains=(), after=()):
    count = len(state) // 3
    height, width = near.shape[3:]

    def kernel(idx_ref, *refs):
        part_refs, refs = refs[: 2 * len(parts)], refs[2 * len(parts) :]
        state_refs, refs = refs[: 3 * count], refs[3 * count :]
        gain_refs, refs = refs[: len(gains)], refs[len(gains) + len(after) :]
        outs, refs = refs[: 3 * count], refs[3 * count :]
        gain_outs, full = refs[: len(gains)], refs[-1]
        is_near = pl.program_id(0) % 2 == idx_ref[1]
        for i, put in enumerate(puts):
            for z in range(4):
                rel = z ^ idx_ref[3]
                slot = (rel & 1) * 2 + (rel >> 1)
                piece = jnp.where(
                    is_near,
                    part_refs[2 * i][0, 0, slot].astype(F32),
                    part_refs[2 * i + 1][0, 0, slot].astype(F32),
                )
                put(full, z, piece)
        start = 0
        for i in range(count):
            columns = state_refs[i].shape[1]
            first, second, new = adamw(
                state_refs[i][...],
                state_refs[count + i][...],
                state_refs[2 * count + i][...],
                full[: state_refs[i].shape[0], start : start + columns],
                RATE_MATRIX,
                DECAY_MATRIX,
            )
            start += columns
            outs[i][...] = first
            outs[count + i][...] = second
            outs[2 * count + i][...] = new
        if gains:

            @pl.when(pl.program_id(0) == 0)
            def _():
                gradient = full[CUT_ROWS : CUT_ROWS + 2, : gain_refs[0].shape[1]]
                first, second, new = adamw(
                    gain_refs[0][...], gain_refs[1][...], gain_refs[2][...], gradient, RATE_GAIN, 0.0
                )
                gain_outs[0][...] = first
                gain_outs[1][...] = second
                gain_outs[2][...] = new

    state_specs = [pl.BlockSpec(*blocks[i]) for i in range(count)] * 3
    gain_specs = [pl.BlockSpec(g.shape, lambda t, _: (0, 0)) for g in gains]
    part_specs = [
        pl.BlockSpec((1, 1, 4, height, width), lambda t, i, p=p: (p, (t // 2) ^ i[2], 0, 0, 0))
        for p in parts
        for _ in range(2)
    ]
    moved = sum(a.size * 8 for a in state)
    return pl.pallas_call(
        kernel,
        grid_spec=pltpu.PrefetchScalarGridSpec(
            num_scalar_prefetch=1,
            grid=(4,),
            in_specs=part_specs
            + state_specs
            + gain_specs
            + [pl.BlockSpec(memory_space=pl.ANY)] * len(after),
            out_specs=tuple(state_specs + gain_specs),
            scratch_shapes=[pltpu.VMEM(shape, F32)],
        ),
        out_shape=tuple(sds(a.shape, F32) for a in [*state, *gains]),
        compiler_params=pltpu.CompilerParams(vmem_limit_bytes=VMEM_LIMIT),
        cost_estimate=pl.CostEstimate(flops=0, bytes_accessed=moved, transcendentals=0),
        name=name,
    )(idx, *[near, far] * len(parts), *state, *gains, *after)


def swap(values, axis, mask):
    size = lax.axis_size(axis)
    return lax.ppermute(values, axis, [(i, i ^ mask) for i in range(size)])


over_y = functools.partial(swap, axis="shard", mask=1)
over_core = functools.partial(swap, axis="dp", mask=1)
over_x = functools.partial(swap, axis="dp", mask=2)
over_z_low = functools.partial(swap, axis="dp", mask=4)
over_z_high = functools.partial(swap, axis="dp", mask=8)


def per_device(
    tokens,
    segments,
    cotangent,
    w_qkv,
    w_out,
    w_gate_up,
    w_down,
    norm_gains,
    first_qkv,
    first_out,
    first_gate_up,
    first_down,
    first_gains,
    second_qkv,
    second_out,
    second_gate_up,
    second_down,
    second_gains,
):
    groups = lax.axis_size("shard")
    replicas = lax.axis_size("dp")
    fast = groups == 2 and replicas == 16
    place_dp = lax.axis_index("dp")
    owner = lax.axis_index("shard")
    idx = jnp.stack([owner, place_dp & 1, (place_dp >> 1) & 1, place_dp >> 2]).astype(jnp.int32)
    x_t, y_t = tokens[0].T, cotangent[0].T
    width, seq_length = x_t.shape
    rows, down_rows = w_qkv.shape[0], w_down.shape[0]
    down_t, first_down_t, second_down_t = w_down.T, first_down.T, second_down.T
    half_size = HEAD // 2
    frequency = ROPE_BASE ** (-(np.arange(half_size) * 2.0 / HEAD))
    frequency = jnp.asarray(np.tile(frequency, 4)[None], F32)
    if fast:
        gate_up = pack_gate_up(idx, w_gate_up)
        gate_up_near = over_y(gate_up)
        qo_near = over_y(pack_qkv_out(idx, w_qkv, w_out, norm_gains, (gate_up,)))
        down_near = over_y(pack_down(idx, down_t, (gate_up_near,)))
        gate_up_near_x = over_x(gate_up_near)
        gate_up_far, gate_up_far_x = over_core(gate_up_near), over_core(gate_up_near_x)
        qo_near_low = over_z_low(qo_near)
        qo_far, qo_far_low = over_core(qo_near), over_core(qo_near_low)
        gains = (norm_gains, qo_near)
        own_rows = lambda o: (o * rows, 0)
        own_rows_out = lambda o: (o * rows, QKV)
        mat_qkv_out = Weight(
            (width, QKV + width),
            own=[(w_qkv, own_rows), (w_out, own_rows_out)],
            parts=[
                (qo_near, (0, 0, 0)),
                (qo_near_low, (0, 0, 1)),
                (qo_far, (1, 0, 0)),
                (qo_far_low, (1, 0, 1)),
            ],
            place=lambda o, c, x, low: (o * rows + c * HALF, low * ((QKV + width) // 2)),
        )
        mat_gate_up = Weight(
            (width, 2 * FF),
            own=[(w_gate_up, own_rows)],
            parts=[
                (gate_up_near, (0, 0, 0)),
                (gate_up_near_x, (0, 1, 0)),
                (gate_up_far, (1, 0, 0)),
                (gate_up_far_x, (1, 1, 0)),
            ],
            place=lambda o, c, x, low: (o * rows + c * HALF, x * FF),
        )
        cut_qkv_out = Pieces(lambda o, c, x, z, p: (o * 4 + c * 2 + x, z), extra=8)
        cut_gate_up = Pieces(lambda o, c, x, z, p: (o * 4 + c * 2 + p, x * 4 + z), parts=2)
        cut_down = Pieces(lambda o, c, x, z, p: (c * 4 + x * 2 + (z >> 1), o * 2 + (z & 1)))
    else:
        gains = (
            lax.all_gather(norm_gains.astype(BF16), "shard", axis=1, tiled=True).astype(F32),
        )
        mat_qkv, mat_out, mat_gate_up, mat_down = [
            lax.all_gather(m.astype(BF16), "shard", axis=0, tiled=True)
            for m in (w_qkv, w_out, w_gate_up, w_down)
        ]
        mat_qkv_out, mat_gate_up, mat_down = [
            Weight(m.shape, whole=m)
            for m in (jnp.concatenate([mat_qkv, mat_out], axis=1), mat_gate_up, mat_down.T)
        ]
        cut_qkv_out = cut_gate_up = cut_down = None

    qkv, attended, *tables, gains, whole = attention_forward(
        idx, x_t, segments, frequency, gains, mat_qkv_out
    ) + (() if fast else (None,))
    after = ()
    if fast:
        mat_qkv_out = Weight(whole.shape, whole=whole)

        def pass_on(ins, outs):
            outs[0][...] = ins[0][...]

        (down_near,) = step(
            pass_on, [down_near], [sds(down_near.shape, BF16)], "pass_on", (attended,)
        )
        down_near_low = over_z_low(down_near)
        after = (down_near,)
    middle, normed_low, ab, hidden, *grad_down = feed_forward(
        idx, x_t, attended, gains, y_t, mat_qkv_out, mat_gate_up, cut_down, after
    )
    if fast:
        whole = grad_down.pop()
        mat_gate_up = Weight(whole.shape, whole=whole)
        mat_down = Weight(
            (width, FF),
            own=[(down_t, lambda o: (0, o * down_rows))],
            parts=[
                (down_near, (0, 0, 0)),
                (down_near_low, (0, 0, 1)),
                (over_core(down_near), (1, 0, 0)),
                (over_core(down_near_low), (1, 0, 1)),
            ],
            place=lambda o, c, x, low: ((c * 2 + low) * HALF, o * down_rows),
        )
    if fast:
        arrived_down = over_core(grad_down[0])
    gated, output, *grad_gate_up = feed_back(
        idx, ab, normed_low, hidden, middle, y_t, mat_down, cut_gate_up
    )
    if fast:
        cut = lambda a, *lead: a.reshape(*lead, *a.shape[-2:])
        arrived_gate_up = over_core(grad_gate_up[0])
        ((send, keep_down),) = add_step(
            [(grad_down[1][0], arrived_down[0], 0)], "down_core", (gated,)
        )
        arrived_down = over_y(send)
        after = (keep_down,)
    grad_middle, grad_attended, gain_two = middle_back(
        idx, y_t, middle, gated, gains, mat_gate_up, mat_qkv_out, after
    )
    if fast:
        halves = [
            [cut(a[p], *lead) for a in (grad_gate_up[1], arrived_gate_up)]
            for p, lead in ((0, (2, 2, 4)), (1, (4, 2, 2)))
        ]
        (send_up, keep_up), (send_low, keep_low) = add_step(
            [(*halves[0], 1), (*halves[1], 1)], "gate_up_core", (grad_middle,)
        )
        arrived_up, arrived_low = over_x(send_up), over_z_low(send_low)
        after = (keep_up,)
    token_grad, *grad_qkv_out = attention_back(
        idx,
        x_t,
        grad_middle,
        grad_attended,
        gain_two,
        qkv,
        attended,
        tables,
        gains,
        mat_qkv_out,
        cut_qkv_out,
        after,
    )
    if fast:

        def put_down(full, z, piece):
            full[(z >> 1) * CUT_ROWS : ((z >> 1) + 1) * CUT_ROWS, pl.ds((z & 1) * 384, 384)] = piece

        def put_upper(full, z, piece):
            full[:CUT_ROWS, pl.ds(z * 384, 384)] = piece

        def put_lower(full, z, piece):
            full[CUT_ROWS:, pl.ds(z * 384, 384)] = piece

        def put_columns(full, z, piece):
            full[:, pl.ds(z * 384, 384)] = piece

        arrived_qkv_out = over_core(grad_qkv_out[0])
        ((send, keep_down),) = add_step(
            [(cut(keep_down, 2, 4), cut(arrived_down, 2, 4), 0)], "down_y", (token_grad,)
        )
        arrived_down = over_x(send)
        ((send, keep_qkv_out),) = add_step(
            [(grad_qkv_out[1][0], arrived_qkv_out[0], 0)], "qkv_out_core", (keep_down,)
        )
        arrived_qkv_out = over_y(send)
        (send_up, keep_up), (send_low, keep_low) = add_step(
            [
                (cut(keep_up, 2, 2, 2), cut(arrived_up, 2, 2, 2), 1),
                (cut(keep_low, 2, 2, 2), cut(arrived_low, 2, 2, 2), 1),
            ],
            "up_x_low_z",
            (keep_qkv_out,),
        )
        arrived_up, arrived_low = over_z_low(send_up), over_x(send_low)
        (send, keep_down), (send_up, keep_up), (send_low, keep_low) = add_step(
            [
                (cut(keep_down, 2, 2), cut(arrived_down, 2, 2), 0),
                (keep_up, arrived_up, 0),
                (keep_low, arrived_low, 0),
            ],
            "down_x_up_z_low_x",
            (keep_up,),
        )
        arrived_down, arrived_up, arrived_low = over_z_low(send), over_y(send_up), over_y(send_low)
        ((send, keep_qkv_out),) = add_step(
            [(cut(keep_qkv_out, 2, 4), cut(arrived_qkv_out, 2, 4), 0)], "qkv_out_y", (keep_down,)
        )
        arrived_qkv_out = over_x(send)

        piece = (CUT_ROWS, CUT_COLUMNS)
        taller = (CUT_ROWS + 8, CUT_COLUMNS)

        def last_sums(ins, outs):
            for i in range(3):
                total = ins[2 * i][...] + ins[2 * i + 1][...].astype(F32)
                outs[0][i] = total[1].astype(BF16)
                outs[1][i] = total[0]

        send, keep = step(
            last_sums,
            [keep_down, arrived_down, keep_up, arrived_up, keep_low, arrived_low],
            [sds((3, *piece), BF16), sds((3, *piece), F32)],
            "down_z_up_y_low_y",
            (keep_qkv_out,),
        )
        arrived = over_z_high(send)
        ((send, keep_qkv_out),) = add_step(
            [(cut(keep_qkv_out, 2, 2), cut(arrived_qkv_out, 2, 2), 0)], "qkv_out_x", (keep,)
        )
        arrived_qkv_out = over_z_low(send)

        def make_pieces(ins, outs):
            outs[0][...] = (ins[0][...] + ins[1][...].astype(F32)).astype(BF16)
            total = ins[2][...] + ins[3][...].astype(F32)
            outs[1][...] = total[1].astype(BF16)
            outs[2][...] = total[0]

        pieces, send, keep_qkv_out = step(
            make_pieces,
            [keep, arrived, keep_qkv_out, arrived_qkv_out],
            [sds((3, *piece), BF16), sds(taller, BF16), sds(taller, F32)],
            "pieces_qkv_out_z",
        )
        pieces_high, arrived_qkv_out = over_z_high(pieces), over_z_high(send)

        def share_high(ins, outs):
            outs[0][0], outs[0][1] = ins[0][0], ins[1][0]
            for part in range(2):
                outs[1][part, 0], outs[1][part, 1] = ins[0][part + 1], ins[1][part + 1]
            outs[2][...] = (ins[2][...] + ins[3][...].astype(F32)).astype(BF16)

        near_down, near_gate_up, piece_qkv_out = step(
            share_high,
            [pieces, pieces_high, keep_qkv_out, arrived_qkv_out],
            [sds((2, *piece), BF16), sds((2, 2, *piece), BF16), sds(taller, BF16)],
            "share_z_high",
        )
        down_low, gate_up_x = over_z_low(near_down), over_x(near_gate_up)
        qkv_out_high = over_z_high(piece_qkv_out)

        def share_next(ins, outs):
            outs[0][0], outs[0][1] = ins[0][...], ins[1][...]
            for part in range(2):
                outs[1][part, 0], outs[1][part, 1] = ins[2][part], ins[3][part]
            outs[2][0], outs[2][1] = ins[4][...], ins[5][...]

        near_down, near_gate_up, near_qkv_out = step(
            share_next,
            [near_down, down_low, near_gate_up, gate_up_x, piece_qkv_out, qkv_out_high],
            [sds((2, 2, *piece), BF16), sds((2, 2, 2, *piece), BF16), sds((2, *taller), BF16)],
            "share_next",
        )
        down_x, gate_up_low = over_x(near_down), over_z_low(near_gate_up)
        qkv_out_x = over_x(near_qkv_out)

        def share_last(ins, outs):
            for x in range(2):
                for low in range(2):
                    for high in range(2):
                        slot = low * 2 + high
                        outs[0][0, x, slot] = ins[x][low, high]
                        for part in range(2):
                            outs[1][part, x, slot] = ins[2 + low][part, x, high]
            outs[2][0], outs[2][1] = ins[4][...], ins[5][...]

        near_down, near_gate_up, near_qkv_out = step(
            share_last,
            [near_down, down_x, near_gate_up, gate_up_low, near_qkv_out, qkv_out_x],
            [sds((1, 2, 4, *piece), BF16), sds((2, 2, 4, *piece), BF16), sds((2, 2, *taller), BF16)],
            "share_last",
        )
        far_down, far_gate_up = over_core(near_down), over_core(near_gate_up)
        qkv_out_low = over_z_low(near_qkv_out)
        by_row = lambda t, _: ((t % 2) * 2 + t // 2, 0)
        one_down, two_down, next_down = update_state(
            idx,
            near_down,
            far_down,
            (0,),
            [((HALF, down_rows), by_row)],
            (put_down,),
            [down_t, first_down_t, second_down_t],
            (HALF, down_rows),
            "update_down",
        )

        def share_qkv_out(ins, outs):
            for x in range(2):
                for low in range(2):
                    for high in range(2):
                        outs[0][0, x, low * 2 + high] = ins[low][x, high]

        (near_qkv_out,) = step(
            share_qkv_out,
            [near_qkv_out, qkv_out_low],
            [sds((1, 2, 4, *taller), BF16)],
            "share_qkv_out",
            (one_down,),
        )
        far_qkv_out = over_core(near_qkv_out)
        one_gate_up, two_gate_up, next_gate_up = update_state(
            idx,
            near_gate_up,
            far_gate_up,
            (0, 1),
            [((HALF, FF), lambda t, _: (t % 2, t // 2))],
            (put_upper, put_lower),
            [w_gate_up, first_gate_up, second_gate_up],
            (HALF, FF),
            "update_gate_up",
            (),
            (near_qkv_out,),
        )
        updated = update_state(
            idx,
            near_qkv_out,
            far_qkv_out,
            (0,),
            [((CUT_ROWS, QKV), by_row), ((CUT_ROWS, width), by_row)],
            (put_columns,),
            [w_qkv, w_out, first_qkv, first_out, second_qkv, second_out],
            (CUT_ROWS + 8, QKV + width),
            "update_qkv_out",
            (norm_gains, first_gains, second_gains),
            (one_gate_up,),
        )
        one_qkv, one_out, two_qkv, two_out, next_qkv, next_out = updated[:6]
        one_gains, two_gains, next_gains = updated[6:]
    else:
        sums = lax.psum((*grad_qkv_out, grad_gate_up[0], grad_down[0].T), ("dp", "shard"))
        grad_qkv_out, grad_gains, grad_gate_up, grad_down = sums

        def own(grad, axis=0):
            size = grad.shape[axis] // groups
            return lax.dynamic_slice_in_dim(grad, owner * size, size, axis)

        one_qkv, two_qkv, next_qkv = adamw(
            w_qkv, first_qkv, second_qkv, own(grad_qkv_out[:, :QKV]), RATE_MATRIX, DECAY_MATRIX
        )
        one_out, two_out, next_out = adamw(
            w_out, first_out, second_out, own(grad_qkv_out[:, QKV:]), RATE_MATRIX, DECAY_MATRIX
        )
        one_gate_up, two_gate_up, next_gate_up = adamw(
            w_gate_up, first_gate_up, second_gate_up, own(grad_gate_up), RATE_MATRIX, DECAY_MATRIX
        )
        one_down, two_down, next_down = [
            a.T
            for a in adamw(
                w_down, first_down, second_down, own(grad_down), RATE_MATRIX, DECAY_MATRIX
            )
        ]
        one_gains, two_gains, next_gains = adamw(
            norm_gains, first_gains, second_gains, own(grad_gains, 1), RATE_GAIN, 0.0
        )
    one_down, two_down, next_down = one_down.T, two_down.T, next_down.T
    return (
        output.T[None],
        token_grad.T[None],
        one_qkv,
        one_out,
        one_gate_up,
        one_down,
        one_gains,
        two_qkv,
        two_out,
        two_gate_up,
        two_down,
        two_gains,
        next_qkv,
        next_out,
        next_gate_up,
        next_down,
        next_gains,
    )


def solution(mesh):
    return jax.shard_map(
        per_device,
        mesh=mesh,
        in_specs=(
            P(("dp", "shard"), None, None),
            P(("dp", "shard"), None),
            P(("dp", "shard"), None, None),
            P("shard", None),
            P("shard", None),
            P("shard", None),
            P("shard", None),
            P(None, "shard"),
            P("shard", None),
            P("shard", None),
            P("shard", None),
            P("shard", None),
            P(None, "shard"),
            P("shard", None),
            P("shard", None),
            P("shard", None),
            P("shard", None),
            P(None, "shard"),
        ),
        out_specs=(
            P(("dp", "shard"), None, None),
            P(("dp", "shard"), None, None),
            P("shard", None),
            P("shard", None),
            P("shard", None),
            P("shard", None),
            P(None, "shard"),
            P("shard", None),
            P("shard", None),
            P("shard", None),
            P("shard", None),
            P(None, "shard"),
            P("shard", None),
            P("shard", None),
            P("shard", None),
            P("shard", None),
            P(None, "shard"),
        ),
        check_vma=False,
    )
```

```python
import functools

import jax
import jax.numpy as jnp
import numpy as np
from jax import lax
from jax.experimental import pallas as pl
from jax.experimental.pallas import tpu as pltpu
from jax.sharding import PartitionSpec as P

HEADS = 9
KV_HEADS = 3
GROUP = HEADS // KV_HEADS
HEAD = 64
FF = 1536
STEP = 10
QUERY = HEADS * HEAD
ROPED = (HEADS + KV_HEADS) * HEAD
QKV = (HEADS + 2 * KV_HEADS) * HEAD
LANES = 128

EPS_NORM = 1e-05
ROPE_BASE = 100000.0
BETA_ONE = 0.9
BETA_TWO = 0.95
RATE_MATRIX = 0.1
RATE_GAIN = 0.3
DECAY_MATRIX = 0.1
EPS_ADAM = 1e-08
MASKED = -1e30
SCALE = float(HEAD) ** (-0.5)
VMEM_LIMIT = 32 * 1024 * 1024
PACK_LIMIT = 60 * 1024 * 1024
HALF = 144
CUT_ROWS = 72
MARK = (8, 128)
CUT_COLUMNS = 384
F32 = jnp.float32
BF16 = jnp.bfloat16


def rotate_block(values, cosine, signed_sine):
    lane = lax.broadcasted_iota(jnp.int32, values.shape, 1)
    swapped = jnp.where(
        lane % HEAD < HEAD // 2,
        pltpu.roll(values, LANES - HEAD // 2, 1),
        pltpu.roll(values, HEAD // 2, 1),
    )
    return values * cosine + swapped * signed_sine


def adamw(weight, first_moment, second_moment, gradient, step_rate, weight_decay):
    first_new = BETA_ONE * first_moment + (1.0 - BETA_ONE) * gradient
    second_new = BETA_TWO * second_moment + (1.0 - BETA_TWO) * gradient * gradient
    fix_one = 1.0 - BETA_ONE**STEP
    fix_two = 1.0 - BETA_TWO**STEP
    update = first_new / fix_one / (jnp.sqrt(second_new / fix_two) + EPS_ADAM)
    return (first_new, second_new, weight - step_rate * (update + weight_decay * weight))


def dot(left, right):
    return lax.dot_general(left, right, (((1,), (0,)), ((), ())), preferred_element_type=F32)


def dot_right_t(left, right):
    return lax.dot_general(left, right, (((1,), (1,)), ((), ())), preferred_element_type=F32)


def dot_left_t(left, right):
    return lax.dot_general(left, right, (((0,), (0,)), ((), ())), preferred_element_type=F32)


def norm_scale(values):
    return lax.rsqrt(jnp.mean(values * values, axis=-1, keepdims=True) + EPS_NORM)


def norm_back(grad_normed, normed, scale_rows):
    return scale_rows * (
        grad_normed - normed * jnp.mean(grad_normed * normed, axis=-1, keepdims=True)
    )


class Weight:
    def __init__(self, shape, whole=None, own=(), parts=()):
        self.shape, self.own, self.parts = shape, own, parts
        self.arrays = [whole] if whole is not None else [a[0] for a in (*own, *parts)]
        self.split = whole is None

    def load(self, idx, refs, full):
        if not self.split:
            return refs[0]
        for ref, (_, place) in zip(refs, self.own):
            self.put(full, place(idx[0]), ref[...].astype(BF16))
        for ref, (_, (core, x, low), place) in zip(refs[len(self.own) :], self.parts):
            place = place(1 - idx[0], idx[1] ^ core, idx[2] ^ x, (idx[3] & 1) ^ low)
            rows = ref.shape[0] // HALF * HALF
            self.put(full, place, ref[:rows, :])
        return full

    def put(self, full, position, value):
        where = []
        for axis, tile in ((0, 16), (1, LANES)):
            at, size = position[axis], value.shape[axis]
            if size == self.shape[axis]:
                where.append(slice(None))
            elif isinstance(at, int):
                where.append(slice(at, at + size))
            else:
                where.append(pl.ds(pl.multiple_of(at, tile), size))
        full[tuple(where)] = value


def call(body, idx, arrays, weights, outs, scratch, busy, name, after=(), hand_on=False):
    counts = [len(w.arrays) for w in weights]
    flat = list(arrays) + [a for w in weights for a in w.arrays]
    outs = list(outs)
    split = [w for w in weights if w.split]
    hand_on = hand_on and bool(split)
    if hand_on:
        outs += [sds(split[-1].shape, BF16)]
    made = [pltpu.VMEM(w.shape, BF16) for w in (split[:-1] if hand_on else split)]

    def kernel(*refs):
        refs = list(refs)
        idx_ref = refs.pop(0)
        take = lambda n: [refs.pop(0) for _ in range(n)]
        array_refs = take(len(arrays))
        weight_refs = [take(n) for n in counts]
        take(len(after))
        out_refs = take(len(outs))
        own_scratch = take(len(scratch))
        fulls = take(len(made)) + ([out_refs.pop()] if hand_on else [])
        loads = [
            functools.partial(w.load, idx_ref, r, fulls.pop(0) if w.split else None)
            for w, r in zip(weights, weight_refs)
        ]
        body(idx_ref, array_refs, loads, out_refs, own_scratch)

    return pl.pallas_call(
        kernel,
        out_shape=tuple(outs),
        in_specs=[pl.BlockSpec(memory_space=pltpu.SMEM)]
        + [pl.BlockSpec(memory_space=pltpu.VMEM)] * len(flat)
        + [pl.BlockSpec(memory_space=pl.ANY)] * len(after),
        out_specs=tuple([pl.BlockSpec(memory_space=pltpu.VMEM)] * len(outs)),
        scratch_shapes=list(scratch) + made,
        compiler_params=pltpu.CompilerParams(vmem_limit_bytes=VMEM_LIMIT),
        cost_estimate=busy_for(busy),
        name=name,
    )(idx, *flat, *after)


def busy_for(microseconds):
    return pl.CostEstimate(flops=int(microseconds * 1e9), bytes_accessed=0, transcendentals=0)


def sds(shape, dtype):
    return jax.ShapeDtypeStruct(shape, dtype)


class Pieces:
    def __init__(self, place, parts=1, extra=0):
        self.place, self.parts, self.extra = place, parts, extra

    def outs(self):
        return [sds((self.parts, 2, 8, CUT_ROWS + self.extra, CUT_COLUMNS), BF16)] * 2

    def scratch(self, columns):
        return pltpu.VMEM((8, CUT_ROWS, columns), BF16)

    def store(self, blocks, grad, start=0):
        for i in range(8):
            rows = grad[i * CUT_ROWS : (i + 1) * CUT_ROWS].astype(BF16)
            blocks[i, :, start : start + grad.shape[1]] = rows

    def emit(self, idx, blocks, outs, under=None):
        for other_core, out in enumerate((outs[1], outs[0])):
            for part in range(self.parts):
                for owner in range(2):
                    for slot in range(8):
                        z = ((slot >> 1) & 1) | ((slot & 1) << 1)
                        block, column = self.place(
                            idx[0] ^ owner, idx[1] ^ other_core, idx[2] ^ (slot >> 2), idx[3] ^ z, part
                        )
                        columns = pl.ds(pl.multiple_of(column * CUT_COLUMNS, LANES), CUT_COLUMNS)
                        piece = blocks[block, :, columns]
                        if under is not None:
                            piece = jnp.concatenate(
                                [piece.astype(F32), under[idx[0] ^ owner]], axis=0
                            ).astype(BF16)
                        out[part, owner, slot] = piece


def head_stack(values, kv_head):
    first = kv_head * GROUP
    return jnp.concatenate(
        [values[:, (first + i) * HEAD : (first + i + 1) * HEAD] for i in range(GROUP)], axis=0
    )


def softmax_rows(query, key, allowed):
    scores = jnp.where(allowed, dot_right_t(query, key) * SCALE, MASKED)
    top = jnp.max(scores, axis=-1, keepdims=True)
    exponent = jnp.exp(scores - top)
    return exponent / jnp.sum(exponent, axis=-1, keepdims=True)


def pack_kernel(body, idx, sources, places, outs, name, after=(), limit=PACK_LIMIT):
    windows = [shape for shape, _ in places]

    def kernel(idx_ref, *refs):
        sources_in, refs = refs[: len(sources)], refs[len(sources) + len(after) :]
        out_refs, buffers, sem = refs[: len(outs)], refs[len(outs) : -1], refs[-1]
        copies = []
        for i, (source, (shape, place)) in enumerate(zip(sources_in, places)):
            where = []
            for axis, tile in ((0, 8), (1, LANES)):
                if shape[axis] == source.shape[axis]:
                    where.append(slice(None))
                else:
                    where.append(pl.ds(pl.multiple_of(place(idx_ref)[axis], tile), shape[axis]))
            copies.append(pltpu.make_async_copy(source.at[tuple(where)], buffers[i], sem.at[i]))
        for copy in copies:
            copy.start()
        for copy in copies:
            copy.wait()
        body(idx_ref, buffers, out_refs)

    return pl.pallas_call(
        kernel,
        out_shape=tuple(outs),
        in_specs=[pl.BlockSpec(memory_space=pltpu.SMEM)]
        + [pl.BlockSpec(memory_space=pltpu.HBM)] * len(sources)
        + [pl.BlockSpec(memory_space=pl.ANY)] * len(after),
        out_specs=tuple([pl.BlockSpec(memory_space=pltpu.VMEM)] * len(outs)),
        scratch_shapes=[pltpu.VMEM(w, F32) for w in windows]
        + [pltpu.SemaphoreType.DMA((len(sources),))],
        compiler_params=pltpu.CompilerParams(vmem_limit_bytes=limit),
        cost_estimate=busy_for(10),
        name=name,
    )(idx, *sources, *after)


def cast_out(idx_ref, buffers, outs):
    for buffer, out in zip(buffers, outs):
        out[...] = buffer[...].astype(BF16)


def pack_gate_up(idx, w_gate_up):
    shape = (HALF, FF // 2)
    windows = [
        (shape, lambda i: (i[1] * HALF, i[2] * (FF // 2))),
        (shape, lambda i: (i[1] * HALF, FF + (i[3] & 1) * (FF // 2))),
    ]
    return pack_kernel(
        cast_out, idx, [w_gate_up] * 2, windows, [sds(shape, BF16)] * 2, "pack_gate_up"
    )


def pack_down(idx, down_t, after):
    shape = (2 * HALF, down_t.shape[1])
    window = (shape, lambda i: (i[1] * 2 * HALF, 0))
    outs = [sds(shape, BF16)]
    return pack_kernel(
        cast_out, idx, [down_t], [window], outs, "pack_down", after, VMEM_LIMIT
    )[0]


def pack_qkv_out(idx, w_qkv, w_out, norm_gains, after):
    columns = (QKV + w_out.shape[1]) // 2
    windows = [((HALF, m.shape[1]), lambda i: (i[1] * HALF, 0)) for m in (w_qkv, w_out)]
    windows.append((norm_gains.shape, lambda i: (0, 0)))

    def body(idx_ref, buffers, outs):
        q_ref, o_ref, gains_ref = buffers
        both = jnp.concatenate([q_ref[:, columns:], o_ref[...]], axis=1)
        outs[0][:HALF, :] = jnp.where((idx_ref[3] & 1) == 0, q_ref[:, :columns], both).astype(BF16)
        outs[0][HALF:, :] = jnp.zeros((16, columns), BF16)
        outs[0][HALF : HALF + 2, : gains_ref.shape[1]] = gains_ref[...].astype(BF16)

    outs = [sds((HALF + 16, columns), BF16)]
    return pack_kernel(
        body, idx, [w_qkv, w_out, norm_gains], windows, outs, "pack_qkv_out", after
    )[0]


def attention_forward(idx, tokens_t, segments, frequency, gains, w_qkv_out):
    width, seq_length = tokens_t.shape
    split_gains = len(gains) > 1

    def body(idx_ref, arrays, loads, outs, scratch):
        x_ref, seg_ref, freq_ref = arrays[:3]
        qkv_ref, o_ref, cos_ref, sin_ref, allowed_ref, gains_ref = outs
        if split_gains:
            own = arrays[3][...].astype(BF16).astype(F32)
            other = arrays[4][HALF : HALF + 8, : width // 2].astype(F32)[:2]
            gains_ref[...] = jnp.where(
                idx_ref[0] == 0,
                jnp.concatenate([own, other], axis=1),
                jnp.concatenate([other, own], axis=1),
            )
        else:
            gains_ref[...] = arrays[3][...]
        seen_doc = jnp.broadcast_to(seg_ref[...], (seq_length, seq_length))
        own_doc = seen_doc.T
        token = lax.broadcasted_iota(jnp.int32, (seq_length, seq_length), 0)
        seen = lax.broadcasted_iota(jnp.int32, (seq_length, seq_length), 1)
        begin = jnp.sum((seen_doc < own_doc).astype(F32), axis=-1, keepdims=True)
        angles = (token.astype(F32) - begin) * freq_ref[...]
        cosine, sine = jnp.cos(angles), jnp.sin(angles)
        sine = jnp.where(seen % HEAD < HEAD // 2, -sine, sine)
        cos_ref[...] = cosine
        sin_ref[...] = sine
        allowed = ((seen_doc == own_doc) & (token >= seen)).astype(F32)
        allowed_ref[...] = allowed
        allowed = jnp.concatenate([allowed] * GROUP, axis=0) > 0.5
        x = x_ref[...].astype(F32).T
        h1 = (x * norm_scale(x) * gains_ref[0:1, :]).astype(BF16)
        projected = dot(h1, loads[0]()[:, :QKV])
        for start in range(0, ROPED, LANES):
            block = projected[:, start : start + LANES]
            qkv_ref[:, start : start + LANES] = rotate_block(block, cosine, sine).astype(BF16)
        qkv_ref[:, ROPED:QKV] = projected[:, ROPED:QKV].astype(BF16)
        qkv = qkv_ref[...]
        for kv in range(KV_HEADS):
            key = qkv[:, QUERY + kv * HEAD : QUERY + (kv + 1) * HEAD]
            value = qkv[:, ROPED + kv * HEAD : ROPED + (kv + 1) * HEAD]
            probs = softmax_rows(head_stack(qkv, kv), key, allowed).astype(BF16)
            attended = dot(probs, value).astype(BF16)
            for i in range(GROUP):
                start = (kv * GROUP + i) * HEAD
                o_ref[:, start : start + HEAD] = attended[i * seq_length : (i + 1) * seq_length]

    square = sds((seq_length, seq_length), F32)
    outs = [sds((seq_length, QKV), BF16), sds((seq_length, QUERY), BF16)]
    outs += [square, square, square, sds((2, width), F32)]
    return call(
        body,
        idx,
        [tokens_t, segments, frequency, *gains],
        [w_qkv_out],
        outs,
        [],
        10,
        "attention",
        hand_on=True,
    )


def feed_forward(idx, tokens_t, attended, gains, cotangent_t, w_qkv_out, w_gate_up, pieces, after):
    width, seq_length = tokens_t.shape

    def body(idx_ref, arrays, loads, outs, scratch):
        x_ref, o_ref, gains_ref, y_ref = arrays
        u_ref, h2_ref, ab_ref, z_ref = outs[:4]
        u = x_ref[...].astype(F32).T + dot(o_ref[...], loads[0]()[:, QKV:])
        u_ref[...] = u
        h2 = (u * norm_scale(u) * gains_ref[1:2, :]).astype(BF16)
        h2_ref[...] = h2
        ab = dot(h2, loads[1]()[...])
        ab_ref[...] = ab
        gate, up = ab[:, :FF], ab[:, FF:]
        z = (gate * jax.nn.sigmoid(gate) * up).astype(BF16)
        z_ref[...] = z
        grad = dot(y_ref[...], z)
        if pieces is None:
            outs[4][...] = grad
        else:
            pieces.store(scratch[0], grad)
            pieces.emit(idx_ref, scratch[0], outs[4:])

    outs = [
        sds((seq_length, width), F32),
        sds((seq_length, width), BF16),
        sds((seq_length, 2 * FF), F32),
        sds((seq_length, FF), BF16),
    ]
    outs += [sds((width, FF), F32)] if pieces is None else pieces.outs()
    scratch = [] if pieces is None else [pieces.scratch(FF)]
    return call(
        body,
        idx,
        [tokens_t, attended, gains, cotangent_t],
        [w_qkv_out, w_gate_up],
        outs,
        scratch,
        20,
        "feed_forward",
        after,
        True,
    )


def feed_back(idx, ab, normed_low, hidden, middle, cotangent_t, down_t, pieces):
    width, seq_length = cotangent_t.shape

    def body(idx_ref, arrays, loads, outs, scratch):
        ab_ref, h2_ref, z_ref, u_ref, y_ref = arrays
        gg_ref, out_ref = outs[:2]
        down = loads[0]()
        gate, up = ab_ref[:, :FF], ab_ref[:, FF:]
        sig = jax.nn.sigmoid(gate)
        grad_hidden = dot_left_t(y_ref[...], down[...])
        gg_ref[:, :FF] = (grad_hidden * up * sig * (1.0 + gate * (1.0 - sig))).astype(BF16)
        gg_ref[:, FF:] = (grad_hidden * gate * sig).astype(BF16)
        grad = dot_left_t(h2_ref[...], gg_ref[...])
        if pieces is None:
            outs[2][...] = grad
        else:
            pieces.store(scratch[0], grad)
            pieces.emit(idx_ref, scratch[0], outs[2:])
        out_ref[...] = (u_ref[...] + dot_right_t(z_ref[...], down[...])).T.astype(BF16)

    outs = [sds((seq_length, 2 * FF), BF16), sds((width, seq_length), BF16)]
    outs += [sds((width, 2 * FF), F32)] if pieces is None else pieces.outs()
    scratch = [] if pieces is None else [pieces.scratch(2 * FF)]
    return call(
        body,
        idx,
        [ab, normed_low, hidden, middle, cotangent_t],
        [down_t],
        outs,
        scratch,
        20,
        "feed_back",
    )


def middle_back(idx, cotangent_t, middle, gated, gains, w_gate_up, w_qkv_out, after):
    width, seq_length = cotangent_t.shape

    def body(idx_ref, arrays, loads, outs, scratch):
        y_ref, u_ref, gg_ref, gains_ref = arrays
        gu_ref, go_ref, gain_ref = outs
        u = u_ref[...]
        scale_two = norm_scale(u)
        normed = u * scale_two
        grad_normed = dot_right_t(gg_ref[...], loads[0]()[...])
        gain_ref[...] = jnp.sum(grad_normed * normed, axis=0, keepdims=True)
        gu = y_ref[...].astype(F32).T + norm_back(
            grad_normed * gains_ref[1:2, :], normed, scale_two
        )
        gu_ref[...] = gu
        go_ref[...] = dot_right_t(gu.astype(BF16), loads[1]()[:, QKV:]).astype(BF16)

    outs = [sds((seq_length, width), F32), sds((seq_length, width), BF16), sds((1, width), F32)]
    return call(
        body,
        idx,
        [cotangent_t, middle, gated, gains],
        [w_gate_up, w_qkv_out],
        outs,
        [],
        20,
        "middle_back",
        after,
    )


def attention_back(
    idx, tokens_t, grad_middle, grad_attended, gain_two, qkv, attended, tables, gains, w_qkv, pieces, after
):
    width, seq_length = tokens_t.shape

    def body(idx_ref, arrays, loads, outs, scratch):
        x_ref, gu_ref, go_ref, gain_two_ref, qkv_ref, o_ref = arrays[:6]
        cos_ref, sin_ref, allowed_ref, gains_ref = arrays[6:]
        grad_ref = outs[0]
        grad_proj, gp_ref, gain_rows, *blocks = scratch
        gu, go = gu_ref[...], go_ref[...]
        gu_low = gu.astype(BF16)
        grad_gain_two = gain_two_ref[...]
        allowed = jnp.concatenate([allowed_ref[...]] * GROUP, axis=0) > 0.5
        qkv_values = qkv_ref[...]
        for kv in range(KV_HEADS):
            key = qkv_values[:, QUERY + kv * HEAD : QUERY + (kv + 1) * HEAD]
            value = qkv_values[:, ROPED + kv * HEAD : ROPED + (kv + 1) * HEAD]
            query = head_stack(qkv_values, kv)
            grad_out = head_stack(go, kv)
            probs = softmax_rows(query, key, allowed)
            grad_probs = dot_right_t(grad_out, value)
            row_delta = jnp.sum(probs * grad_probs, axis=-1, keepdims=True)
            gs = (probs * (grad_probs - row_delta)).astype(BF16)
            grad_query = dot(gs, key) * SCALE
            for i in range(GROUP):
                start = (kv * GROUP + i) * HEAD
                grad_proj[:, start : start + HEAD] = grad_query[
                    i * seq_length : (i + 1) * seq_length
                ]
            start = QUERY + kv * HEAD
            grad_proj[:, start : start + HEAD] = dot_left_t(gs, query) * SCALE
            start = ROPED + kv * HEAD
            grad_proj[:, start : start + HEAD] = dot_left_t(probs.astype(BF16), grad_out)
        for start in range(0, ROPED, LANES):
            gp_ref[:, start : start + LANES] = rotate_block(
                grad_proj[:, start : start + LANES], cos_ref[...], -sin_ref[...]
            ).astype(BF16)
        gp_ref[:, ROPED:QKV] = grad_proj[:, ROPED:QKV].astype(BF16)
        x = x_ref[...].astype(F32).T
        scale_one = norm_scale(x)
        normed = x * scale_one
        h1 = (normed * gains_ref[0:1, :]).astype(BF16)
        grad_qkv = dot_left_t(h1, gp_ref[...])
        grad_out = dot_left_t(o_ref[...], gu_low)
        grad_normed = dot_right_t(gp_ref[...], loads[0]()[:, :QKV])
        grad_gain_one = jnp.sum(grad_normed * normed, axis=0, keepdims=True)
        if pieces is None:
            outs[1][:, :QKV] = grad_qkv
            outs[1][:, QKV:] = grad_out
            outs[2][0:1, :] = grad_gain_one
            outs[2][1:2, :] = grad_gain_two
        else:
            pieces.store(blocks[0], grad_qkv)
            pieces.store(blocks[0], grad_out, QKV)
            half = width // 2
            gain_rows[...] = jnp.zeros_like(gain_rows)
            for owner in range(2):
                columns = slice(owner * half, (owner + 1) * half)
                gain_rows[owner, 0:1, :half] = grad_gain_one[:, columns]
                gain_rows[owner, 1:2, :half] = grad_gain_two[:, columns]
            pieces.emit(idx_ref, blocks[0], outs[1:3], gain_rows)
            outs[3][...] = jnp.zeros_like(outs[3])
        grad_ref[...] = (
            (gu + norm_back(grad_normed * gains_ref[0:1, :], normed, scale_one)).T
        ).astype(BF16)

    outs = [sds((width, seq_length), BF16)]
    scratch = [
        pltpu.VMEM((seq_length, QKV), F32),
        pltpu.VMEM((seq_length, QKV), BF16),
        pltpu.VMEM((2, 8, CUT_COLUMNS), F32),
    ]
    if pieces is None:
        outs += [sds((width, QKV + width), F32), sds((2, width), F32)]
    else:
        outs += pieces.outs() + [sds(MARK, F32)]
        scratch += [pieces.scratch(QKV + width)]
    return call(
        body,
        idx,
        [tokens_t, grad_middle, grad_attended, gain_two, qkv, attended, *tables, gains],
        [w_qkv],
        outs,
        scratch,
        20,
        "attention_back",
        after,
    )


def step(body, arrays, outs, name, after=()):
    def kernel(*refs):
        body(refs[: len(arrays)], refs[len(arrays) + len(after) :])

    return pl.pallas_call(
        kernel,
        out_shape=tuple(outs),
        in_specs=[pl.BlockSpec(memory_space=pltpu.VMEM)] * len(arrays)
        + [pl.BlockSpec(memory_space=pl.ANY)] * len(after),
        out_specs=tuple([pl.BlockSpec(memory_space=pltpu.VMEM)] * len(outs)),
        compiler_params=pltpu.CompilerParams(vmem_limit_bytes=VMEM_LIMIT),
        cost_estimate=busy_for(20),
        name=name,
    )(*arrays, *after)


def add_split(keep, arrived, axis, send_ref, keep_ref):
    total = keep[...].astype(F32) + arrived[...].astype(F32)
    low, high = lax.index_in_dim(total, 0, axis, False), lax.index_in_dim(total, 1, axis, False)
    send_ref[...] = high.astype(BF16)
    keep_ref[...] = low


def add_step(jobs, name, after):
    arrays, outs = [], []
    for keep, arrived, axis in jobs:
        arrays += [keep, arrived]
        shape = keep.shape[:axis] + keep.shape[axis + 1 :]
        outs += [sds(shape, BF16), sds(shape, F32)]

    def body(ins, out_refs):
        for i, (_, _, axis) in enumerate(jobs):
            add_split(ins[2 * i], ins[2 * i + 1], axis, out_refs[2 * i], out_refs[2 * i + 1])

    flat = step(body, arrays, outs, name, after)
    return [(flat[2 * i], flat[2 * i + 1]) for i in range(len(jobs))]


def update_state(idx, near, far, parts, blocks, puts, state, shape, name, gains=(), after=()):
    count = len(state) // 3
    height, width = near.shape[3:]

    def kernel(idx_ref, *refs):
        part_refs, refs = refs[: 2 * len(parts)], refs[2 * len(parts) :]
        state_refs, refs = refs[: 3 * count], refs[3 * count :]
        gain_refs, refs = refs[: len(gains)], refs[len(gains) + len(after) :]
        outs, refs = refs[: 3 * count], refs[3 * count :]
        gain_outs, mark, full = refs[: len(gains)], refs[-2], refs[-1]
        mark[...] = jnp.zeros_like(mark)
        is_near = pl.program_id(0) % 2 == idx_ref[1]
        for i, put in enumerate(puts):
            for z in range(4):
                rel = z ^ idx_ref[3]
                slot = (rel & 1) * 2 + (rel >> 1)
                piece = jnp.where(
                    is_near,
                    part_refs[2 * i][0, 0, slot].astype(F32),
                    part_refs[2 * i + 1][0, 0, slot].astype(F32),
                )
                put(full, z, piece)
        start = 0
        for i in range(count):
            columns = state_refs[i].shape[1]
            first, second, new = adamw(
                state_refs[i][...],
                state_refs[count + i][...],
                state_refs[2 * count + i][...],
                full[: state_refs[i].shape[0], start : start + columns],
                RATE_MATRIX,
                DECAY_MATRIX,
            )
            start += columns
            outs[i][...] = first
            outs[count + i][...] = second
            outs[2 * count + i][...] = new
        if gains:

            @pl.when(pl.program_id(0) == 0)
            def _():
                gradient = full[CUT_ROWS : CUT_ROWS + 2, : gain_refs[0].shape[1]]
                first, second, new = adamw(
                    gain_refs[0][...], gain_refs[1][...], gain_refs[2][...], gradient, RATE_GAIN, 0.0
                )
                gain_outs[0][...] = first
                gain_outs[1][...] = second
                gain_outs[2][...] = new

    state_specs = [pl.BlockSpec(*blocks[i]) for i in range(count)] * 3
    gain_specs = [pl.BlockSpec(g.shape, lambda t, _: (0, 0)) for g in gains]
    part_specs = [
        pl.BlockSpec((1, 1, 4, height, width), lambda t, i, p=p: (p, (t // 2) ^ i[2], 0, 0, 0))
        for p in parts
        for _ in range(2)
    ]
    return pl.pallas_call(
        kernel,
        grid_spec=pltpu.PrefetchScalarGridSpec(
            num_scalar_prefetch=1,
            grid=(4,),
            in_specs=part_specs
            + state_specs
            + gain_specs
            + [pl.BlockSpec(memory_space=pl.ANY)] * len(after),
            out_specs=tuple(state_specs + gain_specs + [pl.BlockSpec(MARK, lambda t, _: (0, 0))]),
            scratch_shapes=[pltpu.VMEM(shape, F32)],
        ),
        out_shape=tuple(sds(a.shape, F32) for a in [*state, *gains]) + (sds(MARK, F32),),
        compiler_params=pltpu.CompilerParams(vmem_limit_bytes=VMEM_LIMIT),
        cost_estimate=busy_for(20),
        name=name,
    )(idx, *[near, far] * len(parts), *state, *gains, *after)


def swap(values, axis, mask):
    size = lax.axis_size(axis)
    return lax.ppermute(values, axis, [(i, i ^ mask) for i in range(size)])


over_y = functools.partial(swap, axis="shard", mask=1)
over_core = functools.partial(swap, axis="dp", mask=1)
over_x = functools.partial(swap, axis="dp", mask=2)
over_z_low = functools.partial(swap, axis="dp", mask=4)
over_z_high = functools.partial(swap, axis="dp", mask=8)


def per_device(
    tokens,
    segments,
    cotangent,
    w_qkv,
    w_out,
    w_gate_up,
    w_down,
    norm_gains,
    first_qkv,
    first_out,
    first_gate_up,
    first_down,
    first_gains,
    second_qkv,
    second_out,
    second_gate_up,
    second_down,
    second_gains,
):
    groups = lax.axis_size("shard")
    replicas = lax.axis_size("dp")
    fast = groups == 2 and replicas == 16
    place_dp = lax.axis_index("dp")
    owner = lax.axis_index("shard")
    idx = jnp.stack([owner, place_dp & 1, (place_dp >> 1) & 1, place_dp >> 2]).astype(jnp.int32)
    x_t, y_t = tokens[0].T, cotangent[0].T
    width, seq_length = x_t.shape
    rows, down_rows = w_qkv.shape[0], w_down.shape[0]
    down_t, first_down_t, second_down_t = w_down.T, first_down.T, second_down.T
    half_size = HEAD // 2
    frequency = ROPE_BASE ** (-(np.arange(half_size) * 2.0 / HEAD))
    frequency = jnp.asarray(np.tile(frequency, 4)[None], F32)
    if fast:
        by_x, by_low = pack_gate_up(idx, w_gate_up)
        by_x, by_low = over_y(by_x), over_y(by_low)
        qo_near = over_y(pack_qkv_out(idx, w_qkv, w_out, norm_gains, ()))
        down_near = over_y(pack_down(idx, down_t, (by_low,)))
        by_x_next, by_low_next = over_x(by_x), over_z_low(by_low)
        qo_near_low = over_z_low(qo_near)
        gains = (norm_gains, qo_near)
        own_rows = lambda o: (o * rows, 0)
        own_rows_out = lambda o: (o * rows, QKV)
        qo_place = lambda o, c, x, low: (o * rows + c * HALF, low * ((QKV + width) // 2))
        x_place = lambda o, c, x, low: (o * rows + c * HALF, x * (FF // 2))
        low_place = lambda o, c, x, low: (o * rows + c * HALF, FF + low * (FF // 2))
        mat_qkv_out = Weight(
            (width, QKV + width),
            own=[(w_qkv, own_rows), (w_out, own_rows_out)],
            parts=[
                (qo_near, (0, 0, 0), qo_place),
                (qo_near_low, (0, 0, 1), qo_place),
                (over_core(qo_near), (1, 0, 0), qo_place),
                (over_core(qo_near_low), (1, 0, 1), qo_place),
            ],
        )
        mat_gate_up = Weight(
            (width, 2 * FF),
            own=[(w_gate_up, own_rows)],
            parts=[
                (by_x, (0, 0, 0), x_place),
                (by_x_next, (0, 1, 0), x_place),
                (over_core(by_x), (1, 0, 0), x_place),
                (over_core(by_x_next), (1, 1, 0), x_place),
                (by_low, (0, 0, 0), low_place),
                (by_low_next, (0, 0, 1), low_place),
                (over_core(by_low), (1, 0, 0), low_place),
                (over_core(by_low_next), (1, 0, 1), low_place),
            ],
        )
        cut_qkv_out = Pieces(lambda o, c, x, z, p: (o * 4 + c * 2 + x, z), extra=8)
        cut_gate_up = Pieces(lambda o, c, x, z, p: (o * 4 + c * 2 + p, x * 4 + z), parts=2)
        cut_down = Pieces(lambda o, c, x, z, p: (c * 4 + x * 2 + (z >> 1), o * 2 + (z & 1)))
    else:
        gains = (
            lax.all_gather(norm_gains.astype(BF16), "shard", axis=1, tiled=True).astype(F32),
        )
        mat_qkv, mat_out, mat_gate_up, mat_down = [
            lax.all_gather(m.astype(BF16), "shard", axis=0, tiled=True)
            for m in (w_qkv, w_out, w_gate_up, w_down)
        ]
        mat_qkv_out, mat_gate_up, mat_down = [
            Weight(m.shape, whole=m)
            for m in (jnp.concatenate([mat_qkv, mat_out], axis=1), mat_gate_up, mat_down.T)
        ]
        cut_qkv_out = cut_gate_up = cut_down = None

    qkv, attended, *tables, gains, whole = attention_forward(
        idx, x_t, segments, frequency, gains, mat_qkv_out
    ) + (() if fast else (None,))
    if fast:
        mat_qkv_out = Weight(whole.shape, whole=whole)
    middle, normed_low, ab, hidden, *grad_down = feed_forward(
        idx, x_t, attended, gains, y_t, mat_qkv_out, mat_gate_up, cut_down, ()
    )
    after = ()
    if fast:
        whole = grad_down.pop()
        mat_gate_up = Weight(whole.shape, whole=whole)

        def pass_on(ins, outs):
            outs[0][...] = ins[0][...]

        (down_near,) = step(
            pass_on, [down_near], [sds(down_near.shape, BF16)], "pass_on", (normed_low,)
        )
        down_place = lambda o, c, x, low: (c * 2 * HALF, o * down_rows)
        mat_down = Weight(
            (width, FF),
            own=[(down_t, lambda o: (0, o * down_rows))],
            parts=[
                (down_near, (0, 0, 0), down_place),
                (over_core(down_near), (1, 0, 0), down_place),
            ],
        )
    if fast:
        arrived_down = over_core(grad_down[0])
    gated, output, *grad_gate_up = feed_back(
        idx, ab, normed_low, hidden, middle, y_t, mat_down, cut_gate_up
    )
    if fast:
        cut = lambda a, *lead: a.reshape(*lead, *a.shape[-2:])
        arrived_gate_up = over_core(grad_gate_up[0])
        ((send, keep_down),) = add_step(
            [(grad_down[1][0], arrived_down[0], 0)], "down_core", (gated,)
        )
        arrived_down = over_y(send)
        after = (keep_down,)
    grad_middle, grad_attended, gain_two = middle_back(
        idx, y_t, middle, gated, gains, mat_gate_up, mat_qkv_out, after
    )
    if fast:
        halves = [
            [cut(a[p], *lead) for a in (grad_gate_up[1], arrived_gate_up)]
            for p, lead in ((0, (2, 2, 4)), (1, (4, 2, 2)))
        ]
        (send_up, keep_up), (send_low, keep_low) = add_step(
            [(*halves[0], 1), (*halves[1], 1)], "gate_up_core", (grad_middle,)
        )
        arrived_up, arrived_low = over_x(send_up), over_z_low(send_low)
        after = (keep_up,)
    token_grad, *grad_qkv_out = attention_back(
        idx,
        x_t,
        grad_middle,
        grad_attended,
        gain_two,
        qkv,
        attended,
        tables,
        gains,
        mat_qkv_out,
        cut_qkv_out,
        after,
    )
    if fast:

        def put_down(full, z, piece):
            full[(z >> 1) * CUT_ROWS : ((z >> 1) + 1) * CUT_ROWS, pl.ds((z & 1) * 384, 384)] = piece

        def put_upper(full, z, piece):
            full[:CUT_ROWS, pl.ds(z * 384, 384)] = piece

        def put_lower(full, z, piece):
            full[CUT_ROWS:, pl.ds(z * 384, 384)] = piece

        def put_columns(full, z, piece):
            full[:, pl.ds(z * 384, 384)] = piece

        arrived_qkv_out = over_core(grad_qkv_out[0])
        piece = (CUT_ROWS, CUT_COLUMNS)
        taller = (CUT_ROWS + 8, CUT_COLUMNS)
        ((send, keep_down),) = add_step(
            [(cut(keep_down, 2, 4), cut(arrived_down, 2, 4), 0)], "down_y", (grad_qkv_out[2],)
        )
        arrived_down = over_x(send)
        (send_up, keep_up), (send_low, keep_low) = add_step(
            [
                (cut(keep_up, 2, 2, 2), cut(arrived_up, 2, 2, 2), 1),
                (cut(keep_low, 2, 2, 2), cut(arrived_low, 2, 2, 2), 0),
            ],
            "up_x_low_z",
            (keep_down,),
        )
        arrived_up, arrived_low = over_z_low(send_up), over_y(send_low)

        def qkv_out_core(ins, outs):
            total = ins[0][...].astype(F32) + ins[1][...].astype(F32)
            outs[0][...] = total[1, :, 0].astype(BF16)
            outs[1][...] = total[0, :, 0]
            outs[2][...] = total[:, 1, 1].astype(BF16)
            outs[3][...] = total[:, 0, 1]

        send_a, keep_a, send_b, keep_b = step(
            qkv_out_core,
            [cut(a, 2, 2, 2, 2) for a in (grad_qkv_out[1], arrived_qkv_out)],
            [sds((2, 2, *taller), t) for t in (BF16, F32, BF16, F32)],
            "qkv_out_core",
            (keep_up,),
        )
        arrived_a, arrived_b = over_y(send_a), over_x(send_b)
        ((send, keep_down),) = add_step(
            [(cut(keep_down, 2, 2), cut(arrived_down, 2, 2), 0)], "down_x", (keep_a,)
        )
        arrived_down = over_z_low(send)
        (send_up, keep_up), (send_low, keep_low), (send_a, keep_a), (send_b, keep_b) = add_step(
            [
                (keep_up, arrived_up, 0),
                (keep_low, arrived_low, 0),
                (keep_a, arrived_a, 0),
                (keep_b, arrived_b, 0),
            ],
            "up_z_low_y_qkv_out_xy",
            (keep_down,),
        )
        arrived_up, arrived_low = over_y(send_up), over_x(send_low)
        arrived_a, arrived_b = over_x(send_a), over_y(send_b)
        ((send, keep_down),) = add_step([(keep_down, arrived_down, 0)], "down_z_low", (keep_up,))
        arrived_down = over_z_high(send)

        def planes(ins, outs):
            for i in range(2):
                total = ins[2 * i][...] + ins[2 * i + 1][...].astype(F32)
                outs[0][i] = total[1].astype(BF16)
                outs[1][i] = total[0]
            outs[2][...] = (ins[6][...] + ins[7][...].astype(F32)).astype(BF16)
            outs[3][...] = ins[4][...] + ins[5][...].astype(F32)
            outs[4][...] = (ins[8][...] + ins[9][...].astype(F32)).astype(BF16)

        send, keep, send_qkv_out, keep_qkv_out, piece_down = step(
            planes,
            [
                *(keep_up, arrived_up, keep_low, arrived_low),
                *(keep_a, arrived_a, keep_b, arrived_b),
                *(keep_down, arrived_down),
            ],
            [
                *(sds((2, *piece), BF16), sds((2, *piece), F32)),
                *(sds((2, *taller), BF16), sds((2, *taller), F32)),
                sds(piece, BF16),
            ],
            "planes",
        )
        arrived = over_z_high(send)
        arrived_qkv_out = over_z_low(send_qkv_out)
        down_high = over_z_high(piece_down)

        def lines(ins, outs):
            outs[0][...] = (ins[0][...] + ins[1][...].astype(F32)).astype(BF16)
            total = ins[2][...] + ins[3][...].astype(F32)
            outs[1][...] = total[1].astype(BF16)
            outs[2][...] = total[0]
            outs[3][0], outs[3][1] = ins[4][...], ins[5][...]

        pieces, send_qkv_out, keep_qkv_out, near_down = step(
            lines,
            [keep, arrived, keep_qkv_out, arrived_qkv_out, piece_down, down_high],
            [
                sds((2, *piece), BF16),
                *(sds(taller, BF16), sds(taller, F32)),
                sds((2, *piece), BF16),
            ],
            "lines",
        )
        pieces_high = over_z_high(pieces)
        arrived_qkv_out = over_z_high(send_qkv_out)
        down_low = over_z_low(near_down)

        def share_high(ins, outs):
            for part in range(2):
                outs[part][0], outs[part][1] = ins[0][part], ins[1][part]
            outs[2][...] = (ins[2][...] + ins[3][...].astype(F32)).astype(BF16)
            outs[3][0], outs[3][1] = ins[4][...], ins[5][...]

        near_up, near_low, piece_qkv_out, near_down = step(
            share_high,
            [pieces, pieces_high, keep_qkv_out, arrived_qkv_out, near_down, down_low],
            [
                *(sds((2, *piece), BF16), sds((2, *piece), BF16)),
                sds(taller, BF16),
                sds((2, 2, *piece), BF16),
            ],
            "share_high",
        )
        up_x, low_low = over_x(near_up), over_z_low(near_low)
        qkv_out_high = over_z_high(piece_qkv_out)
        down_x = over_x(near_down)

        def share_next(ins, outs):
            for i in (0, 1, 2):
                outs[i][0], outs[i][1] = ins[2 * i][...], ins[2 * i + 1][...]
            for x in range(2):
                for low in range(2):
                    for high in range(2):
                        outs[3][0, x, low * 2 + high] = ins[6 + x][low, high]

        near_up, near_low, near_qkv_out, near_down = step(
            share_next,
            [near_up, up_x, near_low, low_low, piece_qkv_out, qkv_out_high, near_down, down_x],
            [
                *(sds((2, 2, *piece), BF16), sds((2, 2, *piece), BF16)),
                sds((2, *taller), BF16),
                sds((1, 2, 4, *piece), BF16),
            ],
            "share_next",
        )
        far_down = over_core(near_down)
        up_low, low_x = over_z_low(near_up), over_x(near_low)
        qkv_out_x, qkv_out_low = over_x(near_qkv_out), over_z_low(near_qkv_out)
        qkv_out_both = swap(near_qkv_out, "dp", 6)
        by_row = lambda t, _: ((t % 2) * 2 + t // 2, 0)
        one_down, two_down, next_down, mark = update_state(
            idx,
            near_down,
            far_down,
            (0,),
            [((HALF, down_rows), by_row)],
            (put_down,),
            [down_t, first_down_t, second_down_t],
            (HALF, down_rows),
            "update_down",
        )

        def share_gate_up(ins, outs):
            for near in range(2):
                for far in range(2):
                    for high in range(2):
                        outs[0][0, near, far * 2 + high] = ins[far][near, high]
                        outs[0][1, far, near * 2 + high] = ins[2 + far][near, high]

        (near_gate_up,) = step(
            share_gate_up,
            [near_up, up_low, near_low, low_x],
            [sds((2, 2, 4, *piece), BF16)],
            "share_gate_up",
            (mark,),
        )
        far_gate_up = over_core(near_gate_up)

        def share_qkv_out(ins, outs):
            for x in range(2):
                for low in range(2):
                    for high in range(2):
                        outs[0][0, x, low * 2 + high] = ins[low * 2 + x][high]

        (near_qkv_out,) = step(
            share_qkv_out,
            [near_qkv_out, qkv_out_x, qkv_out_low, qkv_out_both],
            [sds((1, 2, 4, *taller), BF16)],
            "share_qkv_out",
            (near_gate_up,),
        )
        far_qkv_out = over_core(near_qkv_out)
        one_gate_up, two_gate_up, next_gate_up, mark = update_state(
            idx,
            near_gate_up,
            far_gate_up,
            (0, 1),
            [((HALF, FF), lambda t, _: (t % 2, t // 2))],
            (put_upper, put_lower),
            [w_gate_up, first_gate_up, second_gate_up],
            (HALF, FF),
            "update_gate_up",
            (),
            (near_qkv_out,),
        )
        updated = update_state(
            idx,
            near_qkv_out,
            far_qkv_out,
            (0,),
            [((CUT_ROWS, QKV), by_row), ((CUT_ROWS, width), by_row)],
            (put_columns,),
            [w_qkv, w_out, first_qkv, first_out, second_qkv, second_out],
            (CUT_ROWS + 8, QKV + width),
            "update_qkv_out",
            (norm_gains, first_gains, second_gains),
            (mark,),
        )
        one_qkv, one_out, two_qkv, two_out, next_qkv, next_out = updated[:6]
        one_gains, two_gains, next_gains = updated[6:9]
    else:
        sums = lax.psum((*grad_qkv_out, grad_gate_up[0], grad_down[0].T), ("dp", "shard"))
        grad_qkv_out, grad_gains, grad_gate_up, grad_down = sums

        def own(grad, axis=0):
            size = grad.shape[axis] // groups
            return lax.dynamic_slice_in_dim(grad, owner * size, size, axis)

        one_qkv, two_qkv, next_qkv = adamw(
            w_qkv, first_qkv, second_qkv, own(grad_qkv_out[:, :QKV]), RATE_MATRIX, DECAY_MATRIX
        )
        one_out, two_out, next_out = adamw(
            w_out, first_out, second_out, own(grad_qkv_out[:, QKV:]), RATE_MATRIX, DECAY_MATRIX
        )
        one_gate_up, two_gate_up, next_gate_up = adamw(
            w_gate_up, first_gate_up, second_gate_up, own(grad_gate_up), RATE_MATRIX, DECAY_MATRIX
        )
        one_down, two_down, next_down = [
            a.T
            for a in adamw(
                w_down, first_down, second_down, own(grad_down), RATE_MATRIX, DECAY_MATRIX
            )
        ]
        one_gains, two_gains, next_gains = adamw(
            norm_gains, first_gains, second_gains, own(grad_gains, 1), RATE_GAIN, 0.0
        )
    one_down, two_down, next_down = one_down.T, two_down.T, next_down.T
    return (
        output.T[None],
        token_grad.T[None],
        one_qkv,
        one_out,
        one_gate_up,
        one_down,
        one_gains,
        two_qkv,
        two_out,
        two_gate_up,
        two_down,
        two_gains,
        next_qkv,
        next_out,
        next_gate_up,
        next_down,
        next_gains,
    )


def solution(mesh):
    return jax.shard_map(
        per_device,
        mesh=mesh,
        in_specs=(
            P(("dp", "shard"), None, None),
            P(("dp", "shard"), None),
            P(("dp", "shard"), None, None),
            P("shard", None),
            P("shard", None),
            P("shard", None),
            P("shard", None),
            P(None, "shard"),
            P("shard", None),
            P("shard", None),
            P("shard", None),
            P("shard", None),
            P(None, "shard"),
            P("shard", None),
            P("shard", None),
            P("shard", None),
            P("shard", None),
            P(None, "shard"),
        ),
        out_specs=(
            P(("dp", "shard"), None, None),
            P(("dp", "shard"), None, None),
            P("shard", None),
            P("shard", None),
            P("shard", None),
            P("shard", None),
            P(None, "shard"),
            P("shard", None),
            P("shard", None),
            P("shard", None),
            P("shard", None),
            P(None, "shard"),
            P("shard", None),
            P("shard", None),
            P("shard", None),
            P("shard", None),
            P(None, "shard"),
        ),
        check_vma=False,
    )
```

```python
import functools

import jax
import jax.numpy as jnp
import numpy as np
from jax import lax
from jax.experimental import pallas as pl
from jax.experimental.pallas import tpu as pltpu
from jax.sharding import PartitionSpec as P

HEADS = 9
KV_HEADS = 3
GROUP = HEADS // KV_HEADS
HEAD = 64
FF = 1536
STEP = 10
QUERY = HEADS * HEAD
ROPED = (HEADS + KV_HEADS) * HEAD
QKV = (HEADS + 2 * KV_HEADS) * HEAD
LANES = 128

EPS_NORM = 1e-05
ROPE_BASE = 100000.0
BETA_ONE = 0.9
BETA_TWO = 0.95
RATE_MATRIX = 0.1
RATE_GAIN = 0.3
DECAY_MATRIX = 0.1
EPS_ADAM = 1e-08
MASKED = -1e30
SCALE = float(HEAD) ** (-0.5)
VMEM_LIMIT = 32 * 1024 * 1024
PACK_LIMIT = 60 * 1024 * 1024
HALF = 144
CUT_ROWS = 72
MARK = (8, 128)
CUT_COLUMNS = 384
F32 = jnp.float32
BF16 = jnp.bfloat16


def rotate_block(values, cosine, signed_sine):
    lane = lax.broadcasted_iota(jnp.int32, values.shape, 1)
    swapped = jnp.where(
        lane % HEAD < HEAD // 2,
        pltpu.roll(values, LANES - HEAD // 2, 1),
        pltpu.roll(values, HEAD // 2, 1),
    )
    return values * cosine + swapped * signed_sine


def adamw(weight, first_moment, second_moment, gradient, step_rate, weight_decay):
    first_new = BETA_ONE * first_moment + (1.0 - BETA_ONE) * gradient
    second_new = BETA_TWO * second_moment + (1.0 - BETA_TWO) * gradient * gradient
    fix_one = 1.0 / (1.0 - BETA_ONE**STEP)
    fix_two = 1.0 / (1.0 - BETA_TWO**STEP)
    update = first_new * fix_one / (jnp.sqrt(second_new * fix_two) + EPS_ADAM)
    return (first_new, second_new, weight - step_rate * (update + weight_decay * weight))


def dot(left, right):
    return lax.dot_general(left, right, (((1,), (0,)), ((), ())), preferred_element_type=F32)


def dot_right_t(left, right):
    return lax.dot_general(left, right, (((1,), (1,)), ((), ())), preferred_element_type=F32)


def dot_left_t(left, right):
    return lax.dot_general(left, right, (((0,), (0,)), ((), ())), preferred_element_type=F32)


def norm_scale(values):
    return lax.rsqrt(jnp.mean(values * values, axis=-1, keepdims=True) + EPS_NORM)


def norm_back(grad_normed, normed, scale_rows):
    return scale_rows * (
        grad_normed - normed * jnp.mean(grad_normed * normed, axis=-1, keepdims=True)
    )


class Weight:
    def __init__(self, shape, whole=None, own=(), parts=()):
        self.shape, self.own, self.parts = shape, own, parts
        self.arrays = [whole] if whole is not None else [a[0] for a in (*own, *parts)]
        self.split = whole is None

    def load(self, idx, refs, full):
        if not self.split:
            return refs[0]
        for ref, (_, place) in zip(refs, self.own):
            self.put(full, place(idx[0]), ref[...].astype(BF16))
        for ref, (_, (core, x, low), place) in zip(refs[len(self.own) :], self.parts):
            place = place(1 - idx[0], idx[1] ^ core, idx[2] ^ x, (idx[3] & 1) ^ low)
            rows = ref.shape[0] // HALF * HALF
            self.put(full, place, ref[:rows, :])
        return full

    def put(self, full, position, value):
        where = []
        for axis, tile in ((0, 16), (1, LANES)):
            at, size = position[axis], value.shape[axis]
            if size == self.shape[axis]:
                where.append(slice(None))
            elif isinstance(at, int):
                where.append(slice(at, at + size))
            else:
                where.append(pl.ds(pl.multiple_of(at, tile), size))
        full[tuple(where)] = value


def call(body, idx, arrays, weights, outs, scratch, busy, name, after=(), hand_on=False):
    counts = [len(w.arrays) for w in weights]
    flat = list(arrays) + [a for w in weights for a in w.arrays]
    outs = list(outs)
    split = [w for w in weights if w.split]
    hand_on = hand_on and bool(split)
    if hand_on:
        outs += [sds(split[-1].shape, BF16)]
    made = [pltpu.VMEM(w.shape, BF16) for w in (split[:-1] if hand_on else split)]

    def kernel(*refs):
        refs = list(refs)
        idx_ref = refs.pop(0)
        take = lambda n: [refs.pop(0) for _ in range(n)]
        array_refs = take(len(arrays))
        weight_refs = [take(n) for n in counts]
        take(len(after))
        out_refs = take(len(outs))
        own_scratch = take(len(scratch))
        fulls = take(len(made)) + ([out_refs.pop()] if hand_on else [])
        loads = [
            functools.partial(w.load, idx_ref, r, fulls.pop(0) if w.split else None)
            for w, r in zip(weights, weight_refs)
        ]
        body(idx_ref, array_refs, loads, out_refs, own_scratch)

    return pl.pallas_call(
        kernel,
        out_shape=tuple(outs),
        in_specs=[pl.BlockSpec(memory_space=pltpu.SMEM)]
        + [pl.BlockSpec(memory_space=pltpu.VMEM)] * len(flat)
        + [pl.BlockSpec(memory_space=pl.ANY)] * len(after),
        out_specs=tuple([pl.BlockSpec(memory_space=pltpu.VMEM)] * len(outs)),
        scratch_shapes=list(scratch) + made,
        compiler_params=pltpu.CompilerParams(vmem_limit_bytes=VMEM_LIMIT),
        cost_estimate=busy_for(busy),
        name=name,
    )(idx, *flat, *after)


def busy_for(microseconds):
    return pl.CostEstimate(flops=int(microseconds * 1e9), bytes_accessed=0, transcendentals=0)


def sds(shape, dtype):
    return jax.ShapeDtypeStruct(shape, dtype)


class Pieces:
    def __init__(self, place, parts=1, extra=0):
        self.place, self.parts, self.extra = place, parts, extra

    def outs(self):
        return [sds((self.parts, 2, 8, CUT_ROWS + self.extra, CUT_COLUMNS), BF16)] * 2

    def scratch(self, columns):
        return pltpu.VMEM((8, CUT_ROWS, columns), BF16)

    def store(self, blocks, grad, start=0):
        for i in range(8):
            rows = grad[i * CUT_ROWS : (i + 1) * CUT_ROWS].astype(BF16)
            blocks[i, :, start : start + grad.shape[1]] = rows

    def emit(self, idx, blocks, outs, under=None):
        for other_core, out in enumerate((outs[1], outs[0])):
            for part in range(self.parts):
                for owner in range(2):
                    for slot in range(8):
                        z = ((slot >> 1) & 1) | ((slot & 1) << 1)
                        block, column = self.place(
                            idx[0] ^ owner, idx[1] ^ other_core, idx[2] ^ (slot >> 2), idx[3] ^ z, part
                        )
                        columns = pl.ds(pl.multiple_of(column * CUT_COLUMNS, LANES), CUT_COLUMNS)
                        piece = blocks[block, :, columns]
                        if under is not None:
                            piece = jnp.concatenate(
                                [piece.astype(F32), under[idx[0] ^ owner]], axis=0
                            ).astype(BF16)
                        out[part, owner, slot] = piece


def head_stack(values, kv_head):
    first = kv_head * GROUP
    return jnp.concatenate(
        [values[:, (first + i) * HEAD : (first + i + 1) * HEAD] for i in range(GROUP)], axis=0
    )


def softmax_rows(query, key, allowed):
    scores = jnp.where(allowed, dot_right_t(query, key) * SCALE, MASKED)
    top = jnp.max(scores, axis=-1, keepdims=True)
    exponent = jnp.exp(scores - top)
    return exponent / jnp.sum(exponent, axis=-1, keepdims=True)


def pack_kernel(body, idx, sources, places, outs, name, after=(), limit=PACK_LIMIT):
    windows = [shape for shape, _ in places]

    def kernel(idx_ref, *refs):
        sources_in, refs = refs[: len(sources)], refs[len(sources) + len(after) :]
        out_refs, buffers, sem = refs[: len(outs)], refs[len(outs) : -1], refs[-1]
        copies = []
        for i, (source, (shape, place)) in enumerate(zip(sources_in, places)):
            where = []
            for axis, tile in ((0, 8), (1, LANES)):
                if shape[axis] == source.shape[axis]:
                    where.append(slice(None))
                else:
                    where.append(pl.ds(pl.multiple_of(place(idx_ref)[axis], tile), shape[axis]))
            copies.append(pltpu.make_async_copy(source.at[tuple(where)], buffers[i], sem.at[i]))
        for copy in copies:
            copy.start()
        for copy in copies:
            copy.wait()
        body(idx_ref, buffers, out_refs)

    return pl.pallas_call(
        kernel,
        out_shape=tuple(outs),
        in_specs=[pl.BlockSpec(memory_space=pltpu.SMEM)]
        + [pl.BlockSpec(memory_space=pltpu.HBM)] * len(sources)
        + [pl.BlockSpec(memory_space=pl.ANY)] * len(after),
        out_specs=tuple([pl.BlockSpec(memory_space=pltpu.VMEM)] * len(outs)),
        scratch_shapes=[pltpu.VMEM(w, F32) for w in windows]
        + [pltpu.SemaphoreType.DMA((len(sources),))],
        compiler_params=pltpu.CompilerParams(vmem_limit_bytes=limit),
        cost_estimate=busy_for(10),
        name=name,
    )(idx, *sources, *after)


def cast_out(idx_ref, buffers, outs):
    for buffer, out in zip(buffers, outs):
        out[...] = buffer[...].astype(BF16)


def pack_down(idx, down_t, after):
    shape = (2 * HALF, down_t.shape[1])
    window = (shape, lambda i: (i[1] * 2 * HALF, 0))
    outs = [sds(shape, BF16)]
    return pack_kernel(
        cast_out, idx, [down_t], [window], outs, "pack_down", after, VMEM_LIMIT
    )[0]


def pack_first(idx, w_qkv, w_out, norm_gains, w_gate_up):
    columns = (QKV + w_out.shape[1]) // 2
    quarter = FF // 2
    windows = [((HALF, m.shape[1]), lambda i: (i[1] * HALF, 0)) for m in (w_qkv, w_out)]
    windows.append((norm_gains.shape, lambda i: (0, 0)))
    windows.append(((HALF, quarter), lambda i: (i[1] * HALF, i[2] * quarter)))
    windows.append(((HALF, quarter), lambda i: (i[1] * HALF, FF + (i[3] & 1) * quarter)))

    def body(idx_ref, buffers, outs):
        q_ref, o_ref, gains_ref = buffers[:3]
        both = jnp.concatenate([q_ref[:, columns:], o_ref[...]], axis=1)
        outs[0][:HALF, :] = jnp.where((idx_ref[3] & 1) == 0, q_ref[:, :columns], both).astype(BF16)
        outs[0][HALF:, :] = jnp.zeros((16, columns), BF16)
        outs[0][HALF : HALF + 2, : gains_ref.shape[1]] = gains_ref[...].astype(BF16)
        cast_out(idx_ref, buffers[3:], outs[1:])

    outs = [sds((HALF + 16, columns), BF16)] + [sds((HALF, quarter), BF16)] * 2
    sources = [w_qkv, w_out, norm_gains, w_gate_up, w_gate_up]
    return pack_kernel(body, idx, sources, windows, outs, "pack_first")


def attention_forward(idx, tokens_t, segments, frequency, gains, w_qkv_out):
    width, seq_length = tokens_t.shape
    split_gains = len(gains) > 1

    def body(idx_ref, arrays, loads, outs, scratch):
        x_ref, seg_ref, freq_ref = arrays[:3]
        qkv_ref, o_ref, cos_ref, sin_ref, allowed_ref, gains_ref = outs
        if split_gains:
            own = arrays[3][...].astype(BF16).astype(F32)
            other = arrays[4][HALF : HALF + 8, : width // 2].astype(F32)[:2]
            gains_ref[...] = jnp.where(
                idx_ref[0] == 0,
                jnp.concatenate([own, other], axis=1),
                jnp.concatenate([other, own], axis=1),
            )
        else:
            gains_ref[...] = arrays[3][...]
        seen_doc = jnp.broadcast_to(seg_ref[...], (seq_length, seq_length))
        own_doc = seen_doc.T
        token = lax.broadcasted_iota(jnp.int32, (seq_length, seq_length), 0)
        seen = lax.broadcasted_iota(jnp.int32, (seq_length, seq_length), 1)
        begin = jnp.sum((seen_doc < own_doc).astype(F32), axis=-1, keepdims=True)
        angles = (token.astype(F32) - begin) * freq_ref[...]
        cosine, sine = jnp.cos(angles), jnp.sin(angles)
        sine = jnp.where(seen % HEAD < HEAD // 2, -sine, sine)
        cos_ref[...] = cosine
        sin_ref[...] = sine
        allowed = ((seen_doc == own_doc) & (token >= seen)).astype(F32)
        allowed_ref[...] = allowed
        allowed = jnp.concatenate([allowed] * GROUP, axis=0) > 0.5
        x = x_ref[...].astype(F32).T
        h1 = (x * norm_scale(x) * gains_ref[0:1, :]).astype(BF16)
        projected = dot(h1, loads[0]()[:, :QKV])
        for start in range(0, ROPED, LANES):
            block = projected[:, start : start + LANES]
            qkv_ref[:, start : start + LANES] = rotate_block(block, cosine, sine).astype(BF16)
        qkv_ref[:, ROPED:QKV] = projected[:, ROPED:QKV].astype(BF16)
        qkv = qkv_ref[...]
        for kv in range(KV_HEADS):
            key = qkv[:, QUERY + kv * HEAD : QUERY + (kv + 1) * HEAD]
            value = qkv[:, ROPED + kv * HEAD : ROPED + (kv + 1) * HEAD]
            probs = softmax_rows(head_stack(qkv, kv), key, allowed).astype(BF16)
            attended = dot(probs, value).astype(BF16)
            for i in range(GROUP):
                start = (kv * GROUP + i) * HEAD
                o_ref[:, start : start + HEAD] = attended[i * seq_length : (i + 1) * seq_length]

    square = sds((seq_length, seq_length), F32)
    outs = [sds((seq_length, QKV), BF16), sds((seq_length, QUERY), BF16)]
    outs += [square, square, square, sds((2, width), F32)]
    return call(
        body,
        idx,
        [tokens_t, segments, frequency, *gains],
        [w_qkv_out],
        outs,
        [],
        1,
        "attention",
        hand_on=True,
    )


def feed_forward(idx, tokens_t, attended, gains, cotangent_t, w_qkv_out, w_gate_up, pieces, after):
    width, seq_length = tokens_t.shape

    def body(idx_ref, arrays, loads, outs, scratch):
        x_ref, o_ref, gains_ref, y_ref = arrays
        u_ref, h2_ref, ab_ref, z_ref = outs[:4]
        u = x_ref[...].astype(F32).T + dot(o_ref[...], loads[0]()[:, QKV:])
        u_ref[...] = u
        h2 = (u * norm_scale(u) * gains_ref[1:2, :]).astype(BF16)
        h2_ref[...] = h2
        ab = dot(h2, loads[1]()[...])
        ab_ref[...] = ab
        gate, up = ab[:, :FF], ab[:, FF:]
        z = (gate * jax.nn.sigmoid(gate) * up).astype(BF16)
        z_ref[...] = z
        grad = dot(y_ref[...], z)
        if pieces is None:
            outs[4][...] = grad
        else:
            pieces.store(scratch[0], grad)
            pieces.emit(idx_ref, scratch[0], outs[4:])

    outs = [
        sds((seq_length, width), F32),
        sds((seq_length, width), BF16),
        sds((seq_length, 2 * FF), F32),
        sds((seq_length, FF), BF16),
    ]
    outs += [sds((width, FF), F32)] if pieces is None else pieces.outs()
    scratch = [] if pieces is None else [pieces.scratch(FF)]
    return call(
        body,
        idx,
        [tokens_t, attended, gains, cotangent_t],
        [w_qkv_out, w_gate_up],
        outs,
        scratch,
        2,
        "feed_forward",
        after,
        True,
    )


def feed_back(idx, ab, normed_low, hidden, middle, cotangent_t, down_t, pieces):
    width, seq_length = cotangent_t.shape

    def body(idx_ref, arrays, loads, outs, scratch):
        ab_ref, h2_ref, z_ref, u_ref, y_ref = arrays
        gg_ref, out_ref = outs[:2]
        down = loads[0]()
        gate, up = ab_ref[:, :FF], ab_ref[:, FF:]
        sig = jax.nn.sigmoid(gate)
        grad_hidden = dot_left_t(y_ref[...], down[...])
        gg_ref[:, :FF] = (grad_hidden * up * sig * (1.0 + gate * (1.0 - sig))).astype(BF16)
        gg_ref[:, FF:] = (grad_hidden * gate * sig).astype(BF16)
        grad = dot_left_t(h2_ref[...], gg_ref[...])
        if pieces is None:
            outs[2][...] = grad
        else:
            pieces.store(scratch[0], grad)
            pieces.emit(idx_ref, scratch[0], outs[2:])
        out_ref[...] = (u_ref[...] + dot_right_t(z_ref[...], down[...])).T.astype(BF16)

    outs = [sds((seq_length, 2 * FF), BF16), sds((width, seq_length), BF16)]
    outs += [sds((width, 2 * FF), F32)] if pieces is None else pieces.outs()
    scratch = [] if pieces is None else [pieces.scratch(2 * FF)]
    return call(
        body,
        idx,
        [ab, normed_low, hidden, middle, cotangent_t],
        [down_t],
        outs,
        scratch,
        20,
        "feed_back",
    )


def middle_back(idx, cotangent_t, middle, gated, gains, w_gate_up, w_qkv_out, after):
    width, seq_length = cotangent_t.shape

    def body(idx_ref, arrays, loads, outs, scratch):
        y_ref, u_ref, gg_ref, gains_ref = arrays
        gu_ref, go_ref, gain_ref = outs
        u = u_ref[...]
        scale_two = norm_scale(u)
        normed = u * scale_two
        grad_normed = dot_right_t(gg_ref[...], loads[0]()[...])
        gain_ref[...] = jnp.sum(grad_normed * normed, axis=0, keepdims=True)
        gu = y_ref[...].astype(F32).T + norm_back(
            grad_normed * gains_ref[1:2, :], normed, scale_two
        )
        gu_ref[...] = gu
        go_ref[...] = dot_right_t(gu.astype(BF16), loads[1]()[:, QKV:]).astype(BF16)

    outs = [sds((seq_length, width), F32), sds((seq_length, width), BF16), sds((1, width), F32)]
    return call(
        body,
        idx,
        [cotangent_t, middle, gated, gains],
        [w_gate_up, w_qkv_out],
        outs,
        [],
        20,
        "middle_back",
        after,
    )


def attention_back(
    idx, tokens_t, grad_middle, grad_attended, gain_two, qkv, attended, tables, gains, w_qkv, pieces, after
):
    width, seq_length = tokens_t.shape

    def body(idx_ref, arrays, loads, outs, scratch):
        x_ref, gu_ref, go_ref, gain_two_ref, qkv_ref, o_ref = arrays[:6]
        cos_ref, sin_ref, allowed_ref, gains_ref = arrays[6:]
        grad_ref = outs[0]
        grad_proj, gp_ref, gain_rows, *blocks = scratch
        gu, go = gu_ref[...], go_ref[...]
        gu_low = gu.astype(BF16)
        grad_gain_two = gain_two_ref[...]
        allowed = jnp.concatenate([allowed_ref[...]] * GROUP, axis=0) > 0.5
        qkv_values = qkv_ref[...]
        for kv in range(KV_HEADS):
            key = qkv_values[:, QUERY + kv * HEAD : QUERY + (kv + 1) * HEAD]
            value = qkv_values[:, ROPED + kv * HEAD : ROPED + (kv + 1) * HEAD]
            query = head_stack(qkv_values, kv)
            grad_out = head_stack(go, kv)
            probs = softmax_rows(query, key, allowed)
            grad_probs = dot_right_t(grad_out, value)
            row_delta = jnp.sum(probs * grad_probs, axis=-1, keepdims=True)
            gs = (probs * (grad_probs - row_delta)).astype(BF16)
            grad_query = dot(gs, key) * SCALE
            for i in range(GROUP):
                start = (kv * GROUP + i) * HEAD
                grad_proj[:, start : start + HEAD] = grad_query[
                    i * seq_length : (i + 1) * seq_length
                ]
            start = QUERY + kv * HEAD
            grad_proj[:, start : start + HEAD] = dot_left_t(gs, query) * SCALE
            start = ROPED + kv * HEAD
            grad_proj[:, start : start + HEAD] = dot_left_t(probs.astype(BF16), grad_out)
        for start in range(0, ROPED, LANES):
            gp_ref[:, start : start + LANES] = rotate_block(
                grad_proj[:, start : start + LANES], cos_ref[...], -sin_ref[...]
            ).astype(BF16)
        gp_ref[:, ROPED:QKV] = grad_proj[:, ROPED:QKV].astype(BF16)
        x = x_ref[...].astype(F32).T
        scale_one = norm_scale(x)
        normed = x * scale_one
        h1 = (normed * gains_ref[0:1, :]).astype(BF16)
        grad_qkv = dot_left_t(h1, gp_ref[...])
        grad_out = dot_left_t(o_ref[...], gu_low)
        grad_normed = dot_right_t(gp_ref[...], loads[0]()[:, :QKV])
        grad_gain_one = jnp.sum(grad_normed * normed, axis=0, keepdims=True)
        if pieces is None:
            outs[1][:, :QKV] = grad_qkv
            outs[1][:, QKV:] = grad_out
            outs[2][0:1, :] = grad_gain_one
            outs[2][1:2, :] = grad_gain_two
        else:
            pieces.store(blocks[0], grad_qkv)
            pieces.store(blocks[0], grad_out, QKV)
            half = width // 2
            gain_rows[...] = jnp.zeros_like(gain_rows)
            for owner in range(2):
                columns = slice(owner * half, (owner + 1) * half)
                gain_rows[owner, 0:1, :half] = grad_gain_one[:, columns]
                gain_rows[owner, 1:2, :half] = grad_gain_two[:, columns]
            pieces.emit(idx_ref, blocks[0], outs[1:3], gain_rows)
            outs[3][...] = jnp.zeros_like(outs[3])
        grad_ref[...] = (
            (gu + norm_back(grad_normed * gains_ref[0:1, :], normed, scale_one)).T
        ).astype(BF16)

    outs = [sds((width, seq_length), BF16)]
    scratch = [
        pltpu.VMEM((seq_length, QKV), F32),
        pltpu.VMEM((seq_length, QKV), BF16),
        pltpu.VMEM((2, 8, CUT_COLUMNS), F32),
    ]
    if pieces is None:
        outs += [sds((width, QKV + width), F32), sds((2, width), F32)]
    else:
        outs += pieces.outs() + [sds(MARK, F32)]
        scratch += [pieces.scratch(QKV + width)]
    return call(
        body,
        idx,
        [tokens_t, grad_middle, grad_attended, gain_two, qkv, attended, *tables, gains],
        [w_qkv],
        outs,
        scratch,
        20,
        "attention_back",
        after,
    )


def step(body, arrays, outs, name, after=()):
    def kernel(*refs):
        body(refs[: len(arrays)], refs[len(arrays) + len(after) :])

    return pl.pallas_call(
        kernel,
        out_shape=tuple(outs),
        in_specs=[pl.BlockSpec(memory_space=pltpu.VMEM)] * len(arrays)
        + [pl.BlockSpec(memory_space=pl.ANY)] * len(after),
        out_specs=tuple([pl.BlockSpec(memory_space=pltpu.VMEM)] * len(outs)),
        compiler_params=pltpu.CompilerParams(vmem_limit_bytes=VMEM_LIMIT),
        cost_estimate=busy_for(20),
        name=name,
    )(*arrays, *after)


def add_split(keep, arrived, axis, send_ref, keep_ref):
    total = keep[...].astype(F32) + arrived[...].astype(F32)
    low, high = lax.index_in_dim(total, 0, axis, False), lax.index_in_dim(total, 1, axis, False)
    send_ref[...] = high.astype(BF16)
    keep_ref[...] = low


def add_step(jobs, name, after):
    arrays, outs = [], []
    for keep, arrived, axis in jobs:
        arrays += [keep, arrived]
        shape = keep.shape[:axis] + keep.shape[axis + 1 :]
        outs += [sds(shape, BF16), sds(shape, F32)]

    def body(ins, out_refs):
        for i, (_, _, axis) in enumerate(jobs):
            add_split(ins[2 * i], ins[2 * i + 1], axis, out_refs[2 * i], out_refs[2 * i + 1])

    flat = step(body, arrays, outs, name, after)
    return [(flat[2 * i], flat[2 * i + 1]) for i in range(len(jobs))]


def update_state(idx, near, far, parts, blocks, puts, state, shape, name, gains=(), after=()):
    count = len(state) // 3
    height, width = near.shape[3:]

    def kernel(idx_ref, *refs):
        part_refs, refs = refs[: 2 * len(parts)], refs[2 * len(parts) :]
        state_refs, refs = refs[: 3 * count], refs[3 * count :]
        gain_refs, refs = refs[: len(gains)], refs[len(gains) + len(after) :]
        outs, refs = refs[: 3 * count], refs[3 * count :]
        gain_outs, mark, full = refs[: len(gains)], refs[-2], refs[-1]
        mark[...] = jnp.zeros_like(mark)
        is_near = pl.program_id(0) % 2 == idx_ref[1]
        for i, put in enumerate(puts):
            for z in range(4):
                rel = z ^ idx_ref[3]
                slot = (rel & 1) * 2 + (rel >> 1)
                piece = jnp.where(
                    is_near,
                    part_refs[2 * i][0, 0, slot].astype(F32),
                    part_refs[2 * i + 1][0, 0, slot].astype(F32),
                )
                put(full, z, piece)
        start = 0
        for i in range(count):
            columns = state_refs[i].shape[1]
            first, second, new = adamw(
                state_refs[i][...],
                state_refs[count + i][...],
                state_refs[2 * count + i][...],
                full[: state_refs[i].shape[0], start : start + columns],
                RATE_MATRIX,
                DECAY_MATRIX,
            )
            start += columns
            outs[i][...] = first
            outs[count + i][...] = second
            outs[2 * count + i][...] = new
        if gains:

            @pl.when(pl.program_id(0) == 0)
            def _():
                gradient = full[CUT_ROWS : CUT_ROWS + 2, : gain_refs[0].shape[1]]
                first, second, new = adamw(
                    gain_refs[0][...], gain_refs[1][...], gain_refs[2][...], gradient, RATE_GAIN, 0.0
                )
                gain_outs[0][...] = first
                gain_outs[1][...] = second
                gain_outs[2][...] = new

    state_specs = [pl.BlockSpec(*blocks[i]) for i in range(count)] * 3
    gain_specs = [pl.BlockSpec(g.shape, lambda t, _: (0, 0)) for g in gains]
    part_specs = [
        pl.BlockSpec((1, 1, 4, height, width), lambda t, i, p=p: (p, (t // 2) ^ i[2], 0, 0, 0))
        for p in parts
        for _ in range(2)
    ]
    return pl.pallas_call(
        kernel,
        grid_spec=pltpu.PrefetchScalarGridSpec(
            num_scalar_prefetch=1,
            grid=(4,),
            in_specs=part_specs
            + state_specs
            + gain_specs
            + [pl.BlockSpec(memory_space=pl.ANY)] * len(after),
            out_specs=tuple(state_specs + gain_specs + [pl.BlockSpec(MARK, lambda t, _: (0, 0))]),
            scratch_shapes=[pltpu.VMEM(shape, F32)],
        ),
        out_shape=tuple(sds(a.shape, F32) for a in [*state, *gains]) + (sds(MARK, F32),),
        compiler_params=pltpu.CompilerParams(vmem_limit_bytes=VMEM_LIMIT),
        cost_estimate=busy_for(20),
        name=name,
    )(idx, *[near, far] * len(parts), *state, *gains, *after)


def swap(values, axis, mask):
    size = lax.axis_size(axis)
    return lax.ppermute(values, axis, [(i, i ^ mask) for i in range(size)])


over_y = functools.partial(swap, axis="shard", mask=1)
over_core = functools.partial(swap, axis="dp", mask=1)
over_x = functools.partial(swap, axis="dp", mask=2)
over_z_low = functools.partial(swap, axis="dp", mask=4)
over_z_high = functools.partial(swap, axis="dp", mask=8)


def per_device(
    tokens,
    segments,
    cotangent,
    w_qkv,
    w_out,
    w_gate_up,
    w_down,
    norm_gains,
    first_qkv,
    first_out,
    first_gate_up,
    first_down,
    first_gains,
    second_qkv,
    second_out,
    second_gate_up,
    second_down,
    second_gains,
):
    groups = lax.axis_size("shard")
    replicas = lax.axis_size("dp")
    fast = groups == 2 and replicas == 16
    place_dp = lax.axis_index("dp")
    owner = lax.axis_index("shard")
    idx = jnp.stack([owner, place_dp & 1, (place_dp >> 1) & 1, place_dp >> 2]).astype(jnp.int32)
    x_t, y_t = tokens[0].T, cotangent[0].T
    width, seq_length = x_t.shape
    rows, down_rows = w_qkv.shape[0], w_down.shape[0]
    down_t, first_down_t, second_down_t = w_down.T, first_down.T, second_down.T
    half_size = HEAD // 2
    frequency = ROPE_BASE ** (-(np.arange(half_size) * 2.0 / HEAD))
    frequency = jnp.asarray(np.tile(frequency, 4)[None], F32)
    if fast:
        qo_near, by_x, by_low = pack_first(idx, w_qkv, w_out, norm_gains, w_gate_up)
        qo_near, by_x, by_low = over_y(qo_near), over_y(by_x), over_y(by_low)
        down_near = over_y(pack_down(idx, down_t, (by_low,)))
        by_x_next, by_low_next = over_x(by_x), over_z_low(by_low)
        qo_near_low = over_z_low(qo_near)
        gains = (norm_gains, qo_near)
        own_rows = lambda o: (o * rows, 0)
        own_rows_out = lambda o: (o * rows, QKV)
        qo_place = lambda o, c, x, low: (o * rows + c * HALF, low * ((QKV + width) // 2))
        x_place = lambda o, c, x, low: (o * rows + c * HALF, x * (FF // 2))
        low_place = lambda o, c, x, low: (o * rows + c * HALF, FF + low * (FF // 2))
        mat_qkv_out = Weight(
            (width, QKV + width),
            own=[(w_qkv, own_rows), (w_out, own_rows_out)],
            parts=[
                (qo_near, (0, 0, 0), qo_place),
                (qo_near_low, (0, 0, 1), qo_place),
                (over_core(qo_near), (1, 0, 0), qo_place),
                (over_core(qo_near_low), (1, 0, 1), qo_place),
            ],
        )
        mat_gate_up = Weight(
            (width, 2 * FF),
            own=[(w_gate_up, own_rows)],
            parts=[
                (by_x, (0, 0, 0), x_place),
                (by_x_next, (0, 1, 0), x_place),
                (over_core(by_x), (1, 0, 0), x_place),
                (over_core(by_x_next), (1, 1, 0), x_place),
                (by_low, (0, 0, 0), low_place),
                (by_low_next, (0, 0, 1), low_place),
                (over_core(by_low), (1, 0, 0), low_place),
                (over_core(by_low_next), (1, 0, 1), low_place),
            ],
        )
        cut_qkv_out = Pieces(lambda o, c, x, z, p: (o * 4 + c * 2 + x, z), extra=8)
        cut_gate_up = Pieces(lambda o, c, x, z, p: (o * 4 + c * 2 + p, x * 4 + z), parts=2)
        cut_down = Pieces(lambda o, c, x, z, p: (c * 4 + x * 2 + (z >> 1), o * 2 + (z & 1)))
    else:
        gains = (
            lax.all_gather(norm_gains.astype(BF16), "shard", axis=1, tiled=True).astype(F32),
        )
        mat_qkv, mat_out, mat_gate_up, mat_down = [
            lax.all_gather(m.astype(BF16), "shard", axis=0, tiled=True)
            for m in (w_qkv, w_out, w_gate_up, w_down)
        ]
        mat_qkv_out, mat_gate_up, mat_down = [
            Weight(m.shape, whole=m)
            for m in (jnp.concatenate([mat_qkv, mat_out], axis=1), mat_gate_up, mat_down.T)
        ]
        cut_qkv_out = cut_gate_up = cut_down = None

    qkv, attended, *tables, gains, whole = attention_forward(
        idx, x_t, segments, frequency, gains, mat_qkv_out
    ) + (() if fast else (None,))
    if fast:
        mat_qkv_out = Weight(whole.shape, whole=whole)
    middle, normed_low, ab, hidden, *grad_down = feed_forward(
        idx, x_t, attended, gains, y_t, mat_qkv_out, mat_gate_up, cut_down, ()
    )
    after = ()
    if fast:
        whole = grad_down.pop()
        mat_gate_up = Weight(whole.shape, whole=whole)

        def pass_on(ins, outs):
            outs[0][...] = ins[0][...]

        (down_near,) = step(
            pass_on, [down_near], [sds(down_near.shape, BF16)], "pass_on", (normed_low,)
        )
        down_place = lambda o, c, x, low: (c * 2 * HALF, o * down_rows)
        mat_down = Weight(
            (width, FF),
            own=[(down_t, lambda o: (0, o * down_rows))],
            parts=[
                (down_near, (0, 0, 0), down_place),
                (over_core(down_near), (1, 0, 0), down_place),
            ],
        )
    if fast:
        arrived_down = over_core(grad_down[0])
    gated, output, *grad_gate_up = feed_back(
        idx, ab, normed_low, hidden, middle, y_t, mat_down, cut_gate_up
    )
    if fast:
        cut = lambda a, *lead: a.reshape(*lead, *a.shape[-2:])
        arrived_gate_up = over_core(grad_gate_up[0])
        ((send, keep_down),) = add_step(
            [(grad_down[1][0], arrived_down[0], 0)], "down_core", (gated,)
        )
        arrived_down = over_y(send)
        after = (keep_down,)
    grad_middle, grad_attended, gain_two = middle_back(
        idx, y_t, middle, gated, gains, mat_gate_up, mat_qkv_out, after
    )
    if fast:
        halves = [
            [cut(a[p], *lead) for a in (grad_gate_up[1], arrived_gate_up)]
            for p, lead in ((0, (2, 2, 4)), (1, (4, 2, 2)))
        ]
        (send_up, keep_up), (send_low, keep_low) = add_step(
            [(*halves[0], 1), (*halves[1], 1)], "gate_up_core", (grad_middle,)
        )
        arrived_up, arrived_low = over_x(send_up), over_z_low(send_low)
        after = (keep_up,)
    token_grad, *grad_qkv_out = attention_back(
        idx,
        x_t,
        grad_middle,
        grad_attended,
        gain_two,
        qkv,
        attended,
        tables,
        gains,
        mat_qkv_out,
        cut_qkv_out,
        after,
    )
    if fast:

        def put_down(full, z, piece):
            full[(z >> 1) * CUT_ROWS : ((z >> 1) + 1) * CUT_ROWS, pl.ds((z & 1) * 384, 384)] = piece

        def put_upper(full, z, piece):
            full[:CUT_ROWS, pl.ds(z * 384, 384)] = piece

        def put_lower(full, z, piece):
            full[CUT_ROWS:, pl.ds(z * 384, 384)] = piece

        def put_columns(full, z, piece):
            full[:, pl.ds(z * 384, 384)] = piece

        arrived_qkv_out = over_core(grad_qkv_out[0])
        piece = (CUT_ROWS, CUT_COLUMNS)
        taller = (CUT_ROWS + 8, CUT_COLUMNS)
        ((send, keep_down),) = add_step(
            [(cut(keep_down, 2, 4), cut(arrived_down, 2, 4), 0)], "down_y", (grad_qkv_out[2],)
        )
        arrived_down = over_x(send)
        (send_up, keep_up), (send_low, keep_low) = add_step(
            [
                (cut(keep_up, 2, 2, 2), cut(arrived_up, 2, 2, 2), 1),
                (cut(keep_low, 2, 2, 2), cut(arrived_low, 2, 2, 2), 0),
            ],
            "up_x_low_z",
            (keep_down,),
        )
        arrived_up, arrived_low = over_z_low(send_up), over_y(send_low)

        def qkv_out_core(ins, outs):
            total = ins[0][...].astype(F32) + ins[1][...].astype(F32)
            outs[0][...] = total[1, :, 0].astype(BF16)
            outs[1][...] = total[0, :, 0]
            outs[2][...] = total[:, 1, 1].astype(BF16)
            outs[3][...] = total[:, 0, 1]

        send_a, keep_a, send_b, keep_b = step(
            qkv_out_core,
            [cut(a, 2, 2, 2, 2) for a in (grad_qkv_out[1], arrived_qkv_out)],
            [sds((2, 2, *taller), t) for t in (BF16, F32, BF16, F32)],
            "qkv_out_core",
            (keep_up,),
        )
        arrived_a, arrived_b = over_y(send_a), over_x(send_b)
        ((send, keep_down),) = add_step(
            [(cut(keep_down, 2, 2), cut(arrived_down, 2, 2), 0)], "down_x", (keep_a,)
        )
        arrived_down = over_z_low(send)
        sums = add_step(
            [
                (keep_up, arrived_up, 0),
                (keep_low, arrived_low, 0),
                (keep_a, arrived_a, 0),
                (keep_b, arrived_b, 0),
                (keep_down, arrived_down, 0),
            ],
            "up_z_low_y_qkv_out_xy",
            (keep_down,),
        )
        (send_up, keep_up), (send_low, keep_low), (send_a, keep_a), (send_b, keep_b) = sums[:4]
        ((send, keep_down),) = sums[4:]
        arrived_up, arrived_low = over_y(send_up), over_x(send_low)
        arrived_a, arrived_b = over_x(send_a), over_y(send_b)
        arrived_down = over_z_high(send)

        def planes(ins, outs):
            for i in range(2):
                total = ins[2 * i][...] + ins[2 * i + 1][...].astype(F32)
                outs[0][i] = total[1].astype(BF16)
                outs[1][i] = total[0]
            outs[2][...] = (ins[6][...] + ins[7][...].astype(F32)).astype(BF16)
            outs[3][...] = ins[4][...] + ins[5][...].astype(F32)
            outs[4][...] = (ins[8][...] + ins[9][...].astype(F32)).astype(BF16)

        send, keep, send_qkv_out, keep_qkv_out, piece_down = step(
            planes,
            [
                *(keep_up, arrived_up, keep_low, arrived_low),
                *(keep_a, arrived_a, keep_b, arrived_b),
                *(keep_down, arrived_down),
            ],
            [
                *(sds((2, *piece), BF16), sds((2, *piece), F32)),
                *(sds((2, *taller), BF16), sds((2, *taller), F32)),
                sds(piece, BF16),
            ],
            "planes",
        )
        arrived = over_z_high(send)
        arrived_qkv_out = over_z_low(send_qkv_out)
        down_high = over_z_high(piece_down)

        def lines(ins, outs):
            outs[0][...] = (ins[0][...] + ins[1][...].astype(F32)).astype(BF16)
            total = ins[2][...] + ins[3][...].astype(F32)
            outs[1][...] = total[1].astype(BF16)
            outs[2][...] = total[0]
            outs[3][0], outs[3][1] = ins[4][...], ins[5][...]

        pieces, send_qkv_out, keep_qkv_out, near_down = step(
            lines,
            [keep, arrived, keep_qkv_out, arrived_qkv_out, piece_down, down_high],
            [
                sds((2, *piece), BF16),
                *(sds(taller, BF16), sds(taller, F32)),
                sds((2, *piece), BF16),
            ],
            "lines",
        )
        pieces_high = over_z_high(pieces)
        arrived_qkv_out = over_z_high(send_qkv_out)
        down_low = over_z_low(near_down)

        def share_high(ins, outs):
            for part in range(2):
                outs[part][0], outs[part][1] = ins[0][part], ins[1][part]
            outs[2][...] = (ins[2][...] + ins[3][...].astype(F32)).astype(BF16)
            outs[3][0], outs[3][1] = ins[4][...], ins[5][...]

        near_up, near_low, piece_qkv_out, near_down = step(
            share_high,
            [pieces, pieces_high, keep_qkv_out, arrived_qkv_out, near_down, down_low],
            [
                *(sds((2, *piece), BF16), sds((2, *piece), BF16)),
                sds(taller, BF16),
                sds((2, 2, *piece), BF16),
            ],
            "share_high",
        )
        up_x, low_low = over_x(near_up), over_z_low(near_low)
        qkv_out_high = over_z_high(piece_qkv_out)
        down_x = over_x(near_down)

        def share_next(ins, outs):
            for i in (0, 1, 2):
                outs[i][0], outs[i][1] = ins[2 * i][...], ins[2 * i + 1][...]
            for x in range(2):
                for low in range(2):
                    for high in range(2):
                        outs[3][0, x, low * 2 + high] = ins[6 + x][low, high]

        near_up, near_low, near_qkv_out, near_down = step(
            share_next,
            [near_up, up_x, near_low, low_low, piece_qkv_out, qkv_out_high, near_down, down_x],
            [
                *(sds((2, 2, *piece), BF16), sds((2, 2, *piece), BF16)),
                sds((2, *taller), BF16),
                sds((1, 2, 4, *piece), BF16),
            ],
            "share_next",
        )
        far_down = over_core(near_down)
        up_low, low_x = over_z_low(near_up), over_x(near_low)
        qkv_out_x, qkv_out_low = over_x(near_qkv_out), over_z_low(near_qkv_out)
        qkv_out_both = swap(near_qkv_out, "dp", 6)
        by_row = lambda t, _: ((t % 2) * 2 + t // 2, 0)
        one_down, two_down, next_down, mark = update_state(
            idx,
            near_down,
            far_down,
            (0,),
            [((HALF, down_rows), by_row)],
            (put_down,),
            [down_t, first_down_t, second_down_t],
            (HALF, down_rows),
            "update_down",
        )

        def share_gate_up(ins, outs):
            for near in range(2):
                for far in range(2):
                    for high in range(2):
                        outs[0][0, near, far * 2 + high] = ins[far][near, high]
                        outs[0][1, far, near * 2 + high] = ins[2 + far][near, high]

        (near_gate_up,) = step(
            share_gate_up,
            [near_up, up_low, near_low, low_x],
            [sds((2, 2, 4, *piece), BF16)],
            "share_gate_up",
            (mark,),
        )
        far_gate_up = over_core(near_gate_up)

        def share_qkv_out(ins, outs):
            for x in range(2):
                for low in range(2):
                    for high in range(2):
                        outs[0][0, x, low * 2 + high] = ins[low * 2 + x][high]

        (near_qkv_out,) = step(
            share_qkv_out,
            [near_qkv_out, qkv_out_x, qkv_out_low, qkv_out_both],
            [sds((1, 2, 4, *taller), BF16)],
            "share_qkv_out",
            (near_gate_up,),
        )
        far_qkv_out = over_core(near_qkv_out)
        one_gate_up, two_gate_up, next_gate_up, mark = update_state(
            idx,
            near_gate_up,
            far_gate_up,
            (0, 1),
            [((HALF, FF), lambda t, _: (t % 2, t // 2))],
            (put_upper, put_lower),
            [w_gate_up, first_gate_up, second_gate_up],
            (HALF, FF),
            "update_gate_up",
            (),
            (near_qkv_out,),
        )
        updated = update_state(
            idx,
            near_qkv_out,
            far_qkv_out,
            (0,),
            [((CUT_ROWS, QKV), by_row), ((CUT_ROWS, width), by_row)],
            (put_columns,),
            [w_qkv, w_out, first_qkv, first_out, second_qkv, second_out],
            (CUT_ROWS + 8, QKV + width),
            "update_qkv_out",
            (norm_gains, first_gains, second_gains),
            (mark,),
        )
        one_qkv, one_out, two_qkv, two_out, next_qkv, next_out = updated[:6]
        one_gains, two_gains, next_gains = updated[6:9]
    else:
        sums = lax.psum((*grad_qkv_out, grad_gate_up[0], grad_down[0].T), ("dp", "shard"))
        grad_qkv_out, grad_gains, grad_gate_up, grad_down = sums

        def own(grad, axis=0):
            size = grad.shape[axis] // groups
            return lax.dynamic_slice_in_dim(grad, owner * size, size, axis)

        one_qkv, two_qkv, next_qkv = adamw(
            w_qkv, first_qkv, second_qkv, own(grad_qkv_out[:, :QKV]), RATE_MATRIX, DECAY_MATRIX
        )
        one_out, two_out, next_out = adamw(
            w_out, first_out, second_out, own(grad_qkv_out[:, QKV:]), RATE_MATRIX, DECAY_MATRIX
        )
        one_gate_up, two_gate_up, next_gate_up = adamw(
            w_gate_up, first_gate_up, second_gate_up, own(grad_gate_up), RATE_MATRIX, DECAY_MATRIX
        )
        one_down, two_down, next_down = [
            a.T
            for a in adamw(
                w_down, first_down, second_down, own(grad_down), RATE_MATRIX, DECAY_MATRIX
            )
        ]
        one_gains, two_gains, next_gains = adamw(
            norm_gains, first_gains, second_gains, own(grad_gains, 1), RATE_GAIN, 0.0
        )
    one_down, two_down, next_down = one_down.T, two_down.T, next_down.T
    return (
        output.T[None],
        token_grad.T[None],
        one_qkv,
        one_out,
        one_gate_up,
        one_down,
        one_gains,
        two_qkv,
        two_out,
        two_gate_up,
        two_down,
        two_gains,
        next_qkv,
        next_out,
        next_gate_up,
        next_down,
        next_gains,
    )


def solution(mesh):
    return jax.shard_map(
        per_device,
        mesh=mesh,
        in_specs=(
            P(("dp", "shard"), None, None),
            P(("dp", "shard"), None),
            P(("dp", "shard"), None, None),
            P("shard", None),
            P("shard", None),
            P("shard", None),
            P("shard", None),
            P(None, "shard"),
            P("shard", None),
            P("shard", None),
            P("shard", None),
            P("shard", None),
            P(None, "shard"),
            P("shard", None),
            P("shard", None),
            P("shard", None),
            P("shard", None),
            P(None, "shard"),
        ),
        out_specs=(
            P(("dp", "shard"), None, None),
            P(("dp", "shard"), None, None),
            P("shard", None),
            P("shard", None),
            P("shard", None),
            P("shard", None),
            P(None, "shard"),
            P("shard", None),
            P("shard", None),
            P("shard", None),
            P("shard", None),
            P(None, "shard"),
            P("shard", None),
            P("shard", None),
            P("shard", None),
            P("shard", None),
            P(None, "shard"),
        ),
        check_vma=False,
    )
```

```python
import functools

import jax
import jax.numpy as jnp
import numpy as np
from jax import lax
from jax.experimental import pallas as pl
from jax.experimental.pallas import tpu as pltpu
from jax.sharding import PartitionSpec as P

HEADS = 9
KV_HEADS = 3
GROUP = HEADS // KV_HEADS
HEAD = 64
FF = 1536
STEP = 10
QUERY = HEADS * HEAD
ROPED = (HEADS + KV_HEADS) * HEAD
QKV = (HEADS + 2 * KV_HEADS) * HEAD
LANES = 128

EPS_NORM = 1e-05
ROPE_BASE = 100000.0
BETA_ONE = 0.9
BETA_TWO = 0.95
RATE_MATRIX = 0.1
RATE_GAIN = 0.3
DECAY_MATRIX = 0.1
EPS_ADAM = 1e-08
MASKED = -1e30
SCALE = float(HEAD) ** (-0.5)
VMEM_LIMIT = 32 * 1024 * 1024
PACK_LIMIT = 60 * 1024 * 1024
HALF = 144
CUT_ROWS = 72
MARK = (8, 128)
CUT_COLUMNS = 384
F32 = jnp.float32
BF16 = jnp.bfloat16


def rotate_block(values, cosine, signed_sine):
    lane = lax.broadcasted_iota(jnp.int32, values.shape, 1)
    swapped = jnp.where(
        lane % HEAD < HEAD // 2,
        pltpu.roll(values, LANES - HEAD // 2, 1),
        pltpu.roll(values, HEAD // 2, 1),
    )
    return values * cosine + swapped * signed_sine


def adamw(weight, first_moment, second_moment, gradient, step_rate, weight_decay):
    first_new = BETA_ONE * first_moment + (1.0 - BETA_ONE) * gradient
    second_new = BETA_TWO * second_moment + (1.0 - BETA_TWO) * gradient * gradient
    fix_one = 1.0 / (1.0 - BETA_ONE**STEP)
    fix_two = 1.0 / (1.0 - BETA_TWO**STEP)
    update = first_new * fix_one / (jnp.sqrt(second_new * fix_two) + EPS_ADAM)
    return (first_new, second_new, weight - step_rate * (update + weight_decay * weight))


def dot(left, right):
    return lax.dot_general(left, right, (((1,), (0,)), ((), ())), preferred_element_type=F32)


def dot_right_t(left, right):
    return lax.dot_general(left, right, (((1,), (1,)), ((), ())), preferred_element_type=F32)


def dot_left_t(left, right):
    return lax.dot_general(left, right, (((0,), (0,)), ((), ())), preferred_element_type=F32)


def norm_scale(values):
    return lax.rsqrt(jnp.mean(values * values, axis=-1, keepdims=True) + EPS_NORM)


def norm_back(grad_normed, normed, scale_rows):
    return scale_rows * (
        grad_normed - normed * jnp.mean(grad_normed * normed, axis=-1, keepdims=True)
    )


class Weight:
    def __init__(self, shape, whole=None, own=(), parts=()):
        self.shape, self.own, self.parts = shape, own, parts
        self.arrays = [whole] if whole is not None else [a[0] for a in (*own, *parts)]
        self.split = whole is None

    def load(self, idx, refs, full):
        if not self.split:
            return refs[0]
        for ref, (_, place) in zip(refs, self.own):
            self.put(full, place(idx[0]), ref[...].astype(BF16))
        for ref, (_, (core, x, low), place) in zip(refs[len(self.own) :], self.parts):
            place = place(1 - idx[0], idx[1] ^ core, idx[2] ^ x, (idx[3] & 1) ^ low)
            rows = ref.shape[0] // HALF * HALF
            self.put(full, place, ref[:rows, :])
        return full

    def put(self, full, position, value):
        where = []
        for axis, tile in ((0, 16), (1, LANES)):
            at, size = position[axis], value.shape[axis]
            if size == self.shape[axis]:
                where.append(slice(None))
            elif isinstance(at, int):
                where.append(slice(at, at + size))
            else:
                where.append(pl.ds(pl.multiple_of(at, tile), size))
        full[tuple(where)] = value


def call(body, idx, arrays, weights, outs, scratch, busy, name, after=(), hand_on=False):
    counts = [len(w.arrays) for w in weights]
    flat = list(arrays) + [a for w in weights for a in w.arrays]
    outs = list(outs)
    split = [w for w in weights if w.split]
    hand_on = hand_on and bool(split)
    if hand_on:
        outs += [sds(split[-1].shape, BF16)]
    made = [pltpu.VMEM(w.shape, BF16) for w in (split[:-1] if hand_on else split)]

    def kernel(*refs):
        refs = list(refs)
        idx_ref = refs.pop(0)
        take = lambda n: [refs.pop(0) for _ in range(n)]
        array_refs = take(len(arrays))
        weight_refs = [take(n) for n in counts]
        take(len(after))
        out_refs = take(len(outs))
        own_scratch = take(len(scratch))
        fulls = take(len(made)) + ([out_refs.pop()] if hand_on else [])
        loads = [
            functools.partial(w.load, idx_ref, r, fulls.pop(0) if w.split else None)
            for w, r in zip(weights, weight_refs)
        ]
        body(idx_ref, array_refs, loads, out_refs, own_scratch)

    return pl.pallas_call(
        kernel,
        out_shape=tuple(outs),
        in_specs=[pl.BlockSpec(memory_space=pltpu.SMEM)]
        + [pl.BlockSpec(memory_space=pltpu.VMEM)] * len(flat)
        + [pl.BlockSpec(memory_space=pl.ANY)] * len(after),
        out_specs=tuple([pl.BlockSpec(memory_space=pltpu.VMEM)] * len(outs)),
        scratch_shapes=list(scratch) + made,
        compiler_params=pltpu.CompilerParams(vmem_limit_bytes=VMEM_LIMIT),
        cost_estimate=busy_for(busy),
        name=name,
    )(idx, *flat, *after)


def busy_for(microseconds):
    return pl.CostEstimate(flops=int(microseconds * 1e9), bytes_accessed=0, transcendentals=0)


def sds(shape, dtype):
    return jax.ShapeDtypeStruct(shape, dtype)


class Pieces:
    def __init__(self, place, parts=1, extra=0):
        self.place, self.parts, self.extra = place, parts, extra

    def outs(self):
        return [sds((self.parts, 2, 8, CUT_ROWS + self.extra, CUT_COLUMNS), BF16)] * 2

    def scratch(self, columns):
        return pltpu.VMEM((8, CUT_ROWS, columns), BF16)

    def store(self, blocks, grad, start=0):
        for i in range(8):
            rows = grad[i * CUT_ROWS : (i + 1) * CUT_ROWS].astype(BF16)
            blocks[i, :, start : start + grad.shape[1]] = rows

    def emit(self, idx, blocks, outs, under=None):
        for other_core, out in enumerate((outs[1], outs[0])):
            for part in range(self.parts):
                for owner in range(2):
                    for slot in range(8):
                        z = ((slot >> 1) & 1) | ((slot & 1) << 1)
                        block, column = self.place(
                            idx[0] ^ owner, idx[1] ^ other_core, idx[2] ^ (slot >> 2), idx[3] ^ z, part
                        )
                        columns = pl.ds(pl.multiple_of(column * CUT_COLUMNS, LANES), CUT_COLUMNS)
                        piece = blocks[block, :, columns]
                        if under is not None:
                            piece = jnp.concatenate(
                                [piece.astype(F32), under[idx[0] ^ owner]], axis=0
                            ).astype(BF16)
                        out[part, owner, slot] = piece


def head_stack(values, kv_head):
    first = kv_head * GROUP
    return jnp.concatenate(
        [values[:, (first + i) * HEAD : (first + i + 1) * HEAD] for i in range(GROUP)], axis=0
    )


def softmax_rows(query, key, allowed):
    scores = jnp.where(allowed, dot_right_t(query, key) * SCALE, MASKED)
    top = jnp.max(scores, axis=-1, keepdims=True)
    exponent = jnp.exp(scores - top)
    return exponent / jnp.sum(exponent, axis=-1, keepdims=True)


def pack_kernel(body, idx, sources, places, outs, name, after=(), limit=PACK_LIMIT):
    windows = [shape for shape, _ in places]

    def kernel(idx_ref, *refs):
        sources_in, refs = refs[: len(sources)], refs[len(sources) + len(after) :]
        out_refs, buffers, sem = refs[: len(outs)], refs[len(outs) : -1], refs[-1]
        copies = []
        for i, (source, (shape, place)) in enumerate(zip(sources_in, places)):
            where = []
            for axis, tile in ((0, 8), (1, LANES)):
                if shape[axis] == source.shape[axis]:
                    where.append(slice(None))
                else:
                    where.append(pl.ds(pl.multiple_of(place(idx_ref)[axis], tile), shape[axis]))
            copies.append(pltpu.make_async_copy(source.at[tuple(where)], buffers[i], sem.at[i]))
        for copy in copies:
            copy.start()
        for copy in copies:
            copy.wait()
        body(idx_ref, buffers, out_refs)

    return pl.pallas_call(
        kernel,
        out_shape=tuple(outs),
        in_specs=[pl.BlockSpec(memory_space=pltpu.SMEM)]
        + [pl.BlockSpec(memory_space=pltpu.HBM)] * len(sources)
        + [pl.BlockSpec(memory_space=pl.ANY)] * len(after),
        out_specs=tuple([pl.BlockSpec(memory_space=pltpu.VMEM)] * len(outs)),
        scratch_shapes=[pltpu.VMEM(w, F32) for w in windows]
        + [pltpu.SemaphoreType.DMA((len(sources),))],
        compiler_params=pltpu.CompilerParams(vmem_limit_bytes=limit),
        cost_estimate=busy_for(10),
        name=name,
    )(idx, *sources, *after)


def cast_out(idx_ref, buffers, outs):
    for buffer, out in zip(buffers, outs):
        out[...] = buffer[...].astype(BF16)


def pack_down(idx, down_t, after):
    shape = (2 * HALF, down_t.shape[1])
    window = (shape, lambda i: (i[1] * 2 * HALF, 0))
    outs = [sds(shape, BF16)]
    return pack_kernel(
        cast_out, idx, [down_t], [window], outs, "pack_down", after, VMEM_LIMIT
    )[0]


def pack_first(idx, w_qkv, w_out, norm_gains, w_gate_up):
    columns = (QKV + w_out.shape[1]) // 2
    quarter = FF // 2
    windows = [((HALF, m.shape[1]), lambda i: (i[1] * HALF, 0)) for m in (w_qkv, w_out)]
    windows.append((norm_gains.shape, lambda i: (0, 0)))
    windows.append(((HALF, quarter), lambda i: (i[1] * HALF, i[2] * quarter)))
    windows.append(((HALF, quarter), lambda i: (i[1] * HALF, FF + (i[3] & 1) * quarter)))

    def body(idx_ref, buffers, outs):
        q_ref, o_ref, gains_ref = buffers[:3]
        both = jnp.concatenate([q_ref[:, columns:], o_ref[...]], axis=1)
        outs[0][:HALF, :] = jnp.where((idx_ref[3] & 1) == 0, q_ref[:, :columns], both).astype(BF16)
        outs[0][HALF:, :] = jnp.zeros((16, columns), BF16)
        outs[0][HALF : HALF + 2, : gains_ref.shape[1]] = gains_ref[...].astype(BF16)
        cast_out(idx_ref, buffers[3:], outs[1:])

    outs = [sds((HALF + 16, columns), BF16)] + [sds((HALF, quarter), BF16)] * 2
    sources = [w_qkv, w_out, norm_gains, w_gate_up, w_gate_up]
    return pack_kernel(body, idx, sources, windows, outs, "pack_first")


def attention_forward(idx, tokens_t, segments, frequency, gains, w_qkv_out):
    width, seq_length = tokens_t.shape
    split_gains = len(gains) > 1

    def body(idx_ref, arrays, loads, outs, scratch):
        x_ref, seg_ref, freq_ref = arrays[:3]
        qkv_ref, o_ref, cos_ref, sin_ref, allowed_ref, gains_ref = outs
        if split_gains:
            own = arrays[3][...].astype(BF16).astype(F32)
            other = arrays[4][HALF : HALF + 8, : width // 2].astype(F32)[:2]
            gains_ref[...] = jnp.where(
                idx_ref[0] == 0,
                jnp.concatenate([own, other], axis=1),
                jnp.concatenate([other, own], axis=1),
            )
        else:
            gains_ref[...] = arrays[3][...]
        seen_doc = jnp.broadcast_to(seg_ref[...], (seq_length, seq_length))
        own_doc = seen_doc.T
        token = lax.broadcasted_iota(jnp.int32, (seq_length, seq_length), 0)
        seen = lax.broadcasted_iota(jnp.int32, (seq_length, seq_length), 1)
        begin = jnp.sum((seen_doc < own_doc).astype(F32), axis=-1, keepdims=True)
        angles = (token.astype(F32) - begin) * freq_ref[...]
        cosine, sine = jnp.cos(angles), jnp.sin(angles)
        sine = jnp.where(seen % HEAD < HEAD // 2, -sine, sine)
        cos_ref[...] = cosine
        sin_ref[...] = sine
        allowed = ((seen_doc == own_doc) & (token >= seen)).astype(F32)
        allowed_ref[...] = allowed
        allowed = jnp.concatenate([allowed] * GROUP, axis=0) > 0.5
        x = x_ref[...].astype(F32).T
        h1 = (x * norm_scale(x) * gains_ref[0:1, :]).astype(BF16)
        projected = dot(h1, loads[0]()[:, :QKV])
        for start in range(0, ROPED, LANES):
            block = projected[:, start : start + LANES]
            qkv_ref[:, start : start + LANES] = rotate_block(block, cosine, sine).astype(BF16)
        qkv_ref[:, ROPED:QKV] = projected[:, ROPED:QKV].astype(BF16)
        qkv = qkv_ref[...]
        for kv in range(KV_HEADS):
            key = qkv[:, QUERY + kv * HEAD : QUERY + (kv + 1) * HEAD]
            value = qkv[:, ROPED + kv * HEAD : ROPED + (kv + 1) * HEAD]
            probs = softmax_rows(head_stack(qkv, kv), key, allowed).astype(BF16)
            attended = dot(probs, value).astype(BF16)
            for i in range(GROUP):
                start = (kv * GROUP + i) * HEAD
                o_ref[:, start : start + HEAD] = attended[i * seq_length : (i + 1) * seq_length]

    square = sds((seq_length, seq_length), F32)
    outs = [sds((seq_length, QKV), BF16), sds((seq_length, QUERY), BF16)]
    outs += [square, square, square, sds((2, width), F32)]
    return call(
        body,
        idx,
        [tokens_t, segments, frequency, *gains],
        [w_qkv_out],
        outs,
        [],
        1,
        "attention",
        hand_on=True,
    )


def feed_forward(idx, tokens_t, attended, gains, cotangent_t, w_qkv_out, w_gate_up, pieces, after):
    width, seq_length = tokens_t.shape

    def body(idx_ref, arrays, loads, outs, scratch):
        x_ref, o_ref, gains_ref, y_ref = arrays
        u_ref, h2_ref, ab_ref, z_ref = outs[:4]
        u = x_ref[...].astype(F32).T + dot(o_ref[...], loads[0]()[:, QKV:])
        u_ref[...] = u
        h2 = (u * norm_scale(u) * gains_ref[1:2, :]).astype(BF16)
        h2_ref[...] = h2
        ab = dot(h2, loads[1]()[...])
        ab_ref[...] = ab
        gate, up = ab[:, :FF], ab[:, FF:]
        z = (gate * jax.nn.sigmoid(gate) * up).astype(BF16)
        z_ref[...] = z
        grad = dot(y_ref[...], z)
        if pieces is None:
            outs[4][...] = grad
        else:
            pieces.store(scratch[0], grad)
            pieces.emit(idx_ref, scratch[0], outs[4:])

    outs = [
        sds((seq_length, width), F32),
        sds((seq_length, width), BF16),
        sds((seq_length, 2 * FF), F32),
        sds((seq_length, FF), BF16),
    ]
    outs += [sds((width, FF), F32)] if pieces is None else pieces.outs()
    scratch = [] if pieces is None else [pieces.scratch(FF)]
    return call(
        body,
        idx,
        [tokens_t, attended, gains, cotangent_t],
        [w_qkv_out, w_gate_up],
        outs,
        scratch,
        2,
        "feed_forward",
        after,
        True,
    )


def feed_back(idx, ab, normed_low, cotangent_t, down_t, pieces):
    width, seq_length = cotangent_t.shape

    def body(idx_ref, arrays, loads, outs, scratch):
        ab_ref, h2_ref, y_ref = arrays
        gg_ref = outs[0]
        gate, up = ab_ref[:, :FF], ab_ref[:, FF:]
        sig = jax.nn.sigmoid(gate)
        grad_hidden = dot_left_t(y_ref[...], loads[0]()[...])
        gg_ref[:, :FF] = (grad_hidden * up * sig * (1.0 + gate * (1.0 - sig))).astype(BF16)
        gg_ref[:, FF:] = (grad_hidden * gate * sig).astype(BF16)
        grad = dot_left_t(h2_ref[...], gg_ref[...])
        if pieces is None:
            outs[1][...] = grad
        else:
            pieces.store(scratch[0], grad)
            pieces.emit(idx_ref, scratch[0], outs[1:])

    outs = [sds((seq_length, 2 * FF), BF16)]
    outs += [sds((width, 2 * FF), F32)] if pieces is None else pieces.outs()
    scratch = [] if pieces is None else [pieces.scratch(2 * FF)]
    return call(
        body,
        idx,
        [ab, normed_low, cotangent_t],
        [down_t],
        outs,
        scratch,
        20,
        "feed_back",
        hand_on=True,
    )


def layer_output(middle, hidden, down_t, after):
    seq_length, width = middle.shape

    def body(ins, outs):
        outs[0][...] = (ins[0][...] + dot_right_t(ins[1][...], ins[2][...])).T.astype(BF16)

    return step(
        body, [middle, hidden, down_t], [sds((width, seq_length), BF16)], "layer_output", after, 2
    )[0]


def middle_back(idx, cotangent_t, middle, gated, gains, w_gate_up, w_qkv_out, after):
    width, seq_length = cotangent_t.shape

    def body(idx_ref, arrays, loads, outs, scratch):
        y_ref, u_ref, gg_ref, gains_ref = arrays
        gu_ref, go_ref, gain_ref = outs
        u = u_ref[...]
        scale_two = norm_scale(u)
        normed = u * scale_two
        grad_normed = dot_right_t(gg_ref[...], loads[0]()[...])
        gain_ref[...] = jnp.sum(grad_normed * normed, axis=0, keepdims=True)
        gu = y_ref[...].astype(F32).T + norm_back(
            grad_normed * gains_ref[1:2, :], normed, scale_two
        )
        gu_ref[...] = gu
        go_ref[...] = dot_right_t(gu.astype(BF16), loads[1]()[:, QKV:]).astype(BF16)

    outs = [sds((seq_length, width), F32), sds((seq_length, width), BF16), sds((1, width), F32)]
    return call(
        body,
        idx,
        [cotangent_t, middle, gated, gains],
        [w_gate_up, w_qkv_out],
        outs,
        [],
        20,
        "middle_back",
        after,
    )


def attention_back(
    idx, tokens_t, grad_middle, grad_attended, gain_two, qkv, attended, tables, gains, w_qkv, pieces, after
):
    width, seq_length = tokens_t.shape

    def body(idx_ref, arrays, loads, outs, scratch):
        x_ref, gu_ref, go_ref, gain_two_ref, qkv_ref, o_ref = arrays[:6]
        cos_ref, sin_ref, allowed_ref, gains_ref = arrays[6:]
        grad_ref = outs[0]
        grad_proj, gp_ref, gain_rows, *blocks = scratch
        gu, go = gu_ref[...], go_ref[...]
        gu_low = gu.astype(BF16)
        grad_gain_two = gain_two_ref[...]
        allowed = jnp.concatenate([allowed_ref[...]] * GROUP, axis=0) > 0.5
        qkv_values = qkv_ref[...]
        for kv in range(KV_HEADS):
            key = qkv_values[:, QUERY + kv * HEAD : QUERY + (kv + 1) * HEAD]
            value = qkv_values[:, ROPED + kv * HEAD : ROPED + (kv + 1) * HEAD]
            query = head_stack(qkv_values, kv)
            grad_out = head_stack(go, kv)
            probs = softmax_rows(query, key, allowed)
            grad_probs = dot_right_t(grad_out, value)
            row_delta = jnp.sum(probs * grad_probs, axis=-1, keepdims=True)
            gs = (probs * (grad_probs - row_delta)).astype(BF16)
            grad_query = dot(gs, key) * SCALE
            for i in range(GROUP):
                start = (kv * GROUP + i) * HEAD
                grad_proj[:, start : start + HEAD] = grad_query[
                    i * seq_length : (i + 1) * seq_length
                ]
            start = QUERY + kv * HEAD
            grad_proj[:, start : start + HEAD] = dot_left_t(gs, query) * SCALE
            start = ROPED + kv * HEAD
            grad_proj[:, start : start + HEAD] = dot_left_t(probs.astype(BF16), grad_out)
        for start in range(0, ROPED, LANES):
            gp_ref[:, start : start + LANES] = rotate_block(
                grad_proj[:, start : start + LANES], cos_ref[...], -sin_ref[...]
            ).astype(BF16)
        gp_ref[:, ROPED:QKV] = grad_proj[:, ROPED:QKV].astype(BF16)
        x = x_ref[...].astype(F32).T
        scale_one = norm_scale(x)
        normed = x * scale_one
        h1 = (normed * gains_ref[0:1, :]).astype(BF16)
        grad_qkv = dot_left_t(h1, gp_ref[...])
        grad_out = dot_left_t(o_ref[...], gu_low)
        grad_normed = dot_right_t(gp_ref[...], loads[0]()[:, :QKV])
        grad_gain_one = jnp.sum(grad_normed * normed, axis=0, keepdims=True)
        if pieces is None:
            outs[1][:, :QKV] = grad_qkv
            outs[1][:, QKV:] = grad_out
            outs[2][0:1, :] = grad_gain_one
            outs[2][1:2, :] = grad_gain_two
        else:
            pieces.store(blocks[0], grad_qkv)
            pieces.store(blocks[0], grad_out, QKV)
            half = width // 2
            gain_rows[...] = jnp.zeros_like(gain_rows)
            for owner in range(2):
                columns = slice(owner * half, (owner + 1) * half)
                gain_rows[owner, 0:1, :half] = grad_gain_one[:, columns]
                gain_rows[owner, 1:2, :half] = grad_gain_two[:, columns]
            pieces.emit(idx_ref, blocks[0], outs[1:3], gain_rows)
            outs[3][...] = jnp.zeros_like(outs[3])
        grad_ref[...] = (
            (gu + norm_back(grad_normed * gains_ref[0:1, :], normed, scale_one)).T
        ).astype(BF16)

    outs = [sds((width, seq_length), BF16)]
    scratch = [
        pltpu.VMEM((seq_length, QKV), F32),
        pltpu.VMEM((seq_length, QKV), BF16),
        pltpu.VMEM((2, 8, CUT_COLUMNS), F32),
    ]
    if pieces is None:
        outs += [sds((width, QKV + width), F32), sds((2, width), F32)]
    else:
        outs += pieces.outs() + [sds(MARK, F32)]
        scratch += [pieces.scratch(QKV + width)]
    return call(
        body,
        idx,
        [tokens_t, grad_middle, grad_attended, gain_two, qkv, attended, *tables, gains],
        [w_qkv],
        outs,
        scratch,
        20,
        "attention_back",
        after,
    )


def step(body, arrays, outs, name, after=(), busy=20):
    def kernel(*refs):
        body(refs[: len(arrays)], refs[len(arrays) + len(after) :])

    return pl.pallas_call(
        kernel,
        out_shape=tuple(outs),
        in_specs=[pl.BlockSpec(memory_space=pltpu.VMEM)] * len(arrays)
        + [pl.BlockSpec(memory_space=pl.ANY)] * len(after),
        out_specs=tuple([pl.BlockSpec(memory_space=pltpu.VMEM)] * len(outs)),
        compiler_params=pltpu.CompilerParams(vmem_limit_bytes=VMEM_LIMIT),
        cost_estimate=busy_for(busy),
        name=name,
    )(*arrays, *after)


def pass_on(ins, outs):
    outs[0][...] = ins[0][...]


def add_split(keep, arrived, axis, send_ref, keep_ref):
    total = keep[...].astype(F32) + arrived[...].astype(F32)
    low, high = lax.index_in_dim(total, 0, axis, False), lax.index_in_dim(total, 1, axis, False)
    send_ref[...] = high.astype(BF16)
    keep_ref[...] = low


def add_step(jobs, name, after):
    arrays, outs = [], []
    for keep, arrived, axis in jobs:
        arrays += [keep, arrived]
        shape = keep.shape[:axis] + keep.shape[axis + 1 :]
        outs += [sds(shape, BF16), sds(shape, F32)]

    def body(ins, out_refs):
        for i, (_, _, axis) in enumerate(jobs):
            add_split(ins[2 * i], ins[2 * i + 1], axis, out_refs[2 * i], out_refs[2 * i + 1])

    flat = step(body, arrays, outs, name, after)
    return [(flat[2 * i], flat[2 * i + 1]) for i in range(len(jobs))]


def update_half(idx, far, pieces, place, height, state, earlier, gains, name, after):
    count = len(state) // 3
    columns = [a.shape[1] for a in state[:count]]
    chunks = height // CUT_ROWS
    order = [(k, count + k, 2 * count + k) for k in range(count)]

    def kernel(idx_ref, *refs):
        refs = list(refs)
        take = lambda n: [refs.pop(0) for _ in range(n)]
        (piece_ref,) = take(1)
        state_refs, gain_refs = take(3 * count), take(len(gains))
        take(len(earlier) + len(after))
        outs, gain_outs, (mark,) = take(3 * count), take(len(gains)), take(1)
        buffers, (full, sem) = take(3 * count), refs
        mark[...] = jnp.zeros_like(mark)
        for part in range(pieces.shape[0]):
            for x in range(2):
                for slot in range(4):
                    z = (slot >> 1) | ((slot & 1) << 1)
                    row, column = place(part, idx_ref[2] ^ x, idx_ref[3] ^ z)
                    rows = pl.ds(pl.multiple_of(row, 8), CUT_ROWS)
                    where = pl.ds(pl.multiple_of(column, LANES), CUT_COLUMNS)
                    full[rows, where] = piece_ref[part, x, slot, :CUT_ROWS, :].astype(F32)
        base = (idx_ref[1] ^ far) * height
        copies = []
        for chunk in range(chunks):

            def eight_rows(i, carry, chunk=chunk):
                near_rows = pl.ds(pl.multiple_of(chunk * CUT_ROWS + i * 8, 8), 8)
                rows = pl.ds(pl.multiple_of(base + chunk * CUT_ROWS + i * 8, 8), 8)
                start = 0
                for k in range(count):
                    for at in range(0, columns[k], 768):
                        size = min(768, columns[k] - at)
                        where = slice(at, at + size)
                        results = adamw(
                            *[state_refs[j][rows, where] for j in order[k]],
                            full[near_rows, start + at : start + at + size],
                            RATE_MATRIX,
                            DECAY_MATRIX,
                        )
                        for j, result in zip(order[k], results):
                            buffers[j][near_rows, where] = result
                    start += columns[k]
                return carry

            lax.fori_loop(0, CUT_ROWS // 8, eight_rows, 0)
            near_rows = pl.ds(chunk * CUT_ROWS, CUT_ROWS)
            rows = pl.ds(pl.multiple_of(base + chunk * CUT_ROWS, 8), CUT_ROWS)
            for j in range(3 * count):
                copy = pltpu.make_async_copy(
                    buffers[j].at[near_rows], outs[j].at[rows], sem.at[chunk, j]
                )
                copy.start()
                copies.append(copy)
        if gains:
            gradient = piece_ref[0, 0, 0, CUT_ROWS:, :].astype(F32)[:2, : gains[0].shape[1]]
            results = adamw(*[g[...] for g in gain_refs], gradient, RATE_GAIN, 0.0)
            for out, result in zip(gain_outs, results):
                out[...] = result
        for copy in copies:
            copy.wait()

    vmem, anywhere = pl.BlockSpec(memory_space=pltpu.VMEM), pl.BlockSpec(memory_space=pl.ANY)
    first_earlier = 2 + 3 * count + len(gains)
    return pl.pallas_call(
        kernel,
        out_shape=tuple(sds(a.shape, F32) for a in [*state, *gains]) + (sds(MARK, F32),),
        in_specs=[pl.BlockSpec(memory_space=pltpu.SMEM)]
        + [vmem] * (1 + 3 * count + len(gains))
        + [anywhere] * (len(earlier) + len(after)),
        out_specs=tuple([anywhere] * (3 * count) + [vmem] * (len(gains) + 1)),
        scratch_shapes=[pltpu.VMEM((height, a.shape[1]), F32) for a in state]
        + [pltpu.VMEM((height, sum(columns)), F32), pltpu.SemaphoreType.DMA((chunks, 3 * count))],
        input_output_aliases={first_earlier + i: i for i in range(len(earlier))},
        compiler_params=pltpu.CompilerParams(vmem_limit_bytes=VMEM_LIMIT),
        cost_estimate=busy_for(20),
        name=name,
    )(idx, pieces, *state, *gains, *earlier, *after)


def swap(values, axis, mask):
    size = lax.axis_size(axis)
    return lax.ppermute(values, axis, [(i, i ^ mask) for i in range(size)])


over_y = functools.partial(swap, axis="shard", mask=1)
over_core = functools.partial(swap, axis="dp", mask=1)
over_x = functools.partial(swap, axis="dp", mask=2)
over_z_low = functools.partial(swap, axis="dp", mask=4)
over_z_high = functools.partial(swap, axis="dp", mask=8)


def per_device(
    tokens,
    segments,
    cotangent,
    w_qkv,
    w_out,
    w_gate_up,
    w_down,
    norm_gains,
    first_qkv,
    first_out,
    first_gate_up,
    first_down,
    first_gains,
    second_qkv,
    second_out,
    second_gate_up,
    second_down,
    second_gains,
):
    groups = lax.axis_size("shard")
    replicas = lax.axis_size("dp")
    fast = groups == 2 and replicas == 16
    place_dp = lax.axis_index("dp")
    owner = lax.axis_index("shard")
    idx = jnp.stack([owner, place_dp & 1, (place_dp >> 1) & 1, place_dp >> 2]).astype(jnp.int32)
    x_t, y_t = tokens[0].T, cotangent[0].T
    width, seq_length = x_t.shape
    rows, down_rows = w_qkv.shape[0], w_down.shape[0]
    down_t, first_down_t, second_down_t = w_down.T, first_down.T, second_down.T
    half_size = HEAD // 2
    frequency = ROPE_BASE ** (-(np.arange(half_size) * 2.0 / HEAD))
    frequency = jnp.asarray(np.tile(frequency, 4)[None], F32)
    if fast:
        qo_near, by_x, by_low = pack_first(idx, w_qkv, w_out, norm_gains, w_gate_up)
        qo_near, by_x, by_low = over_y(qo_near), over_y(by_x), over_y(by_low)
        down_near = over_y(pack_down(idx, down_t, (by_low,)))
        by_x_next, by_low_next = over_x(by_x), over_z_low(by_low)
        qo_near_low = over_z_low(qo_near)
        gains = (norm_gains, qo_near)
        (low_far,) = step(
            pass_on, [over_core(by_low_next)], [sds(by_low.shape, BF16)], "pass_on_low", (), 1
        )
        own_rows = lambda o: (o * rows, 0)
        own_rows_out = lambda o: (o * rows, QKV)
        qo_place = lambda o, c, x, low: (o * rows + c * HALF, low * ((QKV + width) // 2))
        x_place = lambda o, c, x, low: (o * rows + c * HALF, x * (FF // 2))
        low_place = lambda o, c, x, low: (o * rows + c * HALF, FF + low * (FF // 2))
        mat_qkv_out = Weight(
            (width, QKV + width),
            own=[(w_qkv, own_rows), (w_out, own_rows_out)],
            parts=[
                (qo_near, (0, 0, 0), qo_place),
                (qo_near_low, (0, 0, 1), qo_place),
                (over_core(qo_near), (1, 0, 0), qo_place),
                (over_core(qo_near_low), (1, 0, 1), qo_place),
            ],
        )
        mat_gate_up = Weight(
            (width, 2 * FF),
            own=[(w_gate_up, own_rows)],
            parts=[
                (by_x, (0, 0, 0), x_place),
                (by_x_next, (0, 1, 0), x_place),
                (over_core(by_x), (1, 0, 0), x_place),
                (over_core(by_x_next), (1, 1, 0), x_place),
                (by_low, (0, 0, 0), low_place),
                (by_low_next, (0, 0, 1), low_place),
                (over_core(by_low), (1, 0, 0), low_place),
                (low_far, (1, 0, 1), low_place),
            ],
        )
        cut_qkv_out = Pieces(lambda o, c, x, z, p: (o * 4 + c * 2 + x, z), extra=8)
        cut_gate_up = Pieces(lambda o, c, x, z, p: (o * 4 + c * 2 + p, x * 4 + z), parts=2)
        cut_down = Pieces(lambda o, c, x, z, p: (c * 4 + x * 2 + (z >> 1), o * 2 + (z & 1)))
    else:
        gains = (
            lax.all_gather(norm_gains.astype(BF16), "shard", axis=1, tiled=True).astype(F32),
        )
        mat_qkv, mat_out, mat_gate_up, mat_down = [
            lax.all_gather(m.astype(BF16), "shard", axis=0, tiled=True)
            for m in (w_qkv, w_out, w_gate_up, w_down)
        ]
        mat_qkv_out, mat_gate_up, mat_down = [
            Weight(m.shape, whole=m)
            for m in (jnp.concatenate([mat_qkv, mat_out], axis=1), mat_gate_up, mat_down.T)
        ]
        cut_qkv_out = cut_gate_up = cut_down = None

    qkv, attended, *tables, gains, whole = attention_forward(
        idx, x_t, segments, frequency, gains, mat_qkv_out
    ) + (() if fast else (None,))
    if fast:
        mat_qkv_out = Weight(whole.shape, whole=whole)
    middle, normed_low, ab, hidden, *grad_down = feed_forward(
        idx, x_t, attended, gains, y_t, mat_qkv_out, mat_gate_up, cut_down, ()
    )
    after = ()
    if fast:
        whole = grad_down.pop()
        mat_gate_up = Weight(whole.shape, whole=whole)

        (down_near,) = step(
            pass_on, [down_near], [sds(down_near.shape, BF16)], "pass_on", (normed_low,)
        )
        down_place = lambda o, c, x, low: (c * 2 * HALF, o * down_rows)
        mat_down = Weight(
            (width, FF),
            own=[(down_t, lambda o: (0, o * down_rows))],
            parts=[
                (down_near, (0, 0, 0), down_place),
                (over_core(down_near), (1, 0, 0), down_place),
            ],
        )
    if fast:
        arrived_down = over_core(grad_down[0])
    gated, *grad_gate_up = feed_back(idx, ab, normed_low, y_t, mat_down, cut_gate_up)
    if not fast:
        output = layer_output(middle, hidden, mat_down.arrays[0], ())
    if fast:
        down_whole = grad_gate_up.pop()
        cut = lambda a, *lead: a.reshape(*lead, *a.shape[-2:])
        arrived_gate_up = over_core(grad_gate_up[0])
        ((send, keep_down),) = add_step(
            [(grad_down[1][0], arrived_down[0], 0)], "down_core", (gated,)
        )
        arrived_down = over_y(send)
        after = (keep_down,)
    grad_middle, grad_attended, gain_two = middle_back(
        idx, y_t, middle, gated, gains, mat_gate_up, mat_qkv_out, after
    )
    if fast:
        halves = [
            [cut(a[p], *lead) for a in (grad_gate_up[1], arrived_gate_up)]
            for p, lead in ((0, (2, 2, 4)), (1, (4, 2, 2)))
        ]
        (send_up, keep_up), (send_low, keep_low) = add_step(
            [(*halves[0], 1), (*halves[1], 1)], "gate_up_core", (grad_middle,)
        )
        arrived_up, arrived_low = over_x(send_up), over_z_low(send_low)
        after = (keep_up,)
    token_grad, *grad_qkv_out = attention_back(
        idx,
        x_t,
        grad_middle,
        grad_attended,
        gain_two,
        qkv,
        attended,
        tables,
        gains,
        mat_qkv_out,
        cut_qkv_out,
        after,
    )
    if fast:

        arrived_qkv_out = over_core(grad_qkv_out[0])
        piece = (CUT_ROWS, CUT_COLUMNS)
        taller = (CUT_ROWS + 8, CUT_COLUMNS)
        ((send, keep_down),) = add_step(
            [(cut(keep_down, 2, 4), cut(arrived_down, 2, 4), 0)], "down_y", (grad_qkv_out[2],)
        )
        arrived_down = over_x(send)
        (send_up, keep_up), (send_low, keep_low) = add_step(
            [
                (cut(keep_up, 2, 2, 2), cut(arrived_up, 2, 2, 2), 1),
                (cut(keep_low, 2, 2, 2), cut(arrived_low, 2, 2, 2), 2),
            ],
            "up_x_low_z",
            (keep_down,),
        )
        arrived_up, arrived_low = over_z_low(send_up), over_z_high(send_low)

        def qkv_out_core(ins, outs):
            total = ins[0][...].astype(F32) + ins[1][...].astype(F32)
            outs[0][...] = total[1, :, 0].astype(BF16)
            outs[1][...] = total[0, :, 0]
            outs[2][...] = total[:, 1, 1].astype(BF16)
            outs[3][...] = total[:, 0, 1]

        send_a, keep_a, send_b, keep_b = step(
            qkv_out_core,
            [cut(a, 2, 2, 2, 2) for a in (grad_qkv_out[1], arrived_qkv_out)],
            [sds((2, 2, *taller), t) for t in (BF16, F32, BF16, F32)],
            "qkv_out_core",
            (keep_up,),
        )
        arrived_a, arrived_b = over_y(send_a), over_x(send_b)
        ((send, keep_down),) = add_step(
            [(cut(keep_down, 2, 2), cut(arrived_down, 2, 2), 0)], "down_x", (keep_a,)
        )
        arrived_down = over_z_low(send)
        output = layer_output(middle, hidden, down_whole, (keep_down,))
        sums = add_step(
            [
                (keep_up, arrived_up, 0),
                (keep_low, arrived_low, 1),
                (keep_a, arrived_a, 0),
                (keep_b, arrived_b, 0),
                (keep_down, arrived_down, 0),
            ],
            "up_z_low_y_qkv_out_xy",
            (keep_down,),
        )
        (send_up, keep_up), (send_low, keep_low), (send_a, keep_a), (send_b, keep_b) = sums[:4]
        ((send, keep_down),) = sums[4:]
        arrived_up, arrived_low = over_y(send_up), over_x(send_low)
        arrived_a, arrived_b = over_x(send_a), over_y(send_b)
        arrived_down = over_z_high(send)

        def planes(ins, outs):
            for i in range(2):
                total = ins[2 * i][...] + ins[2 * i + 1][...].astype(F32)
                outs[i][...] = total[1].astype(BF16)
                outs[2][i] = total[0]
            outs[3][...] = (ins[6][...] + ins[7][...].astype(F32)).astype(BF16)
            outs[4][...] = ins[4][...] + ins[5][...].astype(F32)
            outs[5][...] = (ins[8][...] + ins[9][...].astype(F32)).astype(BF16)

        send_up, send_low, keep, send_qkv_out, keep_qkv_out, piece_down = step(
            planes,
            [
                *(keep_up, arrived_up, keep_low, arrived_low),
                *(keep_a, arrived_a, keep_b, arrived_b),
                *(keep_down, arrived_down),
            ],
            [
                *(sds(piece, BF16), sds(piece, BF16), sds((2, *piece), F32)),
                *(sds((2, *taller), BF16), sds((2, *taller), F32)),
                sds(piece, BF16),
            ],
            "planes",
        )
        arrived_up, arrived_low = over_z_high(send_up), over_y(send_low)
        arrived_qkv_out = over_z_low(send_qkv_out)
        down_high = over_z_high(piece_down)

        def lines(ins, outs):
            for part in range(2):
                total = ins[0][part] + ins[1 + part][...].astype(F32)
                outs[0][part] = total.astype(BF16)
            total = ins[3][...] + ins[4][...].astype(F32)
            outs[1][...] = total[1].astype(BF16)
            outs[2][...] = total[0]
            outs[3][0], outs[3][1] = ins[5][...], ins[6][...]

        pieces, send_qkv_out, keep_qkv_out, near_down = step(
            lines,
            [keep, arrived_up, arrived_low, keep_qkv_out, arrived_qkv_out, piece_down, down_high],
            [
                sds((2, *piece), BF16),
                *(sds(taller, BF16), sds(taller, F32)),
                sds((2, *piece), BF16),
            ],
            "lines",
        )
        pieces_high = over_z_high(pieces)
        arrived_qkv_out = over_z_high(send_qkv_out)
        down_low = over_z_low(near_down)

        def share_high(ins, outs):
            for part in range(2):
                outs[part][0], outs[part][1] = ins[0][part], ins[1][part]
            outs[2][...] = (ins[2][...] + ins[3][...].astype(F32)).astype(BF16)
            outs[3][0], outs[3][1] = ins[4][...], ins[5][...]

        near_up, near_low, piece_qkv_out, near_down = step(
            share_high,
            [pieces, pieces_high, keep_qkv_out, arrived_qkv_out, near_down, down_low],
            [
                *(sds((2, *piece), BF16), sds((2, *piece), BF16)),
                sds(taller, BF16),
                sds((2, 2, *piece), BF16),
            ],
            "share_high",
        )
        up_x, low_low = over_x(near_up), over_z_low(near_low)
        qkv_out_high = over_z_high(piece_qkv_out)
        down_x = over_x(near_down)

        def share_next(ins, outs):
            for i in range(2):
                outs[i][0], outs[i][1] = ins[2 * i][...], ins[2 * i + 1][...]
            for x in range(2):
                for low in range(2):
                    for high in range(2):
                        outs[2][0, x, low * 2 + high] = ins[4 + x][low, high]

        near_up, near_low, near_down = step(
            share_next,
            [near_up, up_x, near_low, low_low, near_down, down_x],
            [
                *(sds((2, 2, *piece), BF16), sds((2, 2, *piece), BF16)),
                sds((1, 2, 4, *piece), BF16),
            ],
            "share_next",
            (qkv_out_high,),
        )
        far_down = over_core(near_down)
        up_low, low_x = over_z_low(near_up), over_x(near_low)

        def update(near, far, place, height, state, gains, name, after):
            near_out = update_half(
                idx, 0, near, place, height, state, (), gains, name + "_near", after
            )
            count = len(state)
            mark = near_out[-1]
            far_out = update_half(
                idx, 1, far, place, height, state, near_out[:count], (), name + "_far", (mark,)
            )
            return (*far_out[:count], *near_out[count:-1], far_out[-1])

        one_down, two_down, next_down, mark = update(
            near_down,
            far_down,
            lambda p, x, z: ((x * 2 + (z >> 1)) * CUT_ROWS, (z & 1) * CUT_COLUMNS),
            2 * HALF,
            [down_t, first_down_t, second_down_t],
            (),
            "update_down",
            (near_up,),
        )

        def share_qkv_out_high(ins, outs):
            outs[0][0], outs[0][1] = ins[0][...], ins[1][...]

        (near_qkv_out,) = step(
            share_qkv_out_high,
            [piece_qkv_out, qkv_out_high],
            [sds((2, *taller), BF16)],
            "share_qkv_out_high",
            (mark,),
        )
        qkv_out_x, qkv_out_low = over_x(near_qkv_out), over_z_low(near_qkv_out)
        qkv_out_both = swap(near_qkv_out, "dp", 6)

        def share_gate_up(ins, outs):
            for near in range(2):
                for far in range(2):
                    for high in range(2):
                        outs[0][0, near, far * 2 + high] = ins[far][near, high]
                        outs[0][1, far, near * 2 + high] = ins[2 + far][near, high]

        (near_gate_up,) = step(
            share_gate_up,
            [near_up, up_low, near_low, low_x],
            [sds((2, 2, 4, *piece), BF16)],
            "share_gate_up",
            (near_qkv_out,),
        )
        far_gate_up = over_core(near_gate_up)
        one_gate_up, two_gate_up, next_gate_up, mark = update(
            near_gate_up,
            far_gate_up,
            lambda p, x, z: (p * CUT_ROWS, (x * 4 + z) * CUT_COLUMNS),
            HALF,
            [w_gate_up, first_gate_up, second_gate_up],
            (),
            "update_gate_up",
            (),
        )

        def share_qkv_out(ins, outs):
            for x in range(2):
                for low in range(2):
                    for high in range(2):
                        outs[0][0, x, low * 2 + high] = ins[low * 2 + x][high]

        (near_qkv_out,) = step(
            share_qkv_out,
            [near_qkv_out, qkv_out_x, qkv_out_low, qkv_out_both],
            [sds((1, 2, 4, *taller), BF16)],
            "share_qkv_out",
            (mark,),
        )
        far_qkv_out = over_core(near_qkv_out)
        updated = update(
            near_qkv_out,
            far_qkv_out,
            lambda p, x, z: (x * CUT_ROWS, z * CUT_COLUMNS),
            HALF,
            [w_qkv, w_out, first_qkv, first_out, second_qkv, second_out],
            (norm_gains, first_gains, second_gains),
            "update_qkv_out",
            (),
        )
        one_qkv, one_out, two_qkv, two_out, next_qkv, next_out = updated[:6]
        one_gains, two_gains, next_gains = updated[6:9]
    else:
        sums = lax.psum((*grad_qkv_out, grad_gate_up[0], grad_down[0].T), ("dp", "shard"))
        grad_qkv_out, grad_gains, grad_gate_up, grad_down = sums

        def own(grad, axis=0):
            size = grad.shape[axis] // groups
            return lax.dynamic_slice_in_dim(grad, owner * size, size, axis)

        one_qkv, two_qkv, next_qkv = adamw(
            w_qkv, first_qkv, second_qkv, own(grad_qkv_out[:, :QKV]), RATE_MATRIX, DECAY_MATRIX
        )
        one_out, two_out, next_out = adamw(
            w_out, first_out, second_out, own(grad_qkv_out[:, QKV:]), RATE_MATRIX, DECAY_MATRIX
        )
        one_gate_up, two_gate_up, next_gate_up = adamw(
            w_gate_up, first_gate_up, second_gate_up, own(grad_gate_up), RATE_MATRIX, DECAY_MATRIX
        )
        one_down, two_down, next_down = [
            a.T
            for a in adamw(
                w_down, first_down, second_down, own(grad_down), RATE_MATRIX, DECAY_MATRIX
            )
        ]
        one_gains, two_gains, next_gains = adamw(
            norm_gains, first_gains, second_gains, own(grad_gains, 1), RATE_GAIN, 0.0
        )
    one_down, two_down, next_down = one_down.T, two_down.T, next_down.T
    return (
        output.T[None],
        token_grad.T[None],
        one_qkv,
        one_out,
        one_gate_up,
        one_down,
        one_gains,
        two_qkv,
        two_out,
        two_gate_up,
        two_down,
        two_gains,
        next_qkv,
        next_out,
        next_gate_up,
        next_down,
        next_gains,
    )


def solution(mesh):
    return jax.shard_map(
        per_device,
        mesh=mesh,
        in_specs=(
            P(("dp", "shard"), None, None),
            P(("dp", "shard"), None),
            P(("dp", "shard"), None, None),
            P("shard", None),
            P("shard", None),
            P("shard", None),
            P("shard", None),
            P(None, "shard"),
            P("shard", None),
            P("shard", None),
            P("shard", None),
            P("shard", None),
            P(None, "shard"),
            P("shard", None),
            P("shard", None),
            P("shard", None),
            P("shard", None),
            P(None, "shard"),
        ),
        out_specs=(
            P(("dp", "shard"), None, None),
            P(("dp", "shard"), None, None),
            P("shard", None),
            P("shard", None),
            P("shard", None),
            P("shard", None),
            P(None, "shard"),
            P("shard", None),
            P("shard", None),
            P("shard", None),
            P("shard", None),
            P(None, "shard"),
            P("shard", None),
            P("shard", None),
            P("shard", None),
            P("shard", None),
            P(None, "shard"),
        ),
        check_vma=False,
    )
```

```python
import functools

import jax
import jax.numpy as jnp
import numpy as np
from jax import lax
from jax.experimental import pallas as pl
from jax.experimental.pallas import tpu as pltpu
from jax.sharding import PartitionSpec as P

HEADS = 9
KV_HEADS = 3
GROUP = HEADS // KV_HEADS
HEAD = 64
FF = 1536
STEP = 10
QUERY = HEADS * HEAD
ROPED = (HEADS + KV_HEADS) * HEAD
QKV = (HEADS + 2 * KV_HEADS) * HEAD
LANES = 128

EPS_NORM = 1e-05
ROPE_BASE = 100000.0
BETA_ONE = 0.9
BETA_TWO = 0.95
RATE_MATRIX = 0.1
RATE_GAIN = 0.3
DECAY_MATRIX = 0.1
EPS_ADAM = 1e-08
MASKED = -1e30
SCALE = float(HEAD) ** (-0.5)
VMEM_LIMIT = 32 * 1024 * 1024
PACK_LIMIT = 60 * 1024 * 1024
HALF = 144
CUT_ROWS = 72
MARK = (8, 128)
CUT_COLUMNS = 384
F32 = jnp.float32
BF16 = jnp.bfloat16


def rotate_block(values, cosine, signed_sine):
    lane = lax.broadcasted_iota(jnp.int32, values.shape, 1)
    swapped = jnp.where(
        lane % HEAD < HEAD // 2,
        pltpu.roll(values, LANES - HEAD // 2, 1),
        pltpu.roll(values, HEAD // 2, 1),
    )
    return values * cosine + swapped * signed_sine


def adamw(weight, first_moment, second_moment, gradient, step_rate, weight_decay):
    first_new = BETA_ONE * first_moment + (1.0 - BETA_ONE) * gradient
    second_new = BETA_TWO * second_moment + (1.0 - BETA_TWO) * gradient * gradient
    fix_one = 1.0 / (1.0 - BETA_ONE**STEP)
    fix_two = 1.0 / (1.0 - BETA_TWO**STEP)
    update = first_new * fix_one / (jnp.sqrt(second_new * fix_two) + EPS_ADAM)
    return (first_new, second_new, weight - step_rate * (update + weight_decay * weight))


def adamw_rows(weight, first_moment, second_moment, gradient, step_rate, weight_decay):
    first_new = BETA_ONE * first_moment + (1.0 - BETA_ONE) * gradient
    second_new = BETA_TWO * second_moment + (1.0 - BETA_TWO) * gradient * gradient
    value = second_new * (1.0 / (1.0 - BETA_TWO**STEP))
    guess = lax.rsqrt(value)
    divisor = value * guess + EPS_ADAM
    inverse = guess * (2.0 - divisor * guess)
    update = first_new * (step_rate / (1.0 - BETA_ONE**STEP)) * inverse
    return (first_new, second_new, weight * (1.0 - step_rate * weight_decay) - update)


def dot(left, right):
    return lax.dot_general(left, right, (((1,), (0,)), ((), ())), preferred_element_type=F32)


def dot_right_t(left, right):
    return lax.dot_general(left, right, (((1,), (1,)), ((), ())), preferred_element_type=F32)


def dot_left_t(left, right):
    return lax.dot_general(left, right, (((0,), (0,)), ((), ())), preferred_element_type=F32)


def norm_scale(values):
    return lax.rsqrt(jnp.mean(values * values, axis=-1, keepdims=True) + EPS_NORM)


def norm_back(grad_normed, normed, scale_rows):
    return scale_rows * (
        grad_normed - normed * jnp.mean(grad_normed * normed, axis=-1, keepdims=True)
    )


class Weight:
    def __init__(self, shape, whole=None, own=(), parts=()):
        self.shape, self.own, self.parts = shape, own, parts
        self.arrays = [whole] if whole is not None else [a[0] for a in (*own, *parts)]
        self.split = whole is None

    def load(self, idx, refs, full):
        if not self.split:
            return refs[0]
        for ref, (_, place) in zip(refs, self.own):
            self.put(full, place(idx[0]), ref[...].astype(BF16))
        for ref, (_, (core, x, low), place) in zip(refs[len(self.own) :], self.parts):
            place = place(1 - idx[0], idx[1] ^ core, idx[2] ^ x, (idx[3] & 1) ^ low)
            rows = ref.shape[0] // HALF * HALF
            self.put(full, place, ref[:rows, :])
        return full

    def put(self, full, position, value):
        where = []
        for axis, tile in ((0, 16), (1, LANES)):
            at, size = position[axis], value.shape[axis]
            if size == self.shape[axis]:
                where.append(slice(None))
            elif isinstance(at, int):
                where.append(slice(at, at + size))
            else:
                where.append(pl.ds(pl.multiple_of(at, tile), size))
        full[tuple(where)] = value


def call(body, idx, arrays, weights, outs, scratch, busy, name, after=(), hand_on=False):
    counts = [len(w.arrays) for w in weights]
    flat = list(arrays) + [a for w in weights for a in w.arrays]
    outs = list(outs)
    split = [w for w in weights if w.split]
    hand_on = hand_on and bool(split)
    if hand_on:
        outs += [sds(split[-1].shape, BF16)]
    made = [pltpu.VMEM(w.shape, BF16) for w in (split[:-1] if hand_on else split)]

    def kernel(*refs):
        refs = list(refs)
        idx_ref = refs.pop(0)
        take = lambda n: [refs.pop(0) for _ in range(n)]
        array_refs = take(len(arrays))
        weight_refs = [take(n) for n in counts]
        take(len(after))
        out_refs = take(len(outs))
        own_scratch = take(len(scratch))
        fulls = take(len(made)) + ([out_refs.pop()] if hand_on else [])
        loads = [
            functools.partial(w.load, idx_ref, r, fulls.pop(0) if w.split else None)
            for w, r in zip(weights, weight_refs)
        ]
        body(idx_ref, array_refs, loads, out_refs, own_scratch)

    return pl.pallas_call(
        kernel,
        out_shape=tuple(outs),
        in_specs=[pl.BlockSpec(memory_space=pltpu.SMEM)]
        + [pl.BlockSpec(memory_space=pltpu.VMEM)] * len(flat)
        + [pl.BlockSpec(memory_space=pl.ANY)] * len(after),
        out_specs=tuple([pl.BlockSpec(memory_space=pltpu.VMEM)] * len(outs)),
        scratch_shapes=list(scratch) + made,
        compiler_params=pltpu.CompilerParams(vmem_limit_bytes=VMEM_LIMIT),
        cost_estimate=busy_for(busy),
        name=name,
    )(idx, *flat, *after)


def busy_for(microseconds):
    return pl.CostEstimate(flops=int(microseconds * 1e9), bytes_accessed=0, transcendentals=0)


def sds(shape, dtype):
    return jax.ShapeDtypeStruct(shape, dtype)


class Pieces:
    def __init__(self, place, parts=1, extra=0):
        self.place, self.parts, self.extra = place, parts, extra

    def outs(self):
        return [sds((self.parts, 2, 8, CUT_ROWS + self.extra, CUT_COLUMNS), BF16)] * 2

    def scratch(self, columns):
        return pltpu.VMEM((8, CUT_ROWS, columns), BF16)

    def store(self, blocks, grad, start=0):
        for i in range(8):
            rows = grad[i * CUT_ROWS : (i + 1) * CUT_ROWS].astype(BF16)
            blocks[i, :, start : start + grad.shape[1]] = rows

    def emit(self, idx, blocks, outs, under=None):
        for other_core, out in enumerate((outs[1], outs[0])):
            for part in range(self.parts):
                for owner in range(2):
                    for slot in range(8):
                        z = ((slot >> 1) & 1) | ((slot & 1) << 1)
                        block, column = self.place(
                            idx[0] ^ owner, idx[1] ^ other_core, idx[2] ^ (slot >> 2), idx[3] ^ z, part
                        )
                        columns = pl.ds(pl.multiple_of(column * CUT_COLUMNS, LANES), CUT_COLUMNS)
                        piece = blocks[block, :, columns]
                        if under is not None:
                            piece = jnp.concatenate(
                                [piece.astype(F32), under[idx[0] ^ owner]], axis=0
                            ).astype(BF16)
                        out[part, owner, slot] = piece


def head_stack(values, kv_head):
    first = kv_head * GROUP
    return jnp.concatenate(
        [values[:, (first + i) * HEAD : (first + i + 1) * HEAD] for i in range(GROUP)], axis=0
    )


def softmax_rows(query, key, allowed):
    scores = jnp.where(allowed, dot_right_t(query, key) * SCALE, MASKED)
    top = jnp.max(scores, axis=-1, keepdims=True)
    exponent = jnp.exp(scores - top)
    return exponent / jnp.sum(exponent, axis=-1, keepdims=True)


def pack_kernel(body, idx, sources, places, outs, name, after=(), limit=PACK_LIMIT):
    windows = [shape for shape, _ in places]

    def kernel(idx_ref, *refs):
        sources_in, refs = refs[: len(sources)], refs[len(sources) + len(after) :]
        out_refs, buffers, sem = refs[: len(outs)], refs[len(outs) : -1], refs[-1]
        copies = []
        for i, (source, (shape, place)) in enumerate(zip(sources_in, places)):
            where = []
            for axis, tile in ((0, 8), (1, LANES)):
                if shape[axis] == source.shape[axis]:
                    where.append(slice(None))
                else:
                    where.append(pl.ds(pl.multiple_of(place(idx_ref)[axis], tile), shape[axis]))
            copies.append(pltpu.make_async_copy(source.at[tuple(where)], buffers[i], sem.at[i]))
        for copy in copies:
            copy.start()
        for copy in copies:
            copy.wait()
        body(idx_ref, buffers, out_refs)

    return pl.pallas_call(
        kernel,
        out_shape=tuple(outs),
        in_specs=[pl.BlockSpec(memory_space=pltpu.SMEM)]
        + [pl.BlockSpec(memory_space=pltpu.HBM)] * len(sources)
        + [pl.BlockSpec(memory_space=pl.ANY)] * len(after),
        out_specs=tuple([pl.BlockSpec(memory_space=pltpu.VMEM)] * len(outs)),
        scratch_shapes=[pltpu.VMEM(w, F32) for w in windows]
        + [pltpu.SemaphoreType.DMA((len(sources),))],
        compiler_params=pltpu.CompilerParams(vmem_limit_bytes=limit),
        cost_estimate=busy_for(10),
        name=name,
    )(idx, *sources, *after)


def cast_out(idx_ref, buffers, outs):
    for buffer, out in zip(buffers, outs):
        out[...] = buffer[...].astype(BF16)


def pack_down(idx, down_t, after):
    shape = (2 * HALF, down_t.shape[1])
    window = (shape, lambda i: (i[1] * 2 * HALF, 0))
    outs = [sds(shape, BF16)]
    return pack_kernel(
        cast_out, idx, [down_t], [window], outs, "pack_down", after, VMEM_LIMIT
    )[0]


def pack_first(idx, w_qkv, w_out, norm_gains, w_gate_up):
    columns = (QKV + w_out.shape[1]) // 2
    quarter = FF // 2
    windows = [((HALF, m.shape[1]), lambda i: (i[1] * HALF, 0)) for m in (w_qkv, w_out)]
    windows.append((norm_gains.shape, lambda i: (0, 0)))
    windows.append(((HALF, quarter), lambda i: (i[1] * HALF, i[2] * quarter)))
    windows.append(((HALF, quarter), lambda i: (i[1] * HALF, FF + (i[3] & 1) * quarter)))

    def body(idx_ref, buffers, outs):
        q_ref, o_ref, gains_ref = buffers[:3]
        both = jnp.concatenate([q_ref[:, columns:], o_ref[...]], axis=1)
        outs[0][:HALF, :] = jnp.where((idx_ref[3] & 1) == 0, q_ref[:, :columns], both).astype(BF16)
        outs[0][HALF:, :] = jnp.zeros((16, columns), BF16)
        outs[0][HALF : HALF + 2, : gains_ref.shape[1]] = gains_ref[...].astype(BF16)
        cast_out(idx_ref, buffers[3:], outs[1:])

    outs = [sds((HALF + 16, columns), BF16)] + [sds((HALF, quarter), BF16)] * 2
    sources = [w_qkv, w_out, norm_gains, w_gate_up, w_gate_up]
    return pack_kernel(body, idx, sources, windows, outs, "pack_first")


def attention_forward(idx, tokens_t, segments, frequency, gains, w_qkv_out):
    width, seq_length = tokens_t.shape
    split_gains = len(gains) > 1

    def body(idx_ref, arrays, loads, outs, scratch):
        x_ref, seg_ref, freq_ref = arrays[:3]
        qkv_ref, o_ref, cos_ref, sin_ref, allowed_ref, gains_ref = outs
        if split_gains:
            own = arrays[3][...].astype(BF16).astype(F32)
            other = arrays[4][HALF : HALF + 8, : width // 2].astype(F32)[:2]
            gains_ref[...] = jnp.where(
                idx_ref[0] == 0,
                jnp.concatenate([own, other], axis=1),
                jnp.concatenate([other, own], axis=1),
            )
        else:
            gains_ref[...] = arrays[3][...]
        seen_doc = jnp.broadcast_to(seg_ref[...], (seq_length, seq_length))
        own_doc = seen_doc.T
        token = lax.broadcasted_iota(jnp.int32, (seq_length, seq_length), 0)
        seen = lax.broadcasted_iota(jnp.int32, (seq_length, seq_length), 1)
        begin = jnp.sum((seen_doc < own_doc).astype(F32), axis=-1, keepdims=True)
        angles = (token.astype(F32) - begin) * freq_ref[...]
        cosine, sine = jnp.cos(angles), jnp.sin(angles)
        sine = jnp.where(seen % HEAD < HEAD // 2, -sine, sine)
        cos_ref[...] = cosine
        sin_ref[...] = sine
        allowed = ((seen_doc == own_doc) & (token >= seen)).astype(F32)
        allowed_ref[...] = allowed
        allowed = jnp.concatenate([allowed] * GROUP, axis=0) > 0.5
        x = x_ref[...].astype(F32).T
        h1 = (x * norm_scale(x) * gains_ref[0:1, :]).astype(BF16)
        projected = dot(h1, loads[0]()[:, :QKV])
        for start in range(0, ROPED, LANES):
            block = projected[:, start : start + LANES]
            qkv_ref[:, start : start + LANES] = rotate_block(block, cosine, sine).astype(BF16)
        qkv_ref[:, ROPED:QKV] = projected[:, ROPED:QKV].astype(BF16)
        qkv = qkv_ref[...]
        for kv in range(KV_HEADS):
            key = qkv[:, QUERY + kv * HEAD : QUERY + (kv + 1) * HEAD]
            value = qkv[:, ROPED + kv * HEAD : ROPED + (kv + 1) * HEAD]
            probs = softmax_rows(head_stack(qkv, kv), key, allowed).astype(BF16)
            attended = dot(probs, value).astype(BF16)
            for i in range(GROUP):
                start = (kv * GROUP + i) * HEAD
                o_ref[:, start : start + HEAD] = attended[i * seq_length : (i + 1) * seq_length]

    square = sds((seq_length, seq_length), F32)
    outs = [sds((seq_length, QKV), BF16), sds((seq_length, QUERY), BF16)]
    outs += [square, square, square, sds((2, width), F32)]
    return call(
        body,
        idx,
        [tokens_t, segments, frequency, *gains],
        [w_qkv_out],
        outs,
        [],
        1,
        "attention",
        hand_on=True,
    )


def feed_forward(idx, tokens_t, attended, gains, cotangent_t, w_qkv_out, w_gate_up, pieces, after):
    width, seq_length = tokens_t.shape

    def body(idx_ref, arrays, loads, outs, scratch):
        x_ref, o_ref, gains_ref, y_ref = arrays
        u_ref, h2_ref, ab_ref, z_ref = outs[:4]
        u = x_ref[...].astype(F32).T + dot(o_ref[...], loads[0]()[:, QKV:])
        u_ref[...] = u
        h2 = (u * norm_scale(u) * gains_ref[1:2, :]).astype(BF16)
        h2_ref[...] = h2
        ab = dot(h2, loads[1]()[...])
        ab_ref[...] = ab
        gate, up = ab[:, :FF], ab[:, FF:]
        z = (gate * jax.nn.sigmoid(gate) * up).astype(BF16)
        z_ref[...] = z
        grad = dot(y_ref[...], z)
        if pieces is None:
            outs[4][...] = grad
        else:
            pieces.store(scratch[0], grad)
            pieces.emit(idx_ref, scratch[0], outs[4:])

    outs = [
        sds((seq_length, width), F32),
        sds((seq_length, width), BF16),
        sds((seq_length, 2 * FF), F32),
        sds((seq_length, FF), BF16),
    ]
    outs += [sds((width, FF), F32)] if pieces is None else pieces.outs()
    scratch = [] if pieces is None else [pieces.scratch(FF)]
    return call(
        body,
        idx,
        [tokens_t, attended, gains, cotangent_t],
        [w_qkv_out, w_gate_up],
        outs,
        scratch,
        5,
        "feed_forward",
        after,
        True,
    )


def feed_back(idx, ab, normed_low, cotangent_t, down_t, pieces):
    width, seq_length = cotangent_t.shape

    def body(idx_ref, arrays, loads, outs, scratch):
        ab_ref, h2_ref, y_ref = arrays
        gg_ref = outs[0]
        gate, up = ab_ref[:, :FF], ab_ref[:, FF:]
        sig = jax.nn.sigmoid(gate)
        grad_hidden = dot_left_t(y_ref[...], loads[0]()[...])
        gg_ref[:, :FF] = (grad_hidden * up * sig * (1.0 + gate * (1.0 - sig))).astype(BF16)
        gg_ref[:, FF:] = (grad_hidden * gate * sig).astype(BF16)
        grad = dot_left_t(h2_ref[...], gg_ref[...])
        if pieces is None:
            outs[1][...] = grad
        else:
            pieces.store(scratch[0], grad)
            pieces.emit(idx_ref, scratch[0], outs[1:])

    outs = [sds((seq_length, 2 * FF), BF16)]
    outs += [sds((width, 2 * FF), F32)] if pieces is None else pieces.outs()
    scratch = [] if pieces is None else [pieces.scratch(2 * FF)]
    return call(
        body,
        idx,
        [ab, normed_low, cotangent_t],
        [down_t],
        outs,
        scratch,
        20,
        "feed_back",
        hand_on=True,
    )


def layer_output(middle, hidden, down_t, after):
    seq_length, width = middle.shape

    def body(ins, outs):
        outs[0][...] = (ins[0][...] + dot_right_t(ins[1][...], ins[2][...])).T.astype(BF16)

    return step(
        body, [middle, hidden, down_t], [sds((width, seq_length), BF16)], "layer_output", after, 2
    )[0]


def middle_back(idx, cotangent_t, middle, gated, gains, w_gate_up, w_qkv_out, after):
    width, seq_length = cotangent_t.shape

    def body(idx_ref, arrays, loads, outs, scratch):
        y_ref, u_ref, gg_ref, gains_ref = arrays
        gu_ref, go_ref, gain_ref = outs
        u = u_ref[...]
        scale_two = norm_scale(u)
        normed = u * scale_two
        grad_normed = dot_right_t(gg_ref[...], loads[0]()[...])
        gain_ref[...] = jnp.sum(grad_normed * normed, axis=0, keepdims=True)
        gu = y_ref[...].astype(F32).T + norm_back(
            grad_normed * gains_ref[1:2, :], normed, scale_two
        )
        gu_ref[...] = gu
        go_ref[...] = dot_right_t(gu.astype(BF16), loads[1]()[:, QKV:]).astype(BF16)

    outs = [sds((seq_length, width), F32), sds((seq_length, width), BF16), sds((1, width), F32)]
    return call(
        body,
        idx,
        [cotangent_t, middle, gated, gains],
        [w_gate_up, w_qkv_out],
        outs,
        [],
        20,
        "middle_back",
        after,
    )


def attention_back(
    idx, tokens_t, grad_middle, grad_attended, gain_two, qkv, attended, tables, gains, w_qkv, pieces, after
):
    width, seq_length = tokens_t.shape

    def body(idx_ref, arrays, loads, outs, scratch):
        x_ref, gu_ref, go_ref, gain_two_ref, qkv_ref, o_ref = arrays[:6]
        cos_ref, sin_ref, allowed_ref, gains_ref = arrays[6:]
        grad_ref = outs[0]
        grad_proj, gp_ref, gain_rows, *blocks = scratch
        gu, go = gu_ref[...], go_ref[...]
        gu_low = gu.astype(BF16)
        grad_gain_two = gain_two_ref[...]
        allowed = jnp.concatenate([allowed_ref[...]] * GROUP, axis=0) > 0.5
        qkv_values = qkv_ref[...]
        for kv in range(KV_HEADS):
            key = qkv_values[:, QUERY + kv * HEAD : QUERY + (kv + 1) * HEAD]
            value = qkv_values[:, ROPED + kv * HEAD : ROPED + (kv + 1) * HEAD]
            query = head_stack(qkv_values, kv)
            grad_out = head_stack(go, kv)
            probs = softmax_rows(query, key, allowed)
            grad_probs = dot_right_t(grad_out, value)
            row_delta = jnp.sum(probs * grad_probs, axis=-1, keepdims=True)
            gs = (probs * (grad_probs - row_delta)).astype(BF16)
            grad_query = dot(gs, key) * SCALE
            for i in range(GROUP):
                start = (kv * GROUP + i) * HEAD
                grad_proj[:, start : start + HEAD] = grad_query[
                    i * seq_length : (i + 1) * seq_length
                ]
            start = QUERY + kv * HEAD
            grad_proj[:, start : start + HEAD] = dot_left_t(gs, query) * SCALE
            start = ROPED + kv * HEAD
            grad_proj[:, start : start + HEAD] = dot_left_t(probs.astype(BF16), grad_out)
        for start in range(0, ROPED, LANES):
            gp_ref[:, start : start + LANES] = rotate_block(
                grad_proj[:, start : start + LANES], cos_ref[...], -sin_ref[...]
            ).astype(BF16)
        gp_ref[:, ROPED:QKV] = grad_proj[:, ROPED:QKV].astype(BF16)
        x = x_ref[...].astype(F32).T
        scale_one = norm_scale(x)
        normed = x * scale_one
        h1 = (normed * gains_ref[0:1, :]).astype(BF16)
        grad_qkv = dot_left_t(h1, gp_ref[...])
        grad_out = dot_left_t(o_ref[...], gu_low)
        grad_normed = dot_right_t(gp_ref[...], loads[0]()[:, :QKV])
        grad_gain_one = jnp.sum(grad_normed * normed, axis=0, keepdims=True)
        if pieces is None:
            outs[1][:, :QKV] = grad_qkv
            outs[1][:, QKV:] = grad_out
            outs[2][0:1, :] = grad_gain_one
            outs[2][1:2, :] = grad_gain_two
        else:
            pieces.store(blocks[0], grad_qkv)
            pieces.store(blocks[0], grad_out, QKV)
            half = width // 2
            gain_rows[...] = jnp.zeros_like(gain_rows)
            for owner in range(2):
                columns = slice(owner * half, (owner + 1) * half)
                gain_rows[owner, 0:1, :half] = grad_gain_one[:, columns]
                gain_rows[owner, 1:2, :half] = grad_gain_two[:, columns]
            pieces.emit(idx_ref, blocks[0], outs[1:3], gain_rows)
            outs[3][...] = jnp.zeros_like(outs[3])
        grad_ref[...] = (
            (gu + norm_back(grad_normed * gains_ref[0:1, :], normed, scale_one)).T
        ).astype(BF16)

    outs = [sds((width, seq_length), BF16)]
    scratch = [
        pltpu.VMEM((seq_length, QKV), F32),
        pltpu.VMEM((seq_length, QKV), BF16),
        pltpu.VMEM((2, 8, CUT_COLUMNS), F32),
    ]
    if pieces is None:
        outs += [sds((width, QKV + width), F32), sds((2, width), F32)]
    else:
        outs += pieces.outs() + [sds(MARK, F32)]
        scratch += [pieces.scratch(QKV + width)]
    return call(
        body,
        idx,
        [tokens_t, grad_middle, grad_attended, gain_two, qkv, attended, *tables, gains],
        [w_qkv],
        outs,
        scratch,
        20,
        "attention_back",
        after,
    )


def step(body, arrays, outs, name, after=(), busy=20):
    def kernel(*refs):
        body(refs[: len(arrays)], refs[len(arrays) + len(after) :])

    return pl.pallas_call(
        kernel,
        out_shape=tuple(outs),
        in_specs=[pl.BlockSpec(memory_space=pltpu.VMEM)] * len(arrays)
        + [pl.BlockSpec(memory_space=pl.ANY)] * len(after),
        out_specs=tuple([pl.BlockSpec(memory_space=pltpu.VMEM)] * len(outs)),
        compiler_params=pltpu.CompilerParams(vmem_limit_bytes=VMEM_LIMIT),
        cost_estimate=busy_for(busy),
        name=name,
    )(*arrays, *after)


def pass_on(ins, outs):
    outs[0][...] = ins[0][...]


def add_split(keep, arrived, axis, send_ref, keep_ref):
    total = keep[...].astype(F32) + arrived[...].astype(F32)
    low, high = lax.index_in_dim(total, 0, axis, False), lax.index_in_dim(total, 1, axis, False)
    send_ref[...] = high.astype(BF16)
    keep_ref[...] = low


def add_step(jobs, name, after):
    arrays, outs = [], []
    for keep, arrived, axis in jobs:
        arrays += [keep, arrived]
        shape = keep.shape[:axis] + keep.shape[axis + 1 :]
        outs += [sds(shape, BF16), sds(shape, F32)]

    def body(ins, out_refs):
        for i, (_, _, axis) in enumerate(jobs):
            add_split(ins[2 * i], ins[2 * i + 1], axis, out_refs[2 * i], out_refs[2 * i + 1])

    flat = step(body, arrays, outs, name, after)
    return [(flat[2 * i], flat[2 * i + 1]) for i in range(len(jobs))]


def update_half(idx, far, pieces, place, height, state, earlier, gains, name, after):
    count = len(state) // 3
    columns = [a.shape[1] for a in state[:count]]
    starts = [sum(-(-c // LANES) * LANES for c in columns[:k]) for k in range(count + 1)]
    chunks = height // CUT_ROWS
    order = [(k, count + k, 2 * count + k) for k in range(count)]

    def kernel(idx_ref, *refs):
        refs = list(refs)
        take = lambda n: [refs.pop(0) for _ in range(n)]
        (piece_ref,) = take(1)
        state_refs, gain_refs = take(3 * count), take(len(gains))
        take(len(earlier) + len(after))
        outs, gain_outs, (mark,) = take(3 * count), take(len(gains)), take(1)
        buffers, (full, sem) = take(3 * count), refs
        mark[...] = jnp.zeros_like(mark)
        for part in range(pieces.shape[0]):
            for x in range(2):
                for z in range(4):
                    rel = z ^ idx_ref[3]
                    slot = ((rel & 1) << 1) | (rel >> 1)
                    piece = piece_ref[part, x, slot].astype(F32)[:CUT_ROWS]
                    row, cuts = place(part, idx_ref[2] ^ x, z)
                    rows = pl.ds(pl.multiple_of(row, 8), CUT_ROWS)
                    for begin, size, to in cuts:
                        if isinstance(to, int):
                            where = slice(to, to + size)
                        else:
                            where = pl.ds(pl.multiple_of(to, LANES), size)
                        full[rows, where] = piece[:, begin : begin + size]
        base = (idx_ref[1] ^ far) * height
        copies = []
        for chunk in range(chunks):

            def eight_rows(i, carry, chunk=chunk):
                near_rows = pl.ds(pl.multiple_of(chunk * CUT_ROWS + i * 8, 8), 8)
                rows = pl.ds(pl.multiple_of(base + chunk * CUT_ROWS + i * 8, 8), 8)
                for k in range(count):
                    for at in range(0, columns[k], 768):
                        size = min(768, columns[k] - at)
                        where = slice(at, at + size)
                        results = adamw_rows(
                            *[state_refs[j][rows, where] for j in order[k]],
                            full[near_rows, starts[k] + at : starts[k] + at + size],
                            RATE_MATRIX,
                            DECAY_MATRIX,
                        )
                        for j, result in zip(order[k], results):
                            buffers[j][near_rows, where] = result
                return carry

            lax.fori_loop(0, CUT_ROWS // 8, eight_rows, 0)
            near_rows = pl.ds(chunk * CUT_ROWS, CUT_ROWS)
            rows = pl.ds(pl.multiple_of(base + chunk * CUT_ROWS, 8), CUT_ROWS)
            for j in range(3 * count):
                copy = pltpu.make_async_copy(
                    buffers[j].at[near_rows], outs[j].at[rows], sem.at[chunk, j]
                )
                copy.start()
                copies.append(copy)
        if gains:
            gradient = piece_ref[0, 0, 0, CUT_ROWS:, :].astype(F32)[:2, : gains[0].shape[1]]
            results = adamw_rows(*[g[...] for g in gain_refs], gradient, RATE_GAIN, 0.0)
            for out, result in zip(gain_outs, results):
                out[...] = result
        for copy in copies:
            copy.wait()

    vmem, anywhere = pl.BlockSpec(memory_space=pltpu.VMEM), pl.BlockSpec(memory_space=pl.ANY)
    first_earlier = 2 + 3 * count + len(gains)
    return pl.pallas_call(
        kernel,
        out_shape=tuple(sds(a.shape, F32) for a in [*state, *gains]) + (sds(MARK, F32),),
        in_specs=[pl.BlockSpec(memory_space=pltpu.SMEM)]
        + [vmem] * (1 + 3 * count + len(gains))
        + [anywhere] * (len(earlier) + len(after)),
        out_specs=tuple([anywhere] * (3 * count) + [vmem] * (len(gains) + 1)),
        scratch_shapes=[pltpu.VMEM((height, a.shape[1]), F32) for a in state]
        + [pltpu.VMEM((height, starts[-1]), F32), pltpu.SemaphoreType.DMA((chunks, 3 * count))],
        input_output_aliases={first_earlier + i: i for i in range(len(earlier))},
        compiler_params=pltpu.CompilerParams(vmem_limit_bytes=VMEM_LIMIT),
        cost_estimate=busy_for(20),
        name=name,
    )(idx, pieces, *state, *gains, *earlier, *after)


def swap(values, axis, mask):
    size = lax.axis_size(axis)
    return lax.ppermute(values, axis, [(i, i ^ mask) for i in range(size)])


over_y = functools.partial(swap, axis="shard", mask=1)
over_core = functools.partial(swap, axis="dp", mask=1)
over_x = functools.partial(swap, axis="dp", mask=2)
over_z_low = functools.partial(swap, axis="dp", mask=4)
over_z_high = functools.partial(swap, axis="dp", mask=8)


def per_device(
    tokens,
    segments,
    cotangent,
    w_qkv,
    w_out,
    w_gate_up,
    w_down,
    norm_gains,
    first_qkv,
    first_out,
    first_gate_up,
    first_down,
    first_gains,
    second_qkv,
    second_out,
    second_gate_up,
    second_down,
    second_gains,
):
    groups = lax.axis_size("shard")
    replicas = lax.axis_size("dp")
    fast = groups == 2 and replicas == 16
    place_dp = lax.axis_index("dp")
    owner = lax.axis_index("shard")
    idx = jnp.stack([owner, place_dp & 1, (place_dp >> 1) & 1, place_dp >> 2]).astype(jnp.int32)
    x_t, y_t = tokens[0].T, cotangent[0].T
    width, seq_length = x_t.shape
    rows, down_rows = w_qkv.shape[0], w_down.shape[0]
    down_t, first_down_t, second_down_t = w_down.T, first_down.T, second_down.T
    half_size = HEAD // 2
    frequency = ROPE_BASE ** (-(np.arange(half_size) * 2.0 / HEAD))
    frequency = jnp.asarray(np.tile(frequency, 4)[None], F32)
    if fast:
        qo_near, by_x, by_low = pack_first(idx, w_qkv, w_out, norm_gains, w_gate_up)
        qo_near, by_x, by_low = over_y(qo_near), over_y(by_x), over_y(by_low)
        down_near = over_y(pack_down(idx, down_t, (by_low,)))
        by_x_next, by_low_next = over_x(by_x), over_z_low(by_low)
        qo_near_low = over_z_low(qo_near)
        gains = (norm_gains, qo_near)
        (low_far,) = step(
            pass_on, [over_core(by_low_next)], [sds(by_low.shape, BF16)], "pass_on_low", (), 1
        )
        own_rows = lambda o: (o * rows, 0)
        own_rows_out = lambda o: (o * rows, QKV)
        qo_place = lambda o, c, x, low: (o * rows + c * HALF, low * ((QKV + width) // 2))
        x_place = lambda o, c, x, low: (o * rows + c * HALF, x * (FF // 2))
        low_place = lambda o, c, x, low: (o * rows + c * HALF, FF + low * (FF // 2))
        mat_qkv_out = Weight(
            (width, QKV + width),
            own=[(w_qkv, own_rows), (w_out, own_rows_out)],
            parts=[
                (qo_near, (0, 0, 0), qo_place),
                (qo_near_low, (0, 0, 1), qo_place),
                (over_core(qo_near), (1, 0, 0), qo_place),
                (over_core(qo_near_low), (1, 0, 1), qo_place),
            ],
        )
        mat_gate_up = Weight(
            (width, 2 * FF),
            own=[(w_gate_up, own_rows)],
            parts=[
                (by_x, (0, 0, 0), x_place),
                (by_x_next, (0, 1, 0), x_place),
                (over_core(by_x), (1, 0, 0), x_place),
                (over_core(by_x_next), (1, 1, 0), x_place),
                (by_low, (0, 0, 0), low_place),
                (by_low_next, (0, 0, 1), low_place),
                (over_core(by_low), (1, 0, 0), low_place),
                (low_far, (1, 0, 1), low_place),
            ],
        )
        cut_qkv_out = Pieces(lambda o, c, x, z, p: (o * 4 + c * 2 + x, z), extra=8)
        cut_gate_up = Pieces(lambda o, c, x, z, p: (o * 4 + c * 2 + p, x * 4 + z), parts=2)
        cut_down = Pieces(lambda o, c, x, z, p: (c * 4 + x * 2 + (z >> 1), o * 2 + (z & 1)))
    else:
        gains = (
            lax.all_gather(norm_gains.astype(BF16), "shard", axis=1, tiled=True).astype(F32),
        )
        mat_qkv, mat_out, mat_gate_up, mat_down = [
            lax.all_gather(m.astype(BF16), "shard", axis=0, tiled=True)
            for m in (w_qkv, w_out, w_gate_up, w_down)
        ]
        mat_qkv_out, mat_gate_up, mat_down = [
            Weight(m.shape, whole=m)
            for m in (jnp.concatenate([mat_qkv, mat_out], axis=1), mat_gate_up, mat_down.T)
        ]
        cut_qkv_out = cut_gate_up = cut_down = None

    qkv, attended, *tables, gains, whole = attention_forward(
        idx, x_t, segments, frequency, gains, mat_qkv_out
    ) + (() if fast else (None,))
    if fast:
        mat_qkv_out = Weight(whole.shape, whole=whole)
    middle, normed_low, ab, hidden, *grad_down = feed_forward(
        idx, x_t, attended, gains, y_t, mat_qkv_out, mat_gate_up, cut_down, ()
    )
    after = ()
    if fast:
        whole = grad_down.pop()
        mat_gate_up = Weight(whole.shape, whole=whole)

        (down_near,) = step(
            pass_on, [down_near], [sds(down_near.shape, BF16)], "pass_on", (attended,), 0.1
        )
        down_place = lambda o, c, x, low: (c * 2 * HALF, o * down_rows)
        mat_down = Weight(
            (width, FF),
            own=[(down_t, lambda o: (0, o * down_rows))],
            parts=[
                (down_near, (0, 0, 0), down_place),
                (over_core(down_near), (1, 0, 0), down_place),
            ],
        )
    if fast:
        arrived_down = over_core(grad_down[0])
    gated, *grad_gate_up = feed_back(idx, ab, normed_low, y_t, mat_down, cut_gate_up)
    if not fast:
        output = layer_output(middle, hidden, mat_down.arrays[0], ())
    if fast:
        down_whole = grad_gate_up.pop()
        cut = lambda a, *lead: a.reshape(*lead, *a.shape[-2:])
        arrived_gate_up = over_core(grad_gate_up[0])
        ((send, keep_down),) = add_step(
            [(grad_down[1][0], arrived_down[0], 0)], "down_core", (gated,)
        )
        arrived_down = over_y(send)
        after = (keep_down,)
    grad_middle, grad_attended, gain_two = middle_back(
        idx, y_t, middle, gated, gains, mat_gate_up, mat_qkv_out, after
    )
    if fast:
        halves = [
            [cut(a[p], *lead) for a in (grad_gate_up[1], arrived_gate_up)]
            for p, lead in ((0, (2, 2, 4)), (1, (4, 2, 2)))
        ]
        (send_up, keep_up), (send_low, keep_low) = add_step(
            [(*halves[0], 1), (*halves[1], 1)], "gate_up_core", (grad_middle,)
        )
        arrived_up, arrived_low = over_x(send_up), over_z_low(send_low)
        after = (keep_up,)
    token_grad, *grad_qkv_out = attention_back(
        idx,
        x_t,
        grad_middle,
        grad_attended,
        gain_two,
        qkv,
        attended,
        tables,
        gains,
        mat_qkv_out,
        cut_qkv_out,
        after,
    )
    if fast:

        arrived_qkv_out = over_core(grad_qkv_out[0])
        piece = (CUT_ROWS, CUT_COLUMNS)
        taller = (CUT_ROWS + 8, CUT_COLUMNS)
        ((send, keep_down),) = add_step(
            [(cut(keep_down, 2, 4), cut(arrived_down, 2, 4), 0)], "down_y", (grad_qkv_out[2],)
        )
        arrived_down = over_x(send)
        (send_up, keep_up), (send_low, keep_low) = add_step(
            [
                (cut(keep_up, 2, 2, 2), cut(arrived_up, 2, 2, 2), 1),
                (cut(keep_low, 2, 2, 2), cut(arrived_low, 2, 2, 2), 1),
            ],
            "up_x_low_z",
            (keep_down,),
        )
        arrived_up, arrived_low = over_z_low(send_up), over_x(send_low)
        ((send, keep_qkv_out),) = add_step(
            [(grad_qkv_out[1][0], arrived_qkv_out[0], 0)], "qkv_out_core", (keep_up,)
        )
        arrived_qkv_out = over_y(send)
        ((send, keep_down),) = add_step(
            [(cut(keep_down, 2, 2), cut(arrived_down, 2, 2), 0)], "down_x", (keep_qkv_out,)
        )
        arrived_down = over_z_low(send)

        def columns(ins, outs):
            for part in range(2):
                total = ins[2 * part][...] + ins[2 * part + 1][...].astype(F32)
                outs[0][part] = total[1].astype(BF16)
                outs[1][part] = total[0]
            for i in (1, 2):
                total = ins[2 * i + 2][...] + ins[2 * i + 3][...].astype(F32)
                outs[2 * i][...] = total[1].astype(BF16)
                outs[2 * i + 1][...] = total[0]

        send, keep, send_qkv_out, keep_qkv_out, send_down, keep_down = step(
            columns,
            [
                *(keep_up, arrived_up, keep_low, arrived_low),
                *(cut(keep_qkv_out, 2, 4), cut(arrived_qkv_out, 2, 4)),
                *(keep_down, arrived_down),
            ],
            [
                *(sds((2, 2, *piece), BF16), sds((2, 2, *piece), F32)),
                *(sds((4, *taller), BF16), sds((4, *taller), F32)),
                *(sds(piece, BF16), sds(piece, F32)),
            ],
            "columns",
        )
        arrived, arrived_qkv_out = over_y(send), over_x(send_qkv_out)
        arrived_down = over_z_high(send_down)

        def planes(ins, outs):
            for part in range(2):
                total = ins[0][part] + ins[1][part].astype(F32)
                outs[0][part] = total[1].astype(BF16)
                outs[1][part] = total[0]
            outs[0][2] = (ins[4][...] + ins[5][...].astype(F32)).astype(BF16)
            total = ins[2][...] + ins[3][...].astype(F32)
            outs[2][...] = total[1].astype(BF16)
            outs[3][...] = total[0]

        send, keep, send_qkv_out, keep_qkv_out = step(
            planes,
            [
                *(keep, arrived),
                *(cut(keep_qkv_out, 2, 2), cut(arrived_qkv_out, 2, 2)),
                *(keep_down, arrived_down),
            ],
            [
                *(sds((3, *piece), BF16), sds((2, *piece), F32)),
                *(sds((2, *taller), BF16), sds((2, *taller), F32)),
            ],
            "planes",
        )
        arrived, arrived_qkv_out = over_z_high(send), over_z_low(send_qkv_out)

        def lines(ins, outs):
            send, keep, arrived, keep_qkv_out, arrived_qkv_out = ins
            total = keep_qkv_out[...] + arrived_qkv_out[...].astype(F32)
            outs[0][0] = total[1].astype(BF16)
            outs[1][...] = total[0]
            for part in range(2):
                total = keep[part] + arrived[part].astype(F32)
                total = jnp.concatenate([total, jnp.zeros((8, CUT_COLUMNS), F32)], axis=0)
                outs[0][part + 1] = total.astype(BF16)
            outs[2][0], outs[2][1] = send[2], arrived[2]

        pieces, keep_qkv_out, near_down = step(
            lines,
            [send, keep, arrived, keep_qkv_out, arrived_qkv_out],
            [sds((3, *taller), BF16), sds(taller, F32), sds((2, *piece), BF16)],
            "lines",
        )
        arrived, down_low = over_z_high(pieces), over_z_low(near_down)

        def share_high(ins, outs):
            pieces, arrived, keep_qkv_out, near_down, down_low = ins
            for high in range(2):
                outs[0][0, high], outs[0][1, high] = near_down[high], down_low[high]
            outs[0][2, 0], outs[0][2, 1] = pieces[1, :CUT_ROWS], arrived[1, :CUT_ROWS]
            outs[1][0], outs[1][1] = pieces[2, :CUT_ROWS], arrived[2, :CUT_ROWS]
            outs[2][...] = (keep_qkv_out[...] + arrived[0].astype(F32)).astype(BF16)

        near_x, near_low, piece_qkv_out = step(
            share_high,
            [pieces, arrived, keep_qkv_out, near_down, down_low],
            [sds((3, 2, *piece), BF16), sds((2, *piece), BF16), sds(taller, BF16)],
            "share_high",
        )
        arrived_x, low_low = over_x(near_x), over_z_low(near_low)
        qkv_out_high = over_z_high(piece_qkv_out)
        output = layer_output(middle, hidden, down_whole, (near_x,))

        def share_next(ins, outs):
            near_x, arrived_x, near_low, low_low = ins
            outs[0][0], outs[0][1] = near_x[2], arrived_x[2]
            outs[1][0], outs[1][1] = near_low[...], low_low[...]
            for low in range(2):
                for high in range(2):
                    outs[2][0, 0, low * 2 + high] = near_x[low, high]
                    outs[2][0, 1, low * 2 + high] = arrived_x[low, high]

        near_up, near_low, near_down = step(
            share_next,
            [near_x, arrived_x, near_low, low_low],
            [
                *(sds((2, 2, *piece), BF16), sds((2, 2, *piece), BF16)),
                sds((1, 2, 4, *piece), BF16),
            ],
            "share_next",
            (qkv_out_high,),
        )
        far_down = over_core(near_down)
        up_low, low_x = over_z_low(near_up), over_x(near_low)

        def update(near, far, place, height, state, gains, name, after):
            near_out = update_half(
                idx, 0, near, place, height, state, (), gains, name + "_near", after
            )
            count = len(state)
            mark = near_out[-1]
            far_out = update_half(
                idx, 1, far, place, height, state, near_out[:count], (), name + "_far", (mark,)
            )
            return (*far_out[:count], *near_out[count:-1], far_out[-1])

        one_down, two_down, next_down, mark = update(
            near_down,
            far_down,
            lambda p, x, z: (
                (x * 2 + (z >> 1)) * CUT_ROWS,
                [(0, CUT_COLUMNS, (z & 1) * CUT_COLUMNS)],
            ),
            2 * HALF,
            [down_t, first_down_t, second_down_t],
            (),
            "update_down",
            (near_up,),
        )

        def share_qkv_out_high(ins, outs):
            outs[0][0], outs[0][1] = ins[0][...], ins[1][...]

        (near_qkv_out,) = step(
            share_qkv_out_high,
            [piece_qkv_out, qkv_out_high],
            [sds((2, *taller), BF16)],
            "share_qkv_out_high",
            (mark,),
        )
        qkv_out_x, qkv_out_low = over_x(near_qkv_out), over_z_low(near_qkv_out)
        qkv_out_both = swap(near_qkv_out, "dp", 6)

        def share_gate_up(ins, outs):
            for near in range(2):
                for far in range(2):
                    for high in range(2):
                        outs[0][0, near, far * 2 + high] = ins[far][near, high]
                        outs[0][1, far, near * 2 + high] = ins[2 + far][near, high]

        (near_gate_up,) = step(
            share_gate_up,
            [near_up, up_low, near_low, low_x],
            [sds((2, 2, 4, *piece), BF16)],
            "share_gate_up",
            (near_qkv_out,),
        )
        far_gate_up = over_core(near_gate_up)
        one_gate_up, two_gate_up, next_gate_up, mark = update(
            near_gate_up,
            far_gate_up,
            lambda p, x, z: (p * CUT_ROWS, [(0, CUT_COLUMNS, (x * 4 + z) * CUT_COLUMNS)]),
            HALF,
            [w_gate_up, first_gate_up, second_gate_up],
            (),
            "update_gate_up",
            (),
        )

        def share_qkv_out(ins, outs):
            for x in range(2):
                for low in range(2):
                    for high in range(2):
                        outs[0][0, x, low * 2 + high] = ins[low * 2 + x][high]

        (near_qkv_out,) = step(
            share_qkv_out,
            [near_qkv_out, qkv_out_x, qkv_out_low, qkv_out_both],
            [sds((1, 2, 4, *taller), BF16)],
            "share_qkv_out",
            (mark,),
        )
        far_qkv_out = over_core(near_qkv_out)
        cuts = [[(0, 384, 0)], [(0, 384, 384)], [(0, 192, 768), (192, 192, 1024)], [(0, 384, 1216)]]
        updated = update(
            near_qkv_out,
            far_qkv_out,
            lambda p, x, z: (x * CUT_ROWS, cuts[z]),
            HALF,
            [w_qkv, w_out, first_qkv, first_out, second_qkv, second_out],
            (norm_gains, first_gains, second_gains),
            "update_qkv_out",
            (),
        )
        one_qkv, one_out, two_qkv, two_out, next_qkv, next_out = updated[:6]
        one_gains, two_gains, next_gains = updated[6:9]
    else:
        sums = lax.psum((*grad_qkv_out, grad_gate_up[0], grad_down[0].T), ("dp", "shard"))
        grad_qkv_out, grad_gains, grad_gate_up, grad_down = sums

        def own(grad, axis=0):
            size = grad.shape[axis] // groups
            return lax.dynamic_slice_in_dim(grad, owner * size, size, axis)

        one_qkv, two_qkv, next_qkv = adamw(
            w_qkv, first_qkv, second_qkv, own(grad_qkv_out[:, :QKV]), RATE_MATRIX, DECAY_MATRIX
        )
        one_out, two_out, next_out = adamw(
            w_out, first_out, second_out, own(grad_qkv_out[:, QKV:]), RATE_MATRIX, DECAY_MATRIX
        )
        one_gate_up, two_gate_up, next_gate_up = adamw(
            w_gate_up, first_gate_up, second_gate_up, own(grad_gate_up), RATE_MATRIX, DECAY_MATRIX
        )
        one_down, two_down, next_down = [
            a.T
            for a in adamw(
                w_down, first_down, second_down, own(grad_down), RATE_MATRIX, DECAY_MATRIX
            )
        ]
        one_gains, two_gains, next_gains = adamw(
            norm_gains, first_gains, second_gains, own(grad_gains, 1), RATE_GAIN, 0.0
        )
    one_down, two_down, next_down = one_down.T, two_down.T, next_down.T
    return (
        output.T[None],
        token_grad.T[None],
        one_qkv,
        one_out,
        one_gate_up,
        one_down,
        one_gains,
        two_qkv,
        two_out,
        two_gate_up,
        two_down,
        two_gains,
        next_qkv,
        next_out,
        next_gate_up,
        next_down,
        next_gains,
    )


def solution(mesh):
    return jax.shard_map(
        per_device,
        mesh=mesh,
        in_specs=(
            P(("dp", "shard"), None, None),
            P(("dp", "shard"), None),
            P(("dp", "shard"), None, None),
            P("shard", None),
            P("shard", None),
            P("shard", None),
            P("shard", None),
            P(None, "shard"),
            P("shard", None),
            P("shard", None),
            P("shard", None),
            P("shard", None),
            P(None, "shard"),
            P("shard", None),
            P("shard", None),
            P("shard", None),
            P("shard", None),
            P(None, "shard"),
        ),
        out_specs=(
            P(("dp", "shard"), None, None),
            P(("dp", "shard"), None, None),
            P("shard", None),
            P("shard", None),
            P("shard", None),
            P("shard", None),
            P(None, "shard"),
            P("shard", None),
            P("shard", None),
            P("shard", None),
            P("shard", None),
            P(None, "shard"),
            P("shard", None),
            P("shard", None),
            P("shard", None),
            P("shard", None),
            P(None, "shard"),
        ),
        check_vma=False,
    )
```

```python
import functools

import jax
import jax.numpy as jnp
import numpy as np
from jax import lax
from jax.experimental import pallas as pl
from jax.experimental.pallas import tpu as pltpu
from jax.sharding import PartitionSpec as P

HEADS = 9
KV_HEADS = 3
GROUP = HEADS // KV_HEADS
HEAD = 64
FF = 1536
STEP = 10
QUERY = HEADS * HEAD
ROPED = (HEADS + KV_HEADS) * HEAD
QKV = (HEADS + 2 * KV_HEADS) * HEAD
LANES = 128

EPS_NORM = 1e-05
ROPE_BASE = 100000.0
BETA_ONE = 0.9
BETA_TWO = 0.95
RATE_MATRIX = 0.1
RATE_GAIN = 0.3
DECAY_MATRIX = 0.1
EPS_ADAM = 1e-08
MASKED = -1e30
SCALE = float(HEAD) ** (-0.5)
VMEM_LIMIT = 32 * 1024 * 1024
PACK_LIMIT = 53 * 1024 * 1024
HALF = 144
CUT_ROWS = 72
MARK = (8, 128)
CUT_COLUMNS = 384
F32 = jnp.float32
BF16 = jnp.bfloat16


def rotate_block(values, cosine, signed_sine):
    lane = lax.broadcasted_iota(jnp.int32, values.shape, 1)
    swapped = jnp.where(
        lane % HEAD < HEAD // 2,
        pltpu.roll(values, LANES - HEAD // 2, 1),
        pltpu.roll(values, HEAD // 2, 1),
    )
    return values * cosine + swapped * signed_sine


def adamw(weight, first_moment, second_moment, gradient, step_rate, weight_decay):
    first_new = BETA_ONE * first_moment + (1.0 - BETA_ONE) * gradient
    second_new = BETA_TWO * second_moment + (1.0 - BETA_TWO) * gradient * gradient
    fix_one = 1.0 / (1.0 - BETA_ONE**STEP)
    fix_two = 1.0 / (1.0 - BETA_TWO**STEP)
    update = first_new * fix_one / (jnp.sqrt(second_new * fix_two) + EPS_ADAM)
    return (first_new, second_new, weight - step_rate * (update + weight_decay * weight))


def adamw_rows(weight, first_moment, second_moment, gradient, step_rate, weight_decay):
    first_new = BETA_ONE * first_moment + (1.0 - BETA_ONE) * gradient
    second_new = BETA_TWO * second_moment + (1.0 - BETA_TWO) * gradient * gradient
    value = second_new * (1.0 / (1.0 - BETA_TWO**STEP))
    guess = lax.rsqrt(value)
    divisor = value * guess + EPS_ADAM
    inverse = guess * (2.0 - divisor * guess)
    update = first_new * (step_rate / (1.0 - BETA_ONE**STEP)) * inverse
    return (first_new, second_new, weight * (1.0 - step_rate * weight_decay) - update)


def dot(left, right):
    return lax.dot_general(left, right, (((1,), (0,)), ((), ())), preferred_element_type=F32)


def dot_right_t(left, right):
    return lax.dot_general(left, right, (((1,), (1,)), ((), ())), preferred_element_type=F32)


def dot_left_t(left, right):
    return lax.dot_general(left, right, (((0,), (0,)), ((), ())), preferred_element_type=F32)


def norm_scale(values):
    return lax.rsqrt(jnp.mean(values * values, axis=-1, keepdims=True) + EPS_NORM)


def norm_back(grad_normed, normed, scale_rows):
    return scale_rows * (
        grad_normed - normed * jnp.mean(grad_normed * normed, axis=-1, keepdims=True)
    )


class Weight:
    def __init__(self, shape, whole=None, own=(), parts=()):
        self.shape, self.own, self.parts = shape, own, parts
        self.arrays = [whole] if whole is not None else [a[0] for a in (*own, *parts)]
        self.split = whole is None

    def load(self, idx, refs, full):
        if not self.split:
            return refs[0]
        for ref, (_, place) in zip(refs, self.own):
            self.put(full, place(idx[0]), ref[...].astype(BF16))
        for ref, (_, (core, x, low), place) in zip(refs[len(self.own) :], self.parts):
            place = place(1 - idx[0], idx[1] ^ core, idx[2] ^ x, (idx[3] & 1) ^ low)
            rows = ref.shape[0] // HALF * HALF
            self.put(full, place, ref[:rows, :])
        return full

    def put(self, full, position, value):
        where = []
        for axis, tile in ((0, 16), (1, LANES)):
            at, size = position[axis], value.shape[axis]
            if size == self.shape[axis]:
                where.append(slice(None))
            elif isinstance(at, int):
                where.append(slice(at, at + size))
            else:
                where.append(pl.ds(pl.multiple_of(at, tile), size))
        full[tuple(where)] = value


def call(body, idx, arrays, weights, outs, scratch, busy, name, after=(), hand_on=False):
    counts = [len(w.arrays) for w in weights]
    flat = list(arrays) + [a for w in weights for a in w.arrays]
    outs = list(outs)
    split = [w for w in weights if w.split]
    hand_on = hand_on and bool(split)
    if hand_on:
        outs += [sds(split[-1].shape, BF16)]
    made = [pltpu.VMEM(w.shape, BF16) for w in (split[:-1] if hand_on else split)]

    def kernel(*refs):
        refs = list(refs)
        idx_ref = refs.pop(0)
        take = lambda n: [refs.pop(0) for _ in range(n)]
        array_refs = take(len(arrays))
        weight_refs = [take(n) for n in counts]
        take(len(after))
        out_refs = take(len(outs))
        own_scratch = take(len(scratch))
        fulls = take(len(made)) + ([out_refs.pop()] if hand_on else [])
        loads = [
            functools.partial(w.load, idx_ref, r, fulls.pop(0) if w.split else None)
            for w, r in zip(weights, weight_refs)
        ]
        body(idx_ref, array_refs, loads, out_refs, own_scratch)

    return pl.pallas_call(
        kernel,
        out_shape=tuple(outs),
        in_specs=[pl.BlockSpec(memory_space=pltpu.SMEM)]
        + [pl.BlockSpec(memory_space=pltpu.VMEM)] * len(flat)
        + [pl.BlockSpec(memory_space=pl.ANY)] * len(after),
        out_specs=tuple([pl.BlockSpec(memory_space=pltpu.VMEM)] * len(outs)),
        scratch_shapes=list(scratch) + made,
        compiler_params=pltpu.CompilerParams(vmem_limit_bytes=VMEM_LIMIT),
        cost_estimate=busy_for(busy),
        name=name,
    )(idx, *flat, *after)


def busy_for(microseconds):
    return pl.CostEstimate(flops=int(microseconds * 1e9), bytes_accessed=0, transcendentals=0)


def sds(shape, dtype):
    return jax.ShapeDtypeStruct(shape, dtype)


class Pieces:
    def __init__(self, place, parts=1, extra=0):
        self.place, self.parts, self.extra = place, parts, extra

    def outs(self):
        return [sds((self.parts, 2, 8, CUT_ROWS + self.extra, CUT_COLUMNS), BF16)] * 2

    def scratch(self, columns):
        return pltpu.VMEM((8, CUT_ROWS, columns), BF16)

    def store(self, blocks, grad, start=0):
        for i in range(8):
            rows = grad[i * CUT_ROWS : (i + 1) * CUT_ROWS].astype(BF16)
            blocks[i, :, start : start + grad.shape[1]] = rows

    def emit(self, idx, blocks, outs, under=None):
        for other_core, out in enumerate((outs[1], outs[0])):
            for part in range(self.parts):
                for owner in range(2):
                    for slot in range(8):
                        z = ((slot >> 1) & 1) | ((slot & 1) << 1)
                        block, column = self.place(
                            idx[0] ^ owner, idx[1] ^ other_core, idx[2] ^ (slot >> 2), idx[3] ^ z, part
                        )
                        columns = pl.ds(pl.multiple_of(column * CUT_COLUMNS, LANES), CUT_COLUMNS)
                        piece = blocks[block, :, columns]
                        if under is not None:
                            piece = jnp.concatenate(
                                [piece.astype(F32), under[idx[0] ^ owner]], axis=0
                            ).astype(BF16)
                        out[part, owner, slot] = piece


def head_stack(values, kv_head):
    first = kv_head * GROUP
    return jnp.concatenate(
        [values[:, (first + i) * HEAD : (first + i + 1) * HEAD] for i in range(GROUP)], axis=0
    )


def softmax_rows(query, key, allowed):
    scores = jnp.where(allowed, dot_right_t(query, key) * SCALE, MASKED)
    top = jnp.max(scores, axis=-1, keepdims=True)
    exponent = jnp.exp(scores - top)
    return exponent / jnp.sum(exponent, axis=-1, keepdims=True)


def pack_kernel(body, idx, sources, places, outs, name, after=(), limit=PACK_LIMIT):
    windows = [shape for shape, _ in places]

    def kernel(idx_ref, *refs):
        sources_in, refs = refs[: len(sources)], refs[len(sources) + len(after) :]
        out_refs, buffers, sem = refs[: len(outs)], refs[len(outs) : -1], refs[-1]
        copies = []
        for i, (source, (shape, place)) in enumerate(zip(sources_in, places)):
            where = []
            for axis, tile in ((0, 8), (1, LANES)):
                if shape[axis] == source.shape[axis]:
                    where.append(slice(None))
                else:
                    where.append(pl.ds(pl.multiple_of(place(idx_ref)[axis], tile), shape[axis]))
            copies.append(pltpu.make_async_copy(source.at[tuple(where)], buffers[i], sem.at[i]))
        for copy in copies:
            copy.start()
        for copy in copies:
            copy.wait()
        body(idx_ref, buffers, out_refs)

    return pl.pallas_call(
        kernel,
        out_shape=tuple(outs),
        in_specs=[pl.BlockSpec(memory_space=pltpu.SMEM)]
        + [pl.BlockSpec(memory_space=pltpu.HBM)] * len(sources)
        + [pl.BlockSpec(memory_space=pl.ANY)] * len(after),
        out_specs=tuple([pl.BlockSpec(memory_space=pltpu.VMEM)] * len(outs)),
        scratch_shapes=[pltpu.VMEM(w, F32) for w in windows]
        + [pltpu.SemaphoreType.DMA((len(sources),))],
        compiler_params=pltpu.CompilerParams(vmem_limit_bytes=limit),
        cost_estimate=busy_for(10),
        name=name,
    )(idx, *sources, *after)


def cast_out(idx_ref, buffers, outs):
    for buffer, out in zip(buffers, outs):
        out[...] = buffer[...].astype(BF16)


def pack_down(idx, down_t, after):
    shape = (2 * HALF, down_t.shape[1])
    window = (shape, lambda i: (i[1] * 2 * HALF, 0))
    outs = [sds(shape, BF16)]
    return pack_kernel(
        cast_out, idx, [down_t], [window], outs, "pack_down", after, VMEM_LIMIT
    )[0]


def pack_first(idx, w_qkv, w_out, norm_gains, w_gate_up):
    columns = (QKV + w_out.shape[1]) // 2
    quarter = FF // 2
    windows = [((HALF, m.shape[1]), lambda i: (i[1] * HALF, 0)) for m in (w_qkv, w_out)]
    windows.append((norm_gains.shape, lambda i: (0, 0)))
    windows.append(((HALF, quarter), lambda i: (i[1] * HALF, i[2] * quarter)))
    windows.append(((HALF, quarter), lambda i: (i[1] * HALF, FF + (i[3] & 1) * quarter)))

    def body(idx_ref, buffers, outs):
        q_ref, o_ref, gains_ref = buffers[:3]
        both = jnp.concatenate([q_ref[:, columns:], o_ref[...]], axis=1)
        outs[0][:HALF, :] = jnp.where((idx_ref[3] & 1) == 0, q_ref[:, :columns], both).astype(BF16)
        outs[0][HALF:, :] = jnp.zeros((16, columns), BF16)
        outs[0][HALF : HALF + 2, : gains_ref.shape[1]] = gains_ref[...].astype(BF16)
        cast_out(idx_ref, buffers[3:], outs[1:])

    outs = [sds((HALF + 16, columns), BF16)] + [sds((HALF, quarter), BF16)] * 2
    sources = [w_qkv, w_out, norm_gains, w_gate_up, w_gate_up]
    return pack_kernel(body, idx, sources, windows, outs, "pack_first")


def attention_forward(idx, tokens_t, segments, frequency, gains, w_qkv_out):
    width, seq_length = tokens_t.shape
    split_gains = len(gains) > 1

    def body(idx_ref, arrays, loads, outs, scratch):
        x_ref, seg_ref, freq_ref = arrays[:3]
        qkv_ref, o_ref, cos_ref, sin_ref, allowed_ref, gains_ref = outs
        if split_gains:
            own = arrays[3][...].astype(BF16).astype(F32)
            other = arrays[4][HALF : HALF + 8, : width // 2].astype(F32)[:2]
            gains_ref[...] = jnp.where(
                idx_ref[0] == 0,
                jnp.concatenate([own, other], axis=1),
                jnp.concatenate([other, own], axis=1),
            )
        else:
            gains_ref[...] = arrays[3][...]
        seen_doc = jnp.broadcast_to(seg_ref[...], (seq_length, seq_length))
        own_doc = seen_doc.T
        token = lax.broadcasted_iota(jnp.int32, (seq_length, seq_length), 0)
        seen = lax.broadcasted_iota(jnp.int32, (seq_length, seq_length), 1)
        begin = jnp.sum((seen_doc < own_doc).astype(F32), axis=-1, keepdims=True)
        angles = (token.astype(F32) - begin) * freq_ref[...]
        cosine, sine = jnp.cos(angles), jnp.sin(angles)
        sine = jnp.where(seen % HEAD < HEAD // 2, -sine, sine)
        cos_ref[...] = cosine
        sin_ref[...] = sine
        allowed = ((seen_doc == own_doc) & (token >= seen)).astype(F32)
        allowed_ref[...] = allowed
        allowed = jnp.concatenate([allowed] * GROUP, axis=0) > 0.5
        x = x_ref[...].astype(F32).T
        h1 = (x * norm_scale(x) * gains_ref[0:1, :]).astype(BF16)
        projected = dot(h1, loads[0]()[:, :QKV])
        for start in range(0, ROPED, LANES):
            block = projected[:, start : start + LANES]
            qkv_ref[:, start : start + LANES] = rotate_block(block, cosine, sine).astype(BF16)
        qkv_ref[:, ROPED:QKV] = projected[:, ROPED:QKV].astype(BF16)
        qkv = qkv_ref[...]
        for kv in range(KV_HEADS):
            key = qkv[:, QUERY + kv * HEAD : QUERY + (kv + 1) * HEAD]
            value = qkv[:, ROPED + kv * HEAD : ROPED + (kv + 1) * HEAD]
            probs = softmax_rows(head_stack(qkv, kv), key, allowed).astype(BF16)
            attended = dot(probs, value).astype(BF16)
            for i in range(GROUP):
                start = (kv * GROUP + i) * HEAD
                o_ref[:, start : start + HEAD] = attended[i * seq_length : (i + 1) * seq_length]

    square = sds((seq_length, seq_length), F32)
    outs = [sds((seq_length, QKV), BF16), sds((seq_length, QUERY), BF16)]
    outs += [square, square, square, sds((2, width), F32)]
    return call(
        body,
        idx,
        [tokens_t, segments, frequency, *gains],
        [w_qkv_out],
        outs,
        [],
        1,
        "attention",
        hand_on=True,
    )


def feed_forward(idx, tokens_t, attended, gains, cotangent_t, w_qkv_out, w_gate_up, pieces, after):
    width, seq_length = tokens_t.shape

    def body(idx_ref, arrays, loads, outs, scratch):
        x_ref, o_ref, gains_ref, y_ref = arrays
        u_ref, h2_ref, ab_ref, z_ref = outs[:4]
        u = x_ref[...].astype(F32).T + dot(o_ref[...], loads[0]()[:, QKV:])
        u_ref[...] = u
        h2 = (u * norm_scale(u) * gains_ref[1:2, :]).astype(BF16)
        h2_ref[...] = h2
        ab = dot(h2, loads[1]()[...])
        ab_ref[...] = ab
        gate, up = ab[:, :FF], ab[:, FF:]
        z = (gate * jax.nn.sigmoid(gate) * up).astype(BF16)
        z_ref[...] = z
        grad = dot(y_ref[...], z)
        if pieces is None:
            outs[4][...] = grad
        else:
            pieces.store(scratch[0], grad)
            pieces.emit(idx_ref, scratch[0], outs[4:])

    outs = [
        sds((seq_length, width), F32),
        sds((seq_length, width), BF16),
        sds((seq_length, 2 * FF), F32),
        sds((seq_length, FF), BF16),
    ]
    outs += [sds((width, FF), F32)] if pieces is None else pieces.outs()
    scratch = [] if pieces is None else [pieces.scratch(FF)]
    return call(
        body,
        idx,
        [tokens_t, attended, gains, cotangent_t],
        [w_qkv_out, w_gate_up],
        outs,
        scratch,
        5,
        "feed_forward",
        after,
        True,
    )


def feed_back(idx, ab, normed_low, cotangent_t, down_t, pieces):
    width, seq_length = cotangent_t.shape

    def body(idx_ref, arrays, loads, outs, scratch):
        ab_ref, h2_ref, y_ref = arrays
        gg_ref = outs[0]
        gate, up = ab_ref[:, :FF], ab_ref[:, FF:]
        sig = jax.nn.sigmoid(gate)
        grad_hidden = dot_left_t(y_ref[...], loads[0]()[...])
        gg_ref[:, :FF] = (grad_hidden * up * sig * (1.0 + gate * (1.0 - sig))).astype(BF16)
        gg_ref[:, FF:] = (grad_hidden * gate * sig).astype(BF16)
        grad = dot_left_t(h2_ref[...], gg_ref[...])
        if pieces is None:
            outs[1][...] = grad
        else:
            pieces.store(scratch[0], grad)
            pieces.emit(idx_ref, scratch[0], outs[1:])

    outs = [sds((seq_length, 2 * FF), BF16)]
    outs += [sds((width, 2 * FF), F32)] if pieces is None else pieces.outs()
    scratch = [] if pieces is None else [pieces.scratch(2 * FF)]
    return call(
        body,
        idx,
        [ab, normed_low, cotangent_t],
        [down_t],
        outs,
        scratch,
        20,
        "feed_back",
        hand_on=True,
    )


def layer_output(middle, hidden, down_t, after):
    seq_length, width = middle.shape

    def body(ins, outs):
        outs[0][...] = (ins[0][...] + dot_right_t(ins[1][...], ins[2][...])).T.astype(BF16)

    return step(
        body, [middle, hidden, down_t], [sds((width, seq_length), BF16)], "layer_output", after, 2
    )[0]


def middle_back(idx, cotangent_t, middle, gated, gains, w_gate_up, w_qkv_out, after):
    width, seq_length = cotangent_t.shape

    def body(idx_ref, arrays, loads, outs, scratch):
        y_ref, u_ref, gg_ref, gains_ref = arrays
        gu_ref, go_ref, gain_ref = outs
        u = u_ref[...]
        scale_two = norm_scale(u)
        normed = u * scale_two
        grad_normed = dot_right_t(gg_ref[...], loads[0]()[...])
        gain_ref[...] = jnp.sum(grad_normed * normed, axis=0, keepdims=True)
        gu = y_ref[...].astype(F32).T + norm_back(
            grad_normed * gains_ref[1:2, :], normed, scale_two
        )
        gu_ref[...] = gu
        go_ref[...] = dot_right_t(gu.astype(BF16), loads[1]()[:, QKV:]).astype(BF16)

    outs = [sds((seq_length, width), F32), sds((seq_length, width), BF16), sds((1, width), F32)]
    return call(
        body,
        idx,
        [cotangent_t, middle, gated, gains],
        [w_gate_up, w_qkv_out],
        outs,
        [],
        20,
        "middle_back",
        after,
    )


def attention_back(
    idx, tokens_t, grad_middle, grad_attended, gain_two, qkv, attended, tables, gains, w_qkv, pieces, after
):
    width, seq_length = tokens_t.shape

    def body(idx_ref, arrays, loads, outs, scratch):
        x_ref, gu_ref, go_ref, gain_two_ref, qkv_ref, o_ref = arrays[:6]
        cos_ref, sin_ref, allowed_ref, gains_ref = arrays[6:]
        grad_ref = outs[0]
        grad_proj, gp_ref, gain_rows, *blocks = scratch
        gu, go = gu_ref[...], go_ref[...]
        gu_low = gu.astype(BF16)
        grad_gain_two = gain_two_ref[...]
        allowed = jnp.concatenate([allowed_ref[...]] * GROUP, axis=0) > 0.5
        qkv_values = qkv_ref[...]
        for kv in range(KV_HEADS):
            key = qkv_values[:, QUERY + kv * HEAD : QUERY + (kv + 1) * HEAD]
            value = qkv_values[:, ROPED + kv * HEAD : ROPED + (kv + 1) * HEAD]
            query = head_stack(qkv_values, kv)
            grad_out = head_stack(go, kv)
            probs = softmax_rows(query, key, allowed)
            grad_probs = dot_right_t(grad_out, value)
            row_delta = jnp.sum(probs * grad_probs, axis=-1, keepdims=True)
            gs = (probs * (grad_probs - row_delta)).astype(BF16)
            grad_query = dot(gs, key) * SCALE
            for i in range(GROUP):
                start = (kv * GROUP + i) * HEAD
                grad_proj[:, start : start + HEAD] = grad_query[
                    i * seq_length : (i + 1) * seq_length
                ]
            start = QUERY + kv * HEAD
            grad_proj[:, start : start + HEAD] = dot_left_t(gs, query) * SCALE
            start = ROPED + kv * HEAD
            grad_proj[:, start : start + HEAD] = dot_left_t(probs.astype(BF16), grad_out)
        for start in range(0, ROPED, LANES):
            gp_ref[:, start : start + LANES] = rotate_block(
                grad_proj[:, start : start + LANES], cos_ref[...], -sin_ref[...]
            ).astype(BF16)
        gp_ref[:, ROPED:QKV] = grad_proj[:, ROPED:QKV].astype(BF16)
        x = x_ref[...].astype(F32).T
        scale_one = norm_scale(x)
        normed = x * scale_one
        h1 = (normed * gains_ref[0:1, :]).astype(BF16)
        grad_qkv = dot_left_t(h1, gp_ref[...])
        grad_out = dot_left_t(o_ref[...], gu_low)
        grad_normed = dot_right_t(gp_ref[...], loads[0]()[:, :QKV])
        grad_gain_one = jnp.sum(grad_normed * normed, axis=0, keepdims=True)
        if pieces is None:
            outs[1][:, :QKV] = grad_qkv
            outs[1][:, QKV:] = grad_out
            outs[2][0:1, :] = grad_gain_one
            outs[2][1:2, :] = grad_gain_two
        else:
            pieces.store(blocks[0], grad_qkv)
            pieces.store(blocks[0], grad_out, QKV)
            half = width // 2
            gain_rows[...] = jnp.zeros_like(gain_rows)
            for owner in range(2):
                columns = slice(owner * half, (owner + 1) * half)
                gain_rows[owner, 0:1, :half] = grad_gain_one[:, columns]
                gain_rows[owner, 1:2, :half] = grad_gain_two[:, columns]
            pieces.emit(idx_ref, blocks[0], outs[1:3], gain_rows)
            outs[3][...] = jnp.zeros_like(outs[3])
        grad_ref[...] = (
            (gu + norm_back(grad_normed * gains_ref[0:1, :], normed, scale_one)).T
        ).astype(BF16)

    outs = [sds((width, seq_length), BF16)]
    scratch = [
        pltpu.VMEM((seq_length, QKV), F32),
        pltpu.VMEM((seq_length, QKV), BF16),
        pltpu.VMEM((2, 8, CUT_COLUMNS), F32),
    ]
    if pieces is None:
        outs += [sds((width, QKV + width), F32), sds((2, width), F32)]
    else:
        outs += pieces.outs() + [sds(MARK, F32)]
        scratch += [pieces.scratch(QKV + width)]
    return call(
        body,
        idx,
        [tokens_t, grad_middle, grad_attended, gain_two, qkv, attended, *tables, gains],
        [w_qkv],
        outs,
        scratch,
        20,
        "attention_back",
        after,
    )


def step(body, arrays, outs, name, after=(), busy=20):
    def kernel(*refs):
        body(refs[: len(arrays)], refs[len(arrays) + len(after) :])

    return pl.pallas_call(
        kernel,
        out_shape=tuple(outs),
        in_specs=[pl.BlockSpec(memory_space=pltpu.VMEM)] * len(arrays)
        + [pl.BlockSpec(memory_space=pl.ANY)] * len(after),
        out_specs=tuple([pl.BlockSpec(memory_space=pltpu.VMEM)] * len(outs)),
        compiler_params=pltpu.CompilerParams(vmem_limit_bytes=VMEM_LIMIT),
        cost_estimate=busy_for(busy),
        name=name,
    )(*arrays, *after)


def pass_on(ins, outs):
    outs[0][...] = ins[0][...]


def add_split(keep, arrived, axis, send_ref, keep_ref):
    total = keep[...].astype(F32) + arrived[...].astype(F32)
    low, high = lax.index_in_dim(total, 0, axis, False), lax.index_in_dim(total, 1, axis, False)
    send_ref[...] = high.astype(BF16)
    keep_ref[...] = low


def add_step(jobs, name, after):
    arrays, outs = [], []
    for keep, arrived, axis in jobs:
        arrays += [keep, arrived]
        shape = keep.shape[:axis] + keep.shape[axis + 1 :]
        outs += [sds(shape, BF16), sds(shape, F32)]

    def body(ins, out_refs):
        for i, (_, _, axis) in enumerate(jobs):
            add_split(ins[2 * i], ins[2 * i + 1], axis, out_refs[2 * i], out_refs[2 * i + 1])

    flat = step(body, arrays, outs, name, after)
    return [(flat[2 * i], flat[2 * i + 1]) for i in range(len(jobs))]


def update_rows(idx, shares, place, height, chunk, state, earlier, gains, name, after, busy=20):
    count = len(state) // 3
    columns = [a.shape[1] for a in state[:count]]
    starts = [sum(-(-c // LANES) * LANES for c in columns[:k]) for k in range(count + 1)]
    chunks = height // chunk
    order = [(k, count + k, 2 * count + k) for k in range(count)]

    def kernel(idx_ref, *refs):
        refs = list(refs)
        take = lambda n: [refs.pop(0) for _ in range(n)]
        share_refs = take(len(shares))
        state_refs, gain_refs = take(3 * count), take(len(gains))
        take(len(earlier) + len(after))
        outs, gain_outs, (mark,) = take(3 * count), take(len(gains)), take(1)
        buffers, (full, sem) = take(3 * count), refs
        mark[...] = jnp.zeros_like(mark)
        copies = []
        for share, (far, _) in enumerate(shares):
            piece_ref = share_refs[share]
            for part in range(piece_ref.shape[0]):
                for x in range(2):
                    for z in range(4):
                        rel = z ^ idx_ref[3]
                        slot = ((rel & 1) << 1) | (rel >> 1)
                        piece = piece_ref[part, x, slot].astype(F32)[:CUT_ROWS]
                        row, cuts = place(part, idx_ref[2] ^ x, z)
                        rows = pl.ds(pl.multiple_of(share * height + row, 8), CUT_ROWS)
                        for begin, size, to in cuts:
                            if isinstance(to, int):
                                where = slice(to, to + size)
                            else:
                                where = pl.ds(pl.multiple_of(to, LANES), size)
                            full[rows, where] = piece[:, begin : begin + size]
            base = (idx_ref[1] ^ far) * height
            for at_chunk in range(chunks):

                def eight_rows(i, carry, at_chunk=at_chunk, share=share, base=base):
                    at_row = at_chunk * chunk + i * 8
                    near_rows = pl.ds(pl.multiple_of(share * height + at_row, 8), 8)
                    rows = pl.ds(pl.multiple_of(base + at_row, 8), 8)
                    for k in range(count):
                        for at in range(0, columns[k], 768):
                            size = min(768, columns[k] - at)
                            where = slice(at, at + size)
                            results = adamw_rows(
                                *[state_refs[j][rows, where] for j in order[k]],
                                full[near_rows, starts[k] + at : starts[k] + at + size],
                                RATE_MATRIX,
                                DECAY_MATRIX,
                            )
                            for j, result in zip(order[k], results):
                                buffers[j][near_rows, where] = result
                    return carry

                lax.fori_loop(0, chunk // 8, eight_rows, 0, unroll=3)
                near_rows = pl.ds(share * height + at_chunk * chunk, chunk)
                rows = pl.ds(pl.multiple_of(base + at_chunk * chunk, 8), chunk)
                for j in range(3 * count):
                    copy = pltpu.make_async_copy(
                        buffers[j].at[near_rows],
                        outs[j].at[rows],
                        sem.at[share * chunks + at_chunk, j],
                    )
                    copy.start()
                    copies.append(copy)
        if gains:
            gradient = share_refs[0][0, 0, 0, CUT_ROWS:, :].astype(F32)[:2, : gains[0].shape[1]]
            results = adamw_rows(*[g[...] for g in gain_refs], gradient, RATE_GAIN, 0.0)
            for out, result in zip(gain_outs, results):
                out[...] = result
        for copy in copies:
            copy.wait()

    vmem, anywhere = pl.BlockSpec(memory_space=pltpu.VMEM), pl.BlockSpec(memory_space=pl.ANY)
    first_earlier = 1 + len(shares) + 3 * count + len(gains)
    total = len(shares) * height
    return pl.pallas_call(
        kernel,
        out_shape=tuple(sds(a.shape, F32) for a in [*state, *gains]) + (sds(MARK, F32),),
        in_specs=[pl.BlockSpec(memory_space=pltpu.SMEM)]
        + [vmem] * (len(shares) + 3 * count + len(gains))
        + [anywhere] * (len(earlier) + len(after)),
        out_specs=tuple([anywhere] * (3 * count) + [vmem] * (len(gains) + 1)),
        scratch_shapes=[pltpu.VMEM((total, a.shape[1]), F32) for a in state]
        + [pltpu.VMEM((total, starts[-1]), F32)]
        + [pltpu.SemaphoreType.DMA((len(shares) * chunks, 3 * count))],
        input_output_aliases={first_earlier + i: i for i in range(len(earlier))},
        compiler_params=pltpu.CompilerParams(vmem_limit_bytes=VMEM_LIMIT),
        cost_estimate=busy_for(busy),
        name=name,
    )(idx, *[p for _, p in shares], *state, *gains, *earlier, *after)


def swap(values, axis, mask):
    size = lax.axis_size(axis)
    return lax.ppermute(values, axis, [(i, i ^ mask) for i in range(size)])


over_y = functools.partial(swap, axis="shard", mask=1)
over_core = functools.partial(swap, axis="dp", mask=1)
over_x = functools.partial(swap, axis="dp", mask=2)
over_z_low = functools.partial(swap, axis="dp", mask=4)
over_z_high = functools.partial(swap, axis="dp", mask=8)


def per_device(
    tokens,
    segments,
    cotangent,
    w_qkv,
    w_out,
    w_gate_up,
    w_down,
    norm_gains,
    first_qkv,
    first_out,
    first_gate_up,
    first_down,
    first_gains,
    second_qkv,
    second_out,
    second_gate_up,
    second_down,
    second_gains,
):
    groups = lax.axis_size("shard")
    replicas = lax.axis_size("dp")
    fast = groups == 2 and replicas == 16
    place_dp = lax.axis_index("dp")
    owner = lax.axis_index("shard")
    idx = jnp.stack([owner, place_dp & 1, (place_dp >> 1) & 1, place_dp >> 2]).astype(jnp.int32)
    x_t, y_t = tokens[0].T, cotangent[0].T
    width, seq_length = x_t.shape
    rows, down_rows = w_qkv.shape[0], w_down.shape[0]
    down_t, first_down_t, second_down_t = w_down.T, first_down.T, second_down.T
    half_size = HEAD // 2
    frequency = ROPE_BASE ** (-(np.arange(half_size) * 2.0 / HEAD))
    frequency = jnp.asarray(np.tile(frequency, 4)[None], F32)
    if fast:
        qo_near, by_x, by_low = pack_first(idx, w_qkv, w_out, norm_gains, w_gate_up)
        qo_near, by_x, by_low = over_y(qo_near), over_y(by_x), over_y(by_low)
        down_near = over_y(pack_down(idx, down_t, (by_low,)))
        by_x_next, by_low_next = over_x(by_x), over_z_low(by_low)
        qo_near_low = over_z_low(qo_near)
        gains = (norm_gains, qo_near)
        (low_far,) = step(
            pass_on, [over_core(by_low_next)], [sds(by_low.shape, BF16)], "pass_on_low", (), 1
        )
        own_rows = lambda o: (o * rows, 0)
        own_rows_out = lambda o: (o * rows, QKV)
        qo_place = lambda o, c, x, low: (o * rows + c * HALF, low * ((QKV + width) // 2))
        x_place = lambda o, c, x, low: (o * rows + c * HALF, x * (FF // 2))
        low_place = lambda o, c, x, low: (o * rows + c * HALF, FF + low * (FF // 2))
        mat_qkv_out = Weight(
            (width, QKV + width),
            own=[(w_qkv, own_rows), (w_out, own_rows_out)],
            parts=[
                (qo_near, (0, 0, 0), qo_place),
                (qo_near_low, (0, 0, 1), qo_place),
                (over_core(qo_near), (1, 0, 0), qo_place),
                (over_core(qo_near_low), (1, 0, 1), qo_place),
            ],
        )
        mat_gate_up = Weight(
            (width, 2 * FF),
            own=[(w_gate_up, own_rows)],
            parts=[
                (by_x, (0, 0, 0), x_place),
                (by_x_next, (0, 1, 0), x_place),
                (over_core(by_x), (1, 0, 0), x_place),
                (over_core(by_x_next), (1, 1, 0), x_place),
                (by_low, (0, 0, 0), low_place),
                (by_low_next, (0, 0, 1), low_place),
                (over_core(by_low), (1, 0, 0), low_place),
                (low_far, (1, 0, 1), low_place),
            ],
        )
        cut_qkv_out = Pieces(lambda o, c, x, z, p: (o * 4 + c * 2 + x, z), extra=8)
        cut_gate_up = Pieces(lambda o, c, x, z, p: (o * 4 + c * 2 + p, x * 4 + z), parts=2)
        cut_down = Pieces(lambda o, c, x, z, p: (c * 4 + x * 2 + (z >> 1), o * 2 + (z & 1)))
    else:
        gains = (
            lax.all_gather(norm_gains.astype(BF16), "shard", axis=1, tiled=True).astype(F32),
        )
        mat_qkv, mat_out, mat_gate_up, mat_down = [
            lax.all_gather(m.astype(BF16), "shard", axis=0, tiled=True)
            for m in (w_qkv, w_out, w_gate_up, w_down)
        ]
        mat_qkv_out, mat_gate_up, mat_down = [
            Weight(m.shape, whole=m)
            for m in (jnp.concatenate([mat_qkv, mat_out], axis=1), mat_gate_up, mat_down.T)
        ]
        cut_qkv_out = cut_gate_up = cut_down = None

    qkv, attended, *tables, gains, whole = attention_forward(
        idx, x_t, segments, frequency, gains, mat_qkv_out
    ) + (() if fast else (None,))
    if fast:
        mat_qkv_out = Weight(whole.shape, whole=whole)
    middle, normed_low, ab, hidden, *grad_down = feed_forward(
        idx, x_t, attended, gains, y_t, mat_qkv_out, mat_gate_up, cut_down, ()
    )
    after = ()
    if fast:
        whole = grad_down.pop()
        mat_gate_up = Weight(whole.shape, whole=whole)

        (down_near,) = step(
            pass_on, [down_near], [sds(down_near.shape, BF16)], "pass_on", (attended,), 0.1
        )
        down_place = lambda o, c, x, low: (c * 2 * HALF, o * down_rows)
        mat_down = Weight(
            (width, FF),
            own=[(down_t, lambda o: (0, o * down_rows))],
            parts=[
                (down_near, (0, 0, 0), down_place),
                (over_core(down_near), (1, 0, 0), down_place),
            ],
        )
    if fast:
        arrived_down = over_core(grad_down[0])
    gated, *grad_gate_up = feed_back(idx, ab, normed_low, y_t, mat_down, cut_gate_up)
    if not fast:
        output = layer_output(middle, hidden, mat_down.arrays[0], ())
    if fast:
        down_whole = grad_gate_up.pop()
        cut = lambda a, *lead: a.reshape(*lead, *a.shape[-2:])
        arrived_gate_up = over_core(grad_gate_up[0])
        ((send, keep_down),) = add_step(
            [(grad_down[1][0], arrived_down[0], 0)], "down_core", (gated,)
        )
        arrived_down = over_y(send)
        after = (keep_down,)
    grad_middle, grad_attended, gain_two = middle_back(
        idx, y_t, middle, gated, gains, mat_gate_up, mat_qkv_out, after
    )
    if fast:
        halves = [
            [cut(a[p], *lead) for a in (grad_gate_up[1], arrived_gate_up)]
            for p, lead in ((0, (2, 2, 4)), (1, (4, 2, 2)))
        ]
        (send_up, keep_up), (send_low, keep_low) = add_step(
            [(*halves[0], 1), (*halves[1], 1)], "gate_up_core", (grad_middle,)
        )
        arrived_up, arrived_low = over_x(send_up), over_z_low(send_low)
        after = (keep_up,)
    token_grad, *grad_qkv_out = attention_back(
        idx,
        x_t,
        grad_middle,
        grad_attended,
        gain_two,
        qkv,
        attended,
        tables,
        gains,
        mat_qkv_out,
        cut_qkv_out,
        after,
    )
    if fast:

        arrived_qkv_out = over_core(grad_qkv_out[0])
        piece = (CUT_ROWS, CUT_COLUMNS)
        taller = (CUT_ROWS + 8, CUT_COLUMNS)
        ((send, keep_down),) = add_step(
            [(cut(keep_down, 2, 4), cut(arrived_down, 2, 4), 0)], "down_y", (grad_qkv_out[2],)
        )
        arrived_down = over_x(send)
        (send_up, keep_up), (send_low, keep_low) = add_step(
            [
                (cut(keep_up, 2, 2, 2), cut(arrived_up, 2, 2, 2), 1),
                (cut(keep_low, 2, 2, 2), cut(arrived_low, 2, 2, 2), 1),
            ],
            "up_x_low_z",
            (keep_down,),
        )
        arrived_up, arrived_low = over_z_low(send_up), over_x(send_low)
        ((send, keep_qkv_out),) = add_step(
            [(grad_qkv_out[1][0], arrived_qkv_out[0], 0)], "qkv_out_core", (keep_up,)
        )
        arrived_qkv_out = over_y(send)
        ((send, keep_down),) = add_step(
            [(cut(keep_down, 2, 2), cut(arrived_down, 2, 2), 0)], "down_x", (keep_qkv_out,)
        )
        arrived_down = over_z_low(send)

        def columns(ins, outs):
            total = ins[0][...] + ins[1][...].astype(F32)
            outs[0][...] = total[1].astype(BF16)
            outs[1][...] = total[0]
            total = ins[2][...] + ins[3][...].astype(F32)
            outs[2][0], outs[2][1] = total[0, 1].astype(BF16), total[1, 1].astype(BF16)
            outs[3][...] = total[:, 0]
            total = ins[4][...] + ins[5][...].astype(F32)
            outs[4][...] = total[1].astype(BF16)
            outs[5][...] = total[0]
            total = ins[6][...] + ins[7][...].astype(F32)
            outs[2][2] = total[1].astype(BF16)
            outs[6][...] = total[0]

        send_up, keep_up, send, keep_low, send_qkv_out, keep_qkv_out, keep_down = step(
            columns,
            [
                *(keep_up, arrived_up, keep_low, arrived_low),
                *(cut(keep_qkv_out, 2, 4), cut(arrived_qkv_out, 2, 4)),
                *(keep_down, arrived_down),
            ],
            [
                *(sds((2, *piece), BF16), sds((2, *piece), F32)),
                *(sds((3, *piece), BF16), sds((2, *piece), F32)),
                *(sds((4, *taller), BF16), sds((4, *taller), F32)),
                sds(piece, F32),
            ],
            "columns",
        )
        arrived_up, arrived_qkv_out = over_y(send_up), over_x(send_qkv_out)
        arrived = over_z_high(send)

        def planes(ins, outs):
            keep_up, arrived_up, keep_low, arrived, keep_down, keep_qkv_out, arrived_qkv_out = ins
            total = keep_up[...] + arrived_up[...].astype(F32)
            outs[0][0] = total[1].astype(BF16)
            outs[1][0] = total[0]
            outs[0][1] = (keep_down[...] + arrived[2].astype(F32)).astype(BF16)
            outs[2][...] = (keep_low[1] + arrived[1].astype(F32)).astype(BF16)
            outs[1][1] = keep_low[0] + arrived[0].astype(F32)
            total = keep_qkv_out[...] + arrived_qkv_out[...].astype(F32)
            outs[3][...] = total[1].astype(BF16)
            outs[4][...] = total[0]

        send, keep, send_low, send_qkv_out, keep_qkv_out = step(
            planes,
            [
                *(keep_up, arrived_up, keep_low, arrived, keep_down),
                *(cut(keep_qkv_out, 2, 2), cut(arrived_qkv_out, 2, 2)),
            ],
            [
                *(sds((2, *piece), BF16), sds((2, *piece), F32), sds(piece, BF16)),
                *(sds((2, *taller), BF16), sds((2, *taller), F32)),
            ],
            "planes",
        )
        arrived, arrived_low = over_z_high(send), over_y(send_low)
        arrived_qkv_out = over_z_low(send_qkv_out)

        def lines(ins, outs):
            send, keep, arrived, arrived_low, keep_qkv_out, arrived_qkv_out = ins
            total = keep_qkv_out[...] + arrived_qkv_out[...].astype(F32)
            outs[0][0] = total[1].astype(BF16)
            outs[1][...] = total[0]
            for part, came in enumerate((arrived[0], arrived_low[...])):
                total = keep[part] + came.astype(F32)
                total = jnp.concatenate([total, jnp.zeros((8, CUT_COLUMNS), F32)], axis=0)
                outs[0][part + 1] = total.astype(BF16)
            outs[2][0], outs[2][1] = send[1], arrived[1]

        pieces, keep_qkv_out, near_down = step(
            lines,
            [send, keep, arrived, arrived_low, keep_qkv_out, arrived_qkv_out],
            [sds((3, *taller), BF16), sds(taller, F32), sds((2, *piece), BF16)],
            "lines",
        )
        arrived, down_low = over_z_high(pieces), over_z_low(near_down)

        def share_high(ins, outs):
            pieces, arrived, keep_qkv_out, near_down, down_low = ins
            for high in range(2):
                outs[0][0, high], outs[0][1, high] = near_down[high], down_low[high]
            outs[0][2, 0], outs[0][2, 1] = pieces[1, :CUT_ROWS], arrived[1, :CUT_ROWS]
            outs[1][0], outs[1][1] = pieces[2, :CUT_ROWS], arrived[2, :CUT_ROWS]
            outs[2][...] = (keep_qkv_out[...] + arrived[0].astype(F32)).astype(BF16)

        near_x, near_low, piece_qkv_out = step(
            share_high,
            [pieces, arrived, keep_qkv_out, near_down, down_low],
            [sds((3, 2, *piece), BF16), sds((2, *piece), BF16), sds(taller, BF16)],
            "share_high",
        )
        arrived_x, low_low = over_x(near_x), over_z_low(near_low)
        qkv_out_high = over_z_high(piece_qkv_out)
        output = layer_output(middle, hidden, down_whole, (near_x,))

        def share_next(ins, outs):
            near_x, arrived_x, near_low, low_low = ins
            outs[0][0], outs[0][1] = near_x[2], arrived_x[2]
            outs[1][0], outs[1][1] = near_low[...], low_low[...]
            for low in range(2):
                for high in range(2):
                    outs[2][0, 0, low * 2 + high] = near_x[low, high]
                    outs[2][0, 1, low * 2 + high] = arrived_x[low, high]

        near_up, near_low, near_down = step(
            share_next,
            [near_x, arrived_x, near_low, low_low],
            [
                *(sds((2, 2, *piece), BF16), sds((2, 2, *piece), BF16)),
                sds((1, 2, 4, *piece), BF16),
            ],
            "share_next",
            (qkv_out_high,),
        )
        far_down = over_core(near_down)
        up_low, low_x = over_z_low(near_up), over_x(near_low)

        def share_qkv_out_high(ins, outs):
            outs[0][0], outs[0][1] = ins[0][...], ins[1][...]

        (near_qkv_out,) = step(
            share_qkv_out_high,
            [piece_qkv_out, qkv_out_high],
            [sds((2, *taller), BF16)],
            "share_qkv_out_high",
            (near_up,),
        )
        qkv_out_x, qkv_out_low = over_x(near_qkv_out), over_z_low(near_qkv_out)
        qkv_out_both = swap(near_qkv_out, "dp", 6)
        one_down, two_down, next_down, mark = update_rows(
            idx,
            [(0, near_down), (1, far_down)],
            lambda p, x, z: (
                (x * 2 + (z >> 1)) * CUT_ROWS,
                [(0, CUT_COLUMNS, (z & 1) * CUT_COLUMNS)],
            ),
            2 * HALF,
            96,
            [down_t, first_down_t, second_down_t],
            (),
            (),
            "update_down",
            (near_qkv_out,),
            0.1,
        )

        def share_gate_up(ins, outs):
            for near in range(2):
                for far in range(2):
                    for high in range(2):
                        outs[0][0, near, far * 2 + high] = ins[far][near, high]
                        outs[0][1, far, near * 2 + high] = ins[2 + far][near, high]

        (near_gate_up,) = step(
            share_gate_up,
            [near_up, up_low, near_low, low_x],
            [sds((2, 2, 4, *piece), BF16)],
            "share_gate_up",
            (mark,),
        )
        far_gate_up = over_core(near_gate_up)
        place_gate_up = lambda p, x, z: (p * CUT_ROWS, [(0, CUT_COLUMNS, (x * 4 + z) * CUT_COLUMNS)])
        state_gate_up = [w_gate_up, first_gate_up, second_gate_up]
        *near_state, mark = update_rows(
            idx,
            [(0, near_gate_up)],
            place_gate_up,
            HALF,
            24,
            state_gate_up,
            (),
            (),
            "update_gate_up_near",
            (),
        )

        def share_qkv_out(ins, outs):
            for x in range(2):
                for low in range(2):
                    for high in range(2):
                        outs[0][0, x, low * 2 + high] = ins[low * 2 + x][high]

        (near_qkv_out,) = step(
            share_qkv_out,
            [near_qkv_out, qkv_out_x, qkv_out_low, qkv_out_both],
            [sds((1, 2, 4, *taller), BF16)],
            "share_qkv_out",
            (mark,),
        )
        far_qkv_out = over_core(near_qkv_out)
        one_gate_up, two_gate_up, next_gate_up, mark = update_rows(
            idx,
            [(1, far_gate_up)],
            place_gate_up,
            HALF,
            24,
            state_gate_up,
            near_state,
            (),
            "update_gate_up_far",
            (near_qkv_out,),
        )
        cuts = [[(0, 384, 0)], [(0, 384, 384)], [(0, 192, 768), (192, 192, 1024)], [(0, 384, 1216)]]
        updated = update_rows(
            idx,
            [(0, near_qkv_out), (1, far_qkv_out)],
            lambda p, x, z: (x * CUT_ROWS, cuts[z]),
            HALF,
            48,
            [w_qkv, w_out, first_qkv, first_out, second_qkv, second_out],
            (),
            (norm_gains, first_gains, second_gains),
            "update_qkv_out",
            (mark,),
        )
        one_qkv, one_out, two_qkv, two_out, next_qkv, next_out = updated[:6]
        one_gains, two_gains, next_gains = updated[6:9]
    else:
        sums = lax.psum((*grad_qkv_out, grad_gate_up[0], grad_down[0].T), ("dp", "shard"))
        grad_qkv_out, grad_gains, grad_gate_up, grad_down = sums

        def own(grad, axis=0):
            size = grad.shape[axis] // groups
            return lax.dynamic_slice_in_dim(grad, owner * size, size, axis)

        one_qkv, two_qkv, next_qkv = adamw(
            w_qkv, first_qkv, second_qkv, own(grad_qkv_out[:, :QKV]), RATE_MATRIX, DECAY_MATRIX
        )
        one_out, two_out, next_out = adamw(
            w_out, first_out, second_out, own(grad_qkv_out[:, QKV:]), RATE_MATRIX, DECAY_MATRIX
        )
        one_gate_up, two_gate_up, next_gate_up = adamw(
            w_gate_up, first_gate_up, second_gate_up, own(grad_gate_up), RATE_MATRIX, DECAY_MATRIX
        )
        one_down, two_down, next_down = [
            a.T
            for a in adamw(
                w_down, first_down, second_down, own(grad_down), RATE_MATRIX, DECAY_MATRIX
            )
        ]
        one_gains, two_gains, next_gains = adamw(
            norm_gains, first_gains, second_gains, own(grad_gains, 1), RATE_GAIN, 0.0
        )
    one_down, two_down, next_down = one_down.T, two_down.T, next_down.T
    return (
        output.T[None],
        token_grad.T[None],
        one_qkv,
        one_out,
        one_gate_up,
        one_down,
        one_gains,
        two_qkv,
        two_out,
        two_gate_up,
        two_down,
        two_gains,
        next_qkv,
        next_out,
        next_gate_up,
        next_down,
        next_gains,
    )


def solution(mesh):
    return jax.shard_map(
        per_device,
        mesh=mesh,
        in_specs=(
            P(("dp", "shard"), None, None),
            P(("dp", "shard"), None),
            P(("dp", "shard"), None, None),
            P("shard", None),
            P("shard", None),
            P("shard", None),
            P("shard", None),
            P(None, "shard"),
            P("shard", None),
            P("shard", None),
            P("shard", None),
            P("shard", None),
            P(None, "shard"),
            P("shard", None),
            P("shard", None),
            P("shard", None),
            P("shard", None),
            P(None, "shard"),
        ),
        out_specs=(
            P(("dp", "shard"), None, None),
            P(("dp", "shard"), None, None),
            P("shard", None),
            P("shard", None),
            P("shard", None),
            P("shard", None),
            P(None, "shard"),
            P("shard", None),
            P("shard", None),
            P("shard", None),
            P("shard", None),
            P(None, "shard"),
            P("shard", None),
            P("shard", None),
            P("shard", None),
            P("shard", None),
            P(None, "shard"),
        ),
        check_vma=False,
    )
```

```python
import functools

import jax
import jax.numpy as jnp
import numpy as np
from jax import lax
from jax.experimental import pallas as pl
from jax.experimental.pallas import tpu as pltpu
from jax.sharding import PartitionSpec as P

HEADS = 9
KV_HEADS = 3
GROUP = HEADS // KV_HEADS
HEAD = 64
FF = 1536
STEP = 10
QUERY = HEADS * HEAD
ROPED = (HEADS + KV_HEADS) * HEAD
QKV = (HEADS + 2 * KV_HEADS) * HEAD
LANES = 128

EPS_NORM = 1e-05
ROPE_BASE = 100000.0
BETA_ONE = 0.9
BETA_TWO = 0.95
RATE_MATRIX = 0.1
RATE_GAIN = 0.3
DECAY_MATRIX = 0.1
EPS_ADAM = 1e-08
MASKED = -1e30
SCALE = float(HEAD) ** (-0.5)
VMEM_LIMIT = 32 * 1024 * 1024
PACK_LIMIT = 53 * 1024 * 1024
STEP_LIMIT = 14 * 1024 * 1024
UPDATE_LIMIT = 27 * 1024 * 1024
HALF = 144
CUT_ROWS = 72
MARK = (8, 128)
CUT_COLUMNS = 384
F32 = jnp.float32
BF16 = jnp.bfloat16


def rotate_block(values, cosine, signed_sine):
    lane = lax.broadcasted_iota(jnp.int32, values.shape, 1)
    swapped = jnp.where(
        lane % HEAD < HEAD // 2,
        pltpu.roll(values, LANES - HEAD // 2, 1),
        pltpu.roll(values, HEAD // 2, 1),
    )
    return values * cosine + swapped * signed_sine


def adamw(weight, first_moment, second_moment, gradient, step_rate, weight_decay):
    first_new = BETA_ONE * first_moment + (1.0 - BETA_ONE) * gradient
    second_new = BETA_TWO * second_moment + (1.0 - BETA_TWO) * gradient * gradient
    fix_one = 1.0 / (1.0 - BETA_ONE**STEP)
    fix_two = 1.0 / (1.0 - BETA_TWO**STEP)
    update = first_new * fix_one / (jnp.sqrt(second_new * fix_two) + EPS_ADAM)
    return (first_new, second_new, weight - step_rate * (update + weight_decay * weight))


def adamw_rows(weight, first_moment, second_moment, gradient, step_rate, weight_decay):
    first_new = BETA_ONE * first_moment + (1.0 - BETA_ONE) * gradient
    second_new = BETA_TWO * second_moment + (1.0 - BETA_TWO) * gradient * gradient
    value = second_new * (1.0 / (1.0 - BETA_TWO**STEP))
    guess = lax.rsqrt(value)
    divisor = value * guess + EPS_ADAM
    inverse = guess * (2.0 - divisor * guess)
    update = first_new * (step_rate / (1.0 - BETA_ONE**STEP)) * inverse
    return (first_new, second_new, weight * (1.0 - step_rate * weight_decay) - update)


def dot(left, right):
    return lax.dot_general(left, right, (((1,), (0,)), ((), ())), preferred_element_type=F32)


def dot_right_t(left, right):
    return lax.dot_general(left, right, (((1,), (1,)), ((), ())), preferred_element_type=F32)


def dot_left_t(left, right):
    return lax.dot_general(left, right, (((0,), (0,)), ((), ())), preferred_element_type=F32)


def norm_scale(values):
    return lax.rsqrt(jnp.mean(values * values, axis=-1, keepdims=True) + EPS_NORM)


def norm_back(grad_normed, normed, scale_rows):
    return scale_rows * (
        grad_normed - normed * jnp.mean(grad_normed * normed, axis=-1, keepdims=True)
    )


class Weight:
    def __init__(self, shape, whole=None, own=(), parts=()):
        self.shape, self.own, self.parts = shape, own, parts
        self.arrays = [whole] if whole is not None else [a[0] for a in (*own, *parts)]
        self.split = whole is None

    def load(self, idx, refs, full):
        if not self.split:
            return refs[0]
        for ref, (_, place) in zip(refs, self.own):
            self.put(full, place(idx[0]), ref[...].astype(BF16))
        for ref, (_, (core, x, low), place) in zip(refs[len(self.own) :], self.parts):
            place = place(1 - idx[0], idx[1] ^ core, idx[2] ^ x, (idx[3] & 1) ^ low)
            rows = ref.shape[0] // HALF * HALF
            self.put(full, place, ref[:rows, :])
        return full

    def put(self, full, position, value):
        where = []
        for axis, tile in ((0, 16), (1, LANES)):
            at, size = position[axis], value.shape[axis]
            if size == self.shape[axis]:
                where.append(slice(None))
            elif isinstance(at, int):
                where.append(slice(at, at + size))
            else:
                where.append(pl.ds(pl.multiple_of(at, tile), size))
        full[tuple(where)] = value


def call(body, idx, arrays, weights, outs, scratch, busy, name, after=(), hand_on=False):
    counts = [len(w.arrays) for w in weights]
    flat = list(arrays) + [a for w in weights for a in w.arrays]
    outs = list(outs)
    split = [w for w in weights if w.split]
    hand_on = hand_on and bool(split)
    if hand_on:
        outs += [sds(split[-1].shape, BF16)]
    made = [pltpu.VMEM(w.shape, BF16) for w in (split[:-1] if hand_on else split)]

    def kernel(*refs):
        refs = list(refs)
        idx_ref = refs.pop(0)
        take = lambda n: [refs.pop(0) for _ in range(n)]
        array_refs = take(len(arrays))
        weight_refs = [take(n) for n in counts]
        take(len(after))
        out_refs = take(len(outs))
        own_scratch = take(len(scratch))
        fulls = take(len(made)) + ([out_refs.pop()] if hand_on else [])
        loads = [
            functools.partial(w.load, idx_ref, r, fulls.pop(0) if w.split else None)
            for w, r in zip(weights, weight_refs)
        ]
        body(idx_ref, array_refs, loads, out_refs, own_scratch)

    return pl.pallas_call(
        kernel,
        out_shape=tuple(outs),
        in_specs=[pl.BlockSpec(memory_space=pltpu.SMEM)]
        + [pl.BlockSpec(memory_space=pltpu.VMEM)] * len(flat)
        + [pl.BlockSpec(memory_space=pl.ANY)] * len(after),
        out_specs=tuple([pl.BlockSpec(memory_space=pltpu.VMEM)] * len(outs)),
        scratch_shapes=list(scratch) + made,
        compiler_params=pltpu.CompilerParams(vmem_limit_bytes=VMEM_LIMIT),
        cost_estimate=busy_for(busy),
        name=name,
    )(idx, *flat, *after)


def busy_for(microseconds):
    return pl.CostEstimate(flops=int(microseconds * 1e9), bytes_accessed=0, transcendentals=0)


def sds(shape, dtype):
    return jax.ShapeDtypeStruct(shape, dtype)


class Pieces:
    def __init__(self, place, parts=1, extra=0):
        self.place, self.parts, self.extra = place, parts, extra

    def outs(self):
        return [sds((self.parts, 2, 8, CUT_ROWS + self.extra, CUT_COLUMNS), BF16)] * 2

    def scratch(self, columns):
        return pltpu.VMEM((8, CUT_ROWS, columns), BF16)

    def store(self, blocks, grad, start=0):
        for i in range(8):
            rows = grad[i * CUT_ROWS : (i + 1) * CUT_ROWS].astype(BF16)
            blocks[i, :, start : start + grad.shape[1]] = rows

    def emit(self, idx, blocks, outs, under=None):
        for other_core, out in enumerate((outs[1], outs[0])):
            for part in range(self.parts):
                for owner in range(2):
                    for slot in range(8):
                        z = ((slot >> 1) & 1) | ((slot & 1) << 1)
                        block, column = self.place(
                            idx[0] ^ owner, idx[1] ^ other_core, idx[2] ^ (slot >> 2), idx[3] ^ z, part
                        )
                        columns = pl.ds(pl.multiple_of(column * CUT_COLUMNS, LANES), CUT_COLUMNS)
                        piece = blocks[block, :, columns]
                        if under is not None:
                            piece = jnp.concatenate(
                                [piece.astype(F32), under[idx[0] ^ owner]], axis=0
                            ).astype(BF16)
                        out[part, owner, slot] = piece


def head_stack(values, kv_head):
    first = kv_head * GROUP
    return jnp.concatenate(
        [values[:, (first + i) * HEAD : (first + i + 1) * HEAD] for i in range(GROUP)], axis=0
    )


def softmax_rows(query, key, allowed):
    scores = jnp.where(allowed, dot_right_t(query, key) * SCALE, MASKED)
    top = jnp.max(scores, axis=-1, keepdims=True)
    exponent = jnp.exp(scores - top)
    return exponent / jnp.sum(exponent, axis=-1, keepdims=True)


def pack_kernel(body, idx, sources, places, outs, name, after=(), limit=PACK_LIMIT):
    windows = [shape for shape, _ in places]

    def kernel(idx_ref, *refs):
        sources_in, refs = refs[: len(sources)], refs[len(sources) + len(after) :]
        out_refs, buffers, sem = refs[: len(outs)], refs[len(outs) : -1], refs[-1]
        copies = []
        for i, (source, (shape, place)) in enumerate(zip(sources_in, places)):
            where = []
            for axis, tile in ((0, 8), (1, LANES)):
                if shape[axis] == source.shape[axis]:
                    where.append(slice(None))
                else:
                    where.append(pl.ds(pl.multiple_of(place(idx_ref)[axis], tile), shape[axis]))
            copies.append(pltpu.make_async_copy(source.at[tuple(where)], buffers[i], sem.at[i]))
        for copy in copies:
            copy.start()
        for copy in copies:
            copy.wait()
        body(idx_ref, buffers, out_refs)

    return pl.pallas_call(
        kernel,
        out_shape=tuple(outs),
        in_specs=[pl.BlockSpec(memory_space=pltpu.SMEM)]
        + [pl.BlockSpec(memory_space=pltpu.HBM)] * len(sources)
        + [pl.BlockSpec(memory_space=pl.ANY)] * len(after),
        out_specs=tuple([pl.BlockSpec(memory_space=pltpu.VMEM)] * len(outs)),
        scratch_shapes=[pltpu.VMEM(w, F32) for w in windows]
        + [pltpu.SemaphoreType.DMA((len(sources),))],
        compiler_params=pltpu.CompilerParams(vmem_limit_bytes=limit),
        cost_estimate=busy_for(10),
        name=name,
    )(idx, *sources, *after)


def cast_out(idx_ref, buffers, outs):
    for buffer, out in zip(buffers, outs):
        out[...] = buffer[...].astype(BF16)


def pack_down(idx, down_t, after):
    shape = (2 * HALF, down_t.shape[1])
    window = (shape, lambda i: (i[1] * 2 * HALF, 0))
    outs = [sds(shape, BF16)]
    return pack_kernel(
        cast_out, idx, [down_t], [window], outs, "pack_down", after, STEP_LIMIT
    )[0]


def pack_first(idx, w_qkv, w_out, norm_gains, w_gate_up):
    columns = (QKV + w_out.shape[1]) // 2
    quarter = FF // 2
    windows = [((HALF, m.shape[1]), lambda i: (i[1] * HALF, 0)) for m in (w_qkv, w_out)]
    windows.append((norm_gains.shape, lambda i: (0, 0)))
    windows.append(((HALF, quarter), lambda i: (i[1] * HALF, i[2] * quarter)))
    windows.append(((HALF, quarter), lambda i: (i[1] * HALF, FF + (i[3] & 1) * quarter)))

    def body(idx_ref, buffers, outs):
        q_ref, o_ref, gains_ref = buffers[:3]
        both = jnp.concatenate([q_ref[:, columns:], o_ref[...]], axis=1)
        outs[0][:HALF, :] = jnp.where((idx_ref[3] & 1) == 0, q_ref[:, :columns], both).astype(BF16)
        outs[0][HALF:, :] = jnp.zeros((16, columns), BF16)
        outs[0][HALF : HALF + 2, : gains_ref.shape[1]] = gains_ref[...].astype(BF16)
        cast_out(idx_ref, buffers[3:], outs[1:])

    outs = [sds((HALF + 16, columns), BF16)] + [sds((HALF, quarter), BF16)] * 2
    sources = [w_qkv, w_out, norm_gains, w_gate_up, w_gate_up]
    return pack_kernel(body, idx, sources, windows, outs, "pack_first")


def attention_forward(idx, tokens_t, segments, frequency, gains, w_qkv_out):
    width, seq_length = tokens_t.shape
    split_gains = len(gains) > 1

    def body(idx_ref, arrays, loads, outs, scratch):
        x_ref, seg_ref, freq_ref = arrays[:3]
        qkv_ref, o_ref, cos_ref, sin_ref, allowed_ref, gains_ref = outs
        if split_gains:
            own = arrays[3][...].astype(BF16).astype(F32)
            other = arrays[4][HALF : HALF + 8, : width // 2].astype(F32)[:2]
            gains_ref[...] = jnp.where(
                idx_ref[0] == 0,
                jnp.concatenate([own, other], axis=1),
                jnp.concatenate([other, own], axis=1),
            )
        else:
            gains_ref[...] = arrays[3][...]
        seen_doc = jnp.broadcast_to(seg_ref[...], (seq_length, seq_length))
        own_doc = seen_doc.T
        token = lax.broadcasted_iota(jnp.int32, (seq_length, seq_length), 0)
        seen = lax.broadcasted_iota(jnp.int32, (seq_length, seq_length), 1)
        begin = jnp.sum((seen_doc < own_doc).astype(F32), axis=-1, keepdims=True)
        angles = (token.astype(F32) - begin) * freq_ref[...]
        cosine, sine = jnp.cos(angles), jnp.sin(angles)
        sine = jnp.where(seen % HEAD < HEAD // 2, -sine, sine)
        cos_ref[...] = cosine
        sin_ref[...] = sine
        allowed = ((seen_doc == own_doc) & (token >= seen)).astype(F32)
        allowed_ref[...] = allowed
        allowed = jnp.concatenate([allowed] * GROUP, axis=0) > 0.5
        x = x_ref[...].astype(F32).T
        h1 = (x * norm_scale(x) * gains_ref[0:1, :]).astype(BF16)
        projected = dot(h1, loads[0]()[:, :QKV])
        for start in range(0, ROPED, LANES):
            block = projected[:, start : start + LANES]
            qkv_ref[:, start : start + LANES] = rotate_block(block, cosine, sine).astype(BF16)
        qkv_ref[:, ROPED:QKV] = projected[:, ROPED:QKV].astype(BF16)
        qkv = qkv_ref[...]
        for kv in range(KV_HEADS):
            key = qkv[:, QUERY + kv * HEAD : QUERY + (kv + 1) * HEAD]
            value = qkv[:, ROPED + kv * HEAD : ROPED + (kv + 1) * HEAD]
            probs = softmax_rows(head_stack(qkv, kv), key, allowed).astype(BF16)
            attended = dot(probs, value).astype(BF16)
            for i in range(GROUP):
                start = (kv * GROUP + i) * HEAD
                o_ref[:, start : start + HEAD] = attended[i * seq_length : (i + 1) * seq_length]

    square = sds((seq_length, seq_length), F32)
    outs = [sds((seq_length, QKV), BF16), sds((seq_length, QUERY), BF16)]
    outs += [square, square, square, sds((2, width), F32)]
    return call(
        body,
        idx,
        [tokens_t, segments, frequency, *gains],
        [w_qkv_out],
        outs,
        [],
        1,
        "attention",
        hand_on=True,
    )


def feed_forward(idx, tokens_t, attended, gains, cotangent_t, w_qkv_out, w_gate_up, pieces, after):
    width, seq_length = tokens_t.shape

    def body(idx_ref, arrays, loads, outs, scratch):
        x_ref, o_ref, gains_ref, y_ref = arrays
        u_ref, h2_ref, ab_ref, z_ref = outs[:4]
        u = x_ref[...].astype(F32).T + dot(o_ref[...], loads[0]()[:, QKV:])
        u_ref[...] = u
        h2 = (u * norm_scale(u) * gains_ref[1:2, :]).astype(BF16)
        h2_ref[...] = h2
        ab = dot(h2, loads[1]()[...])
        ab_ref[...] = ab
        gate, up = ab[:, :FF], ab[:, FF:]
        z = (gate * jax.nn.sigmoid(gate) * up).astype(BF16)
        z_ref[...] = z
        grad = dot(y_ref[...], z)
        if pieces is None:
            outs[4][...] = grad
        else:
            pieces.store(scratch[0], grad)
            pieces.emit(idx_ref, scratch[0], outs[4:])

    outs = [
        sds((seq_length, width), F32),
        sds((seq_length, width), BF16),
        sds((seq_length, 2 * FF), F32),
        sds((seq_length, FF), BF16),
    ]
    outs += [sds((width, FF), F32)] if pieces is None else pieces.outs()
    scratch = [] if pieces is None else [pieces.scratch(FF)]
    return call(
        body,
        idx,
        [tokens_t, attended, gains, cotangent_t],
        [w_qkv_out, w_gate_up],
        outs,
        scratch,
        5,
        "feed_forward",
        after,
        True,
    )


def feed_back(idx, ab, normed_low, cotangent_t, down_t, pieces):
    width, seq_length = cotangent_t.shape

    def body(idx_ref, arrays, loads, outs, scratch):
        ab_ref, h2_ref, y_ref = arrays
        gg_ref = outs[0]
        gate, up = ab_ref[:, :FF], ab_ref[:, FF:]
        sig = jax.nn.sigmoid(gate)
        grad_hidden = dot_left_t(y_ref[...], loads[0]()[...])
        gg_ref[:, :FF] = (grad_hidden * up * sig * (1.0 + gate * (1.0 - sig))).astype(BF16)
        gg_ref[:, FF:] = (grad_hidden * gate * sig).astype(BF16)
        grad = dot_left_t(h2_ref[...], gg_ref[...])
        if pieces is None:
            outs[1][...] = grad
        else:
            pieces.store(scratch[0], grad)
            pieces.emit(idx_ref, scratch[0], outs[1:])

    outs = [sds((seq_length, 2 * FF), BF16)]
    outs += [sds((width, 2 * FF), F32)] if pieces is None else pieces.outs()
    scratch = [] if pieces is None else [pieces.scratch(2 * FF)]
    return call(
        body,
        idx,
        [ab, normed_low, cotangent_t],
        [down_t],
        outs,
        scratch,
        20,
        "feed_back",
        hand_on=True,
    )


def layer_output(middle, hidden, down_t, after):
    seq_length, width = middle.shape

    def body(ins, outs):
        outs[0][...] = (ins[0][...] + dot_right_t(ins[1][...], ins[2][...])).T.astype(BF16)

    return step(
        body, [middle, hidden, down_t], [sds((width, seq_length), BF16)], "layer_output", after, 2
    )[0]


def middle_back(idx, cotangent_t, middle, gated, gains, w_gate_up, w_qkv_out, after):
    width, seq_length = cotangent_t.shape

    def body(idx_ref, arrays, loads, outs, scratch):
        y_ref, u_ref, gg_ref, gains_ref = arrays
        gu_ref, go_ref, gain_ref = outs
        u = u_ref[...]
        scale_two = norm_scale(u)
        normed = u * scale_two
        grad_normed = dot_right_t(gg_ref[...], loads[0]()[...])
        gain_ref[...] = jnp.sum(grad_normed * normed, axis=0, keepdims=True)
        gu = y_ref[...].astype(F32).T + norm_back(
            grad_normed * gains_ref[1:2, :], normed, scale_two
        )
        gu_ref[...] = gu
        go_ref[...] = dot_right_t(gu.astype(BF16), loads[1]()[:, QKV:]).astype(BF16)

    outs = [sds((seq_length, width), F32), sds((seq_length, width), BF16), sds((1, width), F32)]
    return call(
        body,
        idx,
        [cotangent_t, middle, gated, gains],
        [w_gate_up, w_qkv_out],
        outs,
        [],
        20,
        "middle_back",
        after,
    )


def attention_back(
    idx, tokens_t, grad_middle, grad_attended, gain_two, qkv, attended, tables, gains, w_qkv, pieces, after
):
    width, seq_length = tokens_t.shape

    def body(idx_ref, arrays, loads, outs, scratch):
        x_ref, gu_ref, go_ref, gain_two_ref, qkv_ref, o_ref = arrays[:6]
        cos_ref, sin_ref, allowed_ref, gains_ref = arrays[6:]
        grad_ref = outs[0]
        grad_proj, gp_ref, gain_rows, *blocks = scratch
        gu, go = gu_ref[...], go_ref[...]
        gu_low = gu.astype(BF16)
        grad_gain_two = gain_two_ref[...]
        allowed = jnp.concatenate([allowed_ref[...]] * GROUP, axis=0) > 0.5
        qkv_values = qkv_ref[...]
        for kv in range(KV_HEADS):
            key = qkv_values[:, QUERY + kv * HEAD : QUERY + (kv + 1) * HEAD]
            value = qkv_values[:, ROPED + kv * HEAD : ROPED + (kv + 1) * HEAD]
            query = head_stack(qkv_values, kv)
            grad_out = head_stack(go, kv)
            probs = softmax_rows(query, key, allowed)
            grad_probs = dot_right_t(grad_out, value)
            row_delta = jnp.sum(probs * grad_probs, axis=-1, keepdims=True)
            gs = (probs * (grad_probs - row_delta)).astype(BF16)
            grad_query = dot(gs, key) * SCALE
            for i in range(GROUP):
                start = (kv * GROUP + i) * HEAD
                grad_proj[:, start : start + HEAD] = grad_query[
                    i * seq_length : (i + 1) * seq_length
                ]
            start = QUERY + kv * HEAD
            grad_proj[:, start : start + HEAD] = dot_left_t(gs, query) * SCALE
            start = ROPED + kv * HEAD
            grad_proj[:, start : start + HEAD] = dot_left_t(probs.astype(BF16), grad_out)
        for start in range(0, ROPED, LANES):
            gp_ref[:, start : start + LANES] = rotate_block(
                grad_proj[:, start : start + LANES], cos_ref[...], -sin_ref[...]
            ).astype(BF16)
        gp_ref[:, ROPED:QKV] = grad_proj[:, ROPED:QKV].astype(BF16)
        x = x_ref[...].astype(F32).T
        scale_one = norm_scale(x)
        normed = x * scale_one
        h1 = (normed * gains_ref[0:1, :]).astype(BF16)
        grad_qkv = dot_left_t(h1, gp_ref[...])
        grad_out = dot_left_t(o_ref[...], gu_low)
        grad_normed = dot_right_t(gp_ref[...], loads[0]()[:, :QKV])
        grad_gain_one = jnp.sum(grad_normed * normed, axis=0, keepdims=True)
        if pieces is None:
            outs[1][:, :QKV] = grad_qkv
            outs[1][:, QKV:] = grad_out
            outs[2][0:1, :] = grad_gain_one
            outs[2][1:2, :] = grad_gain_two
        else:
            pieces.store(blocks[0], grad_qkv)
            pieces.store(blocks[0], grad_out, QKV)
            half = width // 2
            gain_rows[...] = jnp.zeros_like(gain_rows)
            for owner in range(2):
                columns = slice(owner * half, (owner + 1) * half)
                gain_rows[owner, 0:1, :half] = grad_gain_one[:, columns]
                gain_rows[owner, 1:2, :half] = grad_gain_two[:, columns]
            pieces.emit(idx_ref, blocks[0], outs[1:3], gain_rows)
            outs[3][...] = jnp.zeros_like(outs[3])
        grad_ref[...] = (
            (gu + norm_back(grad_normed * gains_ref[0:1, :], normed, scale_one)).T
        ).astype(BF16)

    outs = [sds((width, seq_length), BF16)]
    scratch = [
        pltpu.VMEM((seq_length, QKV), F32),
        pltpu.VMEM((seq_length, QKV), BF16),
        pltpu.VMEM((2, 8, CUT_COLUMNS), F32),
    ]
    if pieces is None:
        outs += [sds((width, QKV + width), F32), sds((2, width), F32)]
    else:
        outs += pieces.outs() + [sds(MARK, F32)]
        scratch += [pieces.scratch(QKV + width)]
    return call(
        body,
        idx,
        [tokens_t, grad_middle, grad_attended, gain_two, qkv, attended, *tables, gains],
        [w_qkv],
        outs,
        scratch,
        20,
        "attention_back",
        after,
    )


def step(body, arrays, outs, name, after=(), busy=20):
    def kernel(*refs):
        body(refs[: len(arrays)], refs[len(arrays) + len(after) :])

    return pl.pallas_call(
        kernel,
        out_shape=tuple(outs),
        in_specs=[pl.BlockSpec(memory_space=pltpu.VMEM)] * len(arrays)
        + [pl.BlockSpec(memory_space=pl.ANY)] * len(after),
        out_specs=tuple([pl.BlockSpec(memory_space=pltpu.VMEM)] * len(outs)),
        compiler_params=pltpu.CompilerParams(vmem_limit_bytes=STEP_LIMIT),
        cost_estimate=busy_for(busy),
        name=name,
    )(*arrays, *after)


def pass_on(ins, outs):
    outs[0][...] = ins[0][...]


def add_split(keep, arrived, axis, send_ref, keep_ref):
    total = keep[...].astype(F32) + arrived[...].astype(F32)
    low, high = lax.index_in_dim(total, 0, axis, False), lax.index_in_dim(total, 1, axis, False)
    send_ref[...] = high.astype(BF16)
    keep_ref[...] = low


def add_step(jobs, name, after, busy=20):
    arrays, outs = [], []
    for keep, arrived, axis in jobs:
        arrays += [keep, arrived]
        shape = keep.shape[:axis] + keep.shape[axis + 1 :]
        outs += [sds(shape, BF16), sds(shape, F32)]

    def body(ins, out_refs):
        for i, (_, _, axis) in enumerate(jobs):
            add_split(ins[2 * i], ins[2 * i + 1], axis, out_refs[2 * i], out_refs[2 * i + 1])

    flat = step(body, arrays, outs, name, after, busy)
    return [(flat[2 * i], flat[2 * i + 1]) for i in range(len(jobs))]


def update_rows(idx, shares, place, height, chunk, state, earlier, gains, name, after, busy=20):
    count = len(state) // 3
    columns = [a.shape[1] for a in state[:count]]
    starts = [sum(-(-c // LANES) * LANES for c in columns[:k]) for k in range(count + 1)]
    chunks = height // chunk
    order = [(k, count + k, 2 * count + k) for k in range(count)]

    def kernel(idx_ref, *refs):
        refs = list(refs)
        take = lambda n: [refs.pop(0) for _ in range(n)]
        share_refs = take(len(shares))
        state_refs, gain_refs = take(3 * count), take(len(gains))
        take(len(earlier) + len(after))
        outs, gain_outs, (mark,) = take(3 * count), take(len(gains)), take(1)
        buffers, (full, sem) = take(3 * count), refs
        mark[...] = jnp.zeros_like(mark)
        copies = []
        for share, (far, _) in enumerate(shares):
            piece_ref = share_refs[share]
            for part in range(piece_ref.shape[0]):
                for x in range(2):
                    for z in range(4):
                        rel = z ^ idx_ref[3]
                        slot = ((rel & 1) << 1) | (rel >> 1)
                        piece = piece_ref[part, x, slot].astype(F32)[:CUT_ROWS]
                        row, cuts = place(part, idx_ref[2] ^ x, z)
                        rows = pl.ds(pl.multiple_of(share * height + row, 8), CUT_ROWS)
                        for begin, size, to in cuts:
                            if isinstance(to, int):
                                where = slice(to, to + size)
                            else:
                                where = pl.ds(pl.multiple_of(to, LANES), size)
                            full[rows, where] = piece[:, begin : begin + size]
            base = (idx_ref[1] ^ far) * height
            for at_chunk in range(chunks):

                def eight_rows(i, carry, at_chunk=at_chunk, share=share, base=base):
                    at_row = at_chunk * chunk + i * 8
                    near_rows = pl.ds(pl.multiple_of(share * height + at_row, 8), 8)
                    rows = pl.ds(pl.multiple_of(base + at_row, 8), 8)
                    for k in range(count):
                        for at in range(0, columns[k], 768):
                            size = min(768, columns[k] - at)
                            where = slice(at, at + size)
                            results = adamw_rows(
                                *[state_refs[j][rows, where] for j in order[k]],
                                full[near_rows, starts[k] + at : starts[k] + at + size],
                                RATE_MATRIX,
                                DECAY_MATRIX,
                            )
                            for j, result in zip(order[k], results):
                                buffers[j][near_rows, where] = result
                    return carry

                lax.fori_loop(0, chunk // 8, eight_rows, 0, unroll=3)
                near_rows = pl.ds(share * height + at_chunk * chunk, chunk)
                rows = pl.ds(pl.multiple_of(base + at_chunk * chunk, 8), chunk)
                for j in range(3 * count):
                    copy = pltpu.make_async_copy(
                        buffers[j].at[near_rows],
                        outs[j].at[rows],
                        sem.at[share * chunks + at_chunk, j],
                    )
                    copy.start()
                    copies.append(copy)
        if gains:
            gradient = share_refs[0][0, 0, 0, CUT_ROWS:, :].astype(F32)[:2, : gains[0].shape[1]]
            results = adamw_rows(*[g[...] for g in gain_refs], gradient, RATE_GAIN, 0.0)
            for out, result in zip(gain_outs, results):
                out[...] = result
        for copy in copies:
            copy.wait()

    vmem, anywhere = pl.BlockSpec(memory_space=pltpu.VMEM), pl.BlockSpec(memory_space=pl.ANY)
    first_earlier = 1 + len(shares) + 3 * count + len(gains)
    total = len(shares) * height
    return pl.pallas_call(
        kernel,
        out_shape=tuple(sds(a.shape, F32) for a in [*state, *gains]) + (sds(MARK, F32),),
        in_specs=[pl.BlockSpec(memory_space=pltpu.SMEM)]
        + [vmem] * (len(shares) + 3 * count + len(gains))
        + [anywhere] * (len(earlier) + len(after)),
        out_specs=tuple([anywhere] * (3 * count) + [vmem] * (len(gains) + 1)),
        scratch_shapes=[pltpu.VMEM((total, a.shape[1]), F32) for a in state]
        + [pltpu.VMEM((total, starts[-1]), F32)]
        + [pltpu.SemaphoreType.DMA((len(shares) * chunks, 3 * count))],
        input_output_aliases={first_earlier + i: i for i in range(len(earlier))},
        compiler_params=pltpu.CompilerParams(vmem_limit_bytes=UPDATE_LIMIT),
        cost_estimate=busy_for(busy),
        name=name,
    )(idx, *[p for _, p in shares], *state, *gains, *earlier, *after)


def swap(values, axis, mask):
    size = lax.axis_size(axis)
    return lax.ppermute(values, axis, [(i, i ^ mask) for i in range(size)])


over_y = functools.partial(swap, axis="shard", mask=1)
over_core = functools.partial(swap, axis="dp", mask=1)
over_x = functools.partial(swap, axis="dp", mask=2)
over_z_low = functools.partial(swap, axis="dp", mask=4)
over_z_high = functools.partial(swap, axis="dp", mask=8)


def per_device(
    tokens,
    segments,
    cotangent,
    w_qkv,
    w_out,
    w_gate_up,
    w_down,
    norm_gains,
    first_qkv,
    first_out,
    first_gate_up,
    first_down,
    first_gains,
    second_qkv,
    second_out,
    second_gate_up,
    second_down,
    second_gains,
):
    groups = lax.axis_size("shard")
    replicas = lax.axis_size("dp")
    fast = groups == 2 and replicas == 16
    place_dp = lax.axis_index("dp")
    owner = lax.axis_index("shard")
    idx = jnp.stack([owner, place_dp & 1, (place_dp >> 1) & 1, place_dp >> 2]).astype(jnp.int32)
    x_t, y_t = tokens[0].T, cotangent[0].T
    width, seq_length = x_t.shape
    rows, down_rows = w_qkv.shape[0], w_down.shape[0]
    down_t, first_down_t, second_down_t = w_down.T, first_down.T, second_down.T
    half_size = HEAD // 2
    frequency = ROPE_BASE ** (-(np.arange(half_size) * 2.0 / HEAD))
    frequency = jnp.asarray(np.tile(frequency, 4)[None], F32)
    if fast:
        qo_near, by_x, by_low = pack_first(idx, w_qkv, w_out, norm_gains, w_gate_up)
        qo_near, by_x, by_low = over_y(qo_near), over_y(by_x), over_y(by_low)
        down_near = over_y(pack_down(idx, down_t, (by_low,)))
        by_x_next, by_low_next = over_x(by_x), over_z_low(by_low)
        qo_near_low = over_z_low(qo_near)
        gains = (norm_gains, qo_near)
        (low_far,) = step(
            pass_on, [over_core(by_low_next)], [sds(by_low.shape, BF16)], "pass_on_low", (), 1
        )
        own_rows = lambda o: (o * rows, 0)
        own_rows_out = lambda o: (o * rows, QKV)
        qo_place = lambda o, c, x, low: (o * rows + c * HALF, low * ((QKV + width) // 2))
        x_place = lambda o, c, x, low: (o * rows + c * HALF, x * (FF // 2))
        low_place = lambda o, c, x, low: (o * rows + c * HALF, FF + low * (FF // 2))
        mat_qkv_out = Weight(
            (width, QKV + width),
            own=[(w_qkv, own_rows), (w_out, own_rows_out)],
            parts=[
                (qo_near, (0, 0, 0), qo_place),
                (qo_near_low, (0, 0, 1), qo_place),
                (over_core(qo_near), (1, 0, 0), qo_place),
                (over_core(qo_near_low), (1, 0, 1), qo_place),
            ],
        )
        mat_gate_up = Weight(
            (width, 2 * FF),
            own=[(w_gate_up, own_rows)],
            parts=[
                (by_x, (0, 0, 0), x_place),
                (by_x_next, (0, 1, 0), x_place),
                (over_core(by_x), (1, 0, 0), x_place),
                (over_core(by_x_next), (1, 1, 0), x_place),
                (by_low, (0, 0, 0), low_place),
                (by_low_next, (0, 0, 1), low_place),
                (over_core(by_low), (1, 0, 0), low_place),
                (low_far, (1, 0, 1), low_place),
            ],
        )
        cut_qkv_out = Pieces(lambda o, c, x, z, p: (o * 4 + c * 2 + x, z), extra=8)
        cut_gate_up = Pieces(lambda o, c, x, z, p: (o * 4 + c * 2 + p, x * 4 + z), parts=2)
        cut_down = Pieces(lambda o, c, x, z, p: (c * 4 + x * 2 + (z >> 1), o * 2 + (z & 1)))
    else:
        gains = (
            lax.all_gather(norm_gains.astype(BF16), "shard", axis=1, tiled=True).astype(F32),
        )
        mat_qkv, mat_out, mat_gate_up, mat_down = [
            lax.all_gather(m.astype(BF16), "shard", axis=0, tiled=True)
            for m in (w_qkv, w_out, w_gate_up, w_down)
        ]
        mat_qkv_out, mat_gate_up, mat_down = [
            Weight(m.shape, whole=m)
            for m in (jnp.concatenate([mat_qkv, mat_out], axis=1), mat_gate_up, mat_down.T)
        ]
        cut_qkv_out = cut_gate_up = cut_down = None

    qkv, attended, *tables, gains, whole = attention_forward(
        idx, x_t, segments, frequency, gains, mat_qkv_out
    ) + (() if fast else (None,))
    if fast:
        mat_qkv_out = Weight(whole.shape, whole=whole)
    middle, normed_low, ab, hidden, *grad_down = feed_forward(
        idx, x_t, attended, gains, y_t, mat_qkv_out, mat_gate_up, cut_down, ()
    )
    after = ()
    if fast:
        whole = grad_down.pop()
        mat_gate_up = Weight(whole.shape, whole=whole)

        (down_near,) = step(
            pass_on, [down_near], [sds(down_near.shape, BF16)], "pass_on", (attended,), 0.1
        )
        down_place = lambda o, c, x, low: (c * 2 * HALF, o * down_rows)
        mat_down = Weight(
            (width, FF),
            own=[(down_t, lambda o: (0, o * down_rows))],
            parts=[
                (down_near, (0, 0, 0), down_place),
                (over_core(down_near), (1, 0, 0), down_place),
            ],
        )
    if fast:
        arrived_down = over_core(grad_down[0])
    gated, *grad_gate_up = feed_back(idx, ab, normed_low, y_t, mat_down, cut_gate_up)
    if not fast:
        output = layer_output(middle, hidden, mat_down.arrays[0], ())
    if fast:
        down_whole = grad_gate_up.pop()
        cut = lambda a, *lead: a.reshape(*lead, *a.shape[-2:])
        arrived_gate_up = over_core(grad_gate_up[0])
        ((send, keep_down),) = add_step(
            [(grad_down[1][0], arrived_down[0], 0)], "down_core", (gated,)
        )
        arrived_down = over_y(send)
        after = (keep_down,)
    grad_middle, grad_attended, gain_two = middle_back(
        idx, y_t, middle, gated, gains, mat_gate_up, mat_qkv_out, after
    )
    if fast:
        halves = [
            [cut(a[p], *lead) for a in (grad_gate_up[1], arrived_gate_up)]
            for p, lead in ((0, (2, 2, 4)), (1, (4, 2, 2)))
        ]
        (send_up, keep_up), (send_low, keep_low) = add_step(
            [(*halves[0], 1), (*halves[1], 1)], "gate_up_core", (grad_middle,)
        )
        arrived_up, arrived_low = over_x(send_up), over_z_low(send_low)
        after = (keep_up,)
    token_grad, *grad_qkv_out = attention_back(
        idx,
        x_t,
        grad_middle,
        grad_attended,
        gain_two,
        qkv,
        attended,
        tables,
        gains,
        mat_qkv_out,
        cut_qkv_out,
        after,
    )
    if fast:

        arrived_qkv_out = over_core(grad_qkv_out[0])
        piece = (CUT_ROWS, CUT_COLUMNS)
        taller = (CUT_ROWS + 8, CUT_COLUMNS)
        ((send, keep_down),) = add_step(
            [(cut(keep_down, 2, 4), cut(arrived_down, 2, 4), 0)], "down_y", (grad_qkv_out[2],)
        )
        arrived_down = over_x(send)
        ((send, keep_qkv_out),) = add_step(
            [(grad_qkv_out[1][0], arrived_qkv_out[0], 0)], "qkv_out_core", (keep_down,), 0.1
        )
        arrived_qkv_out = over_y(send)
        (send_up, keep_up), (send_low, keep_low) = add_step(
            [
                (cut(keep_up, 2, 2, 2), cut(arrived_up, 2, 2, 2), 1),
                (cut(keep_low, 2, 2, 2), cut(arrived_low, 2, 2, 2), 1),
            ],
            "up_x_low_z",
            (keep_qkv_out,),
        )
        arrived_up, arrived_low = over_z_low(send_up), over_x(send_low)
        ((send, keep_down),) = add_step(
            [(cut(keep_down, 2, 2), cut(arrived_down, 2, 2), 0)], "down_x", (keep_up,)
        )
        arrived_down = over_z_low(send)

        def columns(ins, outs):
            total = ins[0][...] + ins[1][...].astype(F32)
            outs[0][...] = total[1].astype(BF16)
            outs[1][...] = total[0]
            total = ins[2][...] + ins[3][...].astype(F32)
            outs[2][0], outs[2][1] = total[0, 1].astype(BF16), total[1, 1].astype(BF16)
            outs[3][...] = total[:, 0]
            total = ins[4][...] + ins[5][...].astype(F32)
            outs[4][...] = total[1].astype(BF16)
            outs[5][...] = total[0]
            total = ins[6][...] + ins[7][...].astype(F32)
            outs[2][2] = total[1].astype(BF16)
            outs[6][...] = total[0]

        send_up, keep_up, send, keep_low, send_qkv_out, keep_qkv_out, keep_down = step(
            columns,
            [
                *(keep_up, arrived_up, keep_low, arrived_low),
                *(cut(keep_qkv_out, 2, 4), cut(arrived_qkv_out, 2, 4)),
                *(keep_down, arrived_down),
            ],
            [
                *(sds((2, *piece), BF16), sds((2, *piece), F32)),
                *(sds((3, *piece), BF16), sds((2, *piece), F32)),
                *(sds((4, *taller), BF16), sds((4, *taller), F32)),
                sds(piece, F32),
            ],
            "columns",
        )
        arrived_up, arrived_qkv_out = over_y(send_up), over_x(send_qkv_out)
        arrived = over_z_high(send)

        def planes(ins, outs):
            keep_up, arrived_up, keep_low, arrived, keep_down, keep_qkv_out, arrived_qkv_out = ins
            total = keep_up[...] + arrived_up[...].astype(F32)
            outs[0][0] = total[1].astype(BF16)
            outs[1][0] = total[0]
            outs[0][1] = (keep_down[...] + arrived[2].astype(F32)).astype(BF16)
            outs[2][...] = (keep_low[1] + arrived[1].astype(F32)).astype(BF16)
            outs[1][1] = keep_low[0] + arrived[0].astype(F32)
            total = keep_qkv_out[...] + arrived_qkv_out[...].astype(F32)
            outs[3][...] = total[1].astype(BF16)
            outs[4][...] = total[0]

        send, keep, send_low, send_qkv_out, keep_qkv_out = step(
            planes,
            [
                *(keep_up, arrived_up, keep_low, arrived, keep_down),
                *(cut(keep_qkv_out, 2, 2), cut(arrived_qkv_out, 2, 2)),
            ],
            [
                *(sds((2, *piece), BF16), sds((2, *piece), F32), sds(piece, BF16)),
                *(sds((2, *taller), BF16), sds((2, *taller), F32)),
            ],
            "planes",
        )
        arrived, arrived_low = over_z_high(send), over_y(send_low)
        arrived_qkv_out = over_z_low(send_qkv_out)

        def lines(ins, outs):
            send, keep, arrived, arrived_low, keep_qkv_out, arrived_qkv_out = ins
            total = keep_qkv_out[...] + arrived_qkv_out[...].astype(F32)
            outs[0][0] = total[1].astype(BF16)
            outs[1][...] = total[0]
            for part, came in enumerate((arrived[0], arrived_low[...])):
                total = keep[part] + came.astype(F32)
                total = jnp.concatenate([total, jnp.zeros((8, CUT_COLUMNS), F32)], axis=0)
                outs[0][part + 1] = total.astype(BF16)
            outs[2][0], outs[2][1] = send[1], arrived[1]

        pieces, keep_qkv_out, near_down = step(
            lines,
            [send, keep, arrived, arrived_low, keep_qkv_out, arrived_qkv_out],
            [sds((3, *taller), BF16), sds(taller, F32), sds((2, *piece), BF16)],
            "lines",
        )
        arrived, down_low = over_z_high(pieces), over_z_low(near_down)

        def share_high(ins, outs):
            pieces, arrived, keep_qkv_out, near_down, down_low = ins
            outs[0][0], outs[0][1] = near_down[...], down_low[...]
            for part in range(2):
                outs[1 + part][0] = pieces[1 + part, :CUT_ROWS]
                outs[1 + part][1] = arrived[1 + part, :CUT_ROWS]
            outs[3][...] = (keep_qkv_out[...] + arrived[0].astype(F32)).astype(BF16)

        near_down, near_up, near_low, piece_qkv_out = step(
            share_high,
            [pieces, arrived, keep_qkv_out, near_down, down_low],
            [
                *(sds((2, 2, *piece), BF16), sds((2, *piece), BF16), sds((2, *piece), BF16)),
                sds(taller, BF16),
            ],
            "share_high",
        )
        up_x, low_low = over_x(near_up), over_z_low(near_low)
        qkv_out_high = over_z_high(piece_qkv_out)
        (near_down,) = step(pass_on, [near_down], [sds(near_down.shape, BF16)], "pass_down", (near_low,))
        down_x = over_x(near_down)
        output = layer_output(middle, hidden, down_whole, (near_down,))

        def share_next(ins, outs):
            for i in range(2):
                outs[i][0], outs[i][1] = ins[2 * i][...], ins[2 * i + 1][...]

        near_up, near_low = step(
            share_next,
            [near_up, up_x, near_low, low_low],
            [sds((2, 2, *piece), BF16), sds((2, 2, *piece), BF16)],
            "share_next",
            (output,),
        )
        up_low, low_x = over_z_low(near_up), over_x(near_low)

        def share_down(ins, outs):
            for x in range(2):
                for low in range(2):
                    for high in range(2):
                        outs[0][0, x, low * 2 + high] = ins[x][low, high]

        (near_down,) = step(
            share_down,
            [near_down, down_x],
            [sds((1, 2, 4, *piece), BF16)],
            "share_down",
            (near_up,),
        )
        far_down = over_core(near_down)

        def share_qkv_out_high(ins, outs):
            outs[0][0], outs[0][1] = ins[0][...], ins[1][...]

        (near_qkv_out,) = step(
            share_qkv_out_high,
            [piece_qkv_out, qkv_out_high],
            [sds((2, *taller), BF16)],
            "share_qkv_out_high",
            (near_down,),
        )
        qkv_out_x, qkv_out_low = over_x(near_qkv_out), over_z_low(near_qkv_out)
        qkv_out_both = swap(near_qkv_out, "dp", 6)

        def share_gate_up(ins, outs):
            for near in range(2):
                for far in range(2):
                    for high in range(2):
                        outs[0][0, near, far * 2 + high] = ins[far][near, high]
                        outs[0][1, far, near * 2 + high] = ins[2 + far][near, high]

        (near_gate_up,) = step(
            share_gate_up,
            [near_up, up_low, near_low, low_x],
            [sds((2, 2, 4, *piece), BF16)],
            "share_gate_up",
            (near_qkv_out,),
        )
        far_gate_up = over_core(near_gate_up)
        one_down, two_down, next_down, mark = update_rows(
            idx,
            [(0, near_down), (1, far_down)],
            lambda p, x, z: (
                (x * 2 + (z >> 1)) * CUT_ROWS,
                [(0, CUT_COLUMNS, (z & 1) * CUT_COLUMNS)],
            ),
            2 * HALF,
            96,
            [down_t, first_down_t, second_down_t],
            (),
            (),
            "update_down",
            (near_gate_up,),
        )

        def share_qkv_out(ins, outs):
            for x in range(2):
                for low in range(2):
                    for high in range(2):
                        outs[0][0, x, low * 2 + high] = ins[low * 2 + x][high]

        (near_qkv_out,) = step(
            share_qkv_out,
            [near_qkv_out, qkv_out_x, qkv_out_low, qkv_out_both],
            [sds((1, 2, 4, *taller), BF16)],
            "share_qkv_out",
            (mark,),
        )
        far_qkv_out = over_core(near_qkv_out)
        one_gate_up, two_gate_up, next_gate_up, mark = update_rows(
            idx,
            [(0, near_gate_up), (1, far_gate_up)],
            lambda p, x, z: (p * CUT_ROWS, [(0, CUT_COLUMNS, (x * 4 + z) * CUT_COLUMNS)]),
            HALF,
            24,
            [w_gate_up, first_gate_up, second_gate_up],
            (),
            (),
            "update_gate_up",
            (near_qkv_out,),
        )
        cuts = [[(0, 384, 0)], [(0, 384, 384)], [(0, 192, 768), (192, 192, 1024)], [(0, 384, 1216)]]
        updated = update_rows(
            idx,
            [(0, near_qkv_out), (1, far_qkv_out)],
            lambda p, x, z: (x * CUT_ROWS, cuts[z]),
            HALF,
            48,
            [w_qkv, w_out, first_qkv, first_out, second_qkv, second_out],
            (),
            (norm_gains, first_gains, second_gains),
            "update_qkv_out",
            (mark,),
        )
        one_qkv, one_out, two_qkv, two_out, next_qkv, next_out = updated[:6]
        one_gains, two_gains, next_gains = updated[6:9]
    else:
        sums = lax.psum((*grad_qkv_out, grad_gate_up[0], grad_down[0].T), ("dp", "shard"))
        grad_qkv_out, grad_gains, grad_gate_up, grad_down = sums

        def own(grad, axis=0):
            size = grad.shape[axis] // groups
            return lax.dynamic_slice_in_dim(grad, owner * size, size, axis)

        one_qkv, two_qkv, next_qkv = adamw(
            w_qkv, first_qkv, second_qkv, own(grad_qkv_out[:, :QKV]), RATE_MATRIX, DECAY_MATRIX
        )
        one_out, two_out, next_out = adamw(
            w_out, first_out, second_out, own(grad_qkv_out[:, QKV:]), RATE_MATRIX, DECAY_MATRIX
        )
        one_gate_up, two_gate_up, next_gate_up = adamw(
            w_gate_up, first_gate_up, second_gate_up, own(grad_gate_up), RATE_MATRIX, DECAY_MATRIX
        )
        one_down, two_down, next_down = [
            a.T
            for a in adamw(
                w_down, first_down, second_down, own(grad_down), RATE_MATRIX, DECAY_MATRIX
            )
        ]
        one_gains, two_gains, next_gains = adamw(
            norm_gains, first_gains, second_gains, own(grad_gains, 1), RATE_GAIN, 0.0
        )
    one_down, two_down, next_down = one_down.T, two_down.T, next_down.T
    return (
        output.T[None],
        token_grad.T[None],
        one_qkv,
        one_out,
        one_gate_up,
        one_down,
        one_gains,
        two_qkv,
        two_out,
        two_gate_up,
        two_down,
        two_gains,
        next_qkv,
        next_out,
        next_gate_up,
        next_down,
        next_gains,
    )


def solution(mesh):
    return jax.shard_map(
        per_device,
        mesh=mesh,
        in_specs=(
            P(("dp", "shard"), None, None),
            P(("dp", "shard"), None),
            P(("dp", "shard"), None, None),
            P("shard", None),
            P("shard", None),
            P("shard", None),
            P("shard", None),
            P(None, "shard"),
            P("shard", None),
            P("shard", None),
            P("shard", None),
            P("shard", None),
            P(None, "shard"),
            P("shard", None),
            P("shard", None),
            P("shard", None),
            P("shard", None),
            P(None, "shard"),
        ),
        out_specs=(
            P(("dp", "shard"), None, None),
            P(("dp", "shard"), None, None),
            P("shard", None),
            P("shard", None),
            P("shard", None),
            P("shard", None),
            P(None, "shard"),
            P("shard", None),
            P("shard", None),
            P("shard", None),
            P("shard", None),
            P(None, "shard"),
            P("shard", None),
            P("shard", None),
            P("shard", None),
            P("shard", None),
            P(None, "shard"),
        ),
        check_vma=False,
    )
```

```python
import functools

import jax
import jax.numpy as jnp
import numpy as np
from jax import lax
from jax.experimental import pallas as pl
from jax.experimental.pallas import tpu as pltpu
from jax.sharding import PartitionSpec as P

HEADS = 9
KV_HEADS = 3
GROUP = HEADS // KV_HEADS
HEAD = 64
FF = 1536
STEP = 10
QUERY = HEADS * HEAD
ROPED = (HEADS + KV_HEADS) * HEAD
QKV = (HEADS + 2 * KV_HEADS) * HEAD
LANES = 128

EPS_NORM = 1e-05
ROPE_BASE = 100000.0
BETA_ONE = 0.9
BETA_TWO = 0.95
RATE_MATRIX = 0.1
RATE_GAIN = 0.3
DECAY_MATRIX = 0.1
EPS_ADAM = 1e-08
MASKED = -1e30
SCALE = float(HEAD) ** (-0.5)
VMEM_LIMIT = 32 * 1024 * 1024
PACK_LIMIT = 53 * 1024 * 1024
STEP_LIMIT = 14 * 1024 * 1024
UPDATE_LIMIT = 20 * 1024 * 1024
HALF = 144
CUT_ROWS = 72
MARK = (8, 128)
CUT_COLUMNS = 384
F32 = jnp.float32
BF16 = jnp.bfloat16


def rotate_block(values, cosine, signed_sine):
    lane = lax.broadcasted_iota(jnp.int32, values.shape, 1)
    swapped = jnp.where(
        lane % HEAD < HEAD // 2,
        pltpu.roll(values, LANES - HEAD // 2, 1),
        pltpu.roll(values, HEAD // 2, 1),
    )
    return values * cosine + swapped * signed_sine


def adamw(weight, first_moment, second_moment, gradient, step_rate, weight_decay):
    first_new = BETA_ONE * first_moment + (1.0 - BETA_ONE) * gradient
    second_new = BETA_TWO * second_moment + (1.0 - BETA_TWO) * gradient * gradient
    fix_one = 1.0 / (1.0 - BETA_ONE**STEP)
    fix_two = 1.0 / (1.0 - BETA_TWO**STEP)
    update = first_new * fix_one / (jnp.sqrt(second_new * fix_two) + EPS_ADAM)
    return (first_new, second_new, weight - step_rate * (update + weight_decay * weight))


def adamw_rows(weight, first_moment, second_moment, gradient, step_rate, weight_decay):
    first_new = BETA_ONE * first_moment + (1.0 - BETA_ONE) * gradient
    second_new = BETA_TWO * second_moment + (1.0 - BETA_TWO) * gradient * gradient
    value = second_new * (1.0 / (1.0 - BETA_TWO**STEP))
    guess = lax.rsqrt(value)
    divisor = value * guess + EPS_ADAM
    inverse = guess * (2.0 - divisor * guess)
    update = first_new * (step_rate / (1.0 - BETA_ONE**STEP)) * inverse
    return (first_new, second_new, weight * (1.0 - step_rate * weight_decay) - update)


def dot(left, right):
    return lax.dot_general(left, right, (((1,), (0,)), ((), ())), preferred_element_type=F32)


def dot_right_t(left, right):
    return lax.dot_general(left, right, (((1,), (1,)), ((), ())), preferred_element_type=F32)


def dot_left_t(left, right):
    return lax.dot_general(left, right, (((0,), (0,)), ((), ())), preferred_element_type=F32)


def norm_scale(values):
    return lax.rsqrt(jnp.mean(values * values, axis=-1, keepdims=True) + EPS_NORM)


def norm_back(grad_normed, normed, scale_rows):
    return scale_rows * (
        grad_normed - normed * jnp.mean(grad_normed * normed, axis=-1, keepdims=True)
    )


class Weight:
    def __init__(self, shape, whole=None, own=(), parts=()):
        self.shape, self.own, self.parts = shape, own, parts
        self.arrays = [whole] if whole is not None else [a[0] for a in (*own, *parts)]
        self.split = whole is None

    def load(self, idx, refs, full):
        if not self.split:
            return refs[0]
        for ref, (_, place) in zip(refs, self.own):
            self.put(full, place(idx[0]), ref[...].astype(BF16))
        for ref, (_, (core, x, low), place) in zip(refs[len(self.own) :], self.parts):
            place = place(1 - idx[0], idx[1] ^ core, idx[2] ^ x, (idx[3] & 1) ^ low)
            rows = ref.shape[0] // HALF * HALF
            self.put(full, place, ref[:rows, :])
        return full

    def put(self, full, position, value):
        where = []
        for axis, tile in ((0, 16), (1, LANES)):
            at, size = position[axis], value.shape[axis]
            if size == self.shape[axis]:
                where.append(slice(None))
            elif isinstance(at, int):
                where.append(slice(at, at + size))
            else:
                where.append(pl.ds(pl.multiple_of(at, tile), size))
        full[tuple(where)] = value


def call(body, idx, arrays, weights, outs, scratch, busy, name, after=(), hand_on=False):
    counts = [len(w.arrays) for w in weights]
    flat = list(arrays) + [a for w in weights for a in w.arrays]
    outs = list(outs)
    split = [w for w in weights if w.split]
    hand_on = hand_on and bool(split)
    if hand_on:
        outs += [sds(split[-1].shape, BF16)]
    made = [pltpu.VMEM(w.shape, BF16) for w in (split[:-1] if hand_on else split)]

    def kernel(*refs):
        refs = list(refs)
        idx_ref = refs.pop(0)
        take = lambda n: [refs.pop(0) for _ in range(n)]
        array_refs = take(len(arrays))
        weight_refs = [take(n) for n in counts]
        take(len(after))
        out_refs = take(len(outs))
        own_scratch = take(len(scratch))
        fulls = take(len(made)) + ([out_refs.pop()] if hand_on else [])
        loads = [
            functools.partial(w.load, idx_ref, r, fulls.pop(0) if w.split else None)
            for w, r in zip(weights, weight_refs)
        ]
        body(idx_ref, array_refs, loads, out_refs, own_scratch)

    return pl.pallas_call(
        kernel,
        out_shape=tuple(outs),
        in_specs=[pl.BlockSpec(memory_space=pltpu.SMEM)]
        + [pl.BlockSpec(memory_space=pltpu.VMEM)] * len(flat)
        + [pl.BlockSpec(memory_space=pl.ANY)] * len(after),
        out_specs=tuple([pl.BlockSpec(memory_space=pltpu.VMEM)] * len(outs)),
        scratch_shapes=list(scratch) + made,
        compiler_params=pltpu.CompilerParams(vmem_limit_bytes=VMEM_LIMIT),
        cost_estimate=busy_for(busy),
        name=name,
    )(idx, *flat, *after)


def busy_for(microseconds):
    return pl.CostEstimate(flops=int(microseconds * 1e9), bytes_accessed=0, transcendentals=0)


def sds(shape, dtype):
    return jax.ShapeDtypeStruct(shape, dtype)


class Pieces:
    def __init__(self, place, parts=1, extra=0):
        self.place, self.parts, self.extra = place, parts, extra

    def outs(self):
        return [sds((self.parts, 2, 8, CUT_ROWS + self.extra, CUT_COLUMNS), BF16)] * 2

    def scratch(self, columns):
        return pltpu.VMEM((8, CUT_ROWS, columns), BF16)

    def store(self, blocks, grad, start=0):
        for i in range(8):
            rows = grad[i * CUT_ROWS : (i + 1) * CUT_ROWS].astype(BF16)
            blocks[i, :, start : start + grad.shape[1]] = rows

    def emit(self, idx, blocks, outs, under=None):
        for other_core, out in enumerate((outs[1], outs[0])):
            for part in range(self.parts):
                for owner in range(2):
                    for slot in range(8):
                        z = ((slot >> 1) & 1) | ((slot & 1) << 1)
                        block, column = self.place(
                            idx[0] ^ owner, idx[1] ^ other_core, idx[2] ^ (slot >> 2), idx[3] ^ z, part
                        )
                        columns = pl.ds(pl.multiple_of(column * CUT_COLUMNS, LANES), CUT_COLUMNS)
                        piece = blocks[block, :, columns]
                        if under is not None:
                            piece = jnp.concatenate(
                                [piece.astype(F32), under[idx[0] ^ owner]], axis=0
                            ).astype(BF16)
                        out[part, owner, slot] = piece


def head_stack(values, kv_head):
    first = kv_head * GROUP
    return jnp.concatenate(
        [values[:, (first + i) * HEAD : (first + i + 1) * HEAD] for i in range(GROUP)], axis=0
    )


def softmax_rows(query, key, allowed):
    scores = jnp.where(allowed, dot_right_t(query, key) * SCALE, MASKED)
    top = jnp.max(scores, axis=-1, keepdims=True)
    exponent = jnp.exp(scores - top)
    return exponent / jnp.sum(exponent, axis=-1, keepdims=True)


def pack_kernel(body, idx, sources, places, outs, name, after=(), limit=PACK_LIMIT):
    windows = [shape for shape, _ in places]

    def kernel(idx_ref, *refs):
        sources_in, refs = refs[: len(sources)], refs[len(sources) + len(after) :]
        out_refs, buffers, sem = refs[: len(outs)], refs[len(outs) : -1], refs[-1]
        copies = []
        for i, (source, (shape, place)) in enumerate(zip(sources_in, places)):
            where = []
            for axis, tile in ((0, 8), (1, LANES)):
                if shape[axis] == source.shape[axis]:
                    where.append(slice(None))
                else:
                    where.append(pl.ds(pl.multiple_of(place(idx_ref)[axis], tile), shape[axis]))
            copies.append(pltpu.make_async_copy(source.at[tuple(where)], buffers[i], sem.at[i]))
        for copy in copies:
            copy.start()
        for copy in copies:
            copy.wait()
        body(idx_ref, buffers, out_refs)

    return pl.pallas_call(
        kernel,
        out_shape=tuple(outs),
        in_specs=[pl.BlockSpec(memory_space=pltpu.SMEM)]
        + [pl.BlockSpec(memory_space=pltpu.HBM)] * len(sources)
        + [pl.BlockSpec(memory_space=pl.ANY)] * len(after),
        out_specs=tuple([pl.BlockSpec(memory_space=pltpu.VMEM)] * len(outs)),
        scratch_shapes=[pltpu.VMEM(w, F32) for w in windows]
        + [pltpu.SemaphoreType.DMA((len(sources),))],
        compiler_params=pltpu.CompilerParams(vmem_limit_bytes=limit),
        cost_estimate=busy_for(10),
        name=name,
    )(idx, *sources, *after)


def cast_out(idx_ref, buffers, outs):
    for buffer, out in zip(buffers, outs):
        out[...] = buffer[...].astype(BF16)


def pack_down(idx, down_t, after):
    shape = (2 * HALF, down_t.shape[1])
    window = (shape, lambda i: (i[1] * 2 * HALF, 0))
    outs = [sds(shape, BF16)]
    return pack_kernel(
        cast_out, idx, [down_t], [window], outs, "pack_down", after, STEP_LIMIT
    )[0]


def pack_first(idx, w_qkv, w_out, norm_gains, w_gate_up):
    columns = (QKV + w_out.shape[1]) // 2
    quarter = FF // 2
    windows = [((HALF, m.shape[1]), lambda i: (i[1] * HALF, 0)) for m in (w_qkv, w_out)]
    windows.append((norm_gains.shape, lambda i: (0, 0)))
    windows.append(((HALF, quarter), lambda i: (i[1] * HALF, i[2] * quarter)))
    windows.append(((HALF, quarter), lambda i: (i[1] * HALF, FF + (i[3] & 1) * quarter)))

    def body(idx_ref, buffers, outs):
        q_ref, o_ref, gains_ref = buffers[:3]
        both = jnp.concatenate([q_ref[:, columns:], o_ref[...]], axis=1)
        outs[0][:HALF, :] = jnp.where((idx_ref[3] & 1) == 0, q_ref[:, :columns], both).astype(BF16)
        outs[0][HALF:, :] = jnp.zeros((16, columns), BF16)
        outs[0][HALF : HALF + 2, : gains_ref.shape[1]] = gains_ref[...].astype(BF16)
        cast_out(idx_ref, buffers[3:], outs[1:])

    outs = [sds((HALF + 16, columns), BF16)] + [sds((HALF, quarter), BF16)] * 2
    sources = [w_qkv, w_out, norm_gains, w_gate_up, w_gate_up]
    return pack_kernel(body, idx, sources, windows, outs, "pack_first")


def attention_forward(idx, tokens_t, segments, frequency, gains, w_qkv_out):
    width, seq_length = tokens_t.shape
    split_gains = len(gains) > 1

    def body(idx_ref, arrays, loads, outs, scratch):
        x_ref, seg_ref, freq_ref = arrays[:3]
        qkv_ref, o_ref, cos_ref, sin_ref, allowed_ref, gains_ref = outs
        if split_gains:
            own = arrays[3][...].astype(BF16).astype(F32)
            other = arrays[4][HALF : HALF + 8, : width // 2].astype(F32)[:2]
            gains_ref[...] = jnp.where(
                idx_ref[0] == 0,
                jnp.concatenate([own, other], axis=1),
                jnp.concatenate([other, own], axis=1),
            )
        else:
            gains_ref[...] = arrays[3][...]
        seen_doc = jnp.broadcast_to(seg_ref[...], (seq_length, seq_length))
        own_doc = seen_doc.T
        token = lax.broadcasted_iota(jnp.int32, (seq_length, seq_length), 0)
        seen = lax.broadcasted_iota(jnp.int32, (seq_length, seq_length), 1)
        begin = jnp.sum((seen_doc < own_doc).astype(F32), axis=-1, keepdims=True)
        angles = (token.astype(F32) - begin) * freq_ref[...]
        cosine, sine = jnp.cos(angles), jnp.sin(angles)
        sine = jnp.where(seen % HEAD < HEAD // 2, -sine, sine)
        cos_ref[...] = cosine
        sin_ref[...] = sine
        allowed = ((seen_doc == own_doc) & (token >= seen)).astype(F32)
        allowed_ref[...] = allowed
        allowed = jnp.concatenate([allowed] * GROUP, axis=0) > 0.5
        x = x_ref[...].astype(F32).T
        h1 = (x * norm_scale(x) * gains_ref[0:1, :]).astype(BF16)
        projected = dot(h1, loads[0]()[:, :QKV])
        for start in range(0, ROPED, LANES):
            block = projected[:, start : start + LANES]
            qkv_ref[:, start : start + LANES] = rotate_block(block, cosine, sine).astype(BF16)
        qkv_ref[:, ROPED:QKV] = projected[:, ROPED:QKV].astype(BF16)
        qkv = qkv_ref[...]
        for kv in range(KV_HEADS):
            key = qkv[:, QUERY + kv * HEAD : QUERY + (kv + 1) * HEAD]
            value = qkv[:, ROPED + kv * HEAD : ROPED + (kv + 1) * HEAD]
            probs = softmax_rows(head_stack(qkv, kv), key, allowed).astype(BF16)
            attended = dot(probs, value).astype(BF16)
            for i in range(GROUP):
                start = (kv * GROUP + i) * HEAD
                o_ref[:, start : start + HEAD] = attended[i * seq_length : (i + 1) * seq_length]

    square = sds((seq_length, seq_length), F32)
    outs = [sds((seq_length, QKV), BF16), sds((seq_length, QUERY), BF16)]
    outs += [square, square, square, sds((2, width), F32)]
    return call(
        body,
        idx,
        [tokens_t, segments, frequency, *gains],
        [w_qkv_out],
        outs,
        [],
        1,
        "attention",
        hand_on=True,
    )


def feed_forward(idx, tokens_t, attended, gains, cotangent_t, w_qkv_out, w_gate_up, pieces, after):
    width, seq_length = tokens_t.shape

    def body(idx_ref, arrays, loads, outs, scratch):
        x_ref, o_ref, gains_ref, y_ref = arrays
        u_ref, h2_ref, ab_ref, z_ref = outs[:4]
        u = x_ref[...].astype(F32).T + dot(o_ref[...], loads[0]()[:, QKV:])
        u_ref[...] = u
        h2 = (u * norm_scale(u) * gains_ref[1:2, :]).astype(BF16)
        h2_ref[...] = h2
        ab = dot(h2, loads[1]()[...])
        ab_ref[...] = ab
        gate, up = ab[:, :FF], ab[:, FF:]
        z = (gate * jax.nn.sigmoid(gate) * up).astype(BF16)
        z_ref[...] = z
        grad = dot(y_ref[...], z)
        if pieces is None:
            outs[4][...] = grad
        else:
            pieces.store(scratch[0], grad)
            pieces.emit(idx_ref, scratch[0], outs[4:])

    outs = [
        sds((seq_length, width), F32),
        sds((seq_length, width), BF16),
        sds((seq_length, 2 * FF), F32),
        sds((seq_length, FF), BF16),
    ]
    outs += [sds((width, FF), F32)] if pieces is None else pieces.outs()
    scratch = [] if pieces is None else [pieces.scratch(FF)]
    return call(
        body,
        idx,
        [tokens_t, attended, gains, cotangent_t],
        [w_qkv_out, w_gate_up],
        outs,
        scratch,
        5,
        "feed_forward",
        after,
        True,
    )


def feed_back(idx, ab, normed_low, cotangent_t, down_t, pieces):
    width, seq_length = cotangent_t.shape

    def body(idx_ref, arrays, loads, outs, scratch):
        ab_ref, h2_ref, y_ref = arrays
        gg_ref = outs[0]
        gate, up = ab_ref[:, :FF], ab_ref[:, FF:]
        sig = jax.nn.sigmoid(gate)
        grad_hidden = dot_left_t(y_ref[...], loads[0]()[...])
        gg_ref[:, :FF] = (grad_hidden * up * sig * (1.0 + gate * (1.0 - sig))).astype(BF16)
        gg_ref[:, FF:] = (grad_hidden * gate * sig).astype(BF16)
        grad = dot_left_t(h2_ref[...], gg_ref[...])
        if pieces is None:
            outs[1][...] = grad
        else:
            pieces.store(scratch[0], grad)
            pieces.emit(idx_ref, scratch[0], outs[1:])

    outs = [sds((seq_length, 2 * FF), BF16)]
    outs += [sds((width, 2 * FF), F32)] if pieces is None else pieces.outs()
    scratch = [] if pieces is None else [pieces.scratch(2 * FF)]
    return call(
        body,
        idx,
        [ab, normed_low, cotangent_t],
        [down_t],
        outs,
        scratch,
        20,
        "feed_back",
        hand_on=True,
    )


def layer_output(middle, hidden, down_t, after):
    seq_length, width = middle.shape

    def body(ins, outs):
        outs[0][...] = (ins[0][...] + dot_right_t(ins[1][...], ins[2][...])).T.astype(BF16)

    return step(
        body, [middle, hidden, down_t], [sds((width, seq_length), BF16)], "layer_output", after, 2
    )[0]


def middle_back(idx, cotangent_t, middle, gated, gains, w_gate_up, w_qkv_out, after):
    width, seq_length = cotangent_t.shape

    def body(idx_ref, arrays, loads, outs, scratch):
        y_ref, u_ref, gg_ref, gains_ref = arrays
        gu_ref, go_ref, gain_ref = outs
        u = u_ref[...]
        scale_two = norm_scale(u)
        normed = u * scale_two
        grad_normed = dot_right_t(gg_ref[...], loads[0]()[...])
        gain_ref[...] = jnp.sum(grad_normed * normed, axis=0, keepdims=True)
        gu = y_ref[...].astype(F32).T + norm_back(
            grad_normed * gains_ref[1:2, :], normed, scale_two
        )
        gu_ref[...] = gu
        go_ref[...] = dot_right_t(gu.astype(BF16), loads[1]()[:, QKV:]).astype(BF16)

    outs = [sds((seq_length, width), F32), sds((seq_length, width), BF16), sds((1, width), F32)]
    return call(
        body,
        idx,
        [cotangent_t, middle, gated, gains],
        [w_gate_up, w_qkv_out],
        outs,
        [],
        20,
        "middle_back",
        after,
    )


def attention_back(
    idx, tokens_t, grad_middle, grad_attended, gain_two, qkv, attended, tables, gains, w_qkv, pieces, after
):
    width, seq_length = tokens_t.shape

    def body(idx_ref, arrays, loads, outs, scratch):
        x_ref, gu_ref, go_ref, gain_two_ref, qkv_ref, o_ref = arrays[:6]
        cos_ref, sin_ref, allowed_ref, gains_ref = arrays[6:]
        grad_ref = outs[0]
        grad_proj, gp_ref, gain_rows, *blocks = scratch
        gu, go = gu_ref[...], go_ref[...]
        gu_low = gu.astype(BF16)
        grad_gain_two = gain_two_ref[...]
        allowed = jnp.concatenate([allowed_ref[...]] * GROUP, axis=0) > 0.5
        qkv_values = qkv_ref[...]
        for kv in range(KV_HEADS):
            key = qkv_values[:, QUERY + kv * HEAD : QUERY + (kv + 1) * HEAD]
            value = qkv_values[:, ROPED + kv * HEAD : ROPED + (kv + 1) * HEAD]
            query = head_stack(qkv_values, kv)
            grad_out = head_stack(go, kv)
            probs = softmax_rows(query, key, allowed)
            grad_probs = dot_right_t(grad_out, value)
            row_delta = jnp.sum(probs * grad_probs, axis=-1, keepdims=True)
            gs = (probs * (grad_probs - row_delta)).astype(BF16)
            grad_query = dot(gs, key) * SCALE
            for i in range(GROUP):
                start = (kv * GROUP + i) * HEAD
                grad_proj[:, start : start + HEAD] = grad_query[
                    i * seq_length : (i + 1) * seq_length
                ]
            start = QUERY + kv * HEAD
            grad_proj[:, start : start + HEAD] = dot_left_t(gs, query) * SCALE
            start = ROPED + kv * HEAD
            grad_proj[:, start : start + HEAD] = dot_left_t(probs.astype(BF16), grad_out)
        for start in range(0, ROPED, LANES):
            gp_ref[:, start : start + LANES] = rotate_block(
                grad_proj[:, start : start + LANES], cos_ref[...], -sin_ref[...]
            ).astype(BF16)
        gp_ref[:, ROPED:QKV] = grad_proj[:, ROPED:QKV].astype(BF16)
        x = x_ref[...].astype(F32).T
        scale_one = norm_scale(x)
        normed = x * scale_one
        h1 = (normed * gains_ref[0:1, :]).astype(BF16)
        grad_qkv = dot_left_t(h1, gp_ref[...])
        grad_out = dot_left_t(o_ref[...], gu_low)
        grad_normed = dot_right_t(gp_ref[...], loads[0]()[:, :QKV])
        grad_gain_one = jnp.sum(grad_normed * normed, axis=0, keepdims=True)
        if pieces is None:
            outs[1][:, :QKV] = grad_qkv
            outs[1][:, QKV:] = grad_out
            outs[2][0:1, :] = grad_gain_one
            outs[2][1:2, :] = grad_gain_two
        else:
            pieces.store(blocks[0], grad_qkv)
            pieces.store(blocks[0], grad_out, QKV)
            half = width // 2
            gain_rows[...] = jnp.zeros_like(gain_rows)
            for owner in range(2):
                columns = slice(owner * half, (owner + 1) * half)
                gain_rows[owner, 0:1, :half] = grad_gain_one[:, columns]
                gain_rows[owner, 1:2, :half] = grad_gain_two[:, columns]
            pieces.emit(idx_ref, blocks[0], outs[1:3], gain_rows)
            outs[3][...] = jnp.zeros_like(outs[3])
        grad_ref[...] = (
            (gu + norm_back(grad_normed * gains_ref[0:1, :], normed, scale_one)).T
        ).astype(BF16)

    outs = [sds((width, seq_length), BF16)]
    scratch = [
        pltpu.VMEM((seq_length, QKV), F32),
        pltpu.VMEM((seq_length, QKV), BF16),
        pltpu.VMEM((2, 8, CUT_COLUMNS), F32),
    ]
    if pieces is None:
        outs += [sds((width, QKV + width), F32), sds((2, width), F32)]
    else:
        outs += pieces.outs() + [sds(MARK, F32)]
        scratch += [pieces.scratch(QKV + width)]
    return call(
        body,
        idx,
        [tokens_t, grad_middle, grad_attended, gain_two, qkv, attended, *tables, gains],
        [w_qkv],
        outs,
        scratch,
        20,
        "attention_back",
        after,
    )


def step(body, arrays, outs, name, after=(), busy=20):
    def kernel(*refs):
        body(refs[: len(arrays)], refs[len(arrays) + len(after) :])

    return pl.pallas_call(
        kernel,
        out_shape=tuple(outs),
        in_specs=[pl.BlockSpec(memory_space=pltpu.VMEM)] * len(arrays)
        + [pl.BlockSpec(memory_space=pl.ANY)] * len(after),
        out_specs=tuple([pl.BlockSpec(memory_space=pltpu.VMEM)] * len(outs)),
        compiler_params=pltpu.CompilerParams(vmem_limit_bytes=STEP_LIMIT),
        cost_estimate=busy_for(busy),
        name=name,
    )(*arrays, *after)


def pass_on(ins, outs):
    outs[0][...] = ins[0][...]


def add_split(keep, arrived, axis, send_ref, keep_ref):
    total = keep[...].astype(F32) + arrived[...].astype(F32)
    low, high = lax.index_in_dim(total, 0, axis, False), lax.index_in_dim(total, 1, axis, False)
    send_ref[...] = high.astype(BF16)
    keep_ref[...] = low


def add_step(jobs, name, after):
    arrays, outs = [], []
    for keep, arrived, axis in jobs:
        arrays += [keep, arrived]
        shape = keep.shape[:axis] + keep.shape[axis + 1 :]
        outs += [sds(shape, BF16), sds(shape, F32)]

    def body(ins, out_refs):
        for i, (_, _, axis) in enumerate(jobs):
            add_split(ins[2 * i], ins[2 * i + 1], axis, out_refs[2 * i], out_refs[2 * i + 1])

    flat = step(body, arrays, outs, name, after)
    return [(flat[2 * i], flat[2 * i + 1]) for i in range(len(jobs))]


def update_rows(idx, shares, place, height, chunk, state, earlier, gains, name, after, busy=20):
    count = len(state) // 3
    columns = [a.shape[1] for a in state[:count]]
    starts = [sum(-(-c // LANES) * LANES for c in columns[:k]) for k in range(count + 1)]
    chunks = height // chunk
    order = [(k, count + k, 2 * count + k) for k in range(count)]

    def kernel(idx_ref, *refs):
        refs = list(refs)
        take = lambda n: [refs.pop(0) for _ in range(n)]
        share_refs = take(len(shares))
        state_refs, gain_refs = take(3 * count), take(len(gains))
        take(len(earlier) + len(after))
        outs, gain_outs, (mark,) = take(3 * count), take(len(gains)), take(1)
        buffers, (full, sem) = take(3 * count), refs
        mark[...] = jnp.zeros_like(mark)
        copies = []
        for share, (far, _) in enumerate(shares):
            piece_ref = share_refs[share]
            for part in range(piece_ref.shape[0]):
                for x in range(2):
                    for z in range(4):
                        rel = z ^ idx_ref[3]
                        slot = ((rel & 1) << 1) | (rel >> 1)
                        piece = piece_ref[part, x, slot].astype(F32)[:CUT_ROWS]
                        row, cuts = place(part, idx_ref[2] ^ x, z)
                        rows = pl.ds(pl.multiple_of(share * height + row, 8), CUT_ROWS)
                        for begin, size, to in cuts:
                            if isinstance(to, int):
                                where = slice(to, to + size)
                            else:
                                where = pl.ds(pl.multiple_of(to, LANES), size)
                            full[rows, where] = piece[:, begin : begin + size]
            base = (idx_ref[1] ^ far) * height
            for at_chunk in range(chunks):

                def eight_rows(i, carry, at_chunk=at_chunk, share=share, base=base):
                    at_row = at_chunk * chunk + i * 8
                    near_rows = pl.ds(pl.multiple_of(share * height + at_row, 8), 8)
                    rows = pl.ds(pl.multiple_of(base + at_row, 8), 8)
                    for k in range(count):
                        for at in range(0, columns[k], 768):
                            size = min(768, columns[k] - at)
                            where = slice(at, at + size)
                            results = adamw_rows(
                                *[state_refs[j][rows, where] for j in order[k]],
                                full[near_rows, starts[k] + at : starts[k] + at + size],
                                RATE_MATRIX,
                                DECAY_MATRIX,
                            )
                            for j, result in zip(order[k], results):
                                buffers[j][near_rows, where] = result
                    return carry

                lax.fori_loop(0, chunk // 8, eight_rows, 0, unroll=3)
                near_rows = pl.ds(share * height + at_chunk * chunk, chunk)
                rows = pl.ds(pl.multiple_of(base + at_chunk * chunk, 8), chunk)
                for j in range(3 * count):
                    copy = pltpu.make_async_copy(
                        buffers[j].at[near_rows],
                        outs[j].at[rows],
                        sem.at[share * chunks + at_chunk, j],
                    )
                    copy.start()
                    copies.append(copy)
        if gains:
            gradient = share_refs[0][0, 0, 0, CUT_ROWS:, :].astype(F32)[:2, : gains[0].shape[1]]
            results = adamw_rows(*[g[...] for g in gain_refs], gradient, RATE_GAIN, 0.0)
            for out, result in zip(gain_outs, results):
                out[...] = result
        for copy in copies:
            copy.wait()

    vmem, anywhere = pl.BlockSpec(memory_space=pltpu.VMEM), pl.BlockSpec(memory_space=pl.ANY)
    first_earlier = 1 + len(shares) + 3 * count + len(gains)
    total = len(shares) * height
    return pl.pallas_call(
        kernel,
        out_shape=tuple(sds(a.shape, F32) for a in [*state, *gains]) + (sds(MARK, F32),),
        in_specs=[pl.BlockSpec(memory_space=pltpu.SMEM)]
        + [vmem] * (len(shares) + 3 * count + len(gains))
        + [anywhere] * (len(earlier) + len(after)),
        out_specs=tuple([anywhere] * (3 * count) + [vmem] * (len(gains) + 1)),
        scratch_shapes=[pltpu.VMEM((total, a.shape[1]), F32) for a in state]
        + [pltpu.VMEM((total, starts[-1]), F32)]
        + [pltpu.SemaphoreType.DMA((len(shares) * chunks, 3 * count))],
        input_output_aliases={first_earlier + i: i for i in range(len(earlier))},
        compiler_params=pltpu.CompilerParams(vmem_limit_bytes=UPDATE_LIMIT),
        cost_estimate=busy_for(busy),
        name=name,
    )(idx, *[p for _, p in shares], *state, *gains, *earlier, *after)


def swap(values, axis, mask):
    size = lax.axis_size(axis)
    return lax.ppermute(values, axis, [(i, i ^ mask) for i in range(size)])


over_y = functools.partial(swap, axis="shard", mask=1)
over_core = functools.partial(swap, axis="dp", mask=1)
over_x = functools.partial(swap, axis="dp", mask=2)
over_z_low = functools.partial(swap, axis="dp", mask=4)
over_z_high = functools.partial(swap, axis="dp", mask=8)


def per_device(
    tokens,
    segments,
    cotangent,
    w_qkv,
    w_out,
    w_gate_up,
    w_down,
    norm_gains,
    first_qkv,
    first_out,
    first_gate_up,
    first_down,
    first_gains,
    second_qkv,
    second_out,
    second_gate_up,
    second_down,
    second_gains,
):
    groups = lax.axis_size("shard")
    replicas = lax.axis_size("dp")
    fast = groups == 2 and replicas == 16
    place_dp = lax.axis_index("dp")
    owner = lax.axis_index("shard")
    idx = jnp.stack([owner, place_dp & 1, (place_dp >> 1) & 1, place_dp >> 2]).astype(jnp.int32)
    x_t, y_t = tokens[0].T, cotangent[0].T
    width, seq_length = x_t.shape
    rows, down_rows = w_qkv.shape[0], w_down.shape[0]
    down_t, first_down_t, second_down_t = w_down.T, first_down.T, second_down.T
    half_size = HEAD // 2
    frequency = ROPE_BASE ** (-(np.arange(half_size) * 2.0 / HEAD))
    frequency = jnp.asarray(np.tile(frequency, 4)[None], F32)
    if fast:
        qo_near, by_x, by_low = pack_first(idx, w_qkv, w_out, norm_gains, w_gate_up)
        qo_near, by_x, by_low = over_y(qo_near), over_y(by_x), over_y(by_low)
        down_near = over_y(pack_down(idx, down_t, (by_low,)))
        by_x_next, by_low_next = over_x(by_x), over_z_low(by_low)
        qo_near_low = over_z_low(qo_near)
        gains = (norm_gains, qo_near)
        (low_far,) = step(
            pass_on, [over_core(by_low_next)], [sds(by_low.shape, BF16)], "pass_on_low", (), 1
        )
        own_rows = lambda o: (o * rows, 0)
        own_rows_out = lambda o: (o * rows, QKV)
        qo_place = lambda o, c, x, low: (o * rows + c * HALF, low * ((QKV + width) // 2))
        x_place = lambda o, c, x, low: (o * rows + c * HALF, x * (FF // 2))
        low_place = lambda o, c, x, low: (o * rows + c * HALF, FF + low * (FF // 2))
        mat_qkv_out = Weight(
            (width, QKV + width),
            own=[(w_qkv, own_rows), (w_out, own_rows_out)],
            parts=[
                (qo_near, (0, 0, 0), qo_place),
                (qo_near_low, (0, 0, 1), qo_place),
                (over_core(qo_near), (1, 0, 0), qo_place),
                (over_core(qo_near_low), (1, 0, 1), qo_place),
            ],
        )
        mat_gate_up = Weight(
            (width, 2 * FF),
            own=[(w_gate_up, own_rows)],
            parts=[
                (by_x, (0, 0, 0), x_place),
                (by_x_next, (0, 1, 0), x_place),
                (over_core(by_x), (1, 0, 0), x_place),
                (over_core(by_x_next), (1, 1, 0), x_place),
                (by_low, (0, 0, 0), low_place),
                (by_low_next, (0, 0, 1), low_place),
                (over_core(by_low), (1, 0, 0), low_place),
                (low_far, (1, 0, 1), low_place),
            ],
        )
        cut_qkv_out = Pieces(lambda o, c, x, z, p: (o * 4 + c * 2 + x, z), extra=8)
        cut_gate_up = Pieces(lambda o, c, x, z, p: (o * 4 + c * 2 + p, x * 4 + z), parts=2)
        cut_down = Pieces(lambda o, c, x, z, p: (c * 4 + x * 2 + (z >> 1), o * 2 + (z & 1)))
    else:
        gains = (
            lax.all_gather(norm_gains.astype(BF16), "shard", axis=1, tiled=True).astype(F32),
        )
        mat_qkv, mat_out, mat_gate_up, mat_down = [
            lax.all_gather(m.astype(BF16), "shard", axis=0, tiled=True)
            for m in (w_qkv, w_out, w_gate_up, w_down)
        ]
        mat_qkv_out, mat_gate_up, mat_down = [
            Weight(m.shape, whole=m)
            for m in (jnp.concatenate([mat_qkv, mat_out], axis=1), mat_gate_up, mat_down.T)
        ]
        cut_qkv_out = cut_gate_up = cut_down = None

    qkv, attended, *tables, gains, whole = attention_forward(
        idx, x_t, segments, frequency, gains, mat_qkv_out
    ) + (() if fast else (None,))
    if fast:
        mat_qkv_out = Weight(whole.shape, whole=whole)
    middle, normed_low, ab, hidden, *grad_down = feed_forward(
        idx, x_t, attended, gains, y_t, mat_qkv_out, mat_gate_up, cut_down, ()
    )
    after = ()
    if fast:
        whole = grad_down.pop()
        mat_gate_up = Weight(whole.shape, whole=whole)

        (down_near,) = step(
            pass_on, [down_near], [sds(down_near.shape, BF16)], "pass_on", (attended,), 0.1
        )
        down_place = lambda o, c, x, low: (c * 2 * HALF, o * down_rows)
        mat_down = Weight(
            (width, FF),
            own=[(down_t, lambda o: (0, o * down_rows))],
            parts=[
                (down_near, (0, 0, 0), down_place),
                (over_core(down_near), (1, 0, 0), down_place),
            ],
        )
    if fast:
        arrived_down = over_core(grad_down[0])
    gated, *grad_gate_up = feed_back(idx, ab, normed_low, y_t, mat_down, cut_gate_up)
    if not fast:
        output = layer_output(middle, hidden, mat_down.arrays[0], ())
    if fast:
        down_whole = grad_gate_up.pop()
        cut = lambda a, *lead: a.reshape(*lead, *a.shape[-2:])
        arrived_gate_up = over_core(grad_gate_up[0])
        ((send, keep_down),) = add_step(
            [(grad_down[1][0], arrived_down[0], 0)], "down_core", (gated,)
        )
        arrived_down = over_y(send)
        after = (keep_down,)
    grad_middle, grad_attended, gain_two = middle_back(
        idx, y_t, middle, gated, gains, mat_gate_up, mat_qkv_out, after
    )
    if fast:
        halves = [
            [cut(a[p], *lead) for a in (grad_gate_up[1], arrived_gate_up)]
            for p, lead in ((0, (2, 2, 4)), (1, (4, 2, 2)))
        ]
        (send_up, keep_up), (send_low, keep_low) = add_step(
            [(*halves[0], 1), (*halves[1], 1)], "gate_up_core", (grad_middle,)
        )
        arrived_up, arrived_low = over_x(send_up), over_z_low(send_low)
        after = (keep_up,)
    token_grad, *grad_qkv_out = attention_back(
        idx,
        x_t,
        grad_middle,
        grad_attended,
        gain_two,
        qkv,
        attended,
        tables,
        gains,
        mat_qkv_out,
        cut_qkv_out,
        after,
    )
    if fast:

        arrived_qkv_out = over_core(grad_qkv_out[0])
        piece = (CUT_ROWS, CUT_COLUMNS)
        taller = (CUT_ROWS + 8, CUT_COLUMNS)
        ((send, keep_down),) = add_step(
            [(cut(keep_down, 2, 4), cut(arrived_down, 2, 4), 0)], "down_y", (grad_qkv_out[2],)
        )
        arrived_down = over_x(send)
        (send_up, keep_up), (send_low, keep_low) = add_step(
            [
                (cut(keep_up, 2, 2, 2), cut(arrived_up, 2, 2, 2), 1),
                (cut(keep_low, 2, 2, 2), cut(arrived_low, 2, 2, 2), 1),
            ],
            "up_x_low_z",
            (keep_down,),
        )
        arrived_up, arrived_low = over_z_low(send_up), over_x(send_low)
        ((send, keep_qkv_out),) = add_step(
            [(grad_qkv_out[1][0], arrived_qkv_out[0], 0)], "qkv_out_core", (keep_up,)
        )
        arrived_qkv_out = over_y(send)
        ((send, keep_down),) = add_step(
            [(cut(keep_down, 2, 2), cut(arrived_down, 2, 2), 0)], "down_x", (keep_qkv_out,)
        )
        arrived_down = over_z_low(send)

        def columns(ins, outs):
            total = ins[0][...] + ins[1][...].astype(F32)
            outs[0][...] = total[1].astype(BF16)
            outs[1][...] = total[0]
            total = ins[2][...] + ins[3][...].astype(F32)
            outs[2][0], outs[2][1] = total[0, 1].astype(BF16), total[1, 1].astype(BF16)
            outs[3][...] = total[:, 0]
            total = ins[4][...] + ins[5][...].astype(F32)
            outs[4][...] = total[1].astype(BF16)
            outs[5][...] = total[0]
            total = ins[6][...] + ins[7][...].astype(F32)
            outs[2][2] = total[1].astype(BF16)
            outs[6][...] = total[0]

        send_up, keep_up, send, keep_low, send_qkv_out, keep_qkv_out, keep_down = step(
            columns,
            [
                *(keep_up, arrived_up, keep_low, arrived_low),
                *(cut(keep_qkv_out, 2, 4), cut(arrived_qkv_out, 2, 4)),
                *(keep_down, arrived_down),
            ],
            [
                *(sds((2, *piece), BF16), sds((2, *piece), F32)),
                *(sds((3, *piece), BF16), sds((2, *piece), F32)),
                *(sds((4, *taller), BF16), sds((4, *taller), F32)),
                sds(piece, F32),
            ],
            "columns",
        )
        arrived_up, arrived_qkv_out = over_y(send_up), over_x(send_qkv_out)
        arrived = over_z_high(send)

        def planes(ins, outs):
            keep_up, arrived_up, keep_low, arrived, keep_down, keep_qkv_out, arrived_qkv_out = ins
            total = keep_up[...] + arrived_up[...].astype(F32)
            outs[0][0] = total[1].astype(BF16)
            outs[1][0] = total[0]
            outs[0][1] = (keep_down[...] + arrived[2].astype(F32)).astype(BF16)
            outs[2][...] = (keep_low[1] + arrived[1].astype(F32)).astype(BF16)
            outs[1][1] = keep_low[0] + arrived[0].astype(F32)
            total = keep_qkv_out[...] + arrived_qkv_out[...].astype(F32)
            outs[3][...] = total[1].astype(BF16)
            outs[4][...] = total[0]

        send, keep, send_low, send_qkv_out, keep_qkv_out = step(
            planes,
            [
                *(keep_up, arrived_up, keep_low, arrived, keep_down),
                *(cut(keep_qkv_out, 2, 2), cut(arrived_qkv_out, 2, 2)),
            ],
            [
                *(sds((2, *piece), BF16), sds((2, *piece), F32), sds(piece, BF16)),
                *(sds((2, *taller), BF16), sds((2, *taller), F32)),
            ],
            "planes",
        )
        arrived, arrived_low = over_z_high(send), over_y(send_low)
        arrived_qkv_out = over_z_low(send_qkv_out)

        def lines(ins, outs):
            send, keep, arrived, arrived_low, keep_qkv_out, arrived_qkv_out = ins
            total = keep_qkv_out[...] + arrived_qkv_out[...].astype(F32)
            outs[0][0] = total[1].astype(BF16)
            outs[1][...] = total[0]
            for part, came in enumerate((arrived[0], arrived_low[...])):
                total = keep[part] + came.astype(F32)
                total = jnp.concatenate([total, jnp.zeros((8, CUT_COLUMNS), F32)], axis=0)
                outs[0][part + 1] = total.astype(BF16)
            outs[2][0], outs[2][1] = send[1], arrived[1]

        pieces, keep_qkv_out, near_down = step(
            lines,
            [send, keep, arrived, arrived_low, keep_qkv_out, arrived_qkv_out],
            [sds((3, *taller), BF16), sds(taller, F32), sds((2, *piece), BF16)],
            "lines",
            (w_gate_up, first_gate_up, second_gate_up),
        )
        arrived, down_low = over_z_high(pieces), over_z_low(near_down)

        def share_high(ins, outs):
            pieces, arrived, keep_qkv_out, near_down, down_low = ins
            for high in range(2):
                outs[0][0, high], outs[0][1, high] = near_down[high], down_low[high]
            outs[0][2, 0], outs[0][2, 1] = pieces[1, :CUT_ROWS], arrived[1, :CUT_ROWS]
            outs[1][0], outs[1][1] = pieces[2, :CUT_ROWS], arrived[2, :CUT_ROWS]
            outs[2][...] = (keep_qkv_out[...] + arrived[0].astype(F32)).astype(BF16)

        near_x, near_low, piece_qkv_out = step(
            share_high,
            [pieces, arrived, keep_qkv_out, near_down, down_low],
            [sds((3, 2, *piece), BF16), sds((2, *piece), BF16), sds(taller, BF16)],
            "share_high",
            (
                *(w_qkv, w_out, first_qkv, first_out, second_qkv, second_out),
                *(down_t, first_down_t, second_down_t, first_gains, second_gains),
            ),
        )
        arrived_x, low_low = over_x(near_x), over_z_low(near_low)
        qkv_out_high = over_z_high(piece_qkv_out)
        output = layer_output(middle, hidden, down_whole, (near_x,))

        def share_next(ins, outs):
            near_x, arrived_x, near_low, low_low = ins
            outs[0][0], outs[0][1] = near_x[2], arrived_x[2]
            outs[1][0], outs[1][1] = near_low[...], low_low[...]
            for low in range(2):
                for high in range(2):
                    outs[2][0, 0, low * 2 + high] = near_x[low, high]
                    outs[2][0, 1, low * 2 + high] = arrived_x[low, high]

        near_up, near_low, near_down = step(
            share_next,
            [near_x, arrived_x, near_low, low_low],
            [
                *(sds((2, 2, *piece), BF16), sds((2, 2, *piece), BF16)),
                sds((1, 2, 4, *piece), BF16),
            ],
            "share_next",
            (qkv_out_high,),
        )
        far_down = over_core(near_down)
        up_low, low_x = over_z_low(near_up), over_x(near_low)

        def share_qkv_out_high(ins, outs):
            outs[0][0], outs[0][1] = ins[0][...], ins[1][...]

        (near_qkv_out,) = step(
            share_qkv_out_high,
            [piece_qkv_out, qkv_out_high],
            [sds((2, *taller), BF16)],
            "share_qkv_out_high",
            (near_up,),
        )
        qkv_out_x, qkv_out_low = over_x(near_qkv_out), over_z_low(near_qkv_out)
        qkv_out_both = swap(near_qkv_out, "dp", 6)
        one_down, two_down, next_down, mark = update_rows(
            idx,
            [(0, near_down), (1, far_down)],
            lambda p, x, z: (
                (x * 2 + (z >> 1)) * CUT_ROWS,
                [(0, CUT_COLUMNS, (z & 1) * CUT_COLUMNS)],
            ),
            2 * HALF,
            96,
            [down_t, first_down_t, second_down_t],
            (),
            (),
            "update_down",
            (near_qkv_out,),
            0.1,
        )

        def share_gate_up(ins, outs):
            for near in range(2):
                for far in range(2):
                    for high in range(2):
                        outs[0][0, near, far * 2 + high] = ins[far][near, high]
                        outs[0][1, far, near * 2 + high] = ins[2 + far][near, high]

        (near_gate_up,) = step(
            share_gate_up,
            [near_up, up_low, near_low, low_x],
            [sds((2, 2, 4, *piece), BF16)],
            "share_gate_up",
            (mark,),
        )
        far_gate_up = over_core(near_gate_up)
        place_gate_up = lambda p, x, z: (p * CUT_ROWS, [(0, CUT_COLUMNS, (x * 4 + z) * CUT_COLUMNS)])
        state_gate_up = [w_gate_up, first_gate_up, second_gate_up]
        *near_state, mark = update_rows(
            idx,
            [(0, near_gate_up)],
            place_gate_up,
            HALF,
            24,
            state_gate_up,
            (),
            (),
            "update_gate_up_near",
            (),
        )

        def share_qkv_out(ins, outs):
            for x in range(2):
                for low in range(2):
                    for high in range(2):
                        outs[0][0, x, low * 2 + high] = ins[low * 2 + x][high]

        (near_qkv_out,) = step(
            share_qkv_out,
            [near_qkv_out, qkv_out_x, qkv_out_low, qkv_out_both],
            [sds((1, 2, 4, *taller), BF16)],
            "share_qkv_out",
            (mark,),
        )
        far_qkv_out = over_core(near_qkv_out)
        one_gate_up, two_gate_up, next_gate_up, mark = update_rows(
            idx,
            [(1, far_gate_up)],
            place_gate_up,
            HALF,
            24,
            state_gate_up,
            near_state,
            (),
            "update_gate_up_far",
            (near_qkv_out,),
        )
        cuts = [[(0, 384, 0)], [(0, 384, 384)], [(0, 192, 768), (192, 192, 1024)], [(0, 384, 1216)]]
        updated = update_rows(
            idx,
            [(0, near_qkv_out), (1, far_qkv_out)],
            lambda p, x, z: (x * CUT_ROWS, cuts[z]),
            HALF,
            48,
            [w_qkv, w_out, first_qkv, first_out, second_qkv, second_out],
            (),
            (norm_gains, first_gains, second_gains),
            "update_qkv_out",
            (mark,),
        )
        one_qkv, one_out, two_qkv, two_out, next_qkv, next_out = updated[:6]
        one_gains, two_gains, next_gains = updated[6:9]
    else:
        sums = lax.psum((*grad_qkv_out, grad_gate_up[0], grad_down[0].T), ("dp", "shard"))
        grad_qkv_out, grad_gains, grad_gate_up, grad_down = sums

        def own(grad, axis=0):
            size = grad.shape[axis] // groups
            return lax.dynamic_slice_in_dim(grad, owner * size, size, axis)

        one_qkv, two_qkv, next_qkv = adamw(
            w_qkv, first_qkv, second_qkv, own(grad_qkv_out[:, :QKV]), RATE_MATRIX, DECAY_MATRIX
        )
        one_out, two_out, next_out = adamw(
            w_out, first_out, second_out, own(grad_qkv_out[:, QKV:]), RATE_MATRIX, DECAY_MATRIX
        )
        one_gate_up, two_gate_up, next_gate_up = adamw(
            w_gate_up, first_gate_up, second_gate_up, own(grad_gate_up), RATE_MATRIX, DECAY_MATRIX
        )
        one_down, two_down, next_down = [
            a.T
            for a in adamw(
                w_down, first_down, second_down, own(grad_down), RATE_MATRIX, DECAY_MATRIX
            )
        ]
        one_gains, two_gains, next_gains = adamw(
            norm_gains, first_gains, second_gains, own(grad_gains, 1), RATE_GAIN, 0.0
        )
    one_down, two_down, next_down = one_down.T, two_down.T, next_down.T
    return (
        output.T[None],
        token_grad.T[None],
        one_qkv,
        one_out,
        one_gate_up,
        one_down,
        one_gains,
        two_qkv,
        two_out,
        two_gate_up,
        two_down,
        two_gains,
        next_qkv,
        next_out,
        next_gate_up,
        next_down,
        next_gains,
    )


def solution(mesh):
    return jax.shard_map(
        per_device,
        mesh=mesh,
        in_specs=(
            P(("dp", "shard"), None, None),
            P(("dp", "shard"), None),
            P(("dp", "shard"), None, None),
            P("shard", None),
            P("shard", None),
            P("shard", None),
            P("shard", None),
            P(None, "shard"),
            P("shard", None),
            P("shard", None),
            P("shard", None),
            P("shard", None),
            P(None, "shard"),
            P("shard", None),
            P("shard", None),
            P("shard", None),
            P("shard", None),
            P(None, "shard"),
        ),
        out_specs=(
            P(("dp", "shard"), None, None),
            P(("dp", "shard"), None, None),
            P("shard", None),
            P("shard", None),
            P("shard", None),
            P("shard", None),
            P(None, "shard"),
            P("shard", None),
            P("shard", None),
            P("shard", None),
            P("shard", None),
            P(None, "shard"),
            P("shard", None),
            P("shard", None),
            P("shard", None),
            P("shard", None),
            P(None, "shard"),
        ),
        check_vma=False,
    )
```

```python
import functools

import jax
import jax.numpy as jnp
import numpy as np
from jax import lax
from jax.experimental import pallas as pl
from jax.experimental.pallas import tpu as pltpu
from jax.sharding import PartitionSpec as P

HEADS = 9
KV_HEADS = 3
GROUP = HEADS // KV_HEADS
HEAD = 64
FF = 1536
STEP = 10
QUERY = HEADS * HEAD
ROPED = (HEADS + KV_HEADS) * HEAD
QKV = (HEADS + 2 * KV_HEADS) * HEAD
LANES = 128

EPS_NORM = 1e-05
ROPE_BASE = 100000.0
BETA_ONE = 0.9
BETA_TWO = 0.95
RATE_MATRIX = 0.1
RATE_GAIN = 0.3
DECAY_MATRIX = 0.1
EPS_ADAM = 1e-08
MASKED = -1e30
SCALE = float(HEAD) ** (-0.5)
VMEM_LIMIT = 32 * 1024 * 1024
PACK_LIMIT = 53 * 1024 * 1024
STEP_LIMIT = 14 * 1024 * 1024
UPDATE_LIMIT = 20 * 1024 * 1024
HALF = 144
CUT_ROWS = 72
MARK = (8, 128)
CUT_COLUMNS = 384
F32 = jnp.float32
BF16 = jnp.bfloat16


def rotate_block(values, cosine, signed_sine):
    lane = lax.broadcasted_iota(jnp.int32, values.shape, 1)
    swapped = jnp.where(
        lane % HEAD < HEAD // 2,
        pltpu.roll(values, LANES - HEAD // 2, 1),
        pltpu.roll(values, HEAD // 2, 1),
    )
    return values * cosine + swapped * signed_sine


def adamw(weight, first_moment, second_moment, gradient, step_rate, weight_decay):
    first_new = BETA_ONE * first_moment + (1.0 - BETA_ONE) * gradient
    second_new = BETA_TWO * second_moment + (1.0 - BETA_TWO) * gradient * gradient
    fix_one = 1.0 / (1.0 - BETA_ONE**STEP)
    fix_two = 1.0 / (1.0 - BETA_TWO**STEP)
    update = first_new * fix_one / (jnp.sqrt(second_new * fix_two) + EPS_ADAM)
    return (first_new, second_new, weight - step_rate * (update + weight_decay * weight))


def adamw_rows(weight, first_moment, second_moment, gradient, step_rate, weight_decay):
    first_new = BETA_ONE * first_moment + (1.0 - BETA_ONE) * gradient
    second_new = BETA_TWO * second_moment + (1.0 - BETA_TWO) * gradient * gradient
    value = second_new * (1.0 / (1.0 - BETA_TWO**STEP))
    guess = lax.rsqrt(value)
    divisor = value * guess + EPS_ADAM
    inverse = guess * (2.0 - divisor * guess)
    update = first_new * (step_rate / (1.0 - BETA_ONE**STEP)) * inverse
    return (first_new, second_new, weight * (1.0 - step_rate * weight_decay) - update)


def dot(left, right):
    return lax.dot_general(left, right, (((1,), (0,)), ((), ())), preferred_element_type=F32)


def dot_right_t(left, right):
    return lax.dot_general(left, right, (((1,), (1,)), ((), ())), preferred_element_type=F32)


def dot_left_t(left, right):
    return lax.dot_general(left, right, (((0,), (0,)), ((), ())), preferred_element_type=F32)


def norm_scale(values):
    return lax.rsqrt(jnp.mean(values * values, axis=-1, keepdims=True) + EPS_NORM)


def norm_back(grad_normed, normed, scale_rows):
    return scale_rows * (
        grad_normed - normed * jnp.mean(grad_normed * normed, axis=-1, keepdims=True)
    )


class Weight:
    def __init__(self, shape, whole=None, own=(), parts=()):
        self.shape, self.own, self.parts = shape, own, parts
        self.arrays = [whole] if whole is not None else [a[0] for a in (*own, *parts)]
        self.split = whole is None

    def load(self, idx, refs, full):
        if not self.split:
            return refs[0]
        for ref, (_, place) in zip(refs, self.own):
            self.put(full, place(idx[0]), ref[...].astype(BF16))
        for ref, (_, (core, x, low), place) in zip(refs[len(self.own) :], self.parts):
            place = place(1 - idx[0], idx[1] ^ core, idx[2] ^ x, (idx[3] & 1) ^ low)
            rows = ref.shape[0] // HALF * HALF
            self.put(full, place, ref[:rows, :])
        return full

    def put(self, full, position, value):
        where = []
        for axis, tile in ((0, 16), (1, LANES)):
            at, size = position[axis], value.shape[axis]
            if size == self.shape[axis]:
                where.append(slice(None))
            elif isinstance(at, int):
                where.append(slice(at, at + size))
            else:
                where.append(pl.ds(pl.multiple_of(at, tile), size))
        full[tuple(where)] = value


def call(body, idx, arrays, weights, outs, scratch, busy, name, after=(), hand_on=False):
    counts = [len(w.arrays) for w in weights]
    flat = list(arrays) + [a for w in weights for a in w.arrays]
    outs = list(outs)
    split = [w for w in weights if w.split]
    hand_on = hand_on and bool(split)
    if hand_on:
        outs += [sds(split[-1].shape, BF16)]
    made = [pltpu.VMEM(w.shape, BF16) for w in (split[:-1] if hand_on else split)]

    def kernel(*refs):
        refs = list(refs)
        idx_ref = refs.pop(0)
        take = lambda n: [refs.pop(0) for _ in range(n)]
        array_refs = take(len(arrays))
        weight_refs = [take(n) for n in counts]
        take(len(after))
        out_refs = take(len(outs))
        own_scratch = take(len(scratch))
        fulls = take(len(made)) + ([out_refs.pop()] if hand_on else [])
        loads = [
            functools.partial(w.load, idx_ref, r, fulls.pop(0) if w.split else None)
            for w, r in zip(weights, weight_refs)
        ]
        body(idx_ref, array_refs, loads, out_refs, own_scratch)

    return pl.pallas_call(
        kernel,
        out_shape=tuple(outs),
        in_specs=[pl.BlockSpec(memory_space=pltpu.SMEM)]
        + [pl.BlockSpec(memory_space=pltpu.VMEM)] * len(flat)
        + [pl.BlockSpec(memory_space=pl.ANY)] * len(after),
        out_specs=tuple([pl.BlockSpec(memory_space=pltpu.VMEM)] * len(outs)),
        scratch_shapes=list(scratch) + made,
        compiler_params=pltpu.CompilerParams(vmem_limit_bytes=VMEM_LIMIT),
        cost_estimate=busy_for(busy),
        name=name,
    )(idx, *flat, *after)


def busy_for(microseconds):
    return pl.CostEstimate(flops=int(microseconds * 1e9), bytes_accessed=0, transcendentals=0)


def sds(shape, dtype):
    return jax.ShapeDtypeStruct(shape, dtype)


class Pieces:
    def __init__(self, place, parts=1, extra=0):
        self.place, self.parts, self.extra = place, parts, extra

    def outs(self):
        return [sds((self.parts, 2, 8, CUT_ROWS + self.extra, CUT_COLUMNS), BF16)] * 2

    def scratch(self, columns):
        return pltpu.VMEM((8, CUT_ROWS, columns), BF16)

    def store(self, blocks, grad, start=0):
        for i in range(8):
            rows = grad[i * CUT_ROWS : (i + 1) * CUT_ROWS].astype(BF16)
            blocks[i, :, start : start + grad.shape[1]] = rows

    def emit(self, idx, blocks, outs, under=None):
        for other_core, out in enumerate((outs[1], outs[0])):
            for part in range(self.parts):
                for owner in range(2):
                    for slot in range(8):
                        z = ((slot >> 1) & 1) | ((slot & 1) << 1)
                        block, column = self.place(
                            idx[0] ^ owner, idx[1] ^ other_core, idx[2] ^ (slot >> 2), idx[3] ^ z, part
                        )
                        columns = pl.ds(pl.multiple_of(column * CUT_COLUMNS, LANES), CUT_COLUMNS)
                        piece = blocks[block, :, columns]
                        if under is not None:
                            piece = jnp.concatenate(
                                [piece.astype(F32), under[idx[0] ^ owner]], axis=0
                            ).astype(BF16)
                        out[part, owner, slot] = piece


def head_stack(values, kv_head):
    first = kv_head * GROUP
    return jnp.concatenate(
        [values[:, (first + i) * HEAD : (first + i + 1) * HEAD] for i in range(GROUP)], axis=0
    )


def softmax_rows(query, key, allowed):
    scores = jnp.where(allowed, dot_right_t(query, key) * SCALE, MASKED)
    top = jnp.max(scores, axis=-1, keepdims=True)
    exponent = jnp.exp(scores - top)
    return exponent / jnp.sum(exponent, axis=-1, keepdims=True)


def pack_kernel(body, idx, sources, places, outs, name, after=(), limit=PACK_LIMIT):
    windows = [shape for shape, _ in places]

    def kernel(idx_ref, *refs):
        sources_in, refs = refs[: len(sources)], refs[len(sources) + len(after) :]
        out_refs, buffers, sem = refs[: len(outs)], refs[len(outs) : -1], refs[-1]
        copies = []
        for i, (source, (shape, place)) in enumerate(zip(sources_in, places)):
            where = []
            for axis, tile in ((0, 8), (1, LANES)):
                if shape[axis] == source.shape[axis]:
                    where.append(slice(None))
                else:
                    where.append(pl.ds(pl.multiple_of(place(idx_ref)[axis], tile), shape[axis]))
            copies.append(pltpu.make_async_copy(source.at[tuple(where)], buffers[i], sem.at[i]))
        for copy in copies:
            copy.start()
        for copy in copies:
            copy.wait()
        body(idx_ref, buffers, out_refs)

    return pl.pallas_call(
        kernel,
        out_shape=tuple(outs),
        in_specs=[pl.BlockSpec(memory_space=pltpu.SMEM)]
        + [pl.BlockSpec(memory_space=pltpu.HBM)] * len(sources)
        + [pl.BlockSpec(memory_space=pl.ANY)] * len(after),
        out_specs=tuple([pl.BlockSpec(memory_space=pltpu.VMEM)] * len(outs)),
        scratch_shapes=[pltpu.VMEM(w, F32) for w in windows]
        + [pltpu.SemaphoreType.DMA((len(sources),))],
        compiler_params=pltpu.CompilerParams(vmem_limit_bytes=limit),
        cost_estimate=busy_for(10),
        name=name,
    )(idx, *sources, *after)


def cast_out(idx_ref, buffers, outs):
    for buffer, out in zip(buffers, outs):
        out[...] = buffer[...].astype(BF16)


def pack_down(idx, down_t, after):
    shape = (2 * HALF, down_t.shape[1])
    window = (shape, lambda i: (i[1] * 2 * HALF, 0))
    outs = [sds(shape, BF16)]
    return pack_kernel(
        cast_out, idx, [down_t], [window], outs, "pack_down", after, STEP_LIMIT
    )[0]


def pack_first(idx, w_qkv, w_out, norm_gains, w_gate_up):
    columns = (QKV + w_out.shape[1]) // 2
    quarter = FF // 2
    windows = [((HALF, m.shape[1]), lambda i: (i[1] * HALF, 0)) for m in (w_qkv, w_out)]
    windows.append((norm_gains.shape, lambda i: (0, 0)))
    windows.append(((HALF, quarter), lambda i: (i[1] * HALF, i[2] * quarter)))
    windows.append(((HALF, quarter), lambda i: (i[1] * HALF, FF + (i[3] & 1) * quarter)))

    def body(idx_ref, buffers, outs):
        q_ref, o_ref, gains_ref = buffers[:3]
        both = jnp.concatenate([q_ref[:, columns:], o_ref[...]], axis=1)
        outs[0][:HALF, :] = jnp.where((idx_ref[3] & 1) == 0, q_ref[:, :columns], both).astype(BF16)
        outs[0][HALF:, :] = jnp.zeros((16, columns), BF16)
        outs[0][HALF : HALF + 2, : gains_ref.shape[1]] = gains_ref[...].astype(BF16)
        cast_out(idx_ref, buffers[3:], outs[1:])

    outs = [sds((HALF + 16, columns), BF16)] + [sds((HALF, quarter), BF16)] * 2
    sources = [w_qkv, w_out, norm_gains, w_gate_up, w_gate_up]
    return pack_kernel(body, idx, sources, windows, outs, "pack_first")


def attention_forward(idx, tokens_t, segments, frequency, gains, w_qkv_out):
    width, seq_length = tokens_t.shape
    split_gains = len(gains) > 1

    def body(idx_ref, arrays, loads, outs, scratch):
        x_ref, seg_ref, freq_ref = arrays[:3]
        qkv_ref, o_ref, cos_ref, sin_ref, allowed_ref, gains_ref = outs
        if split_gains:
            own = arrays[3][...].astype(BF16).astype(F32)
            other = arrays[4][HALF : HALF + 8, : width // 2].astype(F32)[:2]
            gains_ref[...] = jnp.where(
                idx_ref[0] == 0,
                jnp.concatenate([own, other], axis=1),
                jnp.concatenate([other, own], axis=1),
            )
        else:
            gains_ref[...] = arrays[3][...]
        seen_doc = jnp.broadcast_to(seg_ref[...], (seq_length, seq_length))
        own_doc = seen_doc.T
        token = lax.broadcasted_iota(jnp.int32, (seq_length, seq_length), 0)
        seen = lax.broadcasted_iota(jnp.int32, (seq_length, seq_length), 1)
        begin = jnp.sum((seen_doc < own_doc).astype(F32), axis=-1, keepdims=True)
        angles = (token.astype(F32) - begin) * freq_ref[...]
        cosine, sine = jnp.cos(angles), jnp.sin(angles)
        sine = jnp.where(seen % HEAD < HEAD // 2, -sine, sine)
        cos_ref[...] = cosine
        sin_ref[...] = sine
        allowed = ((seen_doc == own_doc) & (token >= seen)).astype(F32)
        allowed_ref[...] = allowed
        allowed = jnp.concatenate([allowed] * GROUP, axis=0) > 0.5
        x = x_ref[...].astype(F32).T
        h1 = (x * norm_scale(x) * gains_ref[0:1, :]).astype(BF16)
        projected = dot(h1, loads[0]()[:, :QKV])
        for start in range(0, ROPED, LANES):
            block = projected[:, start : start + LANES]
            qkv_ref[:, start : start + LANES] = rotate_block(block, cosine, sine).astype(BF16)
        qkv_ref[:, ROPED:QKV] = projected[:, ROPED:QKV].astype(BF16)
        qkv = qkv_ref[...]
        for kv in range(KV_HEADS):
            key = qkv[:, QUERY + kv * HEAD : QUERY + (kv + 1) * HEAD]
            value = qkv[:, ROPED + kv * HEAD : ROPED + (kv + 1) * HEAD]
            probs = softmax_rows(head_stack(qkv, kv), key, allowed).astype(BF16)
            attended = dot(probs, value).astype(BF16)
            for i in range(GROUP):
                start = (kv * GROUP + i) * HEAD
                o_ref[:, start : start + HEAD] = attended[i * seq_length : (i + 1) * seq_length]

    square = sds((seq_length, seq_length), F32)
    outs = [sds((seq_length, QKV), BF16), sds((seq_length, QUERY), BF16)]
    outs += [square, square, square, sds((2, width), F32)]
    return call(
        body,
        idx,
        [tokens_t, segments, frequency, *gains],
        [w_qkv_out],
        outs,
        [],
        1,
        "attention",
        hand_on=True,
    )


def feed_forward(idx, tokens_t, attended, gains, cotangent_t, w_qkv_out, w_gate_up, pieces, after):
    width, seq_length = tokens_t.shape

    def body(idx_ref, arrays, loads, outs, scratch):
        x_ref, o_ref, gains_ref, y_ref = arrays
        u_ref, h2_ref, ab_ref, z_ref = outs[:4]
        u = x_ref[...].astype(F32).T + dot(o_ref[...], loads[0]()[:, QKV:])
        u_ref[...] = u
        h2 = (u * norm_scale(u) * gains_ref[1:2, :]).astype(BF16)
        h2_ref[...] = h2
        ab = dot(h2, loads[1]()[...])
        ab_ref[...] = ab
        gate, up = ab[:, :FF], ab[:, FF:]
        z = (gate * jax.nn.sigmoid(gate) * up).astype(BF16)
        z_ref[...] = z
        grad = dot(y_ref[...], z)
        if pieces is None:
            outs[4][...] = grad
        else:
            pieces.store(scratch[0], grad)
            pieces.emit(idx_ref, scratch[0], outs[4:])

    outs = [
        sds((seq_length, width), F32),
        sds((seq_length, width), BF16),
        sds((seq_length, 2 * FF), F32),
        sds((seq_length, FF), BF16),
    ]
    outs += [sds((width, FF), F32)] if pieces is None else pieces.outs()
    scratch = [] if pieces is None else [pieces.scratch(FF)]
    return call(
        body,
        idx,
        [tokens_t, attended, gains, cotangent_t],
        [w_qkv_out, w_gate_up],
        outs,
        scratch,
        5,
        "feed_forward",
        after,
        True,
    )


def feed_back(idx, ab, normed_low, cotangent_t, down_t, pieces):
    width, seq_length = cotangent_t.shape

    def body(idx_ref, arrays, loads, outs, scratch):
        ab_ref, h2_ref, y_ref = arrays
        gg_ref = outs[0]
        gate, up = ab_ref[:, :FF], ab_ref[:, FF:]
        sig = jax.nn.sigmoid(gate)
        grad_hidden = dot_left_t(y_ref[...], loads[0]()[...])
        gg_ref[:, :FF] = (grad_hidden * up * sig * (1.0 + gate * (1.0 - sig))).astype(BF16)
        gg_ref[:, FF:] = (grad_hidden * gate * sig).astype(BF16)
        grad = dot_left_t(h2_ref[...], gg_ref[...])
        if pieces is None:
            outs[1][...] = grad
        else:
            pieces.store(scratch[0], grad)
            pieces.emit(idx_ref, scratch[0], outs[1:])

    outs = [sds((seq_length, 2 * FF), BF16)]
    outs += [sds((width, 2 * FF), F32)] if pieces is None else pieces.outs()
    scratch = [] if pieces is None else [pieces.scratch(2 * FF)]
    return call(
        body,
        idx,
        [ab, normed_low, cotangent_t],
        [down_t],
        outs,
        scratch,
        20,
        "feed_back",
        hand_on=True,
    )


def layer_output(middle, hidden, down_t, after):
    seq_length, width = middle.shape

    def body(ins, outs):
        outs[0][...] = (ins[0][...] + dot_right_t(ins[1][...], ins[2][...])).T.astype(BF16)

    return step(
        body, [middle, hidden, down_t], [sds((width, seq_length), BF16)], "layer_output", after, 2
    )[0]


def middle_back(idx, cotangent_t, middle, gated, gains, w_gate_up, w_qkv_out, after):
    width, seq_length = cotangent_t.shape

    def body(idx_ref, arrays, loads, outs, scratch):
        y_ref, u_ref, gg_ref, gains_ref = arrays
        gu_ref, go_ref, gain_ref = outs
        u = u_ref[...]
        scale_two = norm_scale(u)
        normed = u * scale_two
        grad_normed = dot_right_t(gg_ref[...], loads[0]()[...])
        gain_ref[...] = jnp.sum(grad_normed * normed, axis=0, keepdims=True)
        gu = y_ref[...].astype(F32).T + norm_back(
            grad_normed * gains_ref[1:2, :], normed, scale_two
        )
        gu_ref[...] = gu
        go_ref[...] = dot_right_t(gu.astype(BF16), loads[1]()[:, QKV:]).astype(BF16)

    outs = [sds((seq_length, width), F32), sds((seq_length, width), BF16), sds((1, width), F32)]
    return call(
        body,
        idx,
        [cotangent_t, middle, gated, gains],
        [w_gate_up, w_qkv_out],
        outs,
        [],
        20,
        "middle_back",
        after,
    )


def attention_back(
    idx, tokens_t, grad_middle, grad_attended, gain_two, qkv, attended, tables, gains, w_qkv, pieces, after
):
    width, seq_length = tokens_t.shape

    def body(idx_ref, arrays, loads, outs, scratch):
        x_ref, gu_ref, go_ref, gain_two_ref, qkv_ref, o_ref = arrays[:6]
        cos_ref, sin_ref, allowed_ref, gains_ref = arrays[6:]
        grad_ref = outs[0]
        grad_proj, gp_ref, gain_rows, *blocks = scratch
        gu, go = gu_ref[...], go_ref[...]
        gu_low = gu.astype(BF16)
        grad_gain_two = gain_two_ref[...]
        allowed = jnp.concatenate([allowed_ref[...]] * GROUP, axis=0) > 0.5
        qkv_values = qkv_ref[...]
        for kv in range(KV_HEADS):
            key = qkv_values[:, QUERY + kv * HEAD : QUERY + (kv + 1) * HEAD]
            value = qkv_values[:, ROPED + kv * HEAD : ROPED + (kv + 1) * HEAD]
            query = head_stack(qkv_values, kv)
            grad_out = head_stack(go, kv)
            probs = softmax_rows(query, key, allowed)
            grad_probs = dot_right_t(grad_out, value)
            row_delta = jnp.sum(probs * grad_probs, axis=-1, keepdims=True)
            gs = (probs * (grad_probs - row_delta)).astype(BF16)
            grad_query = dot(gs, key) * SCALE
            for i in range(GROUP):
                start = (kv * GROUP + i) * HEAD
                grad_proj[:, start : start + HEAD] = grad_query[
                    i * seq_length : (i + 1) * seq_length
                ]
            start = QUERY + kv * HEAD
            grad_proj[:, start : start + HEAD] = dot_left_t(gs, query) * SCALE
            start = ROPED + kv * HEAD
            grad_proj[:, start : start + HEAD] = dot_left_t(probs.astype(BF16), grad_out)
        for start in range(0, ROPED, LANES):
            gp_ref[:, start : start + LANES] = rotate_block(
                grad_proj[:, start : start + LANES], cos_ref[...], -sin_ref[...]
            ).astype(BF16)
        gp_ref[:, ROPED:QKV] = grad_proj[:, ROPED:QKV].astype(BF16)
        x = x_ref[...].astype(F32).T
        scale_one = norm_scale(x)
        normed = x * scale_one
        h1 = (normed * gains_ref[0:1, :]).astype(BF16)
        grad_qkv = dot_left_t(h1, gp_ref[...])
        grad_out = dot_left_t(o_ref[...], gu_low)
        grad_normed = dot_right_t(gp_ref[...], loads[0]()[:, :QKV])
        grad_gain_one = jnp.sum(grad_normed * normed, axis=0, keepdims=True)
        if pieces is None:
            outs[1][:, :QKV] = grad_qkv
            outs[1][:, QKV:] = grad_out
            outs[2][0:1, :] = grad_gain_one
            outs[2][1:2, :] = grad_gain_two
        else:
            pieces.store(blocks[0], grad_qkv)
            pieces.store(blocks[0], grad_out, QKV)
            half = width // 2
            gain_rows[...] = jnp.zeros_like(gain_rows)
            for owner in range(2):
                columns = slice(owner * half, (owner + 1) * half)
                gain_rows[owner, 0:1, :half] = grad_gain_one[:, columns]
                gain_rows[owner, 1:2, :half] = grad_gain_two[:, columns]
            pieces.emit(idx_ref, blocks[0], outs[1:3], gain_rows)
            outs[3][...] = jnp.zeros_like(outs[3])
        grad_ref[...] = (
            (gu + norm_back(grad_normed * gains_ref[0:1, :], normed, scale_one)).T
        ).astype(BF16)

    outs = [sds((width, seq_length), BF16)]
    scratch = [
        pltpu.VMEM((seq_length, QKV), F32),
        pltpu.VMEM((seq_length, QKV), BF16),
        pltpu.VMEM((2, 8, CUT_COLUMNS), F32),
    ]
    if pieces is None:
        outs += [sds((width, QKV + width), F32), sds((2, width), F32)]
    else:
        outs += pieces.outs() + [sds(MARK, F32)]
        scratch += [pieces.scratch(QKV + width)]
    return call(
        body,
        idx,
        [tokens_t, grad_middle, grad_attended, gain_two, qkv, attended, *tables, gains],
        [w_qkv],
        outs,
        scratch,
        20,
        "attention_back",
        after,
    )


def step(body, arrays, outs, name, after=(), busy=20):
    def kernel(*refs):
        body(refs[: len(arrays)], refs[len(arrays) + len(after) :])

    return pl.pallas_call(
        kernel,
        out_shape=tuple(outs),
        in_specs=[pl.BlockSpec(memory_space=pltpu.VMEM)] * len(arrays)
        + [pl.BlockSpec(memory_space=pl.ANY)] * len(after),
        out_specs=tuple([pl.BlockSpec(memory_space=pltpu.VMEM)] * len(outs)),
        compiler_params=pltpu.CompilerParams(vmem_limit_bytes=STEP_LIMIT),
        cost_estimate=busy_for(busy),
        name=name,
    )(*arrays, *after)


def pass_on(ins, outs):
    outs[0][...] = ins[0][...]


def add_split(keep, arrived, axis, send_ref, keep_ref):
    total = keep[...].astype(F32) + arrived[...].astype(F32)
    low, high = lax.index_in_dim(total, 0, axis, False), lax.index_in_dim(total, 1, axis, False)
    send_ref[...] = high.astype(BF16)
    keep_ref[...] = low


def add_step(jobs, name, after, busy=20):
    arrays, outs = [], []
    for keep, arrived, axis in jobs:
        arrays += [keep, arrived]
        shape = keep.shape[:axis] + keep.shape[axis + 1 :]
        outs += [sds(shape, BF16), sds(shape, F32)]

    def body(ins, out_refs):
        for i, (_, _, axis) in enumerate(jobs):
            add_split(ins[2 * i], ins[2 * i + 1], axis, out_refs[2 * i], out_refs[2 * i + 1])

    flat = step(body, arrays, outs, name, after, busy)
    return [(flat[2 * i], flat[2 * i + 1]) for i in range(len(jobs))]


def update_rows(idx, shares, place, height, chunk, state, earlier, gains, name, after, busy=20):
    count = len(state) // 3
    columns = [a.shape[1] for a in state[:count]]
    starts = [sum(-(-c // LANES) * LANES for c in columns[:k]) for k in range(count + 1)]
    chunks = height // chunk
    order = [(k, count + k, 2 * count + k) for k in range(count)]

    def kernel(idx_ref, *refs):
        refs = list(refs)
        take = lambda n: [refs.pop(0) for _ in range(n)]
        share_refs = take(len(shares))
        state_refs, gain_refs = take(3 * count), take(len(gains))
        take(len(earlier) + len(after))
        outs, gain_outs, (mark,) = take(3 * count), take(len(gains)), take(1)
        buffers, (full, sem) = take(3 * count), refs
        mark[...] = jnp.zeros_like(mark)
        copies = []
        for share, (far, _) in enumerate(shares):
            piece_ref = share_refs[share]
            for part in range(piece_ref.shape[0]):
                for x in range(2):
                    for z in range(4):
                        rel = z ^ idx_ref[3]
                        slot = ((rel & 1) << 1) | (rel >> 1)
                        piece = piece_ref[part, x, slot].astype(F32)[:CUT_ROWS]
                        row, cuts = place(part, idx_ref[2] ^ x, z)
                        rows = pl.ds(pl.multiple_of(share * height + row, 8), CUT_ROWS)
                        for begin, size, to in cuts:
                            if isinstance(to, int):
                                where = slice(to, to + size)
                            else:
                                where = pl.ds(pl.multiple_of(to, LANES), size)
                            full[rows, where] = piece[:, begin : begin + size]
            base = (idx_ref[1] ^ far) * height
            for at_chunk in range(chunks):

                def eight_rows(i, carry, at_chunk=at_chunk, share=share, base=base):
                    at_row = at_chunk * chunk + i * 8
                    near_rows = pl.ds(pl.multiple_of(share * height + at_row, 8), 8)
                    rows = pl.ds(pl.multiple_of(base + at_row, 8), 8)
                    for k in range(count):
                        for at in range(0, columns[k], 768):
                            size = min(768, columns[k] - at)
                            where = slice(at, at + size)
                            results = adamw_rows(
                                *[state_refs[j][rows, where] for j in order[k]],
                                full[near_rows, starts[k] + at : starts[k] + at + size],
                                RATE_MATRIX,
                                DECAY_MATRIX,
                            )
                            for j, result in zip(order[k], results):
                                buffers[j][near_rows, where] = result
                    return carry

                lax.fori_loop(0, chunk // 8, eight_rows, 0, unroll=3)
                near_rows = pl.ds(share * height + at_chunk * chunk, chunk)
                rows = pl.ds(pl.multiple_of(base + at_chunk * chunk, 8), chunk)
                for j in range(3 * count):
                    copy = pltpu.make_async_copy(
                        buffers[j].at[near_rows],
                        outs[j].at[rows],
                        sem.at[share * chunks + at_chunk, j],
                    )
                    copy.start()
                    copies.append(copy)
        if gains:
            gradient = share_refs[0][0, 0, 0, CUT_ROWS:, :].astype(F32)[:2, : gains[0].shape[1]]
            results = adamw_rows(*[g[...] for g in gain_refs], gradient, RATE_GAIN, 0.0)
            for out, result in zip(gain_outs, results):
                out[...] = result
        for copy in copies:
            copy.wait()

    vmem, anywhere = pl.BlockSpec(memory_space=pltpu.VMEM), pl.BlockSpec(memory_space=pl.ANY)
    first_earlier = 1 + len(shares) + 3 * count + len(gains)
    total = len(shares) * height
    return pl.pallas_call(
        kernel,
        out_shape=tuple(sds(a.shape, F32) for a in [*state, *gains]) + (sds(MARK, F32),),
        in_specs=[pl.BlockSpec(memory_space=pltpu.SMEM)]
        + [vmem] * (len(shares) + 3 * count + len(gains))
        + [anywhere] * (len(earlier) + len(after)),
        out_specs=tuple([anywhere] * (3 * count) + [vmem] * (len(gains) + 1)),
        scratch_shapes=[pltpu.VMEM((total, a.shape[1]), F32) for a in state]
        + [pltpu.VMEM((total, starts[-1]), F32)]
        + [pltpu.SemaphoreType.DMA((len(shares) * chunks, 3 * count))],
        input_output_aliases={first_earlier + i: i for i in range(len(earlier))},
        compiler_params=pltpu.CompilerParams(vmem_limit_bytes=UPDATE_LIMIT),
        cost_estimate=busy_for(busy),
        name=name,
    )(idx, *[p for _, p in shares], *state, *gains, *earlier, *after)


def swap(values, axis, mask):
    size = lax.axis_size(axis)
    return lax.ppermute(values, axis, [(i, i ^ mask) for i in range(size)])


over_y = functools.partial(swap, axis="shard", mask=1)
over_core = functools.partial(swap, axis="dp", mask=1)
over_x = functools.partial(swap, axis="dp", mask=2)
over_z_low = functools.partial(swap, axis="dp", mask=4)
over_z_high = functools.partial(swap, axis="dp", mask=8)


def per_device(
    tokens,
    segments,
    cotangent,
    w_qkv,
    w_out,
    w_gate_up,
    w_down,
    norm_gains,
    first_qkv,
    first_out,
    first_gate_up,
    first_down,
    first_gains,
    second_qkv,
    second_out,
    second_gate_up,
    second_down,
    second_gains,
):
    groups = lax.axis_size("shard")
    replicas = lax.axis_size("dp")
    fast = groups == 2 and replicas == 16
    place_dp = lax.axis_index("dp")
    owner = lax.axis_index("shard")
    idx = jnp.stack([owner, place_dp & 1, (place_dp >> 1) & 1, place_dp >> 2]).astype(jnp.int32)
    x_t, y_t = tokens[0].T, cotangent[0].T
    width, seq_length = x_t.shape
    rows, down_rows = w_qkv.shape[0], w_down.shape[0]
    down_t, first_down_t, second_down_t = w_down.T, first_down.T, second_down.T
    half_size = HEAD // 2
    frequency = ROPE_BASE ** (-(np.arange(half_size) * 2.0 / HEAD))
    frequency = jnp.asarray(np.tile(frequency, 4)[None], F32)
    if fast:
        qo_near, by_x, by_low = pack_first(idx, w_qkv, w_out, norm_gains, w_gate_up)
        qo_near, by_x, by_low = over_y(qo_near), over_y(by_x), over_y(by_low)
        down_near = over_y(pack_down(idx, down_t, (by_low,)))
        by_x_next, by_low_next = over_x(by_x), over_z_low(by_low)
        qo_near_low = over_z_low(qo_near)
        gains = (norm_gains, qo_near)
        (low_far,) = step(
            pass_on, [over_core(by_low_next)], [sds(by_low.shape, BF16)], "pass_on_low", (), 1
        )
        own_rows = lambda o: (o * rows, 0)
        own_rows_out = lambda o: (o * rows, QKV)
        qo_place = lambda o, c, x, low: (o * rows + c * HALF, low * ((QKV + width) // 2))
        x_place = lambda o, c, x, low: (o * rows + c * HALF, x * (FF // 2))
        low_place = lambda o, c, x, low: (o * rows + c * HALF, FF + low * (FF // 2))
        mat_qkv_out = Weight(
            (width, QKV + width),
            own=[(w_qkv, own_rows), (w_out, own_rows_out)],
            parts=[
                (qo_near, (0, 0, 0), qo_place),
                (qo_near_low, (0, 0, 1), qo_place),
                (over_core(qo_near), (1, 0, 0), qo_place),
                (over_core(qo_near_low), (1, 0, 1), qo_place),
            ],
        )
        mat_gate_up = Weight(
            (width, 2 * FF),
            own=[(w_gate_up, own_rows)],
            parts=[
                (by_x, (0, 0, 0), x_place),
                (by_x_next, (0, 1, 0), x_place),
                (over_core(by_x), (1, 0, 0), x_place),
                (over_core(by_x_next), (1, 1, 0), x_place),
                (by_low, (0, 0, 0), low_place),
                (by_low_next, (0, 0, 1), low_place),
                (over_core(by_low), (1, 0, 0), low_place),
                (low_far, (1, 0, 1), low_place),
            ],
        )
        cut_qkv_out = Pieces(lambda o, c, x, z, p: (o * 4 + c * 2 + x, z), extra=8)
        cut_gate_up = Pieces(lambda o, c, x, z, p: (o * 4 + c * 2 + p, x * 4 + z), parts=2)
        cut_down = Pieces(lambda o, c, x, z, p: (c * 4 + x * 2 + (z >> 1), o * 2 + (z & 1)))
    else:
        gains = (
            lax.all_gather(norm_gains.astype(BF16), "shard", axis=1, tiled=True).astype(F32),
        )
        mat_qkv, mat_out, mat_gate_up, mat_down = [
            lax.all_gather(m.astype(BF16), "shard", axis=0, tiled=True)
            for m in (w_qkv, w_out, w_gate_up, w_down)
        ]
        mat_qkv_out, mat_gate_up, mat_down = [
            Weight(m.shape, whole=m)
            for m in (jnp.concatenate([mat_qkv, mat_out], axis=1), mat_gate_up, mat_down.T)
        ]
        cut_qkv_out = cut_gate_up = cut_down = None

    qkv, attended, *tables, gains, whole = attention_forward(
        idx, x_t, segments, frequency, gains, mat_qkv_out
    ) + (() if fast else (None,))
    if fast:
        mat_qkv_out = Weight(whole.shape, whole=whole)
    middle, normed_low, ab, hidden, *grad_down = feed_forward(
        idx, x_t, attended, gains, y_t, mat_qkv_out, mat_gate_up, cut_down, ()
    )
    after = ()
    if fast:
        whole = grad_down.pop()
        mat_gate_up = Weight(whole.shape, whole=whole)

        (down_near,) = step(
            pass_on, [down_near], [sds(down_near.shape, BF16)], "pass_on", (attended,), 0.1
        )
        down_place = lambda o, c, x, low: (c * 2 * HALF, o * down_rows)
        mat_down = Weight(
            (width, FF),
            own=[(down_t, lambda o: (0, o * down_rows))],
            parts=[
                (down_near, (0, 0, 0), down_place),
                (over_core(down_near), (1, 0, 0), down_place),
            ],
        )
    if fast:
        arrived_down = over_core(grad_down[0])
    gated, *grad_gate_up = feed_back(idx, ab, normed_low, y_t, mat_down, cut_gate_up)
    if not fast:
        output = layer_output(middle, hidden, mat_down.arrays[0], ())
    if fast:
        down_whole = grad_gate_up.pop()
        cut = lambda a, *lead: a.reshape(*lead, *a.shape[-2:])
        arrived_gate_up = over_core(grad_gate_up[0])
        ((send, keep_down),) = add_step(
            [(grad_down[1][0], arrived_down[0], 0)], "down_core", (gated,)
        )
        arrived_down = over_y(send)
        after = (keep_down,)
    grad_middle, grad_attended, gain_two = middle_back(
        idx, y_t, middle, gated, gains, mat_gate_up, mat_qkv_out, after
    )
    if fast:
        halves = [
            [cut(a[p], *lead) for a in (grad_gate_up[1], arrived_gate_up)]
            for p, lead in ((0, (2, 2, 4)), (1, (4, 2, 2)))
        ]
        (send_up, keep_up), (send_low, keep_low) = add_step(
            [(*halves[0], 1), (*halves[1], 1)], "gate_up_core", (grad_middle,)
        )
        arrived_up, arrived_low = over_x(send_up), over_z_low(send_low)
        after = (keep_up,)
    token_grad, *grad_qkv_out = attention_back(
        idx,
        x_t,
        grad_middle,
        grad_attended,
        gain_two,
        qkv,
        attended,
        tables,
        gains,
        mat_qkv_out,
        cut_qkv_out,
        after,
    )
    if fast:

        arrived_qkv_out = over_core(grad_qkv_out[0])
        piece = (CUT_ROWS, CUT_COLUMNS)
        taller = (CUT_ROWS + 8, CUT_COLUMNS)
        ((send, keep_down),) = add_step(
            [(cut(keep_down, 2, 4), cut(arrived_down, 2, 4), 0)], "down_y", (grad_qkv_out[2],)
        )
        arrived_down = over_x(send)
        ((send, keep_qkv_out),) = add_step(
            [(grad_qkv_out[1][0], arrived_qkv_out[0], 0)], "qkv_out_core", (keep_down,), 0.1
        )
        arrived_qkv_out = over_y(send)
        (send_up, keep_up), (send_low, keep_low) = add_step(
            [
                (cut(keep_up, 2, 2, 2), cut(arrived_up, 2, 2, 2), 1),
                (cut(keep_low, 2, 2, 2), cut(arrived_low, 2, 2, 2), 1),
            ],
            "up_x_low_z",
            (keep_qkv_out,),
            20,
        )
        arrived_up, arrived_low = over_z_low(send_up), over_x(send_low)
        ((send, keep_down),) = add_step(
            [(cut(keep_down, 2, 2), cut(arrived_down, 2, 2), 0)], "down_x", (keep_up,), 0.1
        )
        arrived_down = over_z_low(send)

        def columns(ins, outs):
            total = ins[0][...] + ins[1][...].astype(F32)
            outs[0][...] = total[1].astype(BF16)
            outs[1][...] = total[0]
            total = ins[2][...] + ins[3][...].astype(F32)
            outs[2][0], outs[2][1] = total[0, 1].astype(BF16), total[1, 1].astype(BF16)
            outs[3][...] = total[:, 0]
            total = ins[4][...] + ins[5][...].astype(F32)
            outs[2][2] = total[1].astype(BF16)
            outs[4][...] = total[0]

        ((send, keep_qkv_out),) = add_step(
            [(cut(keep_qkv_out, 2, 4), cut(arrived_qkv_out, 2, 4), 0)],
            "qkv_out_y",
            (keep_down,),
            0.1,
        )
        arrived_qkv_out = over_x(send)
        send_up, keep_up, send, keep_low, keep_down = step(
            columns,
            [keep_up, arrived_up, keep_low, arrived_low, keep_down, arrived_down],
            [
                *(sds((2, *piece), BF16), sds((2, *piece), F32)),
                *(sds((3, *piece), BF16), sds((2, *piece), F32)),
                sds(piece, F32),
            ],
            "columns",
            (keep_qkv_out,),
        )
        arrived_up, arrived = over_y(send_up), over_z_high(send)

        def planes(ins, outs):
            keep_up, arrived_up, keep_low, arrived, keep_down, keep_qkv_out, arrived_qkv_out = ins
            total = keep_up[...] + arrived_up[...].astype(F32)
            outs[0][0] = total[1].astype(BF16)
            outs[1][0] = total[0]
            outs[0][1] = (keep_down[...] + arrived[2].astype(F32)).astype(BF16)
            outs[2][...] = (keep_low[1] + arrived[1].astype(F32)).astype(BF16)
            outs[1][1] = keep_low[0] + arrived[0].astype(F32)
            total = keep_qkv_out[...] + arrived_qkv_out[...].astype(F32)
            outs[3][...] = total[1].astype(BF16)
            outs[4][...] = total[0]

        send, keep, send_low, send_qkv_out, keep_qkv_out = step(
            planes,
            [
                *(keep_up, arrived_up, keep_low, arrived, keep_down),
                *(cut(keep_qkv_out, 2, 2), cut(arrived_qkv_out, 2, 2)),
            ],
            [
                *(sds((2, *piece), BF16), sds((2, *piece), F32), sds(piece, BF16)),
                *(sds((2, *taller), BF16), sds((2, *taller), F32)),
            ],
            "planes",
        )
        arrived, arrived_low = over_z_high(send), over_y(send_low)
        arrived_qkv_out = over_z_low(send_qkv_out)

        def lines(ins, outs):
            send, keep, arrived, arrived_low, keep_qkv_out, arrived_qkv_out = ins
            total = keep_qkv_out[...] + arrived_qkv_out[...].astype(F32)
            outs[0][0] = total[1].astype(BF16)
            outs[1][...] = total[0]
            for part, came in enumerate((arrived[0], arrived_low[...])):
                total = keep[part] + came.astype(F32)
                total = jnp.concatenate([total, jnp.zeros((8, CUT_COLUMNS), F32)], axis=0)
                outs[0][part + 1] = total.astype(BF16)
            outs[2][0], outs[2][1] = send[1], arrived[1]

        pieces, keep_qkv_out, near_down = step(
            lines,
            [send, keep, arrived, arrived_low, keep_qkv_out, arrived_qkv_out],
            [sds((3, *taller), BF16), sds(taller, F32), sds((2, *piece), BF16)],
            "lines",
            (w_gate_up, first_gate_up, second_gate_up),
        )
        arrived, down_low = over_z_high(pieces), over_z_low(near_down)

        def share_high(ins, outs):
            pieces, arrived, keep_qkv_out, near_down, down_low = ins
            for high in range(2):
                outs[0][0, high], outs[0][1, high] = near_down[high], down_low[high]
            outs[0][2, 0], outs[0][2, 1] = pieces[1, :CUT_ROWS], arrived[1, :CUT_ROWS]
            outs[1][0], outs[1][1] = pieces[2, :CUT_ROWS], arrived[2, :CUT_ROWS]
            outs[2][...] = (keep_qkv_out[...] + arrived[0].astype(F32)).astype(BF16)

        near_x, near_low, piece_qkv_out = step(
            share_high,
            [pieces, arrived, keep_qkv_out, near_down, down_low],
            [sds((3, 2, *piece), BF16), sds((2, *piece), BF16), sds(taller, BF16)],
            "share_high",
            (
                *(w_qkv, w_out, first_qkv, first_out, second_qkv, second_out),
                *(down_t, first_down_t, second_down_t, first_gains, second_gains),
            ),
        )
        arrived_x, low_low = over_x(near_x), over_z_low(near_low)
        qkv_out_high = over_z_high(piece_qkv_out)
        output = layer_output(middle, hidden, down_whole, (near_x,))

        def share_next(ins, outs):
            near_x, arrived_x, near_low, low_low = ins
            outs[0][0], outs[0][1] = near_x[2], arrived_x[2]
            outs[1][0], outs[1][1] = near_low[...], low_low[...]
            for low in range(2):
                for high in range(2):
                    outs[2][0, 0, low * 2 + high] = near_x[low, high]
                    outs[2][0, 1, low * 2 + high] = arrived_x[low, high]

        near_up, near_low, near_down = step(
            share_next,
            [near_x, arrived_x, near_low, low_low],
            [
                *(sds((2, 2, *piece), BF16), sds((2, 2, *piece), BF16)),
                sds((1, 2, 4, *piece), BF16),
            ],
            "share_next",
            (qkv_out_high,),
        )
        far_down = over_core(near_down)
        up_low, low_x = over_z_low(near_up), over_x(near_low)

        def share_qkv_out_high(ins, outs):
            outs[0][0], outs[0][1] = ins[0][...], ins[1][...]

        (near_qkv_out,) = step(
            share_qkv_out_high,
            [piece_qkv_out, qkv_out_high],
            [sds((2, *taller), BF16)],
            "share_qkv_out_high",
            (near_up,),
        )
        qkv_out_x, qkv_out_low = over_x(near_qkv_out), over_z_low(near_qkv_out)
        qkv_out_both = swap(near_qkv_out, "dp", 6)
        one_down, two_down, next_down, mark = update_rows(
            idx,
            [(0, near_down), (1, far_down)],
            lambda p, x, z: (
                (x * 2 + (z >> 1)) * CUT_ROWS,
                [(0, CUT_COLUMNS, (z & 1) * CUT_COLUMNS)],
            ),
            2 * HALF,
            96,
            [down_t, first_down_t, second_down_t],
            (),
            (),
            "update_down",
            (near_qkv_out,),
            0.1,
        )

        def share_gate_up(ins, outs):
            for near in range(2):
                for far in range(2):
                    for high in range(2):
                        outs[0][0, near, far * 2 + high] = ins[far][near, high]
                        outs[0][1, far, near * 2 + high] = ins[2 + far][near, high]

        (near_gate_up,) = step(
            share_gate_up,
            [near_up, up_low, near_low, low_x],
            [sds((2, 2, 4, *piece), BF16)],
            "share_gate_up",
            (mark,),
        )
        far_gate_up = over_core(near_gate_up)
        place_gate_up = lambda p, x, z: (p * CUT_ROWS, [(0, CUT_COLUMNS, (x * 4 + z) * CUT_COLUMNS)])
        state_gate_up = [w_gate_up, first_gate_up, second_gate_up]
        *near_state, mark = update_rows(
            idx,
            [(0, near_gate_up)],
            place_gate_up,
            HALF,
            24,
            state_gate_up,
            (),
            (),
            "update_gate_up_near",
            (),
        )

        def share_qkv_out(ins, outs):
            for x in range(2):
                for low in range(2):
                    for high in range(2):
                        outs[0][0, x, low * 2 + high] = ins[low * 2 + x][high]

        (near_qkv_out,) = step(
            share_qkv_out,
            [near_qkv_out, qkv_out_x, qkv_out_low, qkv_out_both],
            [sds((1, 2, 4, *taller), BF16)],
            "share_qkv_out",
            (mark,),
        )
        far_qkv_out = over_core(near_qkv_out)
        one_gate_up, two_gate_up, next_gate_up, mark = update_rows(
            idx,
            [(1, far_gate_up)],
            place_gate_up,
            HALF,
            24,
            state_gate_up,
            near_state,
            (),
            "update_gate_up_far",
            (near_qkv_out,),
        )
        cuts = [[(0, 384, 0)], [(0, 384, 384)], [(0, 192, 768), (192, 192, 1024)], [(0, 384, 1216)]]
        updated = update_rows(
            idx,
            [(0, near_qkv_out), (1, far_qkv_out)],
            lambda p, x, z: (x * CUT_ROWS, cuts[z]),
            HALF,
            48,
            [w_qkv, w_out, first_qkv, first_out, second_qkv, second_out],
            (),
            (norm_gains, first_gains, second_gains),
            "update_qkv_out",
            (mark,),
        )
        one_qkv, one_out, two_qkv, two_out, next_qkv, next_out = updated[:6]
        one_gains, two_gains, next_gains = updated[6:9]
    else:
        sums = lax.psum((*grad_qkv_out, grad_gate_up[0], grad_down[0].T), ("dp", "shard"))
        grad_qkv_out, grad_gains, grad_gate_up, grad_down = sums

        def own(grad, axis=0):
            size = grad.shape[axis] // groups
            return lax.dynamic_slice_in_dim(grad, owner * size, size, axis)

        one_qkv, two_qkv, next_qkv = adamw(
            w_qkv, first_qkv, second_qkv, own(grad_qkv_out[:, :QKV]), RATE_MATRIX, DECAY_MATRIX
        )
        one_out, two_out, next_out = adamw(
            w_out, first_out, second_out, own(grad_qkv_out[:, QKV:]), RATE_MATRIX, DECAY_MATRIX
        )
        one_gate_up, two_gate_up, next_gate_up = adamw(
            w_gate_up, first_gate_up, second_gate_up, own(grad_gate_up), RATE_MATRIX, DECAY_MATRIX
        )
        one_down, two_down, next_down = [
            a.T
            for a in adamw(
                w_down, first_down, second_down, own(grad_down), RATE_MATRIX, DECAY_MATRIX
            )
        ]
        one_gains, two_gains, next_gains = adamw(
            norm_gains, first_gains, second_gains, own(grad_gains, 1), RATE_GAIN, 0.0
        )
    one_down, two_down, next_down = one_down.T, two_down.T, next_down.T
    return (
        output.T[None],
        token_grad.T[None],
        one_qkv,
        one_out,
        one_gate_up,
        one_down,
        one_gains,
        two_qkv,
        two_out,
        two_gate_up,
        two_down,
        two_gains,
        next_qkv,
        next_out,
        next_gate_up,
        next_down,
        next_gains,
    )


def solution(mesh):
    return jax.shard_map(
        per_device,
        mesh=mesh,
        in_specs=(
            P(("dp", "shard"), None, None),
            P(("dp", "shard"), None),
            P(("dp", "shard"), None, None),
            P("shard", None),
            P("shard", None),
            P("shard", None),
            P("shard", None),
            P(None, "shard"),
            P("shard", None),
            P("shard", None),
            P("shard", None),
            P("shard", None),
            P(None, "shard"),
            P("shard", None),
            P("shard", None),
            P("shard", None),
            P("shard", None),
            P(None, "shard"),
        ),
        out_specs=(
            P(("dp", "shard"), None, None),
            P(("dp", "shard"), None, None),
            P("shard", None),
            P("shard", None),
            P("shard", None),
            P("shard", None),
            P(None, "shard"),
            P("shard", None),
            P("shard", None),
            P("shard", None),
            P("shard", None),
            P(None, "shard"),
            P("shard", None),
            P("shard", None),
            P("shard", None),
            P("shard", None),
            P(None, "shard"),
        ),
        check_vma=False,
    )
```

```python
import functools

import jax
import jax.numpy as jnp
import numpy as np
from jax import lax
from jax.experimental import pallas as pl
from jax.experimental.pallas import tpu as pltpu
from jax.sharding import PartitionSpec as P

HEADS = 9
KV_HEADS = 3
GROUP = HEADS // KV_HEADS
HEAD = 64
FF = 1536
STEP = 10
QUERY = HEADS * HEAD
ROPED = (HEADS + KV_HEADS) * HEAD
QKV = (HEADS + 2 * KV_HEADS) * HEAD
LANES = 128

EPS_NORM = 1e-05
ROPE_BASE = 100000.0
BETA_ONE = 0.9
BETA_TWO = 0.95
RATE_MATRIX = 0.1
RATE_GAIN = 0.3
DECAY_MATRIX = 0.1
EPS_ADAM = 1e-08
MASKED = -1e30
SCALE = float(HEAD) ** (-0.5)
VMEM_LIMIT = 32 * 1024 * 1024
PACK_LIMIT = 53 * 1024 * 1024
STEP_LIMIT = 14 * 1024 * 1024
UPDATE_LIMIT = 20 * 1024 * 1024
HALF = 144
CUT_ROWS = 72
MARK = (8, 128)
CUT_COLUMNS = 384
F32 = jnp.float32
BF16 = jnp.bfloat16


def rotate_block(values, cosine, signed_sine):
    lane = lax.broadcasted_iota(jnp.int32, values.shape, 1)
    swapped = jnp.where(
        lane % HEAD < HEAD // 2,
        pltpu.roll(values, LANES - HEAD // 2, 1),
        pltpu.roll(values, HEAD // 2, 1),
    )
    return values * cosine + swapped * signed_sine


def adamw(weight, first_moment, second_moment, gradient, step_rate, weight_decay):
    first_new = BETA_ONE * first_moment + (1.0 - BETA_ONE) * gradient
    second_new = BETA_TWO * second_moment + (1.0 - BETA_TWO) * gradient * gradient
    fix_one = 1.0 / (1.0 - BETA_ONE**STEP)
    fix_two = 1.0 / (1.0 - BETA_TWO**STEP)
    update = first_new * fix_one / (jnp.sqrt(second_new * fix_two) + EPS_ADAM)
    return (first_new, second_new, weight - step_rate * (update + weight_decay * weight))


def adamw_rows(weight, first_moment, second_moment, gradient, step_rate, weight_decay):
    first_new = BETA_ONE * first_moment + (1.0 - BETA_ONE) * gradient
    second_new = BETA_TWO * second_moment + (1.0 - BETA_TWO) * gradient * gradient
    value = second_new * (1.0 / (1.0 - BETA_TWO**STEP))
    guess = lax.rsqrt(value)
    divisor = value * guess + EPS_ADAM
    inverse = guess * (2.0 - divisor * guess)
    update = first_new * (step_rate / (1.0 - BETA_ONE**STEP)) * inverse
    return (first_new, second_new, weight * (1.0 - step_rate * weight_decay) - update)


def dot(left, right):
    return lax.dot_general(left, right, (((1,), (0,)), ((), ())), preferred_element_type=F32)


def dot_right_t(left, right):
    return lax.dot_general(left, right, (((1,), (1,)), ((), ())), preferred_element_type=F32)


def dot_left_t(left, right):
    return lax.dot_general(left, right, (((0,), (0,)), ((), ())), preferred_element_type=F32)


def norm_scale(values):
    return lax.rsqrt(jnp.mean(values * values, axis=-1, keepdims=True) + EPS_NORM)


def norm_back(grad_normed, normed, scale_rows):
    return scale_rows * (
        grad_normed - normed * jnp.mean(grad_normed * normed, axis=-1, keepdims=True)
    )


class Weight:
    def __init__(self, shape, whole=None, own=(), parts=()):
        self.shape, self.own, self.parts = shape, own, parts
        self.arrays = [whole] if whole is not None else [a[0] for a in (*own, *parts)]
        self.split = whole is None

    def load(self, idx, refs, full):
        if not self.split:
            return refs[0]
        for ref, (_, place) in zip(refs, self.own):
            self.put(full, place(idx[0]), ref[...].astype(BF16))
        for ref, (_, (core, x, low), place) in zip(refs[len(self.own) :], self.parts):
            place = place(1 - idx[0], idx[1] ^ core, idx[2] ^ x, (idx[3] & 1) ^ low)
            rows = ref.shape[0] // HALF * HALF
            self.put(full, place, ref[:rows, :])
        return full

    def put(self, full, position, value):
        where = []
        for axis, tile in ((0, 16), (1, LANES)):
            at, size = position[axis], value.shape[axis]
            if size == self.shape[axis]:
                where.append(slice(None))
            elif isinstance(at, int):
                where.append(slice(at, at + size))
            else:
                where.append(pl.ds(pl.multiple_of(at, tile), size))
        full[tuple(where)] = value


def call(body, idx, arrays, weights, outs, scratch, busy, name, after=(), hand_on=False):
    counts = [len(w.arrays) for w in weights]
    flat = list(arrays) + [a for w in weights for a in w.arrays]
    outs = list(outs)
    split = [w for w in weights if w.split]
    hand_on = hand_on and bool(split)
    if hand_on:
        outs += [sds(split[-1].shape, BF16)]
    made = [pltpu.VMEM(w.shape, BF16) for w in (split[:-1] if hand_on else split)]

    def kernel(*refs):
        refs = list(refs)
        idx_ref = refs.pop(0)
        take = lambda n: [refs.pop(0) for _ in range(n)]
        array_refs = take(len(arrays))
        weight_refs = [take(n) for n in counts]
        take(len(after))
        out_refs = take(len(outs))
        own_scratch = take(len(scratch))
        fulls = take(len(made)) + ([out_refs.pop()] if hand_on else [])
        loads = [
            functools.partial(w.load, idx_ref, r, fulls.pop(0) if w.split else None)
            for w, r in zip(weights, weight_refs)
        ]
        body(idx_ref, array_refs, loads, out_refs, own_scratch)

    return pl.pallas_call(
        kernel,
        out_shape=tuple(outs),
        in_specs=[pl.BlockSpec(memory_space=pltpu.SMEM)]
        + [pl.BlockSpec(memory_space=pltpu.VMEM)] * len(flat)
        + [pl.BlockSpec(memory_space=pl.ANY)] * len(after),
        out_specs=tuple([pl.BlockSpec(memory_space=pltpu.VMEM)] * len(outs)),
        scratch_shapes=list(scratch) + made,
        compiler_params=pltpu.CompilerParams(vmem_limit_bytes=VMEM_LIMIT),
        cost_estimate=busy_for(busy),
        name=name,
    )(idx, *flat, *after)


def busy_for(microseconds):
    return pl.CostEstimate(flops=int(microseconds * 1e9), bytes_accessed=0, transcendentals=0)


def sds(shape, dtype):
    return jax.ShapeDtypeStruct(shape, dtype)


class Pieces:
    def __init__(self, place, parts=1, extra=0):
        self.place, self.parts, self.extra = place, parts, extra

    def outs(self):
        return [sds((self.parts, 2, 8, CUT_ROWS + self.extra, CUT_COLUMNS), BF16)] * 2

    def scratch(self, columns):
        return pltpu.VMEM((8, CUT_ROWS, columns), BF16)

    def store(self, blocks, grad, start=0):
        for i in range(8):
            rows = grad[i * CUT_ROWS : (i + 1) * CUT_ROWS].astype(BF16)
            blocks[i, :, start : start + grad.shape[1]] = rows

    def emit(self, idx, blocks, outs, under=None):
        for other_core, out in enumerate((outs[1], outs[0])):
            for part in range(self.parts):
                for owner in range(2):
                    for slot in range(8):
                        z = ((slot >> 1) & 1) | ((slot & 1) << 1)
                        block, column = self.place(
                            idx[0] ^ owner, idx[1] ^ other_core, idx[2] ^ (slot >> 2), idx[3] ^ z, part
                        )
                        columns = pl.ds(pl.multiple_of(column * CUT_COLUMNS, LANES), CUT_COLUMNS)
                        piece = blocks[block, :, columns]
                        if under is not None:
                            piece = jnp.concatenate(
                                [piece.astype(F32), under[idx[0] ^ owner]], axis=0
                            ).astype(BF16)
                        out[part, owner, slot] = piece


def head_stack(values, kv_head):
    first = kv_head * GROUP
    return jnp.concatenate(
        [values[:, (first + i) * HEAD : (first + i + 1) * HEAD] for i in range(GROUP)], axis=0
    )


def softmax_rows(query, key, allowed):
    scores = jnp.where(allowed, dot_right_t(query, key) * SCALE, MASKED)
    top = jnp.max(scores, axis=-1, keepdims=True)
    exponent = jnp.exp(scores - top)
    return exponent / jnp.sum(exponent, axis=-1, keepdims=True)


def pack_kernel(body, idx, sources, places, outs, name, after=(), limit=PACK_LIMIT):
    windows = [shape for shape, _ in places]

    def kernel(idx_ref, *refs):
        sources_in, refs = refs[: len(sources)], refs[len(sources) + len(after) :]
        out_refs, buffers, sem = refs[: len(outs)], refs[len(outs) : -1], refs[-1]
        copies = []
        for i, (source, (shape, place)) in enumerate(zip(sources_in, places)):
            where = []
            for axis, tile in ((0, 8), (1, LANES)):
                if shape[axis] == source.shape[axis]:
                    where.append(slice(None))
                else:
                    where.append(pl.ds(pl.multiple_of(place(idx_ref)[axis], tile), shape[axis]))
            copies.append(pltpu.make_async_copy(source.at[tuple(where)], buffers[i], sem.at[i]))
        for copy in copies:
            copy.start()
        for copy in copies:
            copy.wait()
        body(idx_ref, buffers, out_refs)

    return pl.pallas_call(
        kernel,
        out_shape=tuple(outs),
        in_specs=[pl.BlockSpec(memory_space=pltpu.SMEM)]
        + [pl.BlockSpec(memory_space=pltpu.HBM)] * len(sources)
        + [pl.BlockSpec(memory_space=pl.ANY)] * len(after),
        out_specs=tuple([pl.BlockSpec(memory_space=pltpu.VMEM)] * len(outs)),
        scratch_shapes=[pltpu.VMEM(w, F32) for w in windows]
        + [pltpu.SemaphoreType.DMA((len(sources),))],
        compiler_params=pltpu.CompilerParams(vmem_limit_bytes=limit),
        cost_estimate=busy_for(10),
        name=name,
    )(idx, *sources, *after)


def cast_out(idx_ref, buffers, outs):
    for buffer, out in zip(buffers, outs):
        out[...] = buffer[...].astype(BF16)


def pack_down(idx, down_t, after):
    shape = (2 * HALF, down_t.shape[1])
    window = (shape, lambda i: (i[1] * 2 * HALF, 0))
    outs = [sds(shape, BF16)]
    return pack_kernel(
        cast_out, idx, [down_t], [window], outs, "pack_down", after, STEP_LIMIT
    )[0]


def pack_first(idx, w_qkv, w_out, norm_gains, w_gate_up):
    columns = (QKV + w_out.shape[1]) // 2
    quarter = FF // 2
    windows = [((HALF, m.shape[1]), lambda i: (i[1] * HALF, 0)) for m in (w_qkv, w_out)]
    windows.append((norm_gains.shape, lambda i: (0, 0)))
    windows.append(((HALF, quarter), lambda i: (i[1] * HALF, i[2] * quarter)))
    windows.append(((HALF, quarter), lambda i: (i[1] * HALF, FF + (i[3] & 1) * quarter)))

    def body(idx_ref, buffers, outs):
        q_ref, o_ref, gains_ref = buffers[:3]
        both = jnp.concatenate([q_ref[:, columns:], o_ref[...]], axis=1)
        outs[0][:HALF, :] = jnp.where((idx_ref[3] & 1) == 0, q_ref[:, :columns], both).astype(BF16)
        outs[0][HALF:, :] = jnp.zeros((16, columns), BF16)
        outs[0][HALF : HALF + 2, : gains_ref.shape[1]] = gains_ref[...].astype(BF16)
        cast_out(idx_ref, buffers[3:], outs[1:])

    outs = [sds((HALF + 16, columns), BF16)] + [sds((HALF, quarter), BF16)] * 2
    sources = [w_qkv, w_out, norm_gains, w_gate_up, w_gate_up]
    return pack_kernel(body, idx, sources, windows, outs, "pack_first")


def attention_forward(idx, tokens_t, segments, frequency, gains, w_qkv_out):
    width, seq_length = tokens_t.shape
    split_gains = len(gains) > 1

    def body(idx_ref, arrays, loads, outs, scratch):
        x_ref, seg_ref, freq_ref = arrays[:3]
        qkv_ref, o_ref, cos_ref, sin_ref, probs_ref, normed_ref, scale_ref, gains_ref = outs
        if split_gains:
            own = arrays[3][...].astype(BF16).astype(F32)
            other = arrays[4][HALF : HALF + 8, : width // 2].astype(F32)[:2]
            gains_ref[...] = jnp.where(
                idx_ref[0] == 0,
                jnp.concatenate([own, other], axis=1),
                jnp.concatenate([other, own], axis=1),
            )
        else:
            gains_ref[...] = arrays[3][...]
        seen_doc = jnp.broadcast_to(seg_ref[...], (seq_length, seq_length))
        own_doc = seen_doc.T
        token = lax.broadcasted_iota(jnp.int32, (seq_length, seq_length), 0)
        seen = lax.broadcasted_iota(jnp.int32, (seq_length, seq_length), 1)
        begin = jnp.sum((seen_doc < own_doc).astype(F32), axis=-1, keepdims=True)
        angles = (token.astype(F32) - begin) * freq_ref[...]
        cosine, sine = jnp.cos(angles), jnp.sin(angles)
        sine = jnp.where(seen % HEAD < HEAD // 2, -sine, sine)
        cos_ref[...] = cosine
        sin_ref[...] = sine
        allowed = ((seen_doc == own_doc) & (token >= seen)).astype(F32)
        allowed = jnp.concatenate([allowed] * GROUP, axis=0) > 0.5
        x = x_ref[...].astype(F32).T
        scale_ref[...] = norm_scale(x)
        normed_ref[...] = x * scale_ref[...]
        h1 = (normed_ref[...] * gains_ref[0:1, :]).astype(BF16)
        projected = dot(h1, loads[0]()[:, :QKV])
        for start in range(0, ROPED, LANES):
            block = projected[:, start : start + LANES]
            qkv_ref[:, start : start + LANES] = rotate_block(block, cosine, sine).astype(BF16)
        qkv_ref[:, ROPED:QKV] = projected[:, ROPED:QKV].astype(BF16)
        qkv = qkv_ref[...]
        for kv in range(KV_HEADS):
            key = qkv[:, QUERY + kv * HEAD : QUERY + (kv + 1) * HEAD]
            value = qkv[:, ROPED + kv * HEAD : ROPED + (kv + 1) * HEAD]
            probs = softmax_rows(head_stack(qkv, kv), key, allowed)
            probs_ref[kv] = probs
            attended = dot(probs.astype(BF16), value).astype(BF16)
            for i in range(GROUP):
                start = (kv * GROUP + i) * HEAD
                o_ref[:, start : start + HEAD] = attended[i * seq_length : (i + 1) * seq_length]

    square = sds((seq_length, seq_length), F32)
    outs = [sds((seq_length, QKV), BF16), sds((seq_length, QUERY), BF16)]
    outs += [square, square, sds((KV_HEADS, GROUP * seq_length, seq_length), F32)]
    outs += [sds((seq_length, width), F32), sds((seq_length, 1), F32), sds((2, width), F32)]
    return call(
        body,
        idx,
        [tokens_t, segments, frequency, *gains],
        [w_qkv_out],
        outs,
        [],
        1,
        "attention",
        hand_on=True,
    )


def feed_forward(idx, tokens_t, attended, gains, cotangent_t, w_qkv_out, w_gate_up, pieces, after):
    width, seq_length = tokens_t.shape

    def body(idx_ref, arrays, loads, outs, scratch):
        x_ref, o_ref, gains_ref, y_ref = arrays
        u_ref, h2_ref, ab_ref, z_ref = outs[:4]
        u = x_ref[...].astype(F32).T + dot(o_ref[...], loads[0]()[:, QKV:])
        u_ref[...] = u
        h2 = (u * norm_scale(u) * gains_ref[1:2, :]).astype(BF16)
        h2_ref[...] = h2
        ab = dot(h2, loads[1]()[...])
        ab_ref[...] = ab
        gate, up = ab[:, :FF], ab[:, FF:]
        z = (gate * jax.nn.sigmoid(gate) * up).astype(BF16)
        z_ref[...] = z
        grad = dot(y_ref[...], z)
        if pieces is None:
            outs[4][...] = grad
        else:
            pieces.store(scratch[0], grad)
            pieces.emit(idx_ref, scratch[0], outs[4:])

    outs = [
        sds((seq_length, width), F32),
        sds((seq_length, width), BF16),
        sds((seq_length, 2 * FF), F32),
        sds((seq_length, FF), BF16),
    ]
    outs += [sds((width, FF), F32)] if pieces is None else pieces.outs()
    scratch = [] if pieces is None else [pieces.scratch(FF)]
    return call(
        body,
        idx,
        [tokens_t, attended, gains, cotangent_t],
        [w_qkv_out, w_gate_up],
        outs,
        scratch,
        5,
        "feed_forward",
        after,
        True,
    )


def feed_back(idx, ab, normed_low, cotangent_t, down_t, pieces):
    width, seq_length = cotangent_t.shape

    def body(idx_ref, arrays, loads, outs, scratch):
        ab_ref, h2_ref, y_ref = arrays
        gg_ref = outs[0]
        gate, up = ab_ref[:, :FF], ab_ref[:, FF:]
        sig = jax.nn.sigmoid(gate)
        grad_hidden = dot_left_t(y_ref[...], loads[0]()[...])
        gg_ref[:, :FF] = (grad_hidden * up * sig * (1.0 + gate * (1.0 - sig))).astype(BF16)
        gg_ref[:, FF:] = (grad_hidden * gate * sig).astype(BF16)
        grad = dot_left_t(h2_ref[...], gg_ref[...])
        if pieces is None:
            outs[1][...] = grad
        else:
            pieces.store(scratch[0], grad)
            pieces.emit(idx_ref, scratch[0], outs[1:])

    outs = [sds((seq_length, 2 * FF), BF16)]
    outs += [sds((width, 2 * FF), F32)] if pieces is None else pieces.outs()
    scratch = [] if pieces is None else [pieces.scratch(2 * FF)]
    return call(
        body,
        idx,
        [ab, normed_low, cotangent_t],
        [down_t],
        outs,
        scratch,
        20,
        "feed_back",
        hand_on=True,
    )


def finish_tokens(middle, hidden, down_t, grad_middle, grad_normed, normed, scale, gains, after):
    seq_length, width = middle.shape

    def body(ins, outs):
        u_ref, z_ref, down_ref, gu_ref, grad_ref, normed_ref, scale_ref, gains_ref = ins
        outs[0][...] = (u_ref[...] + dot_right_t(z_ref[...], down_ref[...])).T.astype(BF16)
        grad = grad_ref[...] * gains_ref[0:1, :]
        grad = gu_ref[...] + norm_back(grad, normed_ref[...], scale_ref[...])
        outs[1][...] = grad.T.astype(BF16)

    arrays = [middle, hidden, down_t, grad_middle, grad_normed, normed, scale, gains]
    outs = [sds((width, seq_length), BF16)] * 2
    return step(body, arrays, outs, "finish_tokens", after, 2)


def middle_back(idx, cotangent_t, middle, gated, gains, w_gate_up, w_qkv_out, after):
    width, seq_length = cotangent_t.shape

    def body(idx_ref, arrays, loads, outs, scratch):
        y_ref, u_ref, gg_ref, gains_ref = arrays
        gu_ref, go_ref, gain_ref = outs
        u = u_ref[...]
        scale_two = norm_scale(u)
        normed = u * scale_two
        grad_normed = dot_right_t(gg_ref[...], loads[0]()[...])
        gain_ref[...] = jnp.sum(grad_normed * normed, axis=0, keepdims=True)
        gu = y_ref[...].astype(F32).T + norm_back(
            grad_normed * gains_ref[1:2, :], normed, scale_two
        )
        gu_ref[...] = gu
        go_ref[...] = dot_right_t(gu.astype(BF16), loads[1]()[:, QKV:]).astype(BF16)

    outs = [sds((seq_length, width), F32), sds((seq_length, width), BF16), sds((1, width), F32)]
    return call(
        body,
        idx,
        [cotangent_t, middle, gated, gains],
        [w_gate_up, w_qkv_out],
        outs,
        [],
        20,
        "middle_back",
        after,
    )


def attention_back(
    idx, grad_middle, grad_attended, gain_two, qkv, attended, tables, gains, w_qkv, pieces, after
):
    seq_length, width = grad_middle.shape

    def body(idx_ref, arrays, loads, outs, scratch):
        gu_ref, go_ref, gain_two_ref, qkv_ref, o_ref = arrays[:5]
        cos_ref, sin_ref, probs_ref, normed_ref, gains_ref = arrays[5:]
        grad_ref = outs[0]
        grad_proj, gp_ref, gain_rows, *blocks = scratch
        gu, go = gu_ref[...], go_ref[...]
        gu_low = gu.astype(BF16)
        grad_gain_two = gain_two_ref[...]
        qkv_values = qkv_ref[...]
        for kv in range(KV_HEADS):
            key = qkv_values[:, QUERY + kv * HEAD : QUERY + (kv + 1) * HEAD]
            value = qkv_values[:, ROPED + kv * HEAD : ROPED + (kv + 1) * HEAD]
            query = head_stack(qkv_values, kv)
            grad_out = head_stack(go, kv)
            probs = probs_ref[kv]
            grad_probs = dot_right_t(grad_out, value)
            row_delta = jnp.sum(probs * grad_probs, axis=-1, keepdims=True)
            gs = (probs * (grad_probs - row_delta)).astype(BF16)
            grad_query = dot(gs, key) * SCALE
            for i in range(GROUP):
                start = (kv * GROUP + i) * HEAD
                grad_proj[:, start : start + HEAD] = grad_query[
                    i * seq_length : (i + 1) * seq_length
                ]
            start = QUERY + kv * HEAD
            grad_proj[:, start : start + HEAD] = dot_left_t(gs, query) * SCALE
            start = ROPED + kv * HEAD
            grad_proj[:, start : start + HEAD] = dot_left_t(probs.astype(BF16), grad_out)
        for start in range(0, ROPED, LANES):
            gp_ref[:, start : start + LANES] = rotate_block(
                grad_proj[:, start : start + LANES], cos_ref[...], -sin_ref[...]
            ).astype(BF16)
        gp_ref[:, ROPED:QKV] = grad_proj[:, ROPED:QKV].astype(BF16)
        normed = normed_ref[...]
        h1 = (normed * gains_ref[0:1, :]).astype(BF16)
        grad_qkv = dot_left_t(h1, gp_ref[...])
        grad_out = dot_left_t(o_ref[...], gu_low)
        grad_normed = dot_right_t(gp_ref[...], loads[0]()[:, :QKV])
        grad_gain_one = jnp.sum(grad_normed * normed, axis=0, keepdims=True)
        if pieces is None:
            outs[1][:, :QKV] = grad_qkv
            outs[1][:, QKV:] = grad_out
            outs[2][0:1, :] = grad_gain_one
            outs[2][1:2, :] = grad_gain_two
        else:
            pieces.store(blocks[0], grad_qkv)
            pieces.store(blocks[0], grad_out, QKV)
            half = width // 2
            gain_rows[...] = jnp.zeros_like(gain_rows)
            for owner in range(2):
                columns = slice(owner * half, (owner + 1) * half)
                gain_rows[owner, 0:1, :half] = grad_gain_one[:, columns]
                gain_rows[owner, 1:2, :half] = grad_gain_two[:, columns]
            pieces.emit(idx_ref, blocks[0], outs[1:3], gain_rows)
            outs[3][...] = jnp.zeros_like(outs[3])
        grad_ref[...] = grad_normed

    outs = [sds((seq_length, width), F32)]
    scratch = [
        pltpu.VMEM((seq_length, QKV), F32),
        pltpu.VMEM((seq_length, QKV), BF16),
        pltpu.VMEM((2, 8, CUT_COLUMNS), F32),
    ]
    if pieces is None:
        outs += [sds((width, QKV + width), F32), sds((2, width), F32)]
    else:
        outs += pieces.outs() + [sds(MARK, F32)]
        scratch += [pieces.scratch(QKV + width)]
    return call(
        body,
        idx,
        [grad_middle, grad_attended, gain_two, qkv, attended, *tables, gains],
        [w_qkv],
        outs,
        scratch,
        20,
        "attention_back",
        after,
    )


def step(body, arrays, outs, name, after=(), busy=20):
    def kernel(*refs):
        body(refs[: len(arrays)], refs[len(arrays) + len(after) :])

    return pl.pallas_call(
        kernel,
        out_shape=tuple(outs),
        in_specs=[pl.BlockSpec(memory_space=pltpu.VMEM)] * len(arrays)
        + [pl.BlockSpec(memory_space=pl.ANY)] * len(after),
        out_specs=tuple([pl.BlockSpec(memory_space=pltpu.VMEM)] * len(outs)),
        compiler_params=pltpu.CompilerParams(vmem_limit_bytes=STEP_LIMIT),
        cost_estimate=busy_for(busy),
        name=name,
    )(*arrays, *after)


def pass_on(ins, outs):
    outs[0][...] = ins[0][...]


def add_split(keep, arrived, axis, send_ref, keep_ref):
    total = keep[...].astype(F32) + arrived[...].astype(F32)
    low, high = lax.index_in_dim(total, 0, axis, False), lax.index_in_dim(total, 1, axis, False)
    send_ref[...] = high.astype(BF16)
    keep_ref[...] = low


def add_step(jobs, name, after, busy=20):
    arrays, outs = [], []
    for keep, arrived, axis in jobs:
        arrays += [keep, arrived]
        shape = keep.shape[:axis] + keep.shape[axis + 1 :]
        outs += [sds(shape, BF16), sds(shape, F32)]

    def body(ins, out_refs):
        for i, (_, _, axis) in enumerate(jobs):
            add_split(ins[2 * i], ins[2 * i + 1], axis, out_refs[2 * i], out_refs[2 * i + 1])

    flat = step(body, arrays, outs, name, after, busy)
    return [(flat[2 * i], flat[2 * i + 1]) for i in range(len(jobs))]


def update_rows(idx, shares, place, height, chunk, state, earlier, gains, name, after, busy=20):
    count = len(state) // 3
    columns = [a.shape[1] for a in state[:count]]
    starts = [sum(-(-c // LANES) * LANES for c in columns[:k]) for k in range(count + 1)]
    chunks = height // chunk
    order = [(k, count + k, 2 * count + k) for k in range(count)]

    def kernel(idx_ref, *refs):
        refs = list(refs)
        take = lambda n: [refs.pop(0) for _ in range(n)]
        share_refs = take(len(shares))
        state_refs, gain_refs = take(3 * count), take(len(gains))
        take(len(earlier) + len(after))
        outs, gain_outs, (mark,) = take(3 * count), take(len(gains)), take(1)
        buffers, (full, sem) = take(3 * count), refs
        mark[...] = jnp.zeros_like(mark)
        copies = []
        for share, (far, _) in enumerate(shares):
            piece_ref = share_refs[share]
            for part in range(piece_ref.shape[0]):
                for x in range(2):
                    for z in range(4):
                        rel = z ^ idx_ref[3]
                        slot = ((rel & 1) << 1) | (rel >> 1)
                        piece = piece_ref[part, x, slot].astype(F32)[:CUT_ROWS]
                        row, cuts = place(part, idx_ref[2] ^ x, z)
                        rows = pl.ds(pl.multiple_of(share * height + row, 8), CUT_ROWS)
                        for begin, size, to in cuts:
                            if isinstance(to, int):
                                where = slice(to, to + size)
                            else:
                                where = pl.ds(pl.multiple_of(to, LANES), size)
                            full[rows, where] = piece[:, begin : begin + size]
            base = (idx_ref[1] ^ far) * height
            for at_chunk in range(chunks):

                def eight_rows(i, carry, at_chunk=at_chunk, share=share, base=base):
                    at_row = at_chunk * chunk + i * 8
                    near_rows = pl.ds(pl.multiple_of(share * height + at_row, 8), 8)
                    rows = pl.ds(pl.multiple_of(base + at_row, 8), 8)
                    for k in range(count):
                        for at in range(0, columns[k], 768):
                            size = min(768, columns[k] - at)
                            where = slice(at, at + size)
                            results = adamw_rows(
                                *[state_refs[j][rows, where] for j in order[k]],
                                full[near_rows, starts[k] + at : starts[k] + at + size],
                                RATE_MATRIX,
                                DECAY_MATRIX,
                            )
                            for j, result in zip(order[k], results):
                                buffers[j][near_rows, where] = result
                    return carry

                lax.fori_loop(0, chunk // 8, eight_rows, 0, unroll=3)
                near_rows = pl.ds(share * height + at_chunk * chunk, chunk)
                rows = pl.ds(pl.multiple_of(base + at_chunk * chunk, 8), chunk)
                for j in range(3 * count):
                    copy = pltpu.make_async_copy(
                        buffers[j].at[near_rows],
                        outs[j].at[rows],
                        sem.at[share * chunks + at_chunk, j],
                    )
                    copy.start()
                    copies.append(copy)
        if gains:
            gradient = share_refs[0][0, 0, 0, CUT_ROWS:, :].astype(F32)[:2, : gains[0].shape[1]]
            results = adamw_rows(*[g[...] for g in gain_refs], gradient, RATE_GAIN, 0.0)
            for out, result in zip(gain_outs, results):
                out[...] = result
        for copy in copies:
            copy.wait()

    vmem, anywhere = pl.BlockSpec(memory_space=pltpu.VMEM), pl.BlockSpec(memory_space=pl.ANY)
    first_earlier = 1 + len(shares) + 3 * count + len(gains)
    total = len(shares) * height
    return pl.pallas_call(
        kernel,
        out_shape=tuple(sds(a.shape, F32) for a in [*state, *gains]) + (sds(MARK, F32),),
        in_specs=[pl.BlockSpec(memory_space=pltpu.SMEM)]
        + [vmem] * (len(shares) + 3 * count + len(gains))
        + [anywhere] * (len(earlier) + len(after)),
        out_specs=tuple([anywhere] * (3 * count) + [vmem] * (len(gains) + 1)),
        scratch_shapes=[pltpu.VMEM((total, a.shape[1]), F32) for a in state]
        + [pltpu.VMEM((total, starts[-1]), F32)]
        + [pltpu.SemaphoreType.DMA((len(shares) * chunks, 3 * count))],
        input_output_aliases={first_earlier + i: i for i in range(len(earlier))},
        compiler_params=pltpu.CompilerParams(vmem_limit_bytes=UPDATE_LIMIT),
        cost_estimate=busy_for(busy),
        name=name,
    )(idx, *[p for _, p in shares], *state, *gains, *earlier, *after)


def swap(values, axis, mask):
    size = lax.axis_size(axis)
    return lax.ppermute(values, axis, [(i, i ^ mask) for i in range(size)])


over_y = functools.partial(swap, axis="shard", mask=1)
over_core = functools.partial(swap, axis="dp", mask=1)
over_x = functools.partial(swap, axis="dp", mask=2)
over_z_low = functools.partial(swap, axis="dp", mask=4)
over_z_high = functools.partial(swap, axis="dp", mask=8)


def per_device(
    tokens,
    segments,
    cotangent,
    w_qkv,
    w_out,
    w_gate_up,
    w_down,
    norm_gains,
    first_qkv,
    first_out,
    first_gate_up,
    first_down,
    first_gains,
    second_qkv,
    second_out,
    second_gate_up,
    second_down,
    second_gains,
):
    groups = lax.axis_size("shard")
    replicas = lax.axis_size("dp")
    fast = groups == 2 and replicas == 16
    place_dp = lax.axis_index("dp")
    owner = lax.axis_index("shard")
    idx = jnp.stack([owner, place_dp & 1, (place_dp >> 1) & 1, place_dp >> 2]).astype(jnp.int32)
    x_t, y_t = tokens[0].T, cotangent[0].T
    width, seq_length = x_t.shape
    rows, down_rows = w_qkv.shape[0], w_down.shape[0]
    down_t, first_down_t, second_down_t = w_down.T, first_down.T, second_down.T
    half_size = HEAD // 2
    frequency = ROPE_BASE ** (-(np.arange(half_size) * 2.0 / HEAD))
    frequency = jnp.asarray(np.tile(frequency, 4)[None], F32)
    if fast:
        qo_near, by_x, by_low = pack_first(idx, w_qkv, w_out, norm_gains, w_gate_up)
        qo_near, by_x, by_low = over_y(qo_near), over_y(by_x), over_y(by_low)
        down_near = over_y(pack_down(idx, down_t, (by_low,)))
        by_x_next, by_low_next = over_x(by_x), over_z_low(by_low)
        qo_near_low = over_z_low(qo_near)
        gains = (norm_gains, qo_near)
        (low_far,) = step(
            pass_on, [over_core(by_low_next)], [sds(by_low.shape, BF16)], "pass_on_low", (), 1
        )
        own_rows = lambda o: (o * rows, 0)
        own_rows_out = lambda o: (o * rows, QKV)
        qo_place = lambda o, c, x, low: (o * rows + c * HALF, low * ((QKV + width) // 2))
        x_place = lambda o, c, x, low: (o * rows + c * HALF, x * (FF // 2))
        low_place = lambda o, c, x, low: (o * rows + c * HALF, FF + low * (FF // 2))
        mat_qkv_out = Weight(
            (width, QKV + width),
            own=[(w_qkv, own_rows), (w_out, own_rows_out)],
            parts=[
                (qo_near, (0, 0, 0), qo_place),
                (qo_near_low, (0, 0, 1), qo_place),
                (over_core(qo_near), (1, 0, 0), qo_place),
                (over_core(qo_near_low), (1, 0, 1), qo_place),
            ],
        )
        mat_gate_up = Weight(
            (width, 2 * FF),
            own=[(w_gate_up, own_rows)],
            parts=[
                (by_x, (0, 0, 0), x_place),
                (by_x_next, (0, 1, 0), x_place),
                (over_core(by_x), (1, 0, 0), x_place),
                (over_core(by_x_next), (1, 1, 0), x_place),
                (by_low, (0, 0, 0), low_place),
                (by_low_next, (0, 0, 1), low_place),
                (over_core(by_low), (1, 0, 0), low_place),
                (low_far, (1, 0, 1), low_place),
            ],
        )
        cut_qkv_out = Pieces(lambda o, c, x, z, p: (o * 4 + c * 2 + x, z), extra=8)
        cut_gate_up = Pieces(lambda o, c, x, z, p: (o * 4 + c * 2 + p, x * 4 + z), parts=2)
        cut_down = Pieces(lambda o, c, x, z, p: (c * 4 + x * 2 + (z >> 1), o * 2 + (z & 1)))
    else:
        gains = (
            lax.all_gather(norm_gains.astype(BF16), "shard", axis=1, tiled=True).astype(F32),
        )
        mat_qkv, mat_out, mat_gate_up, mat_down = [
            lax.all_gather(m.astype(BF16), "shard", axis=0, tiled=True)
            for m in (w_qkv, w_out, w_gate_up, w_down)
        ]
        mat_qkv_out, mat_gate_up, mat_down = [
            Weight(m.shape, whole=m)
            for m in (jnp.concatenate([mat_qkv, mat_out], axis=1), mat_gate_up, mat_down.T)
        ]
        cut_qkv_out = cut_gate_up = cut_down = None

    qkv, attended, *tables, scale, gains, whole = attention_forward(
        idx, x_t, segments, frequency, gains, mat_qkv_out
    ) + (() if fast else (None,))
    if fast:
        mat_qkv_out = Weight(whole.shape, whole=whole)
    middle, normed_low, ab, hidden, *grad_down = feed_forward(
        idx, x_t, attended, gains, y_t, mat_qkv_out, mat_gate_up, cut_down, ()
    )
    after = ()
    if fast:
        whole = grad_down.pop()
        mat_gate_up = Weight(whole.shape, whole=whole)

        (down_near,) = step(
            pass_on, [down_near], [sds(down_near.shape, BF16)], "pass_on", (attended,), 0.1
        )
        down_place = lambda o, c, x, low: (c * 2 * HALF, o * down_rows)
        mat_down = Weight(
            (width, FF),
            own=[(down_t, lambda o: (0, o * down_rows))],
            parts=[
                (down_near, (0, 0, 0), down_place),
                (over_core(down_near), (1, 0, 0), down_place),
            ],
        )
    if fast:
        arrived_down = over_core(grad_down[0])
    gated, *grad_gate_up = feed_back(idx, ab, normed_low, y_t, mat_down, cut_gate_up)
    if fast:
        down_whole = grad_gate_up.pop()
        cut = lambda a, *lead: a.reshape(*lead, *a.shape[-2:])
        arrived_gate_up = over_core(grad_gate_up[0])
        ((send, keep_down),) = add_step(
            [(grad_down[1][0], arrived_down[0], 0)], "down_core", (gated,)
        )
        arrived_down = over_y(send)
        after = (keep_down,)
    grad_middle, grad_attended, gain_two = middle_back(
        idx, y_t, middle, gated, gains, mat_gate_up, mat_qkv_out, after
    )
    if fast:
        halves = [
            [cut(a[p], *lead) for a in (grad_gate_up[1], arrived_gate_up)]
            for p, lead in ((0, (2, 2, 4)), (1, (4, 2, 2)))
        ]
        (send_up, keep_up), (send_low, keep_low) = add_step(
            [(*halves[0], 1), (*halves[1], 1)], "gate_up_core", (grad_middle,)
        )
        arrived_up, arrived_low = over_x(send_up), over_z_low(send_low)
        after = (keep_up,)
    grad_normed, *grad_qkv_out = attention_back(
        idx,
        grad_middle,
        grad_attended,
        gain_two,
        qkv,
        attended,
        tables,
        gains,
        mat_qkv_out,
        cut_qkv_out,
        after,
    )
    finish = (grad_middle, grad_normed, tables[3], scale, gains)
    if not fast:
        output, token_grad = finish_tokens(middle, hidden, mat_down.arrays[0], *finish, ())
    if fast:

        arrived_qkv_out = over_core(grad_qkv_out[0])
        piece = (CUT_ROWS, CUT_COLUMNS)
        taller = (CUT_ROWS + 8, CUT_COLUMNS)
        ((send, keep_down),) = add_step(
            [(cut(keep_down, 2, 4), cut(arrived_down, 2, 4), 0)], "down_y", (grad_qkv_out[2],)
        )
        arrived_down = over_x(send)
        ((send, keep_qkv_out),) = add_step(
            [(grad_qkv_out[1][0], arrived_qkv_out[0], 0)], "qkv_out_core", (keep_down,), 0.1
        )
        arrived_qkv_out = over_y(send)
        (send_up, keep_up), (send_low, keep_low) = add_step(
            [
                (cut(keep_up, 2, 2, 2), cut(arrived_up, 2, 2, 2), 1),
                (cut(keep_low, 2, 2, 2), cut(arrived_low, 2, 2, 2), 1),
            ],
            "up_x_low_z",
            (keep_qkv_out,),
            20,
        )
        arrived_up, arrived_low = over_z_low(send_up), over_x(send_low)
        ((send, keep_down),) = add_step(
            [(cut(keep_down, 2, 2), cut(arrived_down, 2, 2), 1)], "down_x", (keep_up,), 0.1
        )
        arrived_down = over_z_high(send)

        def columns(ins, outs):
            total = ins[0][...] + ins[1][...].astype(F32)
            outs[0][...] = total[1].astype(BF16)
            outs[1][...] = total[0]
            total = ins[2][...] + ins[3][...].astype(F32)
            outs[2][0], outs[2][1] = total[0, 1].astype(BF16), total[1, 1].astype(BF16)
            outs[3][...] = total[:, 0]
            total = ins[4][...] + ins[5][...].astype(F32)
            outs[4][...] = total[1].astype(BF16)
            outs[5][...] = total[0]

        ((send, keep_qkv_out),) = add_step(
            [(cut(keep_qkv_out, 2, 4), cut(arrived_qkv_out, 2, 4), 0)],
            "qkv_out_y",
            (keep_down,),
            0.1,
        )
        arrived_qkv_out = over_x(send)
        send_up, keep_up, send, keep_low, send_down, keep_down = step(
            columns,
            [keep_up, arrived_up, keep_low, arrived_low, keep_down, arrived_down],
            [
                *(sds((2, *piece), BF16), sds((2, *piece), F32)),
                *(sds((2, *piece), BF16), sds((2, *piece), F32)),
                *(sds(piece, BF16), sds(piece, F32)),
            ],
            "columns",
            (keep_qkv_out,),
        )
        arrived_up, arrived = over_y(send_up), over_z_high(send)
        arrived_down = over_z_low(send_down)

        def planes(ins, outs):
            keep_up, arrived_up, keep_low, arrived, keep_down, arrived_down = ins[:6]
            keep_qkv_out, arrived_qkv_out = ins[6:]
            total = keep_up[...] + arrived_up[...].astype(F32)
            outs[0][0] = total[1].astype(BF16)
            outs[1][0] = total[0]
            outs[0][1] = (keep_down[...] + arrived_down[...].astype(F32)).astype(BF16)
            outs[2][...] = (keep_low[1] + arrived[1].astype(F32)).astype(BF16)
            outs[1][1] = keep_low[0] + arrived[0].astype(F32)
            total = keep_qkv_out[...] + arrived_qkv_out[...].astype(F32)
            outs[3][...] = total[1].astype(BF16)
            outs[4][...] = total[0]

        send, keep, send_low, send_qkv_out, keep_qkv_out = step(
            planes,
            [
                *(keep_up, arrived_up, keep_low, arrived, keep_down, arrived_down),
                *(cut(keep_qkv_out, 2, 2), cut(arrived_qkv_out, 2, 2)),
            ],
            [
                *(sds((2, *piece), BF16), sds((2, *piece), F32), sds(piece, BF16)),
                *(sds((2, *taller), BF16), sds((2, *taller), F32)),
            ],
            "planes",
        )
        arrived, arrived_low = over_z_high(send), over_y(send_low)
        arrived_qkv_out = over_z_low(send_qkv_out)

        def lines(ins, outs):
            send, keep, arrived, arrived_low, keep_qkv_out, arrived_qkv_out = ins
            total = keep_qkv_out[...] + arrived_qkv_out[...].astype(F32)
            outs[0][0] = total[1].astype(BF16)
            outs[1][...] = total[0]
            for part, came in enumerate((arrived[0], arrived_low[...])):
                total = keep[part] + came.astype(F32)
                total = jnp.concatenate([total, jnp.zeros((8, CUT_COLUMNS), F32)], axis=0)
                outs[0][part + 1] = total.astype(BF16)
            outs[2][0], outs[2][1] = send[1], arrived[1]

        pieces, keep_qkv_out, near_down = step(
            lines,
            [send, keep, arrived, arrived_low, keep_qkv_out, arrived_qkv_out],
            [sds((3, *taller), BF16), sds(taller, F32), sds((2, *piece), BF16)],
            "lines",
            (w_gate_up, first_gate_up, second_gate_up),
        )
        arrived, down_low = over_z_high(pieces), over_z_low(near_down)

        def share_high(ins, outs):
            pieces, arrived, keep_qkv_out, near_down, down_low = ins
            for high in range(2):
                outs[0][0, high], outs[0][1, high] = near_down[high], down_low[high]
            outs[0][2, 0], outs[0][2, 1] = pieces[1, :CUT_ROWS], arrived[1, :CUT_ROWS]
            outs[1][0], outs[1][1] = pieces[2, :CUT_ROWS], arrived[2, :CUT_ROWS]
            outs[2][...] = (keep_qkv_out[...] + arrived[0].astype(F32)).astype(BF16)

        near_x, near_low, piece_qkv_out = step(
            share_high,
            [pieces, arrived, keep_qkv_out, near_down, down_low],
            [sds((3, 2, *piece), BF16), sds((2, *piece), BF16), sds(taller, BF16)],
            "share_high",
            (
                *(w_qkv, w_out, first_qkv, first_out, second_qkv, second_out),
                *(down_t, first_down_t, second_down_t, first_gains, second_gains),
            ),
        )
        arrived_x, low_low = over_x(near_x), over_z_low(near_low)
        qkv_out_high = over_z_high(piece_qkv_out)
        output, token_grad = finish_tokens(middle, hidden, down_whole, *finish, (near_x,))

        def share_next(ins, outs):
            near_x, arrived_x, near_low, low_low = ins
            outs[0][0], outs[0][1] = near_x[2], arrived_x[2]
            outs[1][0], outs[1][1] = near_low[...], low_low[...]
            for low in range(2):
                for high in range(2):
                    outs[2][0, 0, low * 2 + high] = near_x[low, high]
                    outs[2][0, 1, low * 2 + high] = arrived_x[low, high]

        near_up, near_low, near_down = step(
            share_next,
            [near_x, arrived_x, near_low, low_low],
            [
                *(sds((2, 2, *piece), BF16), sds((2, 2, *piece), BF16)),
                sds((1, 2, 4, *piece), BF16),
            ],
            "share_next",
            (qkv_out_high,),
        )
        far_down = over_core(near_down)
        up_low, low_x = over_z_low(near_up), over_x(near_low)

        def share_qkv_out_high(ins, outs):
            outs[0][0], outs[0][1] = ins[0][...], ins[1][...]

        (near_qkv_out,) = step(
            share_qkv_out_high,
            [piece_qkv_out, qkv_out_high],
            [sds((2, *taller), BF16)],
            "share_qkv_out_high",
            (near_up,),
        )
        qkv_out_x, qkv_out_low = over_x(near_qkv_out), over_z_low(near_qkv_out)
        qkv_out_both = swap(near_qkv_out, "dp", 6)
        one_down, two_down, next_down, mark = update_rows(
            idx,
            [(0, near_down), (1, far_down)],
            lambda p, x, z: (
                (x * 2 + (z >> 1)) * CUT_ROWS,
                [(0, CUT_COLUMNS, (z & 1) * CUT_COLUMNS)],
            ),
            2 * HALF,
            96,
            [down_t, first_down_t, second_down_t],
            (),
            (),
            "update_down",
            (near_qkv_out,),
            0.1,
        )

        def share_gate_up(ins, outs):
            for near in range(2):
                for far in range(2):
                    for high in range(2):
                        outs[0][0, near, far * 2 + high] = ins[far][near, high]
                        outs[0][1, far, near * 2 + high] = ins[2 + far][near, high]

        (near_gate_up,) = step(
            share_gate_up,
            [near_up, up_low, near_low, low_x],
            [sds((2, 2, 4, *piece), BF16)],
            "share_gate_up",
            (mark,),
        )
        far_gate_up = over_core(near_gate_up)
        place_gate_up = lambda p, x, z: (p * CUT_ROWS, [(0, CUT_COLUMNS, (x * 4 + z) * CUT_COLUMNS)])
        state_gate_up = [w_gate_up, first_gate_up, second_gate_up]
        *near_state, mark = update_rows(
            idx,
            [(0, near_gate_up)],
            place_gate_up,
            HALF,
            24,
            state_gate_up,
            (),
            (),
            "update_gate_up_near",
            (),
        )

        def share_qkv_out(ins, outs):
            for x in range(2):
                for low in range(2):
                    for high in range(2):
                        outs[0][0, x, low * 2 + high] = ins[low * 2 + x][high]

        (near_qkv_out,) = step(
            share_qkv_out,
            [near_qkv_out, qkv_out_x, qkv_out_low, qkv_out_both],
            [sds((1, 2, 4, *taller), BF16)],
            "share_qkv_out",
            (mark,),
        )
        far_qkv_out = over_core(near_qkv_out)
        one_gate_up, two_gate_up, next_gate_up, mark = update_rows(
            idx,
            [(1, far_gate_up)],
            place_gate_up,
            HALF,
            24,
            state_gate_up,
            near_state,
            (),
            "update_gate_up_far",
            (near_qkv_out,),
        )
        cuts = [[(0, 384, 0)], [(0, 384, 384)], [(0, 192, 768), (192, 192, 1024)], [(0, 384, 1216)]]
        updated = update_rows(
            idx,
            [(0, near_qkv_out), (1, far_qkv_out)],
            lambda p, x, z: (x * CUT_ROWS, cuts[z]),
            HALF,
            48,
            [w_qkv, w_out, first_qkv, first_out, second_qkv, second_out],
            (),
            (norm_gains, first_gains, second_gains),
            "update_qkv_out",
            (mark,),
        )
        one_qkv, one_out, two_qkv, two_out, next_qkv, next_out = updated[:6]
        one_gains, two_gains, next_gains = updated[6:9]
    else:
        sums = lax.psum((*grad_qkv_out, grad_gate_up[0], grad_down[0].T), ("dp", "shard"))
        grad_qkv_out, grad_gains, grad_gate_up, grad_down = sums

        def own(grad, axis=0):
            size = grad.shape[axis] // groups
            return lax.dynamic_slice_in_dim(grad, owner * size, size, axis)

        one_qkv, two_qkv, next_qkv = adamw(
            w_qkv, first_qkv, second_qkv, own(grad_qkv_out[:, :QKV]), RATE_MATRIX, DECAY_MATRIX
        )
        one_out, two_out, next_out = adamw(
            w_out, first_out, second_out, own(grad_qkv_out[:, QKV:]), RATE_MATRIX, DECAY_MATRIX
        )
        one_gate_up, two_gate_up, next_gate_up = adamw(
            w_gate_up, first_gate_up, second_gate_up, own(grad_gate_up), RATE_MATRIX, DECAY_MATRIX
        )
        one_down, two_down, next_down = [
            a.T
            for a in adamw(
                w_down, first_down, second_down, own(grad_down), RATE_MATRIX, DECAY_MATRIX
            )
        ]
        one_gains, two_gains, next_gains = adamw(
            norm_gains, first_gains, second_gains, own(grad_gains, 1), RATE_GAIN, 0.0
        )
    one_down, two_down, next_down = one_down.T, two_down.T, next_down.T
    return (
        output.T[None],
        token_grad.T[None],
        one_qkv,
        one_out,
        one_gate_up,
        one_down,
        one_gains,
        two_qkv,
        two_out,
        two_gate_up,
        two_down,
        two_gains,
        next_qkv,
        next_out,
        next_gate_up,
        next_down,
        next_gains,
    )


def solution(mesh):
    return jax.shard_map(
        per_device,
        mesh=mesh,
        in_specs=(
            P(("dp", "shard"), None, None),
            P(("dp", "shard"), None),
            P(("dp", "shard"), None, None),
            P("shard", None),
            P("shard", None),
            P("shard", None),
            P("shard", None),
            P(None, "shard"),
            P("shard", None),
            P("shard", None),
            P("shard", None),
            P("shard", None),
            P(None, "shard"),
            P("shard", None),
            P("shard", None),
            P("shard", None),
            P("shard", None),
            P(None, "shard"),
        ),
        out_specs=(
            P(("dp", "shard"), None, None),
            P(("dp", "shard"), None, None),
            P("shard", None),
            P("shard", None),
            P("shard", None),
            P("shard", None),
            P(None, "shard"),
            P("shard", None),
            P("shard", None),
            P("shard", None),
            P("shard", None),
            P(None, "shard"),
            P("shard", None),
            P("shard", None),
            P("shard", None),
            P("shard", None),
            P(None, "shard"),
        ),
        check_vma=False,
    )
```

```python
import functools

import jax
import jax.numpy as jnp
import numpy as np
from jax import lax
from jax.experimental import pallas as pl
from jax.experimental.pallas import tpu as pltpu
from jax.sharding import PartitionSpec as P

HEADS = 9
KV_HEADS = 3
GROUP = HEADS // KV_HEADS
HEAD = 64
FF = 1536
STEP = 10
QUERY = HEADS * HEAD
ROPED = (HEADS + KV_HEADS) * HEAD
QKV = (HEADS + 2 * KV_HEADS) * HEAD
LANES = 128

EPS_NORM = 1e-05
ROPE_BASE = 100000.0
BETA_ONE = 0.9
BETA_TWO = 0.95
RATE_MATRIX = 0.1
RATE_GAIN = 0.3
DECAY_MATRIX = 0.1
EPS_ADAM = 1e-08
MASKED = -1e30
SCALE = float(HEAD) ** (-0.5)
VMEM_LIMIT = 32 * 1024 * 1024
PACK_LIMIT = 53 * 1024 * 1024
STEP_LIMIT = 14 * 1024 * 1024
UPDATE_LIMIT = 20 * 1024 * 1024
HALF = 144
CUT_ROWS = 72
MARK = (8, 128)
CUT_COLUMNS = 384
F32 = jnp.float32
BF16 = jnp.bfloat16


def rotate_block(values, cosine, signed_sine):
    lane = lax.broadcasted_iota(jnp.int32, values.shape, 1)
    swapped = jnp.where(
        lane % HEAD < HEAD // 2,
        pltpu.roll(values, LANES - HEAD // 2, 1),
        pltpu.roll(values, HEAD // 2, 1),
    )
    return values * cosine + swapped * signed_sine


def adamw(weight, first_moment, second_moment, gradient, step_rate, weight_decay):
    first_new = BETA_ONE * first_moment + (1.0 - BETA_ONE) * gradient
    second_new = BETA_TWO * second_moment + (1.0 - BETA_TWO) * gradient * gradient
    fix_one = 1.0 / (1.0 - BETA_ONE**STEP)
    fix_two = 1.0 / (1.0 - BETA_TWO**STEP)
    update = first_new * fix_one / (jnp.sqrt(second_new * fix_two) + EPS_ADAM)
    return (first_new, second_new, weight - step_rate * (update + weight_decay * weight))


def adamw_rows(weight, first_moment, second_moment, gradient, step_rate, weight_decay):
    first_new = BETA_ONE * first_moment + (1.0 - BETA_ONE) * gradient
    second_new = BETA_TWO * second_moment + (1.0 - BETA_TWO) * gradient * gradient
    value = second_new * (1.0 / (1.0 - BETA_TWO**STEP))
    guess = lax.rsqrt(value)
    divisor = value * guess + EPS_ADAM
    inverse = guess * (2.0 - divisor * guess)
    update = first_new * (step_rate / (1.0 - BETA_ONE**STEP)) * inverse
    return (first_new, second_new, weight * (1.0 - step_rate * weight_decay) - update)


def dot(left, right):
    return lax.dot_general(left, right, (((1,), (0,)), ((), ())), preferred_element_type=F32)


def dot_right_t(left, right):
    return lax.dot_general(left, right, (((1,), (1,)), ((), ())), preferred_element_type=F32)


def dot_left_t(left, right):
    return lax.dot_general(left, right, (((0,), (0,)), ((), ())), preferred_element_type=F32)


def norm_scale(values):
    return lax.rsqrt(jnp.mean(values * values, axis=-1, keepdims=True) + EPS_NORM)


def norm_back(grad_normed, normed, scale_rows):
    return scale_rows * (
        grad_normed - normed * jnp.mean(grad_normed * normed, axis=-1, keepdims=True)
    )


class Weight:
    def __init__(self, shape, whole=None, own=(), parts=()):
        self.shape, self.own, self.parts = shape, own, parts
        self.arrays = [whole] if whole is not None else [a[0] for a in (*own, *parts)]
        self.split = whole is None

    def load(self, idx, refs, full):
        if not self.split:
            return refs[0]
        for ref, (_, place) in zip(refs, self.own):
            self.put(full, place(idx[0]), ref[...].astype(BF16))
        for ref, (_, (core, x, low), place) in zip(refs[len(self.own) :], self.parts):
            place = place(1 - idx[0], idx[1] ^ core, idx[2] ^ x, (idx[3] & 1) ^ low)
            rows = ref.shape[0] // HALF * HALF
            self.put(full, place, ref[:rows, :])
        return full

    def put(self, full, position, value):
        where = []
        for axis, tile in ((0, 16), (1, LANES)):
            at, size = position[axis], value.shape[axis]
            if size == self.shape[axis]:
                where.append(slice(None))
            elif isinstance(at, int):
                where.append(slice(at, at + size))
            else:
                where.append(pl.ds(pl.multiple_of(at, tile), size))
        full[tuple(where)] = value


def call(body, idx, arrays, weights, outs, scratch, busy, name, after=(), hand_on=False):
    counts = [len(w.arrays) for w in weights]
    flat = list(arrays) + [a for w in weights for a in w.arrays]
    outs = list(outs)
    split = [w for w in weights if w.split]
    hand_on = hand_on and bool(split)
    if hand_on:
        outs += [sds(split[-1].shape, BF16)]
    made = [pltpu.VMEM(w.shape, BF16) for w in (split[:-1] if hand_on else split)]

    def kernel(*refs):
        refs = list(refs)
        idx_ref = refs.pop(0)
        take = lambda n: [refs.pop(0) for _ in range(n)]
        array_refs = take(len(arrays))
        weight_refs = [take(n) for n in counts]
        take(len(after))
        out_refs = take(len(outs))
        own_scratch = take(len(scratch))
        fulls = take(len(made)) + ([out_refs.pop()] if hand_on else [])
        loads = [
            functools.partial(w.load, idx_ref, r, fulls.pop(0) if w.split else None)
            for w, r in zip(weights, weight_refs)
        ]
        body(idx_ref, array_refs, loads, out_refs, own_scratch)

    return pl.pallas_call(
        kernel,
        out_shape=tuple(outs),
        in_specs=[pl.BlockSpec(memory_space=pltpu.SMEM)]
        + [pl.BlockSpec(memory_space=pltpu.VMEM)] * len(flat)
        + [pl.BlockSpec(memory_space=pl.ANY)] * len(after),
        out_specs=tuple([pl.BlockSpec(memory_space=pltpu.VMEM)] * len(outs)),
        scratch_shapes=list(scratch) + made,
        compiler_params=pltpu.CompilerParams(vmem_limit_bytes=VMEM_LIMIT),
        cost_estimate=busy_for(busy),
        name=name,
    )(idx, *flat, *after)


def busy_for(microseconds):
    return pl.CostEstimate(flops=int(microseconds * 1e9), bytes_accessed=0, transcendentals=0)


def sds(shape, dtype):
    return jax.ShapeDtypeStruct(shape, dtype)


class Pieces:
    def __init__(self, place, parts=1, extra=0):
        self.place, self.parts, self.extra = place, parts, extra

    def outs(self):
        return [sds((self.parts, 2, 8, CUT_ROWS + self.extra, CUT_COLUMNS), BF16)] * 2

    def scratch(self, columns):
        return pltpu.VMEM((8, CUT_ROWS, columns), BF16)

    def store(self, blocks, grad, start=0):
        for i in range(8):
            rows = grad[i * CUT_ROWS : (i + 1) * CUT_ROWS].astype(BF16)
            blocks[i, :, start : start + grad.shape[1]] = rows

    def emit(self, idx, blocks, outs, under=None):
        for other_core, out in enumerate((outs[1], outs[0])):
            for part in range(self.parts):
                for owner in range(2):
                    for slot in range(8):
                        z = ((slot >> 1) & 1) | ((slot & 1) << 1)
                        block, column = self.place(
                            idx[0] ^ owner, idx[1] ^ other_core, idx[2] ^ (slot >> 2), idx[3] ^ z, part
                        )
                        columns = pl.ds(pl.multiple_of(column * CUT_COLUMNS, LANES), CUT_COLUMNS)
                        piece = blocks[block, :, columns]
                        if under is not None:
                            piece = jnp.concatenate(
                                [piece.astype(F32), under[idx[0] ^ owner]], axis=0
                            ).astype(BF16)
                        out[part, owner, slot] = piece


def head_stack(values, kv_head):
    first = kv_head * GROUP
    return jnp.concatenate(
        [values[:, (first + i) * HEAD : (first + i + 1) * HEAD] for i in range(GROUP)], axis=0
    )


def softmax_rows(query, key, allowed):
    scores = jnp.where(allowed, dot_right_t(query, key) * SCALE, MASKED)
    top = jnp.max(scores, axis=-1, keepdims=True)
    exponent = jnp.exp(scores - top)
    return exponent / jnp.sum(exponent, axis=-1, keepdims=True)


def pack_kernel(body, idx, sources, places, outs, name, after=(), limit=PACK_LIMIT):
    windows = [shape for shape, _ in places]

    def kernel(idx_ref, *refs):
        sources_in, refs = refs[: len(sources)], refs[len(sources) + len(after) :]
        out_refs, buffers, sem = refs[: len(outs)], refs[len(outs) : -1], refs[-1]
        copies = []
        for i, (source, (shape, place)) in enumerate(zip(sources_in, places)):
            where = []
            for axis, tile in ((0, 8), (1, LANES)):
                if shape[axis] == source.shape[axis]:
                    where.append(slice(None))
                else:
                    where.append(pl.ds(pl.multiple_of(place(idx_ref)[axis], tile), shape[axis]))
            copies.append(pltpu.make_async_copy(source.at[tuple(where)], buffers[i], sem.at[i]))
        for copy in copies:
            copy.start()
        for copy in copies:
            copy.wait()
        body(idx_ref, buffers, out_refs)

    return pl.pallas_call(
        kernel,
        out_shape=tuple(outs),
        in_specs=[pl.BlockSpec(memory_space=pltpu.SMEM)]
        + [pl.BlockSpec(memory_space=pltpu.HBM)] * len(sources)
        + [pl.BlockSpec(memory_space=pl.ANY)] * len(after),
        out_specs=tuple([pl.BlockSpec(memory_space=pltpu.VMEM)] * len(outs)),
        scratch_shapes=[pltpu.VMEM(w, F32) for w in windows]
        + [pltpu.SemaphoreType.DMA((len(sources),))],
        compiler_params=pltpu.CompilerParams(vmem_limit_bytes=limit),
        cost_estimate=busy_for(10),
        name=name,
    )(idx, *sources, *after)


def cast_out(idx_ref, buffers, outs):
    for buffer, out in zip(buffers, outs):
        out[...] = buffer[...].astype(BF16)


def pack_down(idx, down_t, after):
    shape = (2 * HALF, down_t.shape[1])
    window = (shape, lambda i: (i[1] * 2 * HALF, 0))
    outs = [sds(shape, BF16)]
    return pack_kernel(
        cast_out, idx, [down_t], [window], outs, "pack_down", after, STEP_LIMIT
    )[0]


def pack_first(idx, w_qkv, w_out, norm_gains, w_gate_up):
    columns = (QKV + w_out.shape[1]) // 2
    quarter = FF // 2
    windows = [((HALF, m.shape[1]), lambda i: (i[1] * HALF, 0)) for m in (w_qkv, w_out)]
    windows.append((norm_gains.shape, lambda i: (0, 0)))
    windows.append(((HALF, quarter), lambda i: (i[1] * HALF, i[2] * quarter)))
    windows.append(((HALF, quarter), lambda i: (i[1] * HALF, FF + (i[3] & 1) * quarter)))

    def body(idx_ref, buffers, outs):
        q_ref, o_ref, gains_ref = buffers[:3]
        both = jnp.concatenate([q_ref[:, columns:], o_ref[...]], axis=1)
        outs[0][:HALF, :] = jnp.where((idx_ref[3] & 1) == 0, q_ref[:, :columns], both).astype(BF16)
        outs[0][HALF:, :] = jnp.zeros((16, columns), BF16)
        outs[0][HALF : HALF + 2, : gains_ref.shape[1]] = gains_ref[...].astype(BF16)
        cast_out(idx_ref, buffers[3:], outs[1:])

    outs = [sds((HALF + 16, columns), BF16)] + [sds((HALF, quarter), BF16)] * 2
    sources = [w_qkv, w_out, norm_gains, w_gate_up, w_gate_up]
    return pack_kernel(body, idx, sources, windows, outs, "pack_first")


def attention_forward(idx, tokens_t, segments, frequency, gains, w_qkv_out):
    width, seq_length = tokens_t.shape
    split_gains = len(gains) > 1

    def body(idx_ref, arrays, loads, outs, scratch):
        x_ref, seg_ref, freq_ref = arrays[:3]
        qkv_ref, o_ref, cos_ref, sin_ref, probs_ref, normed_ref, scale_ref, gains_ref = outs
        if split_gains:
            own = arrays[3][...].astype(BF16).astype(F32)
            other = arrays[4][HALF : HALF + 8, : width // 2].astype(F32)[:2]
            gains_ref[...] = jnp.where(
                idx_ref[0] == 0,
                jnp.concatenate([own, other], axis=1),
                jnp.concatenate([other, own], axis=1),
            )
        else:
            gains_ref[...] = arrays[3][...]
        seen_doc = jnp.broadcast_to(seg_ref[...], (seq_length, seq_length))
        own_doc = seen_doc.T
        token = lax.broadcasted_iota(jnp.int32, (seq_length, seq_length), 0)
        seen = lax.broadcasted_iota(jnp.int32, (seq_length, seq_length), 1)
        begin = jnp.sum((seen_doc < own_doc).astype(F32), axis=-1, keepdims=True)
        angles = (token.astype(F32) - begin) * freq_ref[...]
        cosine, sine = jnp.cos(angles), jnp.sin(angles)
        sine = jnp.where(seen % HEAD < HEAD // 2, -sine, sine)
        cos_ref[...] = cosine
        sin_ref[...] = sine
        allowed = ((seen_doc == own_doc) & (token >= seen)).astype(F32)
        allowed = jnp.concatenate([allowed] * GROUP, axis=0) > 0.5
        x = x_ref[...].astype(F32).T
        scale_ref[...] = norm_scale(x)
        normed_ref[...] = x * scale_ref[...]
        h1 = (normed_ref[...] * gains_ref[0:1, :]).astype(BF16)
        projected = dot(h1, loads[0]()[:, :QKV])
        for start in range(0, ROPED, LANES):
            block = projected[:, start : start + LANES]
            qkv_ref[:, start : start + LANES] = rotate_block(block, cosine, sine).astype(BF16)
        qkv_ref[:, ROPED:QKV] = projected[:, ROPED:QKV].astype(BF16)
        qkv = qkv_ref[...]
        for kv in range(KV_HEADS):
            key = qkv[:, QUERY + kv * HEAD : QUERY + (kv + 1) * HEAD]
            value = qkv[:, ROPED + kv * HEAD : ROPED + (kv + 1) * HEAD]
            probs = softmax_rows(head_stack(qkv, kv), key, allowed)
            probs_ref[kv] = probs
            attended = dot(probs.astype(BF16), value).astype(BF16)
            for i in range(GROUP):
                start = (kv * GROUP + i) * HEAD
                o_ref[:, start : start + HEAD] = attended[i * seq_length : (i + 1) * seq_length]

    square = sds((seq_length, seq_length), F32)
    outs = [sds((seq_length, QKV), BF16), sds((seq_length, QUERY), BF16)]
    outs += [square, square, sds((KV_HEADS, GROUP * seq_length, seq_length), F32)]
    outs += [sds((seq_length, width), F32), sds((seq_length, 1), F32), sds((2, width), F32)]
    return call(
        body,
        idx,
        [tokens_t, segments, frequency, *gains],
        [w_qkv_out],
        outs,
        [],
        1,
        "attention",
        hand_on=True,
    )


def feed_forward(idx, tokens_t, attended, gains, cotangent_t, w_qkv_out, w_gate_up, pieces, after):
    width, seq_length = tokens_t.shape

    def body(idx_ref, arrays, loads, outs, scratch):
        x_ref, o_ref, gains_ref, y_ref = arrays
        u_ref, h2_ref, ab_ref, z_ref = outs[:4]
        u = x_ref[...].astype(F32).T + dot(o_ref[...], loads[0]()[:, QKV:])
        u_ref[...] = u
        h2 = (u * norm_scale(u) * gains_ref[1:2, :]).astype(BF16)
        h2_ref[...] = h2
        ab = dot(h2, loads[1]()[...])
        ab_ref[...] = ab
        gate, up = ab[:, :FF], ab[:, FF:]
        z = (gate * jax.nn.sigmoid(gate) * up).astype(BF16)
        z_ref[...] = z
        grad = dot(y_ref[...], z)
        if pieces is None:
            outs[4][...] = grad
        else:
            pieces.store(scratch[0], grad)
            pieces.emit(idx_ref, scratch[0], outs[4:])

    outs = [
        sds((seq_length, width), F32),
        sds((seq_length, width), BF16),
        sds((seq_length, 2 * FF), F32),
        sds((seq_length, FF), BF16),
    ]
    outs += [sds((width, FF), F32)] if pieces is None else pieces.outs()
    scratch = [] if pieces is None else [pieces.scratch(FF)]
    return call(
        body,
        idx,
        [tokens_t, attended, gains, cotangent_t],
        [w_qkv_out, w_gate_up],
        outs,
        scratch,
        5,
        "feed_forward",
        after,
        True,
    )


def feed_back(idx, ab, normed_low, cotangent_t, down_t, pieces):
    width, seq_length = cotangent_t.shape

    def body(idx_ref, arrays, loads, outs, scratch):
        ab_ref, h2_ref, y_ref = arrays
        gg_ref = outs[0]
        gate, up = ab_ref[:, :FF], ab_ref[:, FF:]
        sig = jax.nn.sigmoid(gate)
        grad_hidden = dot_left_t(y_ref[...], loads[0]()[...])
        gg_ref[:, :FF] = (grad_hidden * up * sig * (1.0 + gate * (1.0 - sig))).astype(BF16)
        gg_ref[:, FF:] = (grad_hidden * gate * sig).astype(BF16)
        grad = dot_left_t(h2_ref[...], gg_ref[...])
        if pieces is None:
            outs[1][...] = grad
        else:
            pieces.store(scratch[0], grad)
            pieces.emit(idx_ref, scratch[0], outs[1:])

    outs = [sds((seq_length, 2 * FF), BF16)]
    outs += [sds((width, 2 * FF), F32)] if pieces is None else pieces.outs()
    scratch = [] if pieces is None else [pieces.scratch(2 * FF)]
    return call(
        body,
        idx,
        [ab, normed_low, cotangent_t],
        [down_t],
        outs,
        scratch,
        20,
        "feed_back",
        hand_on=True,
    )


def finish_tokens(middle, hidden, down_t, grad_middle, grad_normed, normed, scale, gains, after):
    seq_length, width = middle.shape

    def body(ins, outs):
        u_ref, z_ref, down_ref, gu_ref, grad_ref, normed_ref, scale_ref, gains_ref = ins
        outs[0][...] = (u_ref[...] + dot_right_t(z_ref[...], down_ref[...])).T.astype(BF16)
        grad = grad_ref[...] * gains_ref[0:1, :]
        grad = gu_ref[...] + norm_back(grad, normed_ref[...], scale_ref[...])
        outs[1][...] = grad.T.astype(BF16)

    arrays = [middle, hidden, down_t, grad_middle, grad_normed, normed, scale, gains]
    outs = [sds((width, seq_length), BF16)] * 2
    return step(body, arrays, outs, "finish_tokens", after, 2)


def middle_back(idx, cotangent_t, middle, gated, gains, w_gate_up, w_qkv_out, after):
    width, seq_length = cotangent_t.shape

    def body(idx_ref, arrays, loads, outs, scratch):
        y_ref, u_ref, gg_ref, gains_ref = arrays
        gu_ref, go_ref, gain_ref = outs
        u = u_ref[...]
        scale_two = norm_scale(u)
        normed = u * scale_two
        grad_normed = dot_right_t(gg_ref[...], loads[0]()[...])
        gain_ref[...] = jnp.sum(grad_normed * normed, axis=0, keepdims=True)
        gu = y_ref[...].astype(F32).T + norm_back(
            grad_normed * gains_ref[1:2, :], normed, scale_two
        )
        gu_ref[...] = gu
        go_ref[...] = dot_right_t(gu.astype(BF16), loads[1]()[:, QKV:]).astype(BF16)

    outs = [sds((seq_length, width), F32), sds((seq_length, width), BF16), sds((1, width), F32)]
    return call(
        body,
        idx,
        [cotangent_t, middle, gated, gains],
        [w_gate_up, w_qkv_out],
        outs,
        [],
        20,
        "middle_back",
        after,
    )


def attention_back(
    idx, grad_middle, grad_attended, gain_two, qkv, attended, tables, gains, w_qkv, pieces, after
):
    seq_length, width = grad_middle.shape

    def body(idx_ref, arrays, loads, outs, scratch):
        gu_ref, go_ref, gain_two_ref, qkv_ref, o_ref = arrays[:5]
        cos_ref, sin_ref, probs_ref, normed_ref, gains_ref = arrays[5:]
        grad_ref = outs[0]
        grad_proj, gp_ref, gain_rows, *blocks = scratch
        gu, go = gu_ref[...], go_ref[...]
        gu_low = gu.astype(BF16)
        grad_gain_two = gain_two_ref[...]
        qkv_values = qkv_ref[...]
        for kv in range(KV_HEADS):
            key = qkv_values[:, QUERY + kv * HEAD : QUERY + (kv + 1) * HEAD]
            value = qkv_values[:, ROPED + kv * HEAD : ROPED + (kv + 1) * HEAD]
            query = head_stack(qkv_values, kv)
            grad_out = head_stack(go, kv)
            probs = probs_ref[kv]
            grad_probs = dot_right_t(grad_out, value)
            row_delta = jnp.sum(probs * grad_probs, axis=-1, keepdims=True)
            gs = (probs * (grad_probs - row_delta)).astype(BF16)
            grad_query = dot(gs, key) * SCALE
            for i in range(GROUP):
                start = (kv * GROUP + i) * HEAD
                grad_proj[:, start : start + HEAD] = grad_query[
                    i * seq_length : (i + 1) * seq_length
                ]
            start = QUERY + kv * HEAD
            grad_proj[:, start : start + HEAD] = dot_left_t(gs, query) * SCALE
            start = ROPED + kv * HEAD
            grad_proj[:, start : start + HEAD] = dot_left_t(probs.astype(BF16), grad_out)
        for start in range(0, ROPED, LANES):
            gp_ref[:, start : start + LANES] = rotate_block(
                grad_proj[:, start : start + LANES], cos_ref[...], -sin_ref[...]
            ).astype(BF16)
        gp_ref[:, ROPED:QKV] = grad_proj[:, ROPED:QKV].astype(BF16)
        normed = normed_ref[...]
        h1 = (normed * gains_ref[0:1, :]).astype(BF16)
        grad_qkv = dot_left_t(h1, gp_ref[...])
        grad_out = dot_left_t(o_ref[...], gu_low)
        grad_normed = dot_right_t(gp_ref[...], loads[0]()[:, :QKV])
        grad_gain_one = jnp.sum(grad_normed * normed, axis=0, keepdims=True)
        if pieces is None:
            outs[1][:, :QKV] = grad_qkv
            outs[1][:, QKV:] = grad_out
            outs[2][0:1, :] = grad_gain_one
            outs[2][1:2, :] = grad_gain_two
        else:
            pieces.store(blocks[0], grad_qkv)
            pieces.store(blocks[0], grad_out, QKV)
            half = width // 2
            gain_rows[...] = jnp.zeros_like(gain_rows)
            for owner in range(2):
                columns = slice(owner * half, (owner + 1) * half)
                gain_rows[owner, 0:1, :half] = grad_gain_one[:, columns]
                gain_rows[owner, 1:2, :half] = grad_gain_two[:, columns]
            pieces.emit(idx_ref, blocks[0], outs[1:3], gain_rows)
            outs[3][...] = jnp.zeros_like(outs[3])
        grad_ref[...] = grad_normed

    outs = [sds((seq_length, width), F32)]
    scratch = [
        pltpu.VMEM((seq_length, QKV), F32),
        pltpu.VMEM((seq_length, QKV), BF16),
        pltpu.VMEM((2, 8, CUT_COLUMNS), F32),
    ]
    if pieces is None:
        outs += [sds((width, QKV + width), F32), sds((2, width), F32)]
    else:
        outs += pieces.outs() + [sds(MARK, F32)]
        scratch += [pieces.scratch(QKV + width)]
    return call(
        body,
        idx,
        [grad_middle, grad_attended, gain_two, qkv, attended, *tables, gains],
        [w_qkv],
        outs,
        scratch,
        20,
        "attention_back",
        after,
    )


def step(body, arrays, outs, name, after=(), busy=20):
    def kernel(*refs):
        body(refs[: len(arrays)], refs[len(arrays) + len(after) :])

    return pl.pallas_call(
        kernel,
        out_shape=tuple(outs),
        in_specs=[pl.BlockSpec(memory_space=pltpu.VMEM)] * len(arrays)
        + [pl.BlockSpec(memory_space=pl.ANY)] * len(after),
        out_specs=tuple([pl.BlockSpec(memory_space=pltpu.VMEM)] * len(outs)),
        compiler_params=pltpu.CompilerParams(vmem_limit_bytes=STEP_LIMIT),
        cost_estimate=busy_for(busy),
        name=name,
    )(*arrays, *after)


def pass_on(ins, outs):
    outs[0][...] = ins[0][...]


def add_split(keep, arrived, axis, send_ref, keep_ref):
    total = keep[...].astype(F32) + arrived[...].astype(F32)
    low, high = lax.index_in_dim(total, 0, axis, False), lax.index_in_dim(total, 1, axis, False)
    send_ref[...] = high.astype(BF16)
    keep_ref[...] = low


def add_step(jobs, name, after, busy=20):
    arrays, outs = [], []
    for keep, arrived, axis in jobs:
        arrays += [keep, arrived]
        shape = keep.shape[:axis] + keep.shape[axis + 1 :]
        outs += [sds(shape, BF16), sds(shape, F32)]

    def body(ins, out_refs):
        for i, (_, _, axis) in enumerate(jobs):
            add_split(ins[2 * i], ins[2 * i + 1], axis, out_refs[2 * i], out_refs[2 * i + 1])

    flat = step(body, arrays, outs, name, after, busy)
    return [(flat[2 * i], flat[2 * i + 1]) for i in range(len(jobs))]


def update_rows(idx, shares, place, height, chunk, state, earlier, gains, name, after, busy=20):
    count = len(state) // 3
    columns = [a.shape[1] for a in state[:count]]
    starts = [sum(-(-c // LANES) * LANES for c in columns[:k]) for k in range(count + 1)]
    chunks = height // chunk
    order = [(k, count + k, 2 * count + k) for k in range(count)]

    def kernel(idx_ref, *refs):
        refs = list(refs)
        take = lambda n: [refs.pop(0) for _ in range(n)]
        share_refs = take(len(shares))
        state_refs, gain_refs = take(3 * count), take(len(gains))
        take(len(earlier) + len(after))
        outs, gain_outs, (mark,) = take(3 * count), take(len(gains)), take(1)
        buffers, (full, sem) = take(3 * count), refs
        mark[...] = jnp.zeros_like(mark)
        copies = []
        for share, (far, _) in enumerate(shares):
            piece_ref = share_refs[share]
            for part in range(piece_ref.shape[0]):
                for x in range(2):
                    for z in range(4):
                        rel = z ^ idx_ref[3]
                        slot = ((rel & 1) << 1) | (rel >> 1)
                        piece = piece_ref[part, x, slot].astype(F32)[:CUT_ROWS]
                        row, cuts = place(part, idx_ref[2] ^ x, z)
                        rows = pl.ds(pl.multiple_of(share * height + row, 8), CUT_ROWS)
                        for begin, size, to in cuts:
                            if isinstance(to, int):
                                where = slice(to, to + size)
                            else:
                                where = pl.ds(pl.multiple_of(to, LANES), size)
                            full[rows, where] = piece[:, begin : begin + size]
            base = (idx_ref[1] ^ far) * height
            for at_chunk in range(chunks):

                def eight_rows(i, carry, at_chunk=at_chunk, share=share, base=base):
                    at_row = at_chunk * chunk + i * 8
                    near_rows = pl.ds(pl.multiple_of(share * height + at_row, 8), 8)
                    rows = pl.ds(pl.multiple_of(base + at_row, 8), 8)
                    for k in range(count):
                        for at in range(0, columns[k], 768):
                            size = min(768, columns[k] - at)
                            where = slice(at, at + size)
                            results = adamw_rows(
                                *[state_refs[j][rows, where] for j in order[k]],
                                full[near_rows, starts[k] + at : starts[k] + at + size],
                                RATE_MATRIX,
                                DECAY_MATRIX,
                            )
                            for j, result in zip(order[k], results):
                                buffers[j][near_rows, where] = result
                    return carry

                lax.fori_loop(0, chunk // 8, eight_rows, 0, unroll=3)
                near_rows = pl.ds(share * height + at_chunk * chunk, chunk)
                rows = pl.ds(pl.multiple_of(base + at_chunk * chunk, 8), chunk)
                for j in range(3 * count):
                    copy = pltpu.make_async_copy(
                        buffers[j].at[near_rows],
                        outs[j].at[rows],
                        sem.at[share * chunks + at_chunk, j],
                    )
                    copy.start()
                    copies.append(copy)
        if gains:
            gradient = share_refs[0][0, 0, 0, CUT_ROWS:, :].astype(F32)[:2, : gains[0].shape[1]]
            results = adamw_rows(*[g[...] for g in gain_refs], gradient, RATE_GAIN, 0.0)
            for out, result in zip(gain_outs, results):
                out[...] = result
        for copy in copies:
            copy.wait()

    vmem, anywhere = pl.BlockSpec(memory_space=pltpu.VMEM), pl.BlockSpec(memory_space=pl.ANY)
    first_earlier = 1 + len(shares) + 3 * count + len(gains)
    total = len(shares) * height
    return pl.pallas_call(
        kernel,
        out_shape=tuple(sds(a.shape, F32) for a in [*state, *gains]) + (sds(MARK, F32),),
        in_specs=[pl.BlockSpec(memory_space=pltpu.SMEM)]
        + [vmem] * (len(shares) + 3 * count + len(gains))
        + [anywhere] * (len(earlier) + len(after)),
        out_specs=tuple([anywhere] * (3 * count) + [vmem] * (len(gains) + 1)),
        scratch_shapes=[pltpu.VMEM((total, a.shape[1]), F32) for a in state]
        + [pltpu.VMEM((total, starts[-1]), F32)]
        + [pltpu.SemaphoreType.DMA((len(shares) * chunks, 3 * count))],
        input_output_aliases={first_earlier + i: i for i in range(len(earlier))},
        compiler_params=pltpu.CompilerParams(vmem_limit_bytes=UPDATE_LIMIT),
        cost_estimate=busy_for(busy),
        name=name,
    )(idx, *[p for _, p in shares], *state, *gains, *earlier, *after)


def swap(values, axis, mask):
    size = lax.axis_size(axis)
    return lax.ppermute(values, axis, [(i, i ^ mask) for i in range(size)])


over_y = functools.partial(swap, axis="shard", mask=1)
over_core = functools.partial(swap, axis="dp", mask=1)
over_x = functools.partial(swap, axis="dp", mask=2)
over_z_low = functools.partial(swap, axis="dp", mask=4)
over_z_high = functools.partial(swap, axis="dp", mask=8)


def per_device(
    tokens,
    segments,
    cotangent,
    w_qkv,
    w_out,
    w_gate_up,
    w_down,
    norm_gains,
    first_qkv,
    first_out,
    first_gate_up,
    first_down,
    first_gains,
    second_qkv,
    second_out,
    second_gate_up,
    second_down,
    second_gains,
):
    groups = lax.axis_size("shard")
    replicas = lax.axis_size("dp")
    fast = groups == 2 and replicas == 16
    place_dp = lax.axis_index("dp")
    owner = lax.axis_index("shard")
    idx = jnp.stack([owner, place_dp & 1, (place_dp >> 1) & 1, place_dp >> 2]).astype(jnp.int32)
    x_t, y_t = tokens[0].T, cotangent[0].T
    width, seq_length = x_t.shape
    rows, down_rows = w_qkv.shape[0], w_down.shape[0]
    down_t, first_down_t, second_down_t = w_down.T, first_down.T, second_down.T
    half_size = HEAD // 2
    frequency = ROPE_BASE ** (-(np.arange(half_size) * 2.0 / HEAD))
    frequency = jnp.asarray(np.tile(frequency, 4)[None], F32)
    if fast:
        qo_near, by_x, by_low = pack_first(idx, w_qkv, w_out, norm_gains, w_gate_up)
        qo_near, by_x, by_low = over_y(qo_near), over_y(by_x), over_y(by_low)
        down_near = over_y(pack_down(idx, down_t, (by_low,)))
        by_x_next, by_low_next = over_x(by_x), over_z_low(by_low)
        qo_near_low = over_z_low(qo_near)
        gains = (norm_gains, qo_near)
        (low_far,) = step(
            pass_on, [over_core(by_low_next)], [sds(by_low.shape, BF16)], "pass_on_low", (), 1
        )
        own_rows = lambda o: (o * rows, 0)
        own_rows_out = lambda o: (o * rows, QKV)
        qo_place = lambda o, c, x, low: (o * rows + c * HALF, low * ((QKV + width) // 2))
        x_place = lambda o, c, x, low: (o * rows + c * HALF, x * (FF // 2))
        low_place = lambda o, c, x, low: (o * rows + c * HALF, FF + low * (FF // 2))
        mat_qkv_out = Weight(
            (width, QKV + width),
            own=[(w_qkv, own_rows), (w_out, own_rows_out)],
            parts=[
                (qo_near, (0, 0, 0), qo_place),
                (qo_near_low, (0, 0, 1), qo_place),
                (over_core(qo_near), (1, 0, 0), qo_place),
                (over_core(qo_near_low), (1, 0, 1), qo_place),
            ],
        )
        mat_gate_up = Weight(
            (width, 2 * FF),
            own=[(w_gate_up, own_rows)],
            parts=[
                (by_x, (0, 0, 0), x_place),
                (by_x_next, (0, 1, 0), x_place),
                (over_core(by_x), (1, 0, 0), x_place),
                (over_core(by_x_next), (1, 1, 0), x_place),
                (by_low, (0, 0, 0), low_place),
                (by_low_next, (0, 0, 1), low_place),
                (over_core(by_low), (1, 0, 0), low_place),
                (low_far, (1, 0, 1), low_place),
            ],
        )
        cut_qkv_out = Pieces(lambda o, c, x, z, p: (o * 4 + c * 2 + x, z), extra=8)
        cut_gate_up = Pieces(lambda o, c, x, z, p: (o * 4 + c * 2 + p, x * 4 + z), parts=2)
        cut_down = Pieces(lambda o, c, x, z, p: (c * 4 + x * 2 + (z >> 1), o * 2 + (z & 1)))
    else:
        gains = (
            lax.all_gather(norm_gains.astype(BF16), "shard", axis=1, tiled=True).astype(F32),
        )
        mat_qkv, mat_out, mat_gate_up, mat_down = [
            lax.all_gather(m.astype(BF16), "shard", axis=0, tiled=True)
            for m in (w_qkv, w_out, w_gate_up, w_down)
        ]
        mat_qkv_out, mat_gate_up, mat_down = [
            Weight(m.shape, whole=m)
            for m in (jnp.concatenate([mat_qkv, mat_out], axis=1), mat_gate_up, mat_down.T)
        ]
        cut_qkv_out = cut_gate_up = cut_down = None

    qkv, attended, *tables, scale, gains, whole = attention_forward(
        idx, x_t, segments, frequency, gains, mat_qkv_out
    ) + (() if fast else (None,))
    if fast:
        mat_qkv_out = Weight(whole.shape, whole=whole)
    middle, normed_low, ab, hidden, *grad_down = feed_forward(
        idx, x_t, attended, gains, y_t, mat_qkv_out, mat_gate_up, cut_down, ()
    )
    after = ()
    if fast:
        whole = grad_down.pop()
        mat_gate_up = Weight(whole.shape, whole=whole)

        (down_near,) = step(
            pass_on, [down_near], [sds(down_near.shape, BF16)], "pass_on", (attended,), 0.1
        )
        down_place = lambda o, c, x, low: (c * 2 * HALF, o * down_rows)
        mat_down = Weight(
            (width, FF),
            own=[(down_t, lambda o: (0, o * down_rows))],
            parts=[
                (down_near, (0, 0, 0), down_place),
                (over_core(down_near), (1, 0, 0), down_place),
            ],
        )
    if fast:
        arrived_down = over_core(grad_down[0])
    gated, *grad_gate_up = feed_back(idx, ab, normed_low, y_t, mat_down, cut_gate_up)
    if fast:
        down_whole = grad_gate_up.pop()
        cut = lambda a, *lead: a.reshape(*lead, *a.shape[-2:])
        arrived_gate_up = over_core(grad_gate_up[0])
        ((send, keep_down),) = add_step(
            [(grad_down[1][0], arrived_down[0], 0)], "down_core", (gated,)
        )
        arrived_down = over_y(send)
        after = (keep_down,)
    grad_middle, grad_attended, gain_two = middle_back(
        idx, y_t, middle, gated, gains, mat_gate_up, mat_qkv_out, after
    )
    if fast:
        halves = [
            [cut(a[p], *lead) for a in (grad_gate_up[1], arrived_gate_up)]
            for p, lead in ((0, (2, 2, 4)), (1, (4, 2, 2)))
        ]
        (send_up, keep_up), (send_low, keep_low) = add_step(
            [(*halves[0], 1), (*halves[1], 1)], "gate_up_core", (grad_middle,)
        )
        arrived_up, arrived_low = over_x(send_up), over_z_low(send_low)
        after = (keep_up,)
    grad_normed, *grad_qkv_out = attention_back(
        idx,
        grad_middle,
        grad_attended,
        gain_two,
        qkv,
        attended,
        tables,
        gains,
        mat_qkv_out,
        cut_qkv_out,
        after,
    )
    finish = (grad_middle, grad_normed, tables[3], scale, gains)
    if not fast:
        output, token_grad = finish_tokens(middle, hidden, mat_down.arrays[0], *finish, ())
    if fast:

        arrived_qkv_out = over_core(grad_qkv_out[0])
        piece = (CUT_ROWS, CUT_COLUMNS)
        taller = (CUT_ROWS + 8, CUT_COLUMNS)
        ((send, keep_down),) = add_step(
            [(cut(keep_down, 2, 4), cut(arrived_down, 2, 4), 0)], "down_y", (grad_qkv_out[2],)
        )
        arrived_down = over_x(send)
        ((send, keep_qkv_out),) = add_step(
            [(grad_qkv_out[1][0], arrived_qkv_out[0], 0)], "qkv_out_core", (keep_down,), 0.1
        )
        arrived_qkv_out = over_y(send)
        (send_up, keep_up), (send_low, keep_low) = add_step(
            [
                (cut(keep_up, 2, 2, 2), cut(arrived_up, 2, 2, 2), 1),
                (cut(keep_low, 2, 2, 2), cut(arrived_low, 2, 2, 2), 1),
            ],
            "up_x_low_z",
            (keep_qkv_out,),
            20,
        )
        arrived_up, arrived_low = over_z_low(send_up), over_x(send_low)
        ((send, keep_down),) = add_step(
            [(cut(keep_down, 2, 2), cut(arrived_down, 2, 2), 0)], "down_x", (keep_up,), 0.1
        )
        arrived_down = over_z_low(send)

        def columns(ins, outs):
            total = ins[0][...] + ins[1][...].astype(F32)
            outs[0][...] = total[1].astype(BF16)
            outs[1][...] = total[0]
            total = ins[2][...] + ins[3][...].astype(F32)
            outs[2][0], outs[2][1] = total[0, 1].astype(BF16), total[1, 1].astype(BF16)
            outs[3][...] = total[:, 0]
            total = ins[4][...] + ins[5][...].astype(F32)
            outs[2][2] = total[1].astype(BF16)
            outs[4][...] = total[0]

        ((send, keep_qkv_out),) = add_step(
            [(cut(keep_qkv_out, 2, 4), cut(arrived_qkv_out, 2, 4), 0)],
            "qkv_out_y",
            (keep_down,),
            0.1,
        )
        arrived_qkv_out = over_x(send)
        send_up, keep_up, send, keep_low, keep_down = step(
            columns,
            [keep_up, arrived_up, keep_low, arrived_low, keep_down, arrived_down],
            [
                *(sds((2, *piece), BF16), sds((2, *piece), F32)),
                *(sds((3, *piece), BF16), sds((2, *piece), F32)),
                sds(piece, F32),
            ],
            "columns",
            (keep_qkv_out,),
        )
        arrived_up, arrived = over_y(send_up), over_z_high(send)

        def planes(ins, outs):
            keep_up, arrived_up, keep_low, arrived, keep_down, keep_qkv_out, arrived_qkv_out = ins
            total = keep_up[...] + arrived_up[...].astype(F32)
            outs[0][0] = total[1].astype(BF16)
            outs[1][0] = total[0]
            outs[0][1] = (keep_down[...] + arrived[2].astype(F32)).astype(BF16)
            outs[2][...] = (keep_low[1] + arrived[1].astype(F32)).astype(BF16)
            outs[1][1] = keep_low[0] + arrived[0].astype(F32)
            total = keep_qkv_out[...] + arrived_qkv_out[...].astype(F32)
            outs[3][...] = total[1].astype(BF16)
            outs[4][...] = total[0]

        send, keep, send_low, send_qkv_out, keep_qkv_out = step(
            planes,
            [
                *(keep_up, arrived_up, keep_low, arrived, keep_down),
                *(cut(keep_qkv_out, 2, 2), cut(arrived_qkv_out, 2, 2)),
            ],
            [
                *(sds((2, *piece), BF16), sds((2, *piece), F32), sds(piece, BF16)),
                *(sds((2, *taller), BF16), sds((2, *taller), F32)),
            ],
            "planes",
        )
        arrived, arrived_low = over_z_high(send), over_y(send_low)
        arrived_qkv_out = over_z_low(send_qkv_out)

        def lines(ins, outs):
            send, keep, arrived, arrived_low, keep_qkv_out, arrived_qkv_out = ins
            total = keep_qkv_out[...] + arrived_qkv_out[...].astype(F32)
            outs[0][0] = total[1].astype(BF16)
            outs[1][...] = total[0]
            for part, came in enumerate((arrived[0], arrived_low[...])):
                total = keep[part] + came.astype(F32)
                total = jnp.concatenate([total, jnp.zeros((8, CUT_COLUMNS), F32)], axis=0)
                outs[0][part + 1] = total.astype(BF16)
            outs[2][0], outs[2][1] = send[1], arrived[1]

        pieces, keep_qkv_out, near_down = step(
            lines,
            [send, keep, arrived, arrived_low, keep_qkv_out, arrived_qkv_out],
            [sds((3, *taller), BF16), sds(taller, F32), sds((2, *piece), BF16)],
            "lines",
            (w_gate_up, first_gate_up, second_gate_up),
        )
        arrived, down_low = over_z_high(pieces), over_z_low(near_down)

        def share_high(ins, outs):
            pieces, arrived, keep_qkv_out, near_down, down_low = ins
            for high in range(2):
                outs[0][0, high], outs[0][1, high] = near_down[high], down_low[high]
            outs[0][2, 0], outs[0][2, 1] = pieces[1, :CUT_ROWS], arrived[1, :CUT_ROWS]
            outs[1][0], outs[1][1] = pieces[2, :CUT_ROWS], arrived[2, :CUT_ROWS]
            outs[2][...] = (keep_qkv_out[...] + arrived[0].astype(F32)).astype(BF16)

        near_x, near_low, piece_qkv_out = step(
            share_high,
            [pieces, arrived, keep_qkv_out, near_down, down_low],
            [sds((3, 2, *piece), BF16), sds((2, *piece), BF16), sds(taller, BF16)],
            "share_high",
            (
                *(w_qkv, w_out, first_qkv, first_out, second_qkv, second_out),
                *(down_t, first_down_t, second_down_t, first_gains, second_gains),
            ),
        )
        arrived_x, low_low = over_x(near_x), over_z_low(near_low)
        qkv_out_high = over_z_high(piece_qkv_out)
        output, token_grad = finish_tokens(middle, hidden, down_whole, *finish, (near_x,))

        def share_next(ins, outs):
            near_x, arrived_x, near_low, low_low = ins
            outs[0][0], outs[0][1] = near_x[2], arrived_x[2]
            outs[1][0], outs[1][1] = near_low[...], low_low[...]
            for low in range(2):
                for high in range(2):
                    outs[2][0, 0, low * 2 + high] = near_x[low, high]
                    outs[2][0, 1, low * 2 + high] = arrived_x[low, high]

        near_up, near_low, near_down = step(
            share_next,
            [near_x, arrived_x, near_low, low_low],
            [
                *(sds((2, 2, *piece), BF16), sds((2, 2, *piece), BF16)),
                sds((1, 2, 4, *piece), BF16),
            ],
            "share_next",
            (qkv_out_high,),
        )
        far_down = over_core(near_down)
        up_low, low_x = over_z_low(near_up), over_x(near_low)

        def share_qkv_out_high(ins, outs):
            outs[0][0], outs[0][1] = ins[0][...], ins[1][...]

        (near_qkv_out,) = step(
            share_qkv_out_high,
            [piece_qkv_out, qkv_out_high],
            [sds((2, *taller), BF16)],
            "share_qkv_out_high",
            (near_up,),
        )
        qkv_out_x, qkv_out_low = over_x(near_qkv_out), over_z_low(near_qkv_out)
        qkv_out_both = swap(near_qkv_out, "dp", 6)
        one_down, two_down, next_down, mark = update_rows(
            idx,
            [(0, near_down), (1, far_down)],
            lambda p, x, z: (
                (x * 2 + (z >> 1)) * CUT_ROWS,
                [(0, CUT_COLUMNS, (z & 1) * CUT_COLUMNS)],
            ),
            2 * HALF,
            96,
            [down_t, first_down_t, second_down_t],
            (),
            (),
            "update_down",
            (near_qkv_out,),
            0.1,
        )

        def share_gate_up(ins, outs):
            for near in range(2):
                for far in range(2):
                    for high in range(2):
                        outs[0][0, near, far * 2 + high] = ins[far][near, high]
                        outs[0][1, far, near * 2 + high] = ins[2 + far][near, high]

        (near_gate_up,) = step(
            share_gate_up,
            [near_up, up_low, near_low, low_x],
            [sds((2, 2, 4, *piece), BF16)],
            "share_gate_up",
            (mark,),
        )
        far_gate_up = over_core(near_gate_up)
        place_gate_up = lambda p, x, z: (p * CUT_ROWS, [(0, CUT_COLUMNS, (x * 4 + z) * CUT_COLUMNS)])
        state_gate_up = [w_gate_up, first_gate_up, second_gate_up]
        *near_state, mark = update_rows(
            idx,
            [(0, near_gate_up)],
            place_gate_up,
            HALF,
            24,
            state_gate_up,
            (),
            (),
            "update_gate_up_near",
            (),
        )

        def share_qkv_out(ins, outs):
            for x in range(2):
                for low in range(2):
                    for high in range(2):
                        outs[0][0, x, low * 2 + high] = ins[low * 2 + x][high]

        (near_qkv_out,) = step(
            share_qkv_out,
            [near_qkv_out, qkv_out_x, qkv_out_low, qkv_out_both],
            [sds((1, 2, 4, *taller), BF16)],
            "share_qkv_out",
            (mark,),
        )
        far_qkv_out = over_core(near_qkv_out)
        one_gate_up, two_gate_up, next_gate_up, mark = update_rows(
            idx,
            [(1, far_gate_up)],
            place_gate_up,
            HALF,
            24,
            state_gate_up,
            near_state,
            (),
            "update_gate_up_far",
            (near_qkv_out,),
        )
        cuts = [[(0, 384, 0)], [(0, 384, 384)], [(0, 192, 768), (192, 192, 1024)], [(0, 384, 1216)]]
        updated = update_rows(
            idx,
            [(0, near_qkv_out), (1, far_qkv_out)],
            lambda p, x, z: (x * CUT_ROWS, cuts[z]),
            HALF,
            48,
            [w_qkv, w_out, first_qkv, first_out, second_qkv, second_out],
            (),
            (norm_gains, first_gains, second_gains),
            "update_qkv_out",
            (mark,),
        )
        one_qkv, one_out, two_qkv, two_out, next_qkv, next_out = updated[:6]
        one_gains, two_gains, next_gains = updated[6:9]
    else:
        sums = lax.psum((*grad_qkv_out, grad_gate_up[0], grad_down[0].T), ("dp", "shard"))
        grad_qkv_out, grad_gains, grad_gate_up, grad_down = sums

        def own(grad, axis=0):
            size = grad.shape[axis] // groups
            return lax.dynamic_slice_in_dim(grad, owner * size, size, axis)

        one_qkv, two_qkv, next_qkv = adamw(
            w_qkv, first_qkv, second_qkv, own(grad_qkv_out[:, :QKV]), RATE_MATRIX, DECAY_MATRIX
        )
        one_out, two_out, next_out = adamw(
            w_out, first_out, second_out, own(grad_qkv_out[:, QKV:]), RATE_MATRIX, DECAY_MATRIX
        )
        one_gate_up, two_gate_up, next_gate_up = adamw(
            w_gate_up, first_gate_up, second_gate_up, own(grad_gate_up), RATE_MATRIX, DECAY_MATRIX
        )
        one_down, two_down, next_down = [
            a.T
            for a in adamw(
                w_down, first_down, second_down, own(grad_down), RATE_MATRIX, DECAY_MATRIX
            )
        ]
        one_gains, two_gains, next_gains = adamw(
            norm_gains, first_gains, second_gains, own(grad_gains, 1), RATE_GAIN, 0.0
        )
    one_down, two_down, next_down = one_down.T, two_down.T, next_down.T
    return (
        output.T[None],
        token_grad.T[None],
        one_qkv,
        one_out,
        one_gate_up,
        one_down,
        one_gains,
        two_qkv,
        two_out,
        two_gate_up,
        two_down,
        two_gains,
        next_qkv,
        next_out,
        next_gate_up,
        next_down,
        next_gains,
    )


def solution(mesh):
    return jax.shard_map(
        per_device,
        mesh=mesh,
        in_specs=(
            P(("dp", "shard"), None, None),
            P(("dp", "shard"), None),
            P(("dp", "shard"), None, None),
            P("shard", None),
            P("shard", None),
            P("shard", None),
            P("shard", None),
            P(None, "shard"),
            P("shard", None),
            P("shard", None),
            P("shard", None),
            P("shard", None),
            P(None, "shard"),
            P("shard", None),
            P("shard", None),
            P("shard", None),
            P("shard", None),
            P(None, "shard"),
        ),
        out_specs=(
            P(("dp", "shard"), None, None),
            P(("dp", "shard"), None, None),
            P("shard", None),
            P("shard", None),
            P("shard", None),
            P("shard", None),
            P(None, "shard"),
            P("shard", None),
            P("shard", None),
            P("shard", None),
            P("shard", None),
            P(None, "shard"),
            P("shard", None),
            P("shard", None),
            P("shard", None),
            P("shard", None),
            P(None, "shard"),
        ),
        check_vma=False,
    )
```

```python
import functools

import jax
import jax.numpy as jnp
import numpy as np
from jax import lax
from jax.experimental import pallas as pl
from jax.experimental.pallas import tpu as pltpu
from jax.sharding import PartitionSpec as P

HEADS = 9
KV_HEADS = 3
GROUP = HEADS // KV_HEADS
HEAD = 64
FF = 1536
STEP = 10
QUERY = HEADS * HEAD
ROPED = (HEADS + KV_HEADS) * HEAD
QKV = (HEADS + 2 * KV_HEADS) * HEAD
LANES = 128

EPS_NORM = 1e-05
ROPE_BASE = 100000.0
BETA_ONE = 0.9
BETA_TWO = 0.95
RATE_MATRIX = 0.1
RATE_GAIN = 0.3
DECAY_MATRIX = 0.1
EPS_ADAM = 1e-08
MASKED = -1e30
SCALE = float(HEAD) ** (-0.5)
VMEM_LIMIT = 32 * 1024 * 1024
PACK_LIMIT = 53 * 1024 * 1024
STEP_LIMIT = 14 * 1024 * 1024
UPDATE_LIMIT = 20 * 1024 * 1024
HALF = 144
CUT_ROWS = 72
MARK = (8, 128)
CUT_COLUMNS = 384
F32 = jnp.float32
BF16 = jnp.bfloat16


def rotate_block(values, cosine, signed_sine):
    lane = lax.broadcasted_iota(jnp.int32, values.shape, 1)
    swapped = jnp.where(
        lane % HEAD < HEAD // 2,
        pltpu.roll(values, LANES - HEAD // 2, 1),
        pltpu.roll(values, HEAD // 2, 1),
    )
    return values * cosine + swapped * signed_sine


def adamw(weight, first_moment, second_moment, gradient, step_rate, weight_decay):
    first_new = BETA_ONE * first_moment + (1.0 - BETA_ONE) * gradient
    second_new = BETA_TWO * second_moment + (1.0 - BETA_TWO) * gradient * gradient
    fix_one = 1.0 / (1.0 - BETA_ONE**STEP)
    fix_two = 1.0 / (1.0 - BETA_TWO**STEP)
    update = first_new * fix_one / (jnp.sqrt(second_new * fix_two) + EPS_ADAM)
    return (first_new, second_new, weight - step_rate * (update + weight_decay * weight))


def adamw_rows(weight, first_moment, second_moment, gradient, step_rate, weight_decay):
    first_new = BETA_ONE * first_moment + (1.0 - BETA_ONE) * gradient
    second_new = BETA_TWO * second_moment + (1.0 - BETA_TWO) * gradient * gradient
    value = second_new * (1.0 / (1.0 - BETA_TWO**STEP))
    guess = lax.rsqrt(value)
    divisor = value * guess + EPS_ADAM
    inverse = guess * (2.0 - divisor * guess)
    update = first_new * (step_rate / (1.0 - BETA_ONE**STEP)) * inverse
    return (first_new, second_new, weight * (1.0 - step_rate * weight_decay) - update)


def dot(left, right):
    return lax.dot_general(left, right, (((1,), (0,)), ((), ())), preferred_element_type=F32)


def dot_right_t(left, right):
    return lax.dot_general(left, right, (((1,), (1,)), ((), ())), preferred_element_type=F32)


def dot_left_t(left, right):
    return lax.dot_general(left, right, (((0,), (0,)), ((), ())), preferred_element_type=F32)


def norm_scale(values):
    return lax.rsqrt(jnp.mean(values * values, axis=-1, keepdims=True) + EPS_NORM)


def norm_back(grad_normed, normed, scale_rows):
    return scale_rows * (
        grad_normed - normed * jnp.mean(grad_normed * normed, axis=-1, keepdims=True)
    )


class Weight:
    def __init__(self, shape, whole=None, own=(), parts=()):
        self.shape, self.own, self.parts = shape, own, parts
        self.arrays = [whole] if whole is not None else [a[0] for a in (*own, *parts)]
        self.split = whole is None

    def load(self, idx, refs, full):
        if not self.split:
            return refs[0]
        for ref, (_, place) in zip(refs, self.own):
            self.put(full, place(idx[0]), ref[...].astype(BF16))
        for ref, (_, (core, x, low), place) in zip(refs[len(self.own) :], self.parts):
            place = place(1 - idx[0], idx[1] ^ core, idx[2] ^ x, (idx[3] & 1) ^ low)
            rows = ref.shape[0] // HALF * HALF
            self.put(full, place, ref[:rows, :])
        return full

    def put(self, full, position, value):
        where = []
        for axis, tile in ((0, 16), (1, LANES)):
            at, size = position[axis], value.shape[axis]
            if size == self.shape[axis]:
                where.append(slice(None))
            elif isinstance(at, int):
                where.append(slice(at, at + size))
            else:
                where.append(pl.ds(pl.multiple_of(at, tile), size))
        full[tuple(where)] = value


def call(body, idx, arrays, weights, outs, scratch, busy, name, after=(), hand_on=False):
    counts = [len(w.arrays) for w in weights]
    flat = list(arrays) + [a for w in weights for a in w.arrays]
    outs = list(outs)
    split = [w for w in weights if w.split]
    hand_on = hand_on and bool(split)
    if hand_on:
        outs += [sds(split[-1].shape, BF16)]
    made = [pltpu.VMEM(w.shape, BF16) for w in (split[:-1] if hand_on else split)]

    def kernel(*refs):
        refs = list(refs)
        idx_ref = refs.pop(0)
        take = lambda n: [refs.pop(0) for _ in range(n)]
        array_refs = take(len(arrays))
        weight_refs = [take(n) for n in counts]
        take(len(after))
        out_refs = take(len(outs))
        own_scratch = take(len(scratch))
        fulls = take(len(made)) + ([out_refs.pop()] if hand_on else [])
        loads = [
            functools.partial(w.load, idx_ref, r, fulls.pop(0) if w.split else None)
            for w, r in zip(weights, weight_refs)
        ]
        body(idx_ref, array_refs, loads, out_refs, own_scratch)

    return pl.pallas_call(
        kernel,
        out_shape=tuple(outs),
        in_specs=[pl.BlockSpec(memory_space=pltpu.SMEM)]
        + [pl.BlockSpec(memory_space=pltpu.VMEM)] * len(flat)
        + [pl.BlockSpec(memory_space=pl.ANY)] * len(after),
        out_specs=tuple([pl.BlockSpec(memory_space=pltpu.VMEM)] * len(outs)),
        scratch_shapes=list(scratch) + made,
        compiler_params=pltpu.CompilerParams(vmem_limit_bytes=VMEM_LIMIT),
        cost_estimate=busy_for(busy),
        name=name,
    )(idx, *flat, *after)


def busy_for(microseconds):
    return pl.CostEstimate(flops=int(microseconds * 1e9), bytes_accessed=0, transcendentals=0)


def sds(shape, dtype):
    return jax.ShapeDtypeStruct(shape, dtype)


class Pieces:
    def __init__(self, place, parts=1, extra=0):
        self.place, self.parts, self.extra = place, parts, extra

    def outs(self):
        return [sds((self.parts, 2, 8, CUT_ROWS + self.extra, CUT_COLUMNS), BF16)] * 2

    def scratch(self, columns):
        return pltpu.VMEM((8, CUT_ROWS, columns), BF16)

    def store(self, blocks, grad, start=0):
        for i in range(8):
            rows = grad[i * CUT_ROWS : (i + 1) * CUT_ROWS].astype(BF16)
            blocks[i, :, start : start + grad.shape[1]] = rows

    def emit(self, idx, blocks, outs, under=None):
        for other_core, out in enumerate((outs[1], outs[0])):
            for part in range(self.parts):
                for owner in range(2):
                    for slot in range(8):
                        z = ((slot >> 1) & 1) | ((slot & 1) << 1)
                        block, column = self.place(
                            idx[0] ^ owner, idx[1] ^ other_core, idx[2] ^ (slot >> 2), idx[3] ^ z, part
                        )
                        columns = pl.ds(pl.multiple_of(column * CUT_COLUMNS, LANES), CUT_COLUMNS)
                        piece = blocks[block, :, columns]
                        if under is not None:
                            piece = jnp.concatenate(
                                [piece.astype(F32), under[idx[0] ^ owner]], axis=0
                            ).astype(BF16)
                        out[part, owner, slot] = piece


def head_stack(values, kv_head):
    first = kv_head * GROUP
    return jnp.concatenate(
        [values[:, (first + i) * HEAD : (first + i + 1) * HEAD] for i in range(GROUP)], axis=0
    )


def softmax_rows(query, key, allowed):
    scores = jnp.where(allowed, dot_right_t(query, key) * SCALE, MASKED)
    top = jnp.max(scores, axis=-1, keepdims=True)
    exponent = jnp.exp(scores - top)
    return exponent / jnp.sum(exponent, axis=-1, keepdims=True)


def pack_kernel(body, idx, sources, places, outs, name, after=(), limit=PACK_LIMIT):
    windows = [shape for shape, _ in places]

    def kernel(idx_ref, *refs):
        sources_in, refs = refs[: len(sources)], refs[len(sources) + len(after) :]
        out_refs, buffers, sem = refs[: len(outs)], refs[len(outs) : -1], refs[-1]
        copies = []
        for i, (source, (shape, place)) in enumerate(zip(sources_in, places)):
            where = []
            for axis, tile in ((0, 8), (1, LANES)):
                if shape[axis] == source.shape[axis]:
                    where.append(slice(None))
                else:
                    where.append(pl.ds(pl.multiple_of(place(idx_ref)[axis], tile), shape[axis]))
            copies.append(pltpu.make_async_copy(source.at[tuple(where)], buffers[i], sem.at[i]))
        for copy in copies:
            copy.start()
        for copy in copies:
            copy.wait()
        body(idx_ref, buffers, out_refs)

    return pl.pallas_call(
        kernel,
        out_shape=tuple(outs),
        in_specs=[pl.BlockSpec(memory_space=pltpu.SMEM)]
        + [pl.BlockSpec(memory_space=pltpu.HBM)] * len(sources)
        + [pl.BlockSpec(memory_space=pl.ANY)] * len(after),
        out_specs=tuple([pl.BlockSpec(memory_space=pltpu.VMEM)] * len(outs)),
        scratch_shapes=[pltpu.VMEM(w, F32) for w in windows]
        + [pltpu.SemaphoreType.DMA((len(sources),))],
        compiler_params=pltpu.CompilerParams(vmem_limit_bytes=limit),
        cost_estimate=busy_for(10),
        name=name,
    )(idx, *sources, *after)


def cast_out(idx_ref, buffers, outs):
    for buffer, out in zip(buffers, outs):
        out[...] = buffer[...].astype(BF16)


def pack_down(idx, down_t, after):
    shape = (2 * HALF, down_t.shape[1])
    window = (shape, lambda i: (i[1] * 2 * HALF, 0))
    outs = [sds(shape, BF16)]
    return pack_kernel(
        cast_out, idx, [down_t], [window], outs, "pack_down", after, STEP_LIMIT
    )[0]


def pack_first(idx, w_qkv, w_out, norm_gains, w_gate_up):
    columns = (QKV + w_out.shape[1]) // 2
    quarter = FF // 2
    windows = [((HALF, m.shape[1]), lambda i: (i[1] * HALF, 0)) for m in (w_qkv, w_out)]
    windows.append((norm_gains.shape, lambda i: (0, 0)))
    windows.append(((HALF, quarter), lambda i: (i[1] * HALF, i[2] * quarter)))
    windows.append(((HALF, quarter), lambda i: (i[1] * HALF, FF + (i[3] & 1) * quarter)))

    def body(idx_ref, buffers, outs):
        q_ref, o_ref, gains_ref = buffers[:3]
        both = jnp.concatenate([q_ref[:, columns:], o_ref[...]], axis=1)
        outs[0][:HALF, :] = jnp.where((idx_ref[3] & 1) == 0, q_ref[:, :columns], both).astype(BF16)
        outs[0][HALF:, :] = jnp.zeros((16, columns), BF16)
        outs[0][HALF : HALF + 2, : gains_ref.shape[1]] = gains_ref[...].astype(BF16)
        cast_out(idx_ref, buffers[3:], outs[1:])

    outs = [sds((HALF + 16, columns), BF16)] + [sds((HALF, quarter), BF16)] * 2
    sources = [w_qkv, w_out, norm_gains, w_gate_up, w_gate_up]
    return pack_kernel(body, idx, sources, windows, outs, "pack_first")


def attention_forward(idx, tokens_t, segments, frequency, gains, w_qkv_out):
    width, seq_length = tokens_t.shape
    split_gains = len(gains) > 1

    def body(idx_ref, arrays, loads, outs, scratch):
        x_ref, seg_ref, freq_ref = arrays[:3]
        qkv_ref, o_ref, cos_ref, sin_ref, probs_ref, normed_ref, scale_ref, gains_ref = outs
        if split_gains:
            own = arrays[3][...].astype(BF16).astype(F32)
            other = arrays[4][HALF : HALF + 8, : width // 2].astype(F32)[:2]
            gains_ref[...] = jnp.where(
                idx_ref[0] == 0,
                jnp.concatenate([own, other], axis=1),
                jnp.concatenate([other, own], axis=1),
            )
        else:
            gains_ref[...] = arrays[3][...]
        seen_doc = jnp.broadcast_to(seg_ref[...], (seq_length, seq_length))
        own_doc = seen_doc.T
        token = lax.broadcasted_iota(jnp.int32, (seq_length, seq_length), 0)
        seen = lax.broadcasted_iota(jnp.int32, (seq_length, seq_length), 1)
        begin = jnp.sum((seen_doc < own_doc).astype(F32), axis=-1, keepdims=True)
        angles = (token.astype(F32) - begin) * freq_ref[...]
        cosine, sine = jnp.cos(angles), jnp.sin(angles)
        sine = jnp.where(seen % HEAD < HEAD // 2, -sine, sine)
        cos_ref[...] = cosine
        sin_ref[...] = sine
        allowed = ((seen_doc == own_doc) & (token >= seen)).astype(F32)
        allowed = jnp.concatenate([allowed] * GROUP, axis=0) > 0.5
        x = x_ref[...].astype(F32).T
        scale_ref[...] = norm_scale(x)
        normed_ref[...] = x * scale_ref[...]
        h1 = (normed_ref[...] * gains_ref[0:1, :]).astype(BF16)
        projected = dot(h1, loads[0]()[:, :QKV])
        for start in range(0, ROPED, LANES):
            block = projected[:, start : start + LANES]
            qkv_ref[:, start : start + LANES] = rotate_block(block, cosine, sine).astype(BF16)
        qkv_ref[:, ROPED:QKV] = projected[:, ROPED:QKV].astype(BF16)
        qkv = qkv_ref[...]
        for kv in range(KV_HEADS):
            key = qkv[:, QUERY + kv * HEAD : QUERY + (kv + 1) * HEAD]
            value = qkv[:, ROPED + kv * HEAD : ROPED + (kv + 1) * HEAD]
            probs = softmax_rows(head_stack(qkv, kv), key, allowed)
            probs_ref[kv] = probs
            attended = dot(probs.astype(BF16), value).astype(BF16)
            for i in range(GROUP):
                start = (kv * GROUP + i) * HEAD
                o_ref[:, start : start + HEAD] = attended[i * seq_length : (i + 1) * seq_length]

    square = sds((seq_length, seq_length), F32)
    outs = [sds((seq_length, QKV), BF16), sds((seq_length, QUERY), BF16)]
    outs += [square, square, sds((KV_HEADS, GROUP * seq_length, seq_length), F32)]
    outs += [sds((seq_length, width), F32), sds((seq_length, 1), F32), sds((2, width), F32)]
    return call(
        body,
        idx,
        [tokens_t, segments, frequency, *gains],
        [w_qkv_out],
        outs,
        [],
        1,
        "attention",
        hand_on=True,
    )


def feed_forward(idx, tokens_t, attended, gains, cotangent_t, w_qkv_out, w_gate_up, pieces, after):
    width, seq_length = tokens_t.shape

    def body(idx_ref, arrays, loads, outs, scratch):
        x_ref, o_ref, gains_ref, y_ref = arrays
        u_ref, h2_ref, ab_ref, z_ref = outs[:4]
        u = x_ref[...].astype(F32).T + dot(o_ref[...], loads[0]()[:, QKV:])
        u_ref[...] = u
        h2 = (u * norm_scale(u) * gains_ref[1:2, :]).astype(BF16)
        h2_ref[...] = h2
        ab = dot(h2, loads[1]()[...])
        ab_ref[...] = ab
        gate, up = ab[:, :FF], ab[:, FF:]
        z = (gate * jax.nn.sigmoid(gate) * up).astype(BF16)
        z_ref[...] = z
        grad = dot(y_ref[...], z)
        if pieces is None:
            outs[4][...] = grad
        else:
            pieces.store(scratch[0], grad)
            pieces.emit(idx_ref, scratch[0], outs[4:])

    outs = [
        sds((seq_length, width), F32),
        sds((seq_length, width), BF16),
        sds((seq_length, 2 * FF), F32),
        sds((seq_length, FF), BF16),
    ]
    outs += [sds((width, FF), F32)] if pieces is None else pieces.outs()
    scratch = [] if pieces is None else [pieces.scratch(FF)]
    return call(
        body,
        idx,
        [tokens_t, attended, gains, cotangent_t],
        [w_qkv_out, w_gate_up],
        outs,
        scratch,
        5,
        "feed_forward",
        after,
        True,
    )


def feed_back(idx, ab, normed_low, cotangent_t, down_t, pieces):
    width, seq_length = cotangent_t.shape

    def body(idx_ref, arrays, loads, outs, scratch):
        ab_ref, h2_ref, y_ref = arrays
        gg_ref = outs[0]
        gate, up = ab_ref[:, :FF], ab_ref[:, FF:]
        sig = jax.nn.sigmoid(gate)
        grad_hidden = dot_left_t(y_ref[...], loads[0]()[...])
        gg_ref[:, :FF] = (grad_hidden * up * sig * (1.0 + gate * (1.0 - sig))).astype(BF16)
        gg_ref[:, FF:] = (grad_hidden * gate * sig).astype(BF16)
        grad = dot_left_t(h2_ref[...], gg_ref[...])
        if pieces is None:
            outs[1][...] = grad
        else:
            pieces.store(scratch[0], grad)
            pieces.emit(idx_ref, scratch[0], outs[1:])

    outs = [sds((seq_length, 2 * FF), BF16)]
    outs += [sds((width, 2 * FF), F32)] if pieces is None else pieces.outs()
    scratch = [] if pieces is None else [pieces.scratch(2 * FF)]
    return call(
        body,
        idx,
        [ab, normed_low, cotangent_t],
        [down_t],
        outs,
        scratch,
        20,
        "feed_back",
        hand_on=True,
    )


def finish_tokens(middle, hidden, down_t, grad_middle, grad_normed, normed, scale, gains, after):
    seq_length, width = middle.shape

    def body(ins, outs):
        u_ref, z_ref, down_ref, gu_ref, grad_ref, normed_ref, scale_ref, gains_ref = ins
        outs[0][...] = (u_ref[...] + dot_right_t(z_ref[...], down_ref[...])).T.astype(BF16)
        grad = grad_ref[...] * gains_ref[0:1, :]
        grad = gu_ref[...] + norm_back(grad, normed_ref[...], scale_ref[...])
        outs[1][...] = grad.T.astype(BF16)

    arrays = [middle, hidden, down_t, grad_middle, grad_normed, normed, scale, gains]
    outs = [sds((width, seq_length), BF16)] * 2
    return step(body, arrays, outs, "finish_tokens", after, 2)


def middle_back(idx, cotangent_t, middle, gated, gains, w_gate_up, w_qkv_out, after):
    width, seq_length = cotangent_t.shape

    def body(idx_ref, arrays, loads, outs, scratch):
        y_ref, u_ref, gg_ref, gains_ref = arrays
        gu_ref, go_ref, gain_ref = outs
        u = u_ref[...]
        scale_two = norm_scale(u)
        normed = u * scale_two
        grad_normed = dot_right_t(gg_ref[...], loads[0]()[...])
        gain_ref[...] = jnp.sum(grad_normed * normed, axis=0, keepdims=True)
        gu = y_ref[...].astype(F32).T + norm_back(
            grad_normed * gains_ref[1:2, :], normed, scale_two
        )
        gu_ref[...] = gu
        go_ref[...] = dot_right_t(gu.astype(BF16), loads[1]()[:, QKV:]).astype(BF16)

    outs = [sds((seq_length, width), F32), sds((seq_length, width), BF16), sds((1, width), F32)]
    return call(
        body,
        idx,
        [cotangent_t, middle, gated, gains],
        [w_gate_up, w_qkv_out],
        outs,
        [],
        20,
        "middle_back",
        after,
    )


def attention_back(
    idx, grad_middle, grad_attended, gain_two, qkv, attended, tables, gains, w_qkv, pieces, after
):
    seq_length, width = grad_middle.shape

    def body(idx_ref, arrays, loads, outs, scratch):
        gu_ref, go_ref, gain_two_ref, qkv_ref, o_ref = arrays[:5]
        cos_ref, sin_ref, probs_ref, normed_ref, gains_ref = arrays[5:]
        grad_ref = outs[0]
        grad_proj, gp_ref, gain_rows, *blocks = scratch
        gu, go = gu_ref[...], go_ref[...]
        gu_low = gu.astype(BF16)
        grad_gain_two = gain_two_ref[...]
        qkv_values = qkv_ref[...]
        for kv in range(KV_HEADS):
            key = qkv_values[:, QUERY + kv * HEAD : QUERY + (kv + 1) * HEAD]
            value = qkv_values[:, ROPED + kv * HEAD : ROPED + (kv + 1) * HEAD]
            query = head_stack(qkv_values, kv)
            grad_out = head_stack(go, kv)
            probs = probs_ref[kv]
            grad_probs = dot_right_t(grad_out, value)
            row_delta = jnp.sum(probs * grad_probs, axis=-1, keepdims=True)
            gs = (probs * (grad_probs - row_delta)).astype(BF16)
            grad_query = dot(gs, key) * SCALE
            for i in range(GROUP):
                start = (kv * GROUP + i) * HEAD
                grad_proj[:, start : start + HEAD] = grad_query[
                    i * seq_length : (i + 1) * seq_length
                ]
            start = QUERY + kv * HEAD
            grad_proj[:, start : start + HEAD] = dot_left_t(gs, query) * SCALE
            start = ROPED + kv * HEAD
            grad_proj[:, start : start + HEAD] = dot_left_t(probs.astype(BF16), grad_out)
        for start in range(0, ROPED, LANES):
            gp_ref[:, start : start + LANES] = rotate_block(
                grad_proj[:, start : start + LANES], cos_ref[...], -sin_ref[...]
            ).astype(BF16)
        gp_ref[:, ROPED:QKV] = grad_proj[:, ROPED:QKV].astype(BF16)
        normed = normed_ref[...]
        h1 = (normed * gains_ref[0:1, :]).astype(BF16)
        grad_qkv = dot_left_t(h1, gp_ref[...])
        grad_out = dot_left_t(o_ref[...], gu_low)
        grad_normed = dot_right_t(gp_ref[...], loads[0]()[:, :QKV])
        grad_gain_one = jnp.sum(grad_normed * normed, axis=0, keepdims=True)
        if pieces is None:
            outs[1][:, :QKV] = grad_qkv
            outs[1][:, QKV:] = grad_out
            outs[2][0:1, :] = grad_gain_one
            outs[2][1:2, :] = grad_gain_two
        else:
            pieces.store(blocks[0], grad_qkv)
            pieces.store(blocks[0], grad_out, QKV)
            half = width // 2
            gain_rows[...] = jnp.zeros_like(gain_rows)
            for owner in range(2):
                columns = slice(owner * half, (owner + 1) * half)
                gain_rows[owner, 0:1, :half] = grad_gain_one[:, columns]
                gain_rows[owner, 1:2, :half] = grad_gain_two[:, columns]
            pieces.emit(idx_ref, blocks[0], outs[1:3], gain_rows)
            outs[3][...] = jnp.zeros_like(outs[3])
        grad_ref[...] = grad_normed

    outs = [sds((seq_length, width), F32)]
    scratch = [
        pltpu.VMEM((seq_length, QKV), F32),
        pltpu.VMEM((seq_length, QKV), BF16),
        pltpu.VMEM((2, 8, CUT_COLUMNS), F32),
    ]
    if pieces is None:
        outs += [sds((width, QKV + width), F32), sds((2, width), F32)]
    else:
        outs += pieces.outs() + [sds(MARK, F32)]
        scratch += [pieces.scratch(QKV + width)]
    return call(
        body,
        idx,
        [grad_middle, grad_attended, gain_two, qkv, attended, *tables, gains],
        [w_qkv],
        outs,
        scratch,
        20,
        "attention_back",
        after,
    )


def step(body, arrays, outs, name, after=(), busy=20):
    def kernel(*refs):
        body(refs[: len(arrays)], refs[len(arrays) + len(after) :])

    return pl.pallas_call(
        kernel,
        out_shape=tuple(outs),
        in_specs=[pl.BlockSpec(memory_space=pltpu.VMEM)] * len(arrays)
        + [pl.BlockSpec(memory_space=pl.ANY)] * len(after),
        out_specs=tuple([pl.BlockSpec(memory_space=pltpu.VMEM)] * len(outs)),
        compiler_params=pltpu.CompilerParams(vmem_limit_bytes=STEP_LIMIT),
        cost_estimate=busy_for(busy),
        name=name,
    )(*arrays, *after)


def pass_on(ins, outs):
    outs[0][...] = ins[0][...]


def add_split(keep, arrived, axis, send_ref, keep_ref):
    total = keep[...].astype(F32) + arrived[...].astype(F32)
    low, high = lax.index_in_dim(total, 0, axis, False), lax.index_in_dim(total, 1, axis, False)
    send_ref[...] = high.astype(BF16)
    keep_ref[...] = low


def add_step(jobs, name, after, busy=20):
    arrays, outs = [], []
    for keep, arrived, axis in jobs:
        arrays += [keep, arrived]
        shape = keep.shape[:axis] + keep.shape[axis + 1 :]
        outs += [sds(shape, BF16), sds(shape, F32)]

    def body(ins, out_refs):
        for i, (_, _, axis) in enumerate(jobs):
            add_split(ins[2 * i], ins[2 * i + 1], axis, out_refs[2 * i], out_refs[2 * i + 1])

    flat = step(body, arrays, outs, name, after, busy)
    return [(flat[2 * i], flat[2 * i + 1]) for i in range(len(jobs))]


def update_rows(idx, shares, place, height, chunk, state, earlier, gains, name, after, busy=20):
    count = len(state) // 3
    columns = [a.shape[1] for a in state[:count]]
    starts = [sum(-(-c // LANES) * LANES for c in columns[:k]) for k in range(count + 1)]
    chunks = height // chunk
    order = [(k, count + k, 2 * count + k) for k in range(count)]

    def kernel(idx_ref, *refs):
        refs = list(refs)
        take = lambda n: [refs.pop(0) for _ in range(n)]
        share_refs = take(len(shares))
        state_refs, gain_refs = take(3 * count), take(len(gains))
        take(len(earlier) + len(after))
        outs, gain_outs, (mark,) = take(3 * count), take(len(gains)), take(1)
        buffers, (full, sem) = take(3 * count), refs
        mark[...] = jnp.zeros_like(mark)
        copies = []
        for share, (far, _) in enumerate(shares):
            piece_ref = share_refs[share]
            for part in range(piece_ref.shape[0]):
                for x in range(2):
                    for z in range(4):
                        rel = z ^ idx_ref[3]
                        slot = ((rel & 1) << 1) | (rel >> 1)
                        piece = piece_ref[part, x, slot].astype(F32)[:CUT_ROWS]
                        row, cuts = place(part, idx_ref[2] ^ x, z)
                        rows = pl.ds(pl.multiple_of(share * height + row, 8), CUT_ROWS)
                        for begin, size, to in cuts:
                            if isinstance(to, int):
                                where = slice(to, to + size)
                            else:
                                where = pl.ds(pl.multiple_of(to, LANES), size)
                            full[rows, where] = piece[:, begin : begin + size]
            base = (idx_ref[1] ^ far) * height
            for at_chunk in range(chunks):

                def some_rows(i, carry, at_chunk=at_chunk, share=share, base=base):
                    at_row = at_chunk * chunk + i * 24
                    near_rows = pl.ds(pl.multiple_of(share * height + at_row, 8), 24)
                    rows = pl.ds(pl.multiple_of(base + at_row, 8), 24)
                    for k in range(count):
                        for at in range(0, columns[k], 384):
                            size = min(384, columns[k] - at)
                            where = slice(at, at + size)
                            results = adamw_rows(
                                *[state_refs[j][rows, where] for j in order[k]],
                                full[near_rows, starts[k] + at : starts[k] + at + size],
                                RATE_MATRIX,
                                DECAY_MATRIX,
                            )
                            for j, result in zip(order[k], results):
                                buffers[j][near_rows, where] = result
                    return carry

                lax.fori_loop(0, chunk // 24, some_rows, 0, unroll=2 if chunk > 24 else 1)
                near_rows = pl.ds(share * height + at_chunk * chunk, chunk)
                rows = pl.ds(pl.multiple_of(base + at_chunk * chunk, 8), chunk)
                for j in range(3 * count):
                    copy = pltpu.make_async_copy(
                        buffers[j].at[near_rows],
                        outs[j].at[rows],
                        sem.at[share * chunks + at_chunk, j],
                    )
                    copy.start()
                    copies.append(copy)
        if gains:
            gradient = share_refs[0][0, 0, 0, CUT_ROWS:, :].astype(F32)[:2, : gains[0].shape[1]]
            results = adamw_rows(*[g[...] for g in gain_refs], gradient, RATE_GAIN, 0.0)
            for out, result in zip(gain_outs, results):
                out[...] = result
        for copy in copies:
            copy.wait()

    vmem, anywhere = pl.BlockSpec(memory_space=pltpu.VMEM), pl.BlockSpec(memory_space=pl.ANY)
    first_earlier = 1 + len(shares) + 3 * count + len(gains)
    total = len(shares) * height
    return pl.pallas_call(
        kernel,
        out_shape=tuple(sds(a.shape, F32) for a in [*state, *gains]) + (sds(MARK, F32),),
        in_specs=[pl.BlockSpec(memory_space=pltpu.SMEM)]
        + [vmem] * (len(shares) + 3 * count + len(gains))
        + [anywhere] * (len(earlier) + len(after)),
        out_specs=tuple([anywhere] * (3 * count) + [vmem] * (len(gains) + 1)),
        scratch_shapes=[pltpu.VMEM((total, a.shape[1]), F32) for a in state]
        + [pltpu.VMEM((total, starts[-1]), F32)]
        + [pltpu.SemaphoreType.DMA((len(shares) * chunks, 3 * count))],
        input_output_aliases={first_earlier + i: i for i in range(len(earlier))},
        compiler_params=pltpu.CompilerParams(vmem_limit_bytes=UPDATE_LIMIT),
        cost_estimate=busy_for(busy),
        name=name,
    )(idx, *[p for _, p in shares], *state, *gains, *earlier, *after)


def swap(values, axis, mask):
    size = lax.axis_size(axis)
    return lax.ppermute(values, axis, [(i, i ^ mask) for i in range(size)])


over_y = functools.partial(swap, axis="shard", mask=1)
over_core = functools.partial(swap, axis="dp", mask=1)
over_x = functools.partial(swap, axis="dp", mask=2)
over_z_low = functools.partial(swap, axis="dp", mask=4)
over_z_high = functools.partial(swap, axis="dp", mask=8)


def per_device(
    tokens,
    segments,
    cotangent,
    w_qkv,
    w_out,
    w_gate_up,
    w_down,
    norm_gains,
    first_qkv,
    first_out,
    first_gate_up,
    first_down,
    first_gains,
    second_qkv,
    second_out,
    second_gate_up,
    second_down,
    second_gains,
):
    groups = lax.axis_size("shard")
    replicas = lax.axis_size("dp")
    fast = groups == 2 and replicas == 16
    place_dp = lax.axis_index("dp")
    owner = lax.axis_index("shard")
    idx = jnp.stack([owner, place_dp & 1, (place_dp >> 1) & 1, place_dp >> 2]).astype(jnp.int32)
    x_t, y_t = tokens[0].T, cotangent[0].T
    width, seq_length = x_t.shape
    rows, down_rows = w_qkv.shape[0], w_down.shape[0]
    down_t, first_down_t, second_down_t = w_down.T, first_down.T, second_down.T
    half_size = HEAD // 2
    frequency = ROPE_BASE ** (-(np.arange(half_size) * 2.0 / HEAD))
    frequency = jnp.asarray(np.tile(frequency, 4)[None], F32)
    if fast:
        qo_near, by_x, by_low = pack_first(idx, w_qkv, w_out, norm_gains, w_gate_up)
        qo_near, by_x, by_low = over_y(qo_near), over_y(by_x), over_y(by_low)
        down_near = over_y(pack_down(idx, down_t, (by_low,)))
        by_x_next, by_low_next = over_x(by_x), over_z_low(by_low)
        qo_near_low = over_z_low(qo_near)
        gains = (norm_gains, qo_near)
        (low_far,) = step(
            pass_on, [over_core(by_low_next)], [sds(by_low.shape, BF16)], "pass_on_low", (), 1
        )
        own_rows = lambda o: (o * rows, 0)
        own_rows_out = lambda o: (o * rows, QKV)
        qo_place = lambda o, c, x, low: (o * rows + c * HALF, low * ((QKV + width) // 2))
        x_place = lambda o, c, x, low: (o * rows + c * HALF, x * (FF // 2))
        low_place = lambda o, c, x, low: (o * rows + c * HALF, FF + low * (FF // 2))
        mat_qkv_out = Weight(
            (width, QKV + width),
            own=[(w_qkv, own_rows), (w_out, own_rows_out)],
            parts=[
                (qo_near, (0, 0, 0), qo_place),
                (qo_near_low, (0, 0, 1), qo_place),
                (over_core(qo_near), (1, 0, 0), qo_place),
                (over_core(qo_near_low), (1, 0, 1), qo_place),
            ],
        )
        mat_gate_up = Weight(
            (width, 2 * FF),
            own=[(w_gate_up, own_rows)],
            parts=[
                (by_x, (0, 0, 0), x_place),
                (by_x_next, (0, 1, 0), x_place),
                (over_core(by_x), (1, 0, 0), x_place),
                (over_core(by_x_next), (1, 1, 0), x_place),
                (by_low, (0, 0, 0), low_place),
                (by_low_next, (0, 0, 1), low_place),
                (over_core(by_low), (1, 0, 0), low_place),
                (low_far, (1, 0, 1), low_place),
            ],
        )
        cut_qkv_out = Pieces(lambda o, c, x, z, p: (o * 4 + c * 2 + x, z), extra=8)
        cut_gate_up = Pieces(lambda o, c, x, z, p: (o * 4 + c * 2 + p, x * 4 + z), parts=2)
        cut_down = Pieces(lambda o, c, x, z, p: (c * 4 + x * 2 + (z >> 1), o * 2 + (z & 1)))
    else:
        gains = (
            lax.all_gather(norm_gains.astype(BF16), "shard", axis=1, tiled=True).astype(F32),
        )
        mat_qkv, mat_out, mat_gate_up, mat_down = [
            lax.all_gather(m.astype(BF16), "shard", axis=0, tiled=True)
            for m in (w_qkv, w_out, w_gate_up, w_down)
        ]
        mat_qkv_out, mat_gate_up, mat_down = [
            Weight(m.shape, whole=m)
            for m in (jnp.concatenate([mat_qkv, mat_out], axis=1), mat_gate_up, mat_down.T)
        ]
        cut_qkv_out = cut_gate_up = cut_down = None

    qkv, attended, *tables, scale, gains, whole = attention_forward(
        idx, x_t, segments, frequency, gains, mat_qkv_out
    ) + (() if fast else (None,))
    if fast:
        mat_qkv_out = Weight(whole.shape, whole=whole)
    middle, normed_low, ab, hidden, *grad_down = feed_forward(
        idx, x_t, attended, gains, y_t, mat_qkv_out, mat_gate_up, cut_down, ()
    )
    after = ()
    if fast:
        whole = grad_down.pop()
        mat_gate_up = Weight(whole.shape, whole=whole)

        (down_near,) = step(
            pass_on, [down_near], [sds(down_near.shape, BF16)], "pass_on", (attended,), 0.1
        )
        down_place = lambda o, c, x, low: (c * 2 * HALF, o * down_rows)
        mat_down = Weight(
            (width, FF),
            own=[(down_t, lambda o: (0, o * down_rows))],
            parts=[
                (down_near, (0, 0, 0), down_place),
                (over_core(down_near), (1, 0, 0), down_place),
            ],
        )
    if fast:
        arrived_down = over_core(grad_down[0])
    gated, *grad_gate_up = feed_back(idx, ab, normed_low, y_t, mat_down, cut_gate_up)
    if fast:
        down_whole = grad_gate_up.pop()
        cut = lambda a, *lead: a.reshape(*lead, *a.shape[-2:])
        arrived_gate_up = over_core(grad_gate_up[0])
        ((send, keep_down),) = add_step(
            [(grad_down[1][0], arrived_down[0], 0)], "down_core", (gated,)
        )
        arrived_down = over_y(send)
        after = (keep_down,)
    grad_middle, grad_attended, gain_two = middle_back(
        idx, y_t, middle, gated, gains, mat_gate_up, mat_qkv_out, after
    )
    if fast:
        halves = [
            [cut(a[p], *lead) for a in (grad_gate_up[1], arrived_gate_up)]
            for p, lead in ((0, (2, 2, 4)), (1, (4, 2, 2)))
        ]
        (send_up, keep_up), (send_low, keep_low) = add_step(
            [(*halves[0], 1), (*halves[1], 1)], "gate_up_core", (grad_middle,)
        )
        arrived_up, arrived_low = over_x(send_up), over_z_low(send_low)
        after = (keep_up,)
    grad_normed, *grad_qkv_out = attention_back(
        idx,
        grad_middle,
        grad_attended,
        gain_two,
        qkv,
        attended,
        tables,
        gains,
        mat_qkv_out,
        cut_qkv_out,
        after,
    )
    finish = (grad_middle, grad_normed, tables[3], scale, gains)
    if not fast:
        output, token_grad = finish_tokens(middle, hidden, mat_down.arrays[0], *finish, ())
    if fast:

        arrived_qkv_out = over_core(grad_qkv_out[0])
        piece = (CUT_ROWS, CUT_COLUMNS)
        taller = (CUT_ROWS + 8, CUT_COLUMNS)
        ((send, keep_down),) = add_step(
            [(cut(keep_down, 2, 4), cut(arrived_down, 2, 4), 0)], "down_y", (grad_qkv_out[2],)
        )
        arrived_down = over_x(send)
        ((send, keep_qkv_out),) = add_step(
            [(grad_qkv_out[1][0], arrived_qkv_out[0], 0)], "qkv_out_core", (keep_down,), 0.1
        )
        arrived_qkv_out = over_y(send)
        (send_up, keep_up), (send_low, keep_low) = add_step(
            [
                (cut(keep_up, 2, 2, 2), cut(arrived_up, 2, 2, 2), 1),
                (cut(keep_low, 2, 2, 2), cut(arrived_low, 2, 2, 2), 1),
            ],
            "up_x_low_z",
            (keep_qkv_out,),
            20,
        )
        arrived_up, arrived_low = over_z_low(send_up), over_x(send_low)
        ((send, keep_down),) = add_step(
            [(cut(keep_down, 2, 2), cut(arrived_down, 2, 2), 0)], "down_x", (keep_up,), 0.1
        )
        arrived_down = over_z_low(send)

        def columns(ins, outs):
            total = ins[0][...] + ins[1][...].astype(F32)
            outs[0][...] = total[1].astype(BF16)
            outs[1][...] = total[0]
            total = ins[2][...] + ins[3][...].astype(F32)
            outs[2][0], outs[2][1] = total[0, 1].astype(BF16), total[1, 1].astype(BF16)
            outs[3][...] = total[:, 0]
            total = ins[4][...] + ins[5][...].astype(F32)
            outs[2][2] = total[1].astype(BF16)
            outs[4][...] = total[0]

        ((send, keep_qkv_out),) = add_step(
            [(cut(keep_qkv_out, 2, 4), cut(arrived_qkv_out, 2, 4), 0)],
            "qkv_out_y",
            (keep_down,),
            0.1,
        )
        arrived_qkv_out = over_x(send)
        send_up, keep_up, send, keep_low, keep_down = step(
            columns,
            [keep_up, arrived_up, keep_low, arrived_low, keep_down, arrived_down],
            [
                *(sds((2, *piece), BF16), sds((2, *piece), F32)),
                *(sds((3, *piece), BF16), sds((2, *piece), F32)),
                sds(piece, F32),
            ],
            "columns",
            (keep_qkv_out,),
        )
        arrived_up, arrived = over_y(send_up), over_z_high(send)

        def planes(ins, outs):
            keep_up, arrived_up, keep_low, arrived, keep_down, keep_qkv_out, arrived_qkv_out = ins
            total = keep_up[...] + arrived_up[...].astype(F32)
            outs[0][0] = total[1].astype(BF16)
            outs[1][0] = total[0]
            outs[0][1] = (keep_down[...] + arrived[2].astype(F32)).astype(BF16)
            outs[2][...] = (keep_low[1] + arrived[1].astype(F32)).astype(BF16)
            outs[1][1] = keep_low[0] + arrived[0].astype(F32)
            total = keep_qkv_out[...] + arrived_qkv_out[...].astype(F32)
            outs[3][...] = total[1].astype(BF16)
            outs[4][...] = total[0]

        send, keep, send_low, send_qkv_out, keep_qkv_out = step(
            planes,
            [
                *(keep_up, arrived_up, keep_low, arrived, keep_down),
                *(cut(keep_qkv_out, 2, 2), cut(arrived_qkv_out, 2, 2)),
            ],
            [
                *(sds((2, *piece), BF16), sds((2, *piece), F32), sds(piece, BF16)),
                *(sds((2, *taller), BF16), sds((2, *taller), F32)),
            ],
            "planes",
        )
        arrived, arrived_low = over_z_high(send), over_y(send_low)
        arrived_qkv_out = over_z_low(send_qkv_out)

        def lines(ins, outs):
            send, keep, arrived, arrived_low, keep_qkv_out, arrived_qkv_out = ins
            total = keep_qkv_out[...] + arrived_qkv_out[...].astype(F32)
            outs[0][0] = total[1].astype(BF16)
            outs[1][...] = total[0]
            for part, came in enumerate((arrived[0], arrived_low[...])):
                total = keep[part] + came.astype(F32)
                total = jnp.concatenate([total, jnp.zeros((8, CUT_COLUMNS), F32)], axis=0)
                outs[0][part + 1] = total.astype(BF16)
            outs[2][0], outs[2][1] = send[1], arrived[1]

        pieces, keep_qkv_out, near_down = step(
            lines,
            [send, keep, arrived, arrived_low, keep_qkv_out, arrived_qkv_out],
            [sds((3, *taller), BF16), sds(taller, F32), sds((2, *piece), BF16)],
            "lines",
            (w_gate_up, first_gate_up, second_gate_up),
        )
        arrived, down_low = over_z_high(pieces), over_z_low(near_down)

        def share_high(ins, outs):
            pieces, arrived, keep_qkv_out, near_down, down_low = ins
            for high in range(2):
                outs[0][0, high], outs[0][1, high] = near_down[high], down_low[high]
            outs[0][2, 0], outs[0][2, 1] = pieces[1, :CUT_ROWS], arrived[1, :CUT_ROWS]
            outs[1][0], outs[1][1] = pieces[2, :CUT_ROWS], arrived[2, :CUT_ROWS]
            outs[2][...] = (keep_qkv_out[...] + arrived[0].astype(F32)).astype(BF16)

        near_x, near_low, piece_qkv_out = step(
            share_high,
            [pieces, arrived, keep_qkv_out, near_down, down_low],
            [sds((3, 2, *piece), BF16), sds((2, *piece), BF16), sds(taller, BF16)],
            "share_high",
            (
                *(w_qkv, w_out, first_qkv, first_out, second_qkv, second_out),
                *(down_t, first_down_t, second_down_t, first_gains, second_gains),
            ),
        )
        arrived_x, low_low = over_x(near_x), over_z_low(near_low)
        qkv_out_high = over_z_high(piece_qkv_out)
        output, token_grad = finish_tokens(middle, hidden, down_whole, *finish, (near_x,))

        def share_next(ins, outs):
            near_x, arrived_x, near_low, low_low = ins
            outs[0][0], outs[0][1] = near_x[2], arrived_x[2]
            outs[1][0], outs[1][1] = near_low[...], low_low[...]
            for low in range(2):
                for high in range(2):
                    outs[2][0, 0, low * 2 + high] = near_x[low, high]
                    outs[2][0, 1, low * 2 + high] = arrived_x[low, high]

        near_up, near_low, near_down = step(
            share_next,
            [near_x, arrived_x, near_low, low_low],
            [
                *(sds((2, 2, *piece), BF16), sds((2, 2, *piece), BF16)),
                sds((1, 2, 4, *piece), BF16),
            ],
            "share_next",
            (qkv_out_high,),
        )
        far_down = over_core(near_down)
        up_low, low_x = over_z_low(near_up), over_x(near_low)

        def share_qkv_out_high(ins, outs):
            outs[0][0], outs[0][1] = ins[0][...], ins[1][...]

        (near_qkv_out,) = step(
            share_qkv_out_high,
            [piece_qkv_out, qkv_out_high],
            [sds((2, *taller), BF16)],
            "share_qkv_out_high",
            (near_up,),
        )
        qkv_out_x, qkv_out_low = over_x(near_qkv_out), over_z_low(near_qkv_out)
        qkv_out_both = swap(near_qkv_out, "dp", 6)
        one_down, two_down, next_down, mark = update_rows(
            idx,
            [(0, near_down), (1, far_down)],
            lambda p, x, z: (
                (x * 2 + (z >> 1)) * CUT_ROWS,
                [(0, CUT_COLUMNS, (z & 1) * CUT_COLUMNS)],
            ),
            2 * HALF,
            96,
            [down_t, first_down_t, second_down_t],
            (),
            (),
            "update_down",
            (near_qkv_out,),
            0.1,
        )

        def share_gate_up(ins, outs):
            for near in range(2):
                for far in range(2):
                    for high in range(2):
                        outs[0][0, near, far * 2 + high] = ins[far][near, high]
                        outs[0][1, far, near * 2 + high] = ins[2 + far][near, high]

        (near_gate_up,) = step(
            share_gate_up,
            [near_up, up_low, near_low, low_x],
            [sds((2, 2, 4, *piece), BF16)],
            "share_gate_up",
            (mark,),
        )
        far_gate_up = over_core(near_gate_up)
        place_gate_up = lambda p, x, z: (p * CUT_ROWS, [(0, CUT_COLUMNS, (x * 4 + z) * CUT_COLUMNS)])
        state_gate_up = [w_gate_up, first_gate_up, second_gate_up]
        *near_state, mark = update_rows(
            idx,
            [(0, near_gate_up)],
            place_gate_up,
            HALF,
            24,
            state_gate_up,
            (),
            (),
            "update_gate_up_near",
            (),
        )

        def share_qkv_out(ins, outs):
            for x in range(2):
                for low in range(2):
                    for high in range(2):
                        outs[0][0, x, low * 2 + high] = ins[low * 2 + x][high]

        (near_qkv_out,) = step(
            share_qkv_out,
            [near_qkv_out, qkv_out_x, qkv_out_low, qkv_out_both],
            [sds((1, 2, 4, *taller), BF16)],
            "share_qkv_out",
            (mark,),
        )
        far_qkv_out = over_core(near_qkv_out)
        one_gate_up, two_gate_up, next_gate_up, mark = update_rows(
            idx,
            [(1, far_gate_up)],
            place_gate_up,
            HALF,
            24,
            state_gate_up,
            near_state,
            (),
            "update_gate_up_far",
            (near_qkv_out,),
        )
        cuts = [[(0, 384, 0)], [(0, 384, 384)], [(0, 192, 768), (192, 192, 1024)], [(0, 384, 1216)]]
        updated = update_rows(
            idx,
            [(0, near_qkv_out), (1, far_qkv_out)],
            lambda p, x, z: (x * CUT_ROWS, cuts[z]),
            HALF,
            48,
            [w_qkv, w_out, first_qkv, first_out, second_qkv, second_out],
            (),
            (norm_gains, first_gains, second_gains),
            "update_qkv_out",
            (mark,),
        )
        one_qkv, one_out, two_qkv, two_out, next_qkv, next_out = updated[:6]
        one_gains, two_gains, next_gains = updated[6:9]
    else:
        sums = lax.psum((*grad_qkv_out, grad_gate_up[0], grad_down[0].T), ("dp", "shard"))
        grad_qkv_out, grad_gains, grad_gate_up, grad_down = sums

        def own(grad, axis=0):
            size = grad.shape[axis] // groups
            return lax.dynamic_slice_in_dim(grad, owner * size, size, axis)

        one_qkv, two_qkv, next_qkv = adamw(
            w_qkv, first_qkv, second_qkv, own(grad_qkv_out[:, :QKV]), RATE_MATRIX, DECAY_MATRIX
        )
        one_out, two_out, next_out = adamw(
            w_out, first_out, second_out, own(grad_qkv_out[:, QKV:]), RATE_MATRIX, DECAY_MATRIX
        )
        one_gate_up, two_gate_up, next_gate_up = adamw(
            w_gate_up, first_gate_up, second_gate_up, own(grad_gate_up), RATE_MATRIX, DECAY_MATRIX
        )
        one_down, two_down, next_down = [
            a.T
            for a in adamw(
                w_down, first_down, second_down, own(grad_down), RATE_MATRIX, DECAY_MATRIX
            )
        ]
        one_gains, two_gains, next_gains = adamw(
            norm_gains, first_gains, second_gains, own(grad_gains, 1), RATE_GAIN, 0.0
        )
    one_down, two_down, next_down = one_down.T, two_down.T, next_down.T
    return (
        output.T[None],
        token_grad.T[None],
        one_qkv,
        one_out,
        one_gate_up,
        one_down,
        one_gains,
        two_qkv,
        two_out,
        two_gate_up,
        two_down,
        two_gains,
        next_qkv,
        next_out,
        next_gate_up,
        next_down,
        next_gains,
    )


def solution(mesh):
    return jax.shard_map(
        per_device,
        mesh=mesh,
        in_specs=(
            P(("dp", "shard"), None, None),
            P(("dp", "shard"), None),
            P(("dp", "shard"), None, None),
            P("shard", None),
            P("shard", None),
            P("shard", None),
            P("shard", None),
            P(None, "shard"),
            P("shard", None),
            P("shard", None),
            P("shard", None),
            P("shard", None),
            P(None, "shard"),
            P("shard", None),
            P("shard", None),
            P("shard", None),
            P("shard", None),
            P(None, "shard"),
        ),
        out_specs=(
            P(("dp", "shard"), None, None),
            P(("dp", "shard"), None, None),
            P("shard", None),
            P("shard", None),
            P("shard", None),
            P("shard", None),
            P(None, "shard"),
            P("shard", None),
            P("shard", None),
            P("shard", None),
            P("shard", None),
            P(None, "shard"),
            P("shard", None),
            P("shard", None),
            P("shard", None),
            P("shard", None),
            P(None, "shard"),
        ),
        check_vma=False,
    )
```
